32 devices in a mesh: grp: 2 (over core), dp: 16 (over z, y, x).
Axes of the slice: x: 2, y: 2, z: 4, core: 2. Of those that a mesh axis runs over, the one named last changes fastest.
Arguments:
- tokens: bfloat16 [4096, 2048], P(('grp', 'dp')), may hold values from -6 to 6
- segments: int32 [4096], P('grp'), may hold values from 0 to 66, as said below
- routes: int32 [4096, 8], P(('grp', 'dp')), may hold values from 0 to 15, all different within a row; in each aligned block of 128 rows (0 to 127, 128 to 255, ...) at most 80 rows name the same one
- route_weight: float32 [4096, 8], P(('grp', 'dp')), may hold values from 0.06 to 0.19
- capacity: int32 [1], replicated, may hold values from 768 to 1279
- norm_gain: float32 [2, 2048], replicated, may hold values from 0.5 to 1.5
- qkv_weight: bfloat16 [6144, 2048], P('dp'), may hold values from -0.125 to 0.125
- out_weight: bfloat16 [2048, 2048], P('dp'), may hold values from -1 to 1
- gate_weight: bfloat16 [16, 2048, 1024], P('dp'), may hold values from -0.125 to 0.125
- up_weight: bfloat16 [16, 2048, 1024], P('dp'), may hold values from -0.125 to 0.125
- down_weight: bfloat16 [16, 1024, 2048], P('dp'), may hold values from -0.75 to 0.75
- cotangent: bfloat16 [4096, 2048], P(('grp', 'dp')), may hold values from -6 to 6
Outputs:
- layer_out: bfloat16 [4096, 2048], P(('grp', 'dp'))
- tokens_grad: float32 [4096, 2048], P(('grp', 'dp'))
- qkv_weight_grad: float32 [6144, 2048], P('dp')
- out_weight_grad: float32 [2048, 2048], P('dp')
- gate_weight_grad: float32 [16, 2048, 1024], P('dp')
- up_weight_grad: float32 [16, 2048, 1024], P('dp')
- down_weight_grad: float32 [16, 1024, 2048], P('dp')
- norm_gain_grad: float32 [2, 2048], replicated
- stats: float32 [2, 3], P('grp')
The draws below stay inside these ranges and needn't reach their ends.
Inputs may be any that keep to these rules, and one draw needn't show every extreme that they name: `segments`: in each sequence of 2048 tokens, numbers never fall except to 0, which marks the padding that ends the sequence; one document covers all but at most 64 tokens at each end. `routes`: A token names 8 different experts; among the 128 tokens of one device no expert is named more than 80 times.
All inputs are finite; a program needn't handle non-finite values.
Results may differ from the reference program's by a relative error of at most 0.023.
Values may be sent and summed in bfloat16 or wider, within the bound.
A program may use at most 384 MiB of HBM per device.

```python
import math
import jax
import jax.numpy as jnp
import numpy as np
from jax import lax

D = 2048
H = 16
HD = 128
FF = 1024
TOPK = 8
TOK_DEV = 128
EXPERTS = 16
SEQ_LEN = 2048
TOKENS = 4096
MOST = 80
N_DP = 16


def draw_segments(key, part):
    key = jax.random.fold_in(key, 11)
    groups = TOKENS // SEQ_LEN
    quarter = TOK_DEV // 4
    top_number = TOK_DEV // 2 + 2

    def one_sequence(seq_key):
        key_pad, key_start, key_stop, key_flags = jax.random.split(seq_key, 4)
        padding = jax.random.randint(key_pad, (), 1, quarter + 1)
        start_at = jax.random.randint(key_start, (), 1, quarter + 1)
        stop_at = SEQ_LEN - padding - jax.random.randint(key_stop, (), 0, quarter)
        position = jnp.arange(SEQ_LEN, dtype=jnp.int32)
        flags = (jax.random.randint(key_flags, (SEQ_LEN,), 0, 6) == 0).astype(jnp.int32)
        inside = (position > start_at) & (position < stop_at)
        flags = jnp.where(inside, 0, flags)
        flags = jnp.where((position == 0) | (position == start_at) | (position == stop_at), 1, flags)
        live = position < SEQ_LEN - padding
        flags = jnp.where(live, flags, 0)
        numbers = jnp.cumsum(flags).astype(jnp.int32)
        last_number = jnp.sum(flags).astype(jnp.int32)
        numbers = numbers + (top_number - last_number)
        return jnp.where(live, numbers, 0).astype(jnp.int32)
    return jax.vmap(one_sequence)(jax.random.split(key, groups)).reshape(TOKENS)


def block_levels(rng, extent, cuts, low, largest):
    level, own = 1.0, jax.random.fold_in(rng, 6)
    for dim, blocks in cuts:
        draws = jnp.exp(jax.random.uniform(jax.random.fold_in(own, dim), (blocks,), jnp.float32, low / len(cuts), largest / len(cuts)))
        level = level * jnp.repeat(draws, extent[dim] // blocks).reshape([-1 if axis == dim else 1 for axis in range(len(extent))])
    return level


def deal_out(stream_key, own, number, rows, count, top, bound, lean):
    sequence = jax.random.permutation(stream_key, count)
    packed, common = load_shares(count, rows * top, bound, lean, True), load_shares(count, rows * top, bound, lean, False)
    places = jnp.arange(count)

    def named(sizes, rotation):
        used = int((sizes > 0).sum())
        fixed = max(1, used // 4)
        shifted = fixed + (places - fixed + rotation * (used - fixed)) % max(1, count - fixed)
        return jnp.zeros((count,), jnp.int32).at[sequence[jnp.where(places < fixed, places, shifted)]].set(jnp.asarray(sizes, jnp.int32))

    sizes = jnp.where(number % 4 == 0, named(packed, number // 4), named(common, number - number // 4 - 1))
    mixed = jax.random.permutation(jax.random.fold_in(own, 3), count)
    giver, taker = mixed[0:count // 2 * 2:2], mixed[1:count // 2 * 2:2]
    margin = jnp.minimum(sizes[giver] - 1, bound - sizes[taker]) // 2
    margin = jnp.where((giver == sequence[0]) | (taker == sequence[0]) | (sizes[taker] == 0), 0, jnp.maximum(margin, 0))
    shifted = jax.random.randint(jax.random.fold_in(own, 4), (count // 2,), 0, 1 << 20) % (margin + 1)
    sizes = sizes.at[giver].add(-shifted).at[taker].add(shifted)
    labels = jnp.searchsorted(jnp.cumsum(sizes), jnp.arange(rows * top), side="right").astype(jnp.int32)
    table = labels.reshape(top, rows).T
    table = table[jax.random.permutation(jax.random.fold_in(own, 1), rows)]
    rotation = jax.random.randint(jax.random.fold_in(own, 2), (rows, 1), 0, top)
    return jnp.take_along_axis(table, (jnp.arange(top)[None, :] + rotation) % top, axis=1)


def load_shares(number_of, total, limit, lean, full):
    loads = [(1 << 20) // math.isqrt(standing ** lean) + 1 for standing in range(1, number_of + 1)]
    largest = limit if full else min(limit, max(-(-total // number_of), total * loads[0] // sum(loads)))
    least = 1 if total - largest >= number_of - 1 else 0
    given, rest = [largest] + [least] * (number_of - 1), total - largest - least * (number_of - 1)
    while rest > 0:
        candidates = [i for i in range(1, number_of) if given[i] < largest] or [i for i in range(1, number_of) if given[i] < limit]
        whole, left = sum([loads[i] for i in candidates]), rest
        for i in candidates:
            more = min(limit - given[i], max(1, left * loads[i] // whole), rest)
            given[i] = given[i] + more
            rest = rest - more
    return np.array(given)


def noise(stream_key, dims, deviation, most, pieces=(), kind=jnp.bfloat16):
    factor_of = block_levels(stream_key, dims, pieces, -0.22, 0.18) if pieces else 1.0
    values = jax.random.normal(stream_key, dims, jnp.float32) * deviation * factor_of
    return jnp.minimum(jnp.maximum(values, -most), most).astype(kind)


def setup_inputs(seed: int = 0) -> dict:
    key_of = jax.random.split(jax.random.key(seed), 13)
    tokens = noise(key_of[0], (TOKENS, D), 1.0, 6.0, ((0, 32),))
    segments = draw_segments(jax.random.fold_in(key_of[12], 71), 0)
    routes_keys = jax.random.split(jax.random.fold_in(key_of[2], 1), TOKENS // TOK_DEV)
    routes_turns = jax.random.permutation(jax.random.fold_in(key_of[2], 3), TOKENS // TOK_DEV)
    routes = jax.vmap(lambda own, number: deal_out(jax.random.fold_in(key_of[2], 2), own, number, TOK_DEV, EXPERTS, TOPK, MOST, 2))(routes_keys, routes_turns).reshape((TOKENS, TOPK))
    route_weight = jnp.clip(0.06 + 0.13 * jax.random.uniform(key_of[3], (TOKENS, TOPK), jnp.float32) ** block_levels(key_of[3], (TOKENS, TOPK), ((0, 32),), -0.2, 0.2), 0.06, 0.19)
    capacity = jax.random.randint(key_of[4], (1,), SEQ_LEN * TOPK // EXPERTS * 3 // 4, SEQ_LEN * TOPK // EXPERTS * 5 // 4).astype(jnp.int32)
    norm_gain = jnp.clip(1.0 + 0.1 * jax.random.normal(key_of[5], (2, D), jnp.float32), 0.5, 1.5)
    qkv_weight = noise(key_of[6], (3 * D, D), D ** -0.5, 0.125, ((0, 16),))
    out_weight = noise(key_of[7], (D, D), (D // 64) ** -0.5, 1.0, ((0, 16),))
    gate_weight = noise(key_of[8], (EXPERTS, D, FF), D ** -0.5, 0.125, ((0, 16),))
    up_weight = noise(key_of[9], (EXPERTS, D, FF), D ** -0.5, 0.125, ((0, 16),))
    down_weight = noise(key_of[10], (EXPERTS, FF, D), (FF // 16) ** -0.5, 0.75, ((0, 16),))
    cotangent = noise(key_of[11], (TOKENS, D), 1.0, 6.0, ((0, 32),))
    return dict(tokens=tokens, segments=segments, routes=routes, route_weight=route_weight, capacity=capacity, norm_gain=norm_gain, qkv_weight=qkv_weight, out_weight=out_weight, gate_weight=gate_weight, up_weight=up_weight, down_weight=down_weight, cotangent=cotangent)


@jax.custom_vjp
def low(v):
    return lax.optimization_barrier(v.astype(jnp.bfloat16)).astype(jnp.float32)

@jax.custom_vjp
def low_back(v):
    return v

def low_keep(v):
    return (low(v), None)

def low_pass(kept, grad):
    return (grad,)

def back_keep(v):
    return (v, None)

def back_low(kept, grad):
    return (low(grad),)
low.defvjp(low_keep, low_pass)
low_back.defvjp(back_keep, back_low)
HIGH = lax.Precision.HIGHEST
EPS = 1e-06
THETA = 50000.0

def rmsnorm(field, gain_row):
    return field * lax.rsqrt(lax.optimization_barrier(jnp.mean(field * field, -1, keepdims=True)) + EPS) * gain_row

def rotary_tables(length):
    position = jnp.arange(length).astype(jnp.float32)
    freq = THETA ** (-(jnp.arange(HD // 2).astype(jnp.float32) * 2.0 / HD))
    angle = position[:, None] * freq[None, :]
    return (jnp.cos(angle)[:, None, :], jnp.sin(angle)[:, None, :])

def rotate(heads_in, cos_table, sin_table):
    half_size = heads_in.shape[-1] // 2
    first = heads_in[..., :half_size]
    second = heads_in[..., half_size:]
    return jnp.concatenate([first * cos_table - second * sin_table, second * cos_table + first * sin_table], -1)

def attend(queries, keys, values, seg):
    block_rows = min(512, SEQ_LEN)
    blocks = SEQ_LEN // block_rows
    scale_factor = HD ** (-0.5)

    def one_block(block_data):
        query_block, seg_block = block_data
        scores = jnp.einsum('qhd,khd->hqk', query_block, keys, precision=HIGH) * scale_factor
        scores = low_back(scores)
        allowed = (seg_block[:, None] == seg[None, :]) & (seg[None, :] != 0)
        masked = jnp.where(allowed[None], scores, -1e+30)
        peak = lax.optimization_barrier(jnp.max(masked, -1, keepdims=True))
        expo = jnp.where(allowed[None], jnp.exp(masked - peak), 0.0)
        row_total = lax.optimization_barrier(jnp.sum(expo, -1, keepdims=True))
        attn_prob = expo / jnp.maximum(row_total, 1.0)
        return jnp.einsum('hqk,khd->qhd', low(attn_prob), values, precision=HIGH)
    outs = lax.map(jax.checkpoint(one_block), (queries.reshape(blocks, block_rows, H, HD), seg.reshape(blocks, block_rows)))
    return outs.reshape(SEQ_LEN, H * HD)

def expert_mix(normed2, routes, route_weight, capacity, gate_w, up_w, down_w):
    pair_count = SEQ_LEN * TOPK
    buffer_rows = min(N_DP * MOST, SEQ_LEN * TOPK // EXPERTS * 5 // 4)
    flat_routes = routes.reshape(-1).astype(jnp.int32)
    one_hot = (flat_routes[:, None] == jnp.arange(EXPERTS, dtype=jnp.int32)[None, :]).astype(jnp.int32)
    running = jnp.cumsum(one_hot, 0).astype(jnp.int32) - one_hot
    rank_of = lax.optimization_barrier(jnp.sum(running * one_hot, 1)).astype(jnp.int32)
    keep_mask = rank_of < capacity[0]
    slot_index = (flat_routes * buffer_rows + rank_of).astype(jnp.int32)
    order = jnp.arange(pair_count, dtype=jnp.int32)
    target = jnp.where(keep_mask, slot_index, EXPERTS * buffer_rows).astype(jnp.int32)
    slot_table = jnp.full((EXPERTS * buffer_rows,), pair_count, jnp.int32).at[target].set(order, mode='drop')
    live_slot = slot_table < pair_count
    token_of = (jnp.minimum(slot_table, pair_count - 1) // TOPK).astype(jnp.int32)
    expert_rows = jnp.where(live_slot[:, None], normed2[token_of], 0.0).reshape(EXPERTS, buffer_rows, D)
    expert_rows = low_back(expert_rows)
    gate_act = low_back(jnp.einsum('erd,edf->erf', expert_rows, gate_w, precision=HIGH))
    up_act = low_back(jnp.einsum('erd,edf->erf', expert_rows, up_w, precision=HIGH))
    hidden = low(jax.nn.silu(gate_act) * up_act)
    expert_out = low(low_back(jnp.einsum('erf,efd->erd', hidden, down_w, precision=HIGH)))
    picked = expert_out.reshape(EXPERTS * buffer_rows, D)[jnp.where(keep_mask, slot_index, 0).astype(jnp.int32)]
    route_coef = jnp.where(keep_mask, route_weight.reshape(-1), 0.0)
    return lax.optimization_barrier(jnp.sum((route_coef[:, None] * picked).reshape(SEQ_LEN, TOPK, D), 1))

def layer_forward(stream, seg, routes, route_weight, capacity, gains, qkv_w, out_w, gate_w, up_w, down_w):
    cos_table, sin_table = rotary_tables(SEQ_LEN)
    normed = low(rmsnorm(stream, gains[0]))
    projected = jnp.dot(normed, qkv_w.T, precision=HIGH)
    queries = low(rotate(low_back(projected[:, :D]).reshape(SEQ_LEN, H, HD), cos_table, sin_table))
    keys = low(rotate(low_back(projected[:, D:2 * D]).reshape(SEQ_LEN, H, HD), cos_table, sin_table))
    values = low(low_back(projected[:, 2 * D:])).reshape(SEQ_LEN, H, HD)
    context = low(low_back(attend(queries, keys, values, seg)))
    attended = low_back(jnp.dot(context, out_w.T, precision=HIGH))
    middle = stream + attended
    normed2 = low(rmsnorm(middle, gains[1]))
    mixture = expert_mix(normed2, routes, route_weight, capacity, gate_w, up_w, down_w)
    layer_sum = middle + mixture
    valid_rows = (seg != 0).astype(jnp.float32)
    stat_sums = jnp.stack([jnp.sum(valid_rows * lax.optimization_barrier(jnp.sum(layer_sum * layer_sum, -1))), jnp.sum(valid_rows * lax.optimization_barrier(jnp.sum(attended * attended, -1))), jnp.sum(valid_rows * lax.optimization_barrier(jnp.sum(mixture * mixture, -1))), jnp.sum(valid_rows) * D])
    return (layer_sum, stat_sums)

def reference(tokens, segments, routes, route_weight, capacity, norm_gain, qkv_weight, out_weight, gate_weight, up_weight, down_weight, cotangent):
    groups = TOKENS // SEQ_LEN
    weights_f = tuple((w.astype(jnp.float32) for w in (qkv_weight, out_weight, gate_weight, up_weight, down_weight)))
    gains = norm_gain.astype(jnp.float32)
    group_inputs = (tokens.reshape(groups, SEQ_LEN, D), segments.reshape(groups, SEQ_LEN), routes.reshape(groups, SEQ_LEN, TOPK), route_weight.reshape(groups, SEQ_LEN, TOPK), cotangent.reshape(groups, SEQ_LEN, D))

    def per_group(totals_in, group_data):
        stream_in, seg, group_routes, group_weight, group_cot = group_data

        def forward(stream, gain_pair, qkv_w, out_w, gate_w, up_w, down_w):
            return layer_forward(stream, seg, group_routes, group_weight, capacity, gain_pair, qkv_w, out_w, gate_w, up_w, down_w)
        layer_sum, pullback, stat_sums = jax.vjp(forward, stream_in.astype(jnp.float32), gains, *weights_f, has_aux=True)
        gradients = pullback(group_cot.astype(jnp.float32))
        totals_out = tuple((a + b for a, b in zip(totals_in, gradients[1:])))
        stat_row = jnp.sqrt(stat_sums[:3] / stat_sums[3])
        return (totals_out, (layer_sum.astype(jnp.bfloat16), gradients[0], stat_row))
    zero_grads = tuple((jnp.zeros(w.shape, jnp.float32) for w in (gains,) + weights_f))
    totals, (outs, input_grads, stat_rows) = lax.scan(per_group, zero_grads, group_inputs)
    return (outs.reshape(TOKENS, D), input_grads.reshape(TOKENS, D), totals[1], totals[2], totals[3], totals[4], totals[5], totals[0], stat_rows)
```

```python
import functools

import jax
import jax.numpy as jnp
import numpy as np
from jax import lax
from jax.experimental import pallas as pl
from jax.experimental.pallas import tpu as pltpu
from jax.sharding import PartitionSpec as P

H = 16
HD = 128
TOPK = 8
EPS = 1e-06
THETA = 50000.0
MESH = pl.DeviceIdType.MESH
MIB = 2**20
BF = jnp.bfloat16
F32 = jnp.float32
SCALE = HD**-0.5
LOG2E = 1.4426950408889634


def places():
    me = lax.axis_index("dp")
    z, y, x = me // 4, (me // 2) % 2, me % 2
    xor = [z, z + 1 - 2 * (z % 2), (z + 2) % 4, 3 - z]
    at = lambda k, yy, xx: xor[k] * 4 + yy * 2 + xx
    return dict(
        me=me,
        col=[at(k, y, x) for k in range(4)],
        X=[at(k, y, 1 - x) for k in range(4)],
        Y=[at(k, 1 - y, x) for k in range(4)],
        D=[at(k, 1 - y, 1 - x) for k in range(4)],
    )


def barrier(targets, pair=False):
    sem = pltpu.get_barrier_semaphore()
    for t in targets:
        pl.semaphore_signal(sem, inc=1, device_id={"dp": t}, device_id_type=MESH)
    count = len(targets)
    if pair:
        pl.semaphore_signal(sem, inc=1, device_id={"grp": partner()}, device_id_type=MESH)
        count += 1
    pl.semaphore_wait(sem, count)


def partner():
    g = lax.axis_index("grp")
    return g + 1 - 2 * (g % 2)


def push(src, dst, send, recv, to):
    c = pltpu.make_async_remote_copy(
        src_ref=src, dst_ref=dst, send_sem=send, recv_sem=recv,
        device_id={"dp": to}, device_id_type=MESH,
    )
    c.start()
    return c


def push_pair(src, dst, send, recv):
    c = pltpu.make_async_remote_copy(
        src_ref=src, dst_ref=dst, send_sem=send, recv_sem=recv,
        device_id={"grp": partner()}, device_id_type=MESH,
    )
    c.start()
    return c


GATHER_SEMS = [pltpu.SemaphoreType.DMA((4,))] * 6 + [pltpu.SemaphoreType.DMA((4, 2))] * 2 + [pltpu.SemaphoreType.DMA]


def gather_steps(src, dst, rows, sems):
    zs, zr, xs, xr, ys, yr, ds, dr, own = sems
    p = places()
    half = rows // 2
    blk = lambda b: dst.at[pl.ds(pl.multiple_of(b * rows, rows), rows)]
    part = lambda b, h: dst.at[pl.ds(pl.multiple_of(b * rows + h * half, half), half)]
    me, xn, yn = p["me"], p["X"][0], p["Y"][0]
    mine = pltpu.make_async_copy(src, blk(me), own)
    mine.start()
    xc = [push(src, blk(me), xs.at[0], xr.at[0], xn)]
    yc = [push(src, blk(me), ys.at[0], yr.at[0], yn)]
    zc = [push(src, blk(me), zs.at[k], zr.at[k], p["col"][k]) for k in (1, 2, 3)]
    dc = []
    mine.wait()
    yield
    for k in range(4):
        if k < 3:
            zc[k].wait_recv()
            b = p["col"][k + 1]
            xc.append(push(blk(b), blk(b), xs.at[k + 1], xr.at[k + 1], xn))
            yc.append(push(blk(b), blk(b), ys.at[k + 1], yr.at[k + 1], yn))
        xc[k].wait_recv()
        dc.append(push(part(p["X"][k], 0), part(p["X"][k], 0), ds.at[k, 0], dr.at[k, 0], yn))
        yc[k].wait_recv()
        dc.append(push(part(p["Y"][k], 1), part(p["Y"][k], 1), ds.at[k, 1], dr.at[k, 1], xn))
        yield
    for c in dc:
        c.wait_recv()
    for c in xc + yc + zc + dc:
        c.wait_send()


def gather_targets():
    p = places()
    return [p["col"][1], p["col"][2], p["col"][3], p["X"][0], p["Y"][0]]


def run(*steps):
    live = list(steps)
    while live:
        for s in list(live):
            try:
                next(s)
            except StopIteration:
                live.remove(s)


SCATTER_SEMS = [pltpu.SemaphoreType.DMA((4, 2))] * 2 + [pltpu.SemaphoreType.DMA((4,))] * 6


def scatter_bufs(rows, width):
    return [
        pltpu.VMEM((8, rows // 2, width), BF),
        pltpu.VMEM((4, rows, width), BF),
        pltpu.VMEM((4, rows, width), BF),
        pltpu.VMEM((4, rows, width), BF),
    ]


def scatter_sum(part, out, rows, bufs, sems):
    rd, rx, ry, rz = bufs
    ds, dr, xs, xr, ys, yr, zs, zr = sems
    p = places()
    half = rows // 2
    xn, yn = p["X"][0], p["Y"][0]
    order = (1, 2, 3, 0)
    sent = []
    da, db, xc, yc, zc = {}, {}, {}, {}, {}
    for k in order:
        b = p["D"][k]
        da[k] = push(part.at[b, pl.ds(0, half)], rd.at[2 * k], ds.at[k, 0], dr.at[k, 0], yn)
        db[k] = push(part.at[b, pl.ds(half, half)], rd.at[2 * k + 1], ds.at[k, 1], dr.at[k, 1], xn)
    for k in order:
        b = p["X"][k]
        da[k].wait_recv()
        part[b, pl.ds(0, half)] = (part[b, pl.ds(0, half)].astype(F32) + rd[2 * k].astype(F32)).astype(BF)
        xc[k] = push(part.at[b], rx.at[k], xs.at[k], xr.at[k], xn)
        b = p["Y"][k]
        db[k].wait_recv()
        part[b, pl.ds(half, half)] = (part[b, pl.ds(half, half)].astype(F32) + rd[2 * k + 1].astype(F32)).astype(BF)
        yc[k] = push(part.at[b], ry.at[k], ys.at[k], yr.at[k], yn)
    for k in order:
        b = p["col"][k]
        xc[k].wait_recv()
        yc[k].wait_recv()
        total = part[b].astype(F32) + rx[k].astype(F32) + ry[k].astype(F32)
        if k:
            part[b] = total.astype(BF)
            zc[k] = push(part.at[b], rz.at[k], zs.at[k], zr.at[k], b)
        else:
            out[...] = total
    for k in (1, 2, 3):
        zc[k].wait_recv()
        out[...] += rz[k].astype(F32)
    for group in (da, db, xc, yc, zc):
        for c in group.values():
            c.wait_send()


ANY = pl.BlockSpec(memory_space=pl.ANY)
VM = pl.BlockSpec(memory_space=pltpu.VMEM)


def params(cid, vmem=60):
    return pltpu.CompilerParams(collective_id=cid, has_side_effects=True, vmem_limit_bytes=vmem * MIB)


def front_kernel(n_ref, m_ref, w_ref, nall, mall, wh, *sems):
    g_sems, (ms, mr, mo, ws, wr, ps, pr, wo) = sems[:9], sems[9:]
    me = lax.axis_index("dp")
    core = lax.axis_index("grp") % 2
    barrier([lax.rem(me + d, 16) for d in range(1, 16)], pair=True)
    hr = HD // 2
    g = gather_steps(n_ref, nall, n_ref.shape[0], g_sems)
    next(g)
    own = pltpu.make_async_copy(m_ref, mall.at[me], mo)
    own.start()
    mc = []
    for d in range(1, 16):
        to = lax.rem(me + d, 16)
        mc.append(push(m_ref, mall.at[me], ms.at[d], mr.at[d], to))
    off = core * hr
    for l in range(3):
        b = 3 * me + l
        to, slot = lax.rem(b, 16), b // 16
        src = w_ref.at[pl.ds(pl.multiple_of(l * HD + off, hr), hr)]
        dst = wh.at[pl.ds(pl.multiple_of(slot * HD + off, hr), hr)]

        @pl.when(to != me)
        def _():
            push(src, dst, ws.at[l], wr.at[slot], to)

        @pl.when(to == me)
        def _():
            pltpu.make_async_copy(src, dst, wr.at[slot]).start()

    for s in range(3):
        dst = wh.at[pl.ds(pl.multiple_of(s * HD + off, hr), hr)]
        pltpu.make_async_copy(dst, dst, wr.at[s]).wait()
        push_pair(dst, dst, ps.at[s], pr.at[s])
    for _ in g:
        pass
    own.wait()
    for c in mc:
        c.wait()
    for l in range(3):
        b = 3 * me + l
        src = w_ref.at[pl.ds(pl.multiple_of(l * HD + off, hr), hr)]

        @pl.when(lax.rem(b, 16) != me)
        def _():
            pltpu.make_async_copy(src, src, ws.at[l]).wait()

    for s in range(3):
        dst = wh.at[pl.ds(pl.multiple_of(s * HD + off, hr), hr)]
        other = wh.at[pl.ds(pl.multiple_of(s * HD + (hr - off), hr), hr)]
        pltpu.make_async_copy(dst, dst, ps.at[s]).wait()
        pltpu.make_async_copy(other, other, pr.at[s]).wait()


def front(normed, meta, w):
    rows, width = normed.shape
    return pl.pallas_call(
        front_kernel,
        out_shape=[
            jax.ShapeDtypeStruct((16 * rows, width), BF),
            jax.ShapeDtypeStruct((16,) + meta.shape, F32),
            jax.ShapeDtypeStruct((3 * HD, width), BF),
        ],
        in_specs=[ANY] * 3,
        out_specs=[ANY] * 3,
        scratch_shapes=GATHER_SEMS
        + [pltpu.SemaphoreType.DMA((16,)), pltpu.SemaphoreType.DMA((16,)), pltpu.SemaphoreType.DMA]
        + [pltpu.SemaphoreType.DMA((3,))] * 4
        + [pltpu.SemaphoreType.DMA],
        compiler_params=params(0),
        name="front",
    )(normed, meta, w)


def gather_kernel(x_ref, o_ref, *sems):
    barrier(gather_targets())
    run(gather_steps(x_ref, o_ref, x_ref.shape[0], sems))


def gather(x, cid):
    rows, width = x.shape
    return pl.pallas_call(
        gather_kernel,
        out_shape=jax.ShapeDtypeStruct((16 * rows, width), x.dtype),
        in_specs=[ANY],
        out_specs=ANY,
        scratch_shapes=GATHER_SEMS,
        compiler_params=params(cid),
        name=f"gather_{cid}",
    )(x)


def scatter_kernel(p_ref, o_ref, part, load, *rest):
    bufs, sems = rest[:4], rest[4:]
    c = pltpu.make_async_copy(p_ref, part, load)
    c.start()
    barrier(gather_targets())
    c.wait()
    scatter_sum(part, o_ref, part.shape[1], bufs, sems)


def scatter(x, cid):
    rows, width = x.shape[0] // 16, x.shape[1]
    return pl.pallas_call(
        scatter_kernel,
        out_shape=jax.ShapeDtypeStruct((rows, width), F32),
        in_specs=[ANY],
        out_specs=VM,
        scratch_shapes=[pltpu.VMEM((16, rows, width), BF), pltpu.SemaphoreType.DMA]
        + scatter_bufs(rows, width)
        + SCATTER_SEMS,
        compiler_params=params(cid),
        name=f"scatter_{cid}",
    )(x.reshape(16, rows, width))


def swap_kernel(x_ref, o_ref, ss, rs, lo):
    me = lax.axis_index("dp")
    barrier([lax.rem(me + d, 16) for d in range(1, 16)])
    own = pltpu.make_async_copy(x_ref.at[me], o_ref.at[me], lo)
    own.start()
    sent = []
    for d in range(1, 16):
        to = lax.rem(me + d, 16)
        sent.append(push(x_ref.at[to], o_ref.at[me], ss.at[d], rs.at[d], to))
    own.wait()
    for c in sent:
        c.wait()


def swap(x, cid):
    return pl.pallas_call(
        swap_kernel,
        out_shape=jax.ShapeDtypeStruct(x.shape, x.dtype),
        in_specs=[ANY],
        out_specs=ANY,
        scratch_shapes=[pltpu.SemaphoreType.DMA((16,))] * 2 + [pltpu.SemaphoreType.DMA],
        compiler_params=params(cid),
        name=f"swap_{cid}",
    )(x)


def return_kernel(x_ref, o_ref, ss, rs):
    me = lax.axis_index("dp")
    barrier([lax.rem(me + d, 16) for d in range(1, 16)])
    for s in range(3):
        b = 16 * s + me
        to, slot = b // 3, lax.rem(b, 3)

        @pl.when(to != me)
        def _():
            push(x_ref.at[s], o_ref.at[slot], ss.at[s], rs.at[slot], to)

        @pl.when(to == me)
        def _():
            pltpu.make_async_copy(x_ref.at[s], o_ref.at[slot], rs.at[slot]).start()

    for s in range(3):
        pltpu.make_async_copy(x_ref.at[s], o_ref.at[s], rs.at[s]).wait()

        @pl.when((16 * s + me) // 3 != me)
        def _():
            pltpu.make_async_copy(x_ref.at[s], o_ref.at[s], ss.at[s]).wait()


def give_back(x, cid):
    return pl.pallas_call(
        return_kernel,
        out_shape=jax.ShapeDtypeStruct(x.shape, x.dtype),
        in_specs=[ANY],
        out_specs=ANY,
        scratch_shapes=[pltpu.SemaphoreType.DMA((3,))] * 2,
        compiler_params=params(cid),
        name="give_back",
    )(x)


QB = 256


def attend_kernel(q, k, v, sq, sk, ctx, lse):
    s = lax.dot_general(q[...], k[...], (((1,), (1,)), ((), ())), preferred_element_type=F32)
    s = jnp.where(sq[...] == sk[...], s, -1e30)
    peak = jnp.maximum(jnp.max(s, -1, keepdims=True), -1e29)
    ex = jnp.exp2((s - peak) * (SCALE * LOG2E))
    total = jnp.maximum(jnp.sum(ex, -1, keepdims=True), 1.0)
    prob = (ex * (1.0 / total)).astype(BF)
    ctx[...] = jnp.dot(prob, v[...], preferred_element_type=F32).astype(BF)
    lse[...] = peak * (SCALE * LOG2E) + jnp.log2(total)


def attend(q, k, v, sq, sk):
    n = q.shape[0]
    row = lambda w: pl.BlockSpec((QB, w), lambda i: (i, 0))
    full = lambda r, w: pl.BlockSpec((r, w), lambda i: (0, 0))
    return pl.pallas_call(
        attend_kernel,
        grid=(n // QB,),
        out_shape=[jax.ShapeDtypeStruct((n, HD), BF), jax.ShapeDtypeStruct((n, 1), F32)],
        in_specs=[row(HD), full(n, HD), full(n, HD), row(1), full(1, n)],
        out_specs=[row(HD), row(1)],
        compiler_params=pltpu.CompilerParams(vmem_limit_bytes=48 * MIB),
        name="attend",
    )(q, k, v, sq, sk)


def attend_back_kernel(q, k, v, sq, sk, lse, dc, dq, dkt, dvt):
    @pl.when(pl.program_id(0) == 0)
    def _():
        dkt[...] = jnp.zeros_like(dkt)
        dvt[...] = jnp.zeros_like(dvt)

    s = lax.dot_general(q[...], k[...], (((1,), (1,)), ((), ())), preferred_element_type=F32)
    prob = jnp.where(sq[...] == sk[...], jnp.exp2(s * (SCALE * LOG2E) - lse[...]), 0.0)
    dp = lax.dot_general(dc[...], v[...], (((1,), (1,)), ((), ())), preferred_element_type=F32)
    delta = jnp.sum(prob * dp, -1, keepdims=True)
    ds = (prob * (dp - delta)).astype(BF)
    dq[...] = jnp.dot(ds, k[...], preferred_element_type=F32) * SCALE
    dkt[...] += lax.dot_general(q[...], ds, (((0,), (0,)), ((), ())), preferred_element_type=F32) * SCALE
    dvt[...] += lax.dot_general(dc[...], prob.astype(BF), (((0,), (0,)), ((), ())), preferred_element_type=F32)


def attend_back(q, k, v, sq, sk, lse, dc):
    n = q.shape[0]
    row = lambda w: pl.BlockSpec((QB, w), lambda i: (i, 0))
    full = lambda r, w: pl.BlockSpec((r, w), lambda i: (0, 0))
    return pl.pallas_call(
        attend_back_kernel,
        grid=(n // QB,),
        out_shape=[jax.ShapeDtypeStruct((n, HD), F32), jax.ShapeDtypeStruct((HD, n), F32), jax.ShapeDtypeStruct((HD, n), F32)],
        in_specs=[row(HD), full(n, HD), full(n, HD), row(1), full(1, n), row(1), row(HD)],
        out_specs=[row(HD), full(HD, n), full(HD, n)],
        compiler_params=pltpu.CompilerParams(vmem_limit_bytes=48 * MIB),
        name="attend_back",
    )(q, k, v, sq, sk, lse, dc)


def rmsnorm(field, gain_row):
    return field * lax.rsqrt(jnp.mean(field * field, -1, keepdims=True) + EPS) * gain_row


def rotate(field, cos_table, sin_table):
    half = field.shape[-1] // 2
    first, second = field[..., :half], field[..., half:]
    return jnp.concatenate(
        [first * cos_table - second * sin_table, second * cos_table + first * sin_table], -1
    )


def rotary_tables(length):
    position = jnp.arange(length).astype(F32)
    freq = THETA ** (-(jnp.arange(HD // 2).astype(F32) * 2.0 / HD))
    angle = position[:, None] * freq[None, :]
    return jnp.cos(angle), jnp.sin(angle)


def dot(a, b, ca, cb):
    return lax.dot_general(a, b, (((ca,), (cb,)), ((), ())), preferred_element_type=F32)


def per_device(
    tokens, segments, routes, route_weight, capacity, norm_gain,
    qkv_weight, out_weight, gate_weight, up_weight, down_weight, cotangent,
):
    rows, width = tokens.shape
    seq = segments.shape[0]
    me = lax.axis_index("dp")
    slots = 80
    stream = tokens.astype(F32)
    normed = rmsnorm(stream, norm_gain[0]).astype(BF)
    meta = jnp.concatenate([routes.astype(F32).T, route_weight.T], 0)
    normed_all, meta_all, w_head = front(normed, meta, qkv_weight)
    projected = dot(normed_all, w_head, 1, 1)
    cos_table, sin_table = rotary_tables(seq)
    q = rotate(projected[:, :HD], cos_table, sin_table).astype(BF)
    k = rotate(projected[:, HD : 2 * HD], cos_table, sin_table).astype(BF)
    v = projected[:, 2 * HD :].astype(BF)
    sq = segments[:, None]
    sk = jnp.where(segments == 0, -1, segments)[None, :]
    ctx_h, lse = attend(q, k, v, sq, sk)
    context = swap(ctx_h.reshape(16, rows, HD), 1).transpose(1, 0, 2).reshape(rows, width)
    dense_out = gather(out_weight, 2)
    attended = dot(context, dense_out, 1, 1)
    middle = stream + attended
    normed2 = rmsnorm(middle, norm_gain[1]).astype(BF)
    normed2_all = gather(normed2, 3)
    cot_all = gather(cotangent, 4)
    mine = meta_all[:, :TOPK] == me.astype(F32)
    member = jnp.sum(mine.astype(F32), 1)
    weight = jnp.sum(jnp.where(mine, meta_all[:, TOPK:], 0.0), 1)
    local = jnp.cumsum(member, 1) - member
    before = jnp.cumsum(jnp.sum(member, 1)) - jnp.sum(member, 1)
    kept = (member > 0) & (local + before[:, None] < capacity[0].astype(F32))
    pick = (jnp.arange(slots, dtype=F32)[None, :, None] == local[:, None, :]) & kept[:, None, :]
    slot_weight = jnp.sum(jnp.where(pick, weight[:, None, :], 0.0), 2).reshape(16 * slots, 1)
    pick = pick.astype(BF)
    take = lambda a: jnp.einsum("jst,jtd->jsd", pick, a.reshape(16, rows, width), preferred_element_type=F32).reshape(16 * slots, width)
    put = lambda a: jnp.einsum("jst,jsd->jtd", pick, a.reshape(16, slots, width), preferred_element_type=F32).reshape(seq, width).astype(BF)
    xr = take(normed2_all).astype(BF)
    pg = (take(cot_all) * slot_weight).astype(BF)
    gate = dot(xr, gate_weight[0], 1, 0)
    up = dot(xr, up_weight[0], 1, 0)
    sig = jax.nn.sigmoid(gate)
    hidden = (gate * sig * up).astype(BF)
    eo = dot(hidden, down_weight[0], 1, 0).astype(BF)
    mix_part = put((eo.astype(F32) * slot_weight).astype(BF))
    hg = dot(pg, down_weight[0], 1, 1)
    gg = (hg * up * sig * (1.0 + gate * (1.0 - sig))).astype(BF)
    ug = (hg * gate * sig).astype(BF)
    rg = (dot(gg, gate_weight[0], 1, 1) + dot(ug, up_weight[0], 1, 1)).astype(BF)
    back_part = put(rg)
    down_g = dot(hidden, pg, 0, 0)
    gate_g = dot(xr, gg, 0, 0)
    up_g = dot(xr, ug, 0, 0)
    mixture = scatter(mix_part, 5)
    n2g = scatter(back_part, 6)
    layer = middle + mixture
    own_seg = lax.dynamic_slice_in_dim(segments, me * rows, rows)
    valid = (own_seg != 0).astype(F32)
    sums = jnp.stack(
        [
            jnp.sum(valid * jnp.sum(layer * layer, -1)),
            jnp.sum(valid * jnp.sum(attended * attended, -1)),
            jnp.sum(valid * jnp.sum(mixture * mixture, -1)),
            jnp.sum(valid) * width,
        ]
    )
    grad = cotangent.astype(F32)
    mg, gain2 = jax.vjp(rmsnorm, middle, norm_gain[1])[1](n2g)
    middle_grad = grad + mg
    attended_grad = middle_grad.astype(BF)
    context_grad = dot(attended_grad, dense_out, 1, 0).astype(BF)
    cg_h = swap(context_grad.reshape(rows, H, HD).transpose(1, 0, 2), 7).reshape(seq, HD)
    dq, dkt, dvt = attend_back(q, k, v, sq, sk, lse, cg_h)
    pgrad = jnp.concatenate(
        [rotate(dq, cos_table, -sin_table), rotate(dkt.T, cos_table, -sin_table), dvt.T], 1
    ).astype(BF)
    qkv_part = dot(pgrad, normed_all, 0, 0)
    qkv_sum = lax.psum(qkv_part.astype(BF), "grp")
    qkv_total = give_back(qkv_sum.reshape(3, HD, width), 8).reshape(3 * HD, width).astype(F32)
    normed_grad = scatter(dot(pgrad, w_head, 1, 0).astype(BF), 9)
    out_part = scatter(dot(attended_grad, context, 0, 0).astype(BF), 10)
    sg, gain1 = jax.vjp(rmsnorm, stream, norm_gain[0])[1](normed_grad)
    tokens_grad = middle_grad + sg
    seq_sums, gain_dp = lax.psum((sums, jnp.stack([gain1, gain2])), "dp")
    stat_row = jnp.sqrt(seq_sums[:3] / seq_sums[3]).reshape(1, 3)
    over = lambda a: lax.psum(a.astype(BF), "grp").astype(F32)
    return (
        layer.astype(BF),
        tokens_grad,
        qkv_total,
        over(out_part),
        over(gate_g)[None],
        over(up_g)[None],
        over(down_g)[None],
        over(gain_dp),
        stat_row,
    )


def solution(mesh):
    both = ("grp", "dp")
    in_specs = (
        P(both, None), P("grp"), P(both, None), P(both, None), P(), P(),
        P("dp", None), P("dp", None), P("dp", None, None), P("dp", None, None), P("dp", None, None),
        P(both, None),
    )
    out_specs = (
        P(both, None), P(both, None), P("dp", None), P("dp", None),
        P("dp", None, None), P("dp", None, None), P("dp", None, None), P(), P("grp", None),
    )
    return jax.shard_map(per_device, mesh=mesh, in_specs=in_specs, out_specs=out_specs, check_vma=False)
```

```python
import functools

import jax
import jax.numpy as jnp
import numpy as np
from jax import lax
from jax.experimental import pallas as pl
from jax.experimental.pallas import tpu as pltpu
from jax.sharding import PartitionSpec as P

H = 16
HD = 128
TOPK = 8
EPS = 1e-06
THETA = 50000.0
MESH = pl.DeviceIdType.MESH
MIB = 2**20
BF = jnp.bfloat16
F32 = jnp.float32
SCALE = HD**-0.5
LOG2E = 1.4426950408889634


def places():
    me = lax.axis_index("dp")
    z, y, x = me // 4, (me // 2) % 2, me % 2
    xor = [z, z + 1 - 2 * (z % 2), (z + 2) % 4, 3 - z]
    at = lambda k, yy, xx: xor[k] * 4 + yy * 2 + xx
    return dict(
        me=me,
        col=[at(k, y, x) for k in range(4)],
        X=[at(k, y, 1 - x) for k in range(4)],
        Y=[at(k, 1 - y, x) for k in range(4)],
        D=[at(k, 1 - y, 1 - x) for k in range(4)],
    )


def barrier(targets, pair=False):
    sem = pltpu.get_barrier_semaphore()
    for t in targets:
        pl.semaphore_signal(sem, inc=1, device_id={"dp": t}, device_id_type=MESH)
    count = len(targets)
    if pair:
        pl.semaphore_signal(sem, inc=1, device_id={"grp": partner()}, device_id_type=MESH)
        count += 1
    pl.semaphore_wait(sem, count)


def partner():
    g = lax.axis_index("grp")
    return g + 1 - 2 * (g % 2)


def push(src, dst, send, recv, to):
    c = pltpu.make_async_remote_copy(
        src_ref=src, dst_ref=dst, send_sem=send, recv_sem=recv,
        device_id={"dp": to}, device_id_type=MESH,
    )
    c.start()
    return c


def push_pair(src, dst, send, recv):
    c = pltpu.make_async_remote_copy(
        src_ref=src, dst_ref=dst, send_sem=send, recv_sem=recv,
        device_id={"grp": partner()}, device_id_type=MESH,
    )
    c.start()
    return c


GATHER_SEMS = [pltpu.SemaphoreType.DMA((4,))] * 6 + [pltpu.SemaphoreType.DMA((4, 2))] * 2 + [pltpu.SemaphoreType.DMA]


class Gather:
    def __init__(self, src, dst, rows, sems):
        self.src, self.dst, self.rows, self.sems, self.p = src, dst, rows, sems, places()

    def block(self, b):
        return self.dst.at[pl.ds(pl.multiple_of(b * self.rows, self.rows), self.rows)]

    def part(self, b, h):
        half = self.rows // 2
        return self.dst.at[pl.ds(pl.multiple_of(b * self.rows + h * half, half), half)]

    def begin(self):
        zs, zr, xs, xr, ys, yr, _, _, own = self.sems
        p, src = self.p, self.src
        me = p["me"]
        self.mine = pltpu.make_async_copy(src, self.block(me), own)
        self.mine.start()
        self.xc = [push(src, self.block(me), xs.at[0], xr.at[0], p["X"][0])]
        self.yc = [push(src, self.block(me), ys.at[0], yr.at[0], p["Y"][0])]
        self.zc = [push(src, self.block(me), zs.at[k], zr.at[k], p["col"][k]) for k in (1, 2, 3)]
        self.dc = []

    def step(self, k):
        zs, zr, xs, xr, ys, yr, ds, dr, own = self.sems
        p = self.p
        if k < 3:
            self.zc[k].wait_recv()
            b = self.block(p["col"][k + 1])
            self.xc.append(push(b, b, xs.at[k + 1], xr.at[k + 1], p["X"][0]))
            self.yc.append(push(b, b, ys.at[k + 1], yr.at[k + 1], p["Y"][0]))
        b = self.part(p["X"][k], 0)
        self.xc[k].wait_recv()
        self.dc.append(push(b, b, ds.at[k, 0], dr.at[k, 0], p["Y"][0]))
        b = self.part(p["Y"][k], 1)
        self.yc[k].wait_recv()
        self.dc.append(push(b, b, ds.at[k, 1], dr.at[k, 1], p["X"][0]))

    def ready(self, k):
        if k == 0:
            self.mine.wait()
        self.dc[2 * k].wait_recv()
        self.dc[2 * k + 1].wait_recv()

    def end(self):
        for c in self.xc + self.yc + self.zc + self.dc:
            c.wait_send()

    def all(self):
        for k in range(4):
            self.step(k)
        for k in range(4):
            self.ready(k)
        self.end()


def gather_targets():
    p = places()
    return [p["col"][1], p["col"][2], p["col"][3], p["X"][0], p["Y"][0]]


SCATTER_SEMS = [pltpu.SemaphoreType.DMA((4, 2))] * 2 + [pltpu.SemaphoreType.DMA((4,))] * 6


def scatter_bufs(rows, width):
    return [
        pltpu.VMEM((8, rows // 2, width), BF),
        pltpu.VMEM((4, rows, width), BF),
        pltpu.VMEM((4, rows, width), BF),
        pltpu.VMEM((4, rows, width), BF),
    ]


class Scatter:
    def __init__(self, part, out, rows, bufs, sems):
        self.part, self.out, self.half, self.bufs, self.sems, self.p = part, out, rows // 2, bufs, sems, places()
        self.da, self.db, self.xc, self.yc, self.zc = {}, {}, {}, {}, {}

    def far(self, k):
        ds, dr = self.sems[:2]
        rd, h, p = self.bufs[0], self.half, self.p
        b = p["D"][k]
        self.da[k] = push(self.part.at[b, pl.ds(0, h)], rd.at[2 * k], ds.at[k, 0], dr.at[k, 0], p["Y"][0])
        self.db[k] = push(self.part.at[b, pl.ds(h, h)], rd.at[2 * k + 1], ds.at[k, 1], dr.at[k, 1], p["X"][0])

    def near(self, k):
        _, _, xs, xr, ys, yr, _, _ = self.sems
        rd, rx, ry, _ = self.bufs
        part, h, p = self.part, self.half, self.p
        b = p["X"][k]
        self.da[k].wait_recv()
        part[b, pl.ds(0, h)] = (part[b, pl.ds(0, h)].astype(F32) + rd[2 * k].astype(F32)).astype(BF)
        self.xc[k] = push(part.at[b], rx.at[k], xs.at[k], xr.at[k], p["X"][0])
        b = p["Y"][k]
        self.db[k].wait_recv()
        part[b, pl.ds(h, h)] = (part[b, pl.ds(h, h)].astype(F32) + rd[2 * k + 1].astype(F32)).astype(BF)
        self.yc[k] = push(part.at[b], ry.at[k], ys.at[k], yr.at[k], p["Y"][0])

    def along(self, k):
        zs, zr = self.sems[6:]
        _, rx, ry, rz = self.bufs
        part = self.part
        b = self.p["col"][k]
        self.xc[k].wait_recv()
        self.yc[k].wait_recv()
        total = part[b].astype(F32) + rx[k].astype(F32) + ry[k].astype(F32)
        if k:
            part[b] = total.astype(BF)
            self.zc[k] = push(part.at[b], rz.at[k], zs.at[k], zr.at[k], b)
        else:
            self.out[...] = total

    def end(self):
        for k in (1, 2, 3):
            self.zc[k].wait_recv()
            self.out[...] += self.bufs[3][k].astype(F32)
        for group in (self.da, self.db, self.xc, self.yc, self.zc):
            for c in group.values():
                c.wait_send()

    def all(self):
        order = (1, 2, 3, 0)
        for k in order:
            self.far(k)
        for k in order:
            self.near(k)
        for k in order:
            self.along(k)
        self.end()


ANY = pl.BlockSpec(memory_space=pl.ANY)
VM = pl.BlockSpec(memory_space=pltpu.VMEM)


def params(cid, vmem=60):
    return pltpu.CompilerParams(collective_id=cid, has_side_effects=True, vmem_limit_bytes=vmem * MIB)


def front_kernel(n_ref, m_ref, w_ref, nall, mall, wh, *sems):
    g_sems, (ms, mr, mo, ws, wr, ps, pr, wo) = sems[:9], sems[9:]
    me = lax.axis_index("dp")
    core = lax.axis_index("grp") % 2
    barrier([lax.rem(me + d, 16) for d in range(1, 16)], pair=True)
    hr = HD // 2
    g = Gather(n_ref, nall, n_ref.shape[0], g_sems)
    g.begin()
    own = pltpu.make_async_copy(m_ref, mall.at[me], mo)
    own.start()
    mc = []
    for d in range(1, 16):
        to = lax.rem(me + d, 16)
        mc.append(push(m_ref, mall.at[me], ms.at[d], mr.at[d], to))
    off = core * hr
    for l in range(3):
        b = 3 * me + l
        to, slot = lax.rem(b, 16), b // 16
        src = w_ref.at[pl.ds(pl.multiple_of(l * HD + off, hr), hr)]
        dst = wh.at[pl.ds(pl.multiple_of(slot * HD + off, hr), hr)]

        @pl.when(to != me)
        def _():
            push(src, dst, ws.at[l], wr.at[slot], to)

        @pl.when(to == me)
        def _():
            pltpu.make_async_copy(src, dst, wr.at[slot]).start()

    for s in range(3):
        dst = wh.at[pl.ds(pl.multiple_of(s * HD + off, hr), hr)]
        pltpu.make_async_copy(dst, dst, wr.at[s]).wait()
        push_pair(dst, dst, ps.at[s], pr.at[s])
    g.all()
    own.wait()
    for c in mc:
        c.wait()
    for l in range(3):
        b = 3 * me + l
        src = w_ref.at[pl.ds(pl.multiple_of(l * HD + off, hr), hr)]

        @pl.when(lax.rem(b, 16) != me)
        def _():
            pltpu.make_async_copy(src, src, ws.at[l]).wait()

    for s in range(3):
        dst = wh.at[pl.ds(pl.multiple_of(s * HD + off, hr), hr)]
        other = wh.at[pl.ds(pl.multiple_of(s * HD + (hr - off), hr), hr)]
        pltpu.make_async_copy(dst, dst, ps.at[s]).wait()
        pltpu.make_async_copy(other, other, pr.at[s]).wait()


def front(normed, meta, w):
    rows, width = normed.shape
    return pl.pallas_call(
        front_kernel,
        out_shape=[
            jax.ShapeDtypeStruct((16 * rows, width), BF),
            jax.ShapeDtypeStruct((16,) + meta.shape, F32),
            jax.ShapeDtypeStruct((3 * HD, width), BF),
        ],
        in_specs=[ANY] * 3,
        out_specs=[ANY] * 3,
        scratch_shapes=GATHER_SEMS
        + [pltpu.SemaphoreType.DMA((16,)), pltpu.SemaphoreType.DMA((16,)), pltpu.SemaphoreType.DMA]
        + [pltpu.SemaphoreType.DMA((3,))] * 4
        + [pltpu.SemaphoreType.DMA],
        compiler_params=params(0),
        name="front",
    )(normed, meta, w)


def gather_kernel(x_ref, o_ref, *sems):
    barrier(gather_targets())
    g = Gather(x_ref, o_ref, x_ref.shape[0], sems)
    g.begin()
    g.all()


def gather(x, cid):
    rows, width = x.shape
    return pl.pallas_call(
        gather_kernel,
        out_shape=jax.ShapeDtypeStruct((16 * rows, width), x.dtype),
        in_specs=[ANY],
        out_specs=ANY,
        scratch_shapes=GATHER_SEMS,
        compiler_params=params(cid),
        name=f"gather_{cid}",
    )(x)


def scatter_kernel(p_ref, o_ref, part, load, *rest):
    bufs, sems = rest[:4], rest[4:]
    c = pltpu.make_async_copy(p_ref, part, load)
    c.start()
    barrier(gather_targets())
    c.wait()
    Scatter(part, o_ref, part.shape[1], bufs, sems).all()


def scatter(x, cid):
    rows, width = x.shape[0] // 16, x.shape[1]
    return pl.pallas_call(
        scatter_kernel,
        out_shape=jax.ShapeDtypeStruct((rows, width), F32),
        in_specs=[ANY],
        out_specs=VM,
        scratch_shapes=[pltpu.VMEM((16, rows, width), BF), pltpu.SemaphoreType.DMA]
        + scatter_bufs(rows, width)
        + SCATTER_SEMS,
        compiler_params=params(cid),
        name=f"scatter_{cid}",
    )(x.reshape(16, rows, width))


def swap_kernel(x_ref, o_ref, ss, rs, lo):
    me = lax.axis_index("dp")
    barrier([lax.rem(me + d, 16) for d in range(1, 16)])
    own = pltpu.make_async_copy(x_ref.at[me], o_ref.at[me], lo)
    own.start()
    sent = []
    for d in range(1, 16):
        to = lax.rem(me + d, 16)
        sent.append(push(x_ref.at[to], o_ref.at[me], ss.at[d], rs.at[d], to))
    own.wait()
    for c in sent:
        c.wait()


def swap(x, cid):
    return pl.pallas_call(
        swap_kernel,
        out_shape=jax.ShapeDtypeStruct(x.shape, x.dtype),
        in_specs=[ANY],
        out_specs=ANY,
        scratch_shapes=[pltpu.SemaphoreType.DMA((16,))] * 2 + [pltpu.SemaphoreType.DMA],
        compiler_params=params(cid),
        name=f"swap_{cid}",
    )(x)


def return_kernel(x_ref, o_ref, ss, rs):
    me = lax.axis_index("dp")
    barrier([lax.rem(me + d, 16) for d in range(1, 16)])
    for s in range(3):
        b = 16 * s + me
        to, slot = b // 3, lax.rem(b, 3)

        @pl.when(to != me)
        def _():
            push(x_ref.at[s], o_ref.at[slot], ss.at[s], rs.at[slot], to)

        @pl.when(to == me)
        def _():
            pltpu.make_async_copy(x_ref.at[s], o_ref.at[slot], rs.at[slot]).start()

    for s in range(3):
        pltpu.make_async_copy(x_ref.at[s], o_ref.at[s], rs.at[s]).wait()

        @pl.when((16 * s + me) // 3 != me)
        def _():
            pltpu.make_async_copy(x_ref.at[s], o_ref.at[s], ss.at[s]).wait()


def give_back(x, cid):
    return pl.pallas_call(
        return_kernel,
        out_shape=jax.ShapeDtypeStruct(x.shape, x.dtype),
        in_specs=[ANY],
        out_specs=ANY,
        scratch_shapes=[pltpu.SemaphoreType.DMA((3,))] * 2,
        compiler_params=params(cid),
        name="give_back",
    )(x)


QB = 256


def attend_kernel(q, k, v, sq, sk, ctx, lse):
    s = lax.dot_general(q[...], k[...], (((1,), (1,)), ((), ())), preferred_element_type=F32)
    s = jnp.where(sq[...] == sk[...], s, -1e30)
    peak = jnp.maximum(jnp.max(s, -1, keepdims=True), -1e29)
    ex = jnp.exp2((s - peak) * (SCALE * LOG2E))
    total = jnp.maximum(jnp.sum(ex, -1, keepdims=True), 1.0)
    prob = (ex * (1.0 / total)).astype(BF)
    ctx[...] = jnp.dot(prob, v[...], preferred_element_type=F32).astype(BF)
    lse[...] = peak * (SCALE * LOG2E) + jnp.log2(total)


def attend(q, k, v, sq, sk):
    n = q.shape[0]
    row = lambda w: pl.BlockSpec((QB, w), lambda i: (i, 0))
    full = lambda r, w: pl.BlockSpec((r, w), lambda i: (0, 0))
    return pl.pallas_call(
        attend_kernel,
        grid=(n // QB,),
        out_shape=[jax.ShapeDtypeStruct((n, HD), BF), jax.ShapeDtypeStruct((n, 1), F32)],
        in_specs=[row(HD), full(n, HD), full(n, HD), row(1), full(1, n)],
        out_specs=[row(HD), row(1)],
        compiler_params=pltpu.CompilerParams(vmem_limit_bytes=48 * MIB),
        name="attend",
    )(q, k, v, sq, sk)


def attend_back_kernel(q, k, v, sq, sk, lse, dc, dq, dkt, dvt):
    @pl.when(pl.program_id(0) == 0)
    def _():
        dkt[...] = jnp.zeros_like(dkt)
        dvt[...] = jnp.zeros_like(dvt)

    s = lax.dot_general(q[...], k[...], (((1,), (1,)), ((), ())), preferred_element_type=F32)
    prob = jnp.where(sq[...] == sk[...], jnp.exp2(s * (SCALE * LOG2E) - lse[...]), 0.0)
    dp = lax.dot_general(dc[...], v[...], (((1,), (1,)), ((), ())), preferred_element_type=F32)
    delta = jnp.sum(prob * dp, -1, keepdims=True)
    ds = (prob * (dp - delta)).astype(BF)
    dq[...] = jnp.dot(ds, k[...], preferred_element_type=F32) * SCALE
    dkt[...] += lax.dot_general(q[...], ds, (((0,), (0,)), ((), ())), preferred_element_type=F32) * SCALE
    dvt[...] += lax.dot_general(dc[...], prob.astype(BF), (((0,), (0,)), ((), ())), preferred_element_type=F32)


def attend_back(q, k, v, sq, sk, lse, dc):
    n = q.shape[0]
    row = lambda w: pl.BlockSpec((QB, w), lambda i: (i, 0))
    full = lambda r, w: pl.BlockSpec((r, w), lambda i: (0, 0))
    return pl.pallas_call(
        attend_back_kernel,
        grid=(n // QB,),
        out_shape=[jax.ShapeDtypeStruct((n, HD), F32), jax.ShapeDtypeStruct((HD, n), F32), jax.ShapeDtypeStruct((HD, n), F32)],
        in_specs=[row(HD), full(n, HD), full(n, HD), row(1), full(1, n), row(1), row(HD)],
        out_specs=[row(HD), full(HD, n), full(HD, n)],
        compiler_params=pltpu.CompilerParams(vmem_limit_bytes=48 * MIB),
        name="attend_back",
    )(q, k, v, sq, sk, lse, dc)


SLOTS = 80
COLS = 256


def place_of(k, j):
    me = lax.axis_index("dp")
    z, y, x = me // 4, (me // 2) % 2, me % 2
    zk = [z, z + 1 - 2 * (z % 2), (z + 2) % 4, 3 - z][k]
    jy, jx = j // 2, j % 2
    return zk * 4 + (y + jy - 2 * y * jy) * 2 + (x + jx - 2 * x * jx)


def expert_kernel(
    n2, cot, pick, pickt, sw, wg_h, wu_h, wd_h,
    n2g, p1, xr_o, pg_o, hid_o, gg_o, ug_o,
    nall, call, part, stage, wg, wu, wd, xr, pg, hid, gg, ug, rd, rx, ry, rz, wsem, osem, psem, *sems,
):
    rows = n2.shape[0]
    chunk = 4 * SLOTS
    loads = [pltpu.make_async_copy(a, b, wsem.at[i]) for i, (a, b) in enumerate([(wg_h, wg), (wu_h, wu), (wd_h, wd)])]
    for c in loads:
        c.start()
    barrier(gather_targets())
    gn = Gather(n2, nall, rows, sems[:9])
    gc = Gather(cot, call, rows, sems[9:18])
    sc = Scatter(part, n2g, rows, (rd, rx, ry, rz), sems[18:])
    gn.begin()
    gc.begin()
    saves = []
    for k in range(4):
        gn.step(k)
        gc.step(k)
        gn.ready(k)
        gc.ready(k)
        for c in saves:
            c.wait()
        if k == 0:
            for c in loads:
                c.wait()

        def collect(j, carry):
            b = place_of(k, j)
            row = pl.ds(pl.multiple_of(b * rows, rows), rows)
            to = pl.ds(pl.multiple_of(j * SLOTS, SLOTS), SLOTS)

            def cols(n, c):
                w = pl.ds(pl.multiple_of(n * 512, 512), 512)
                xr[to, w] = dot(pick[b], nall[row, w], 1, 0).astype(BF)
                pg[to, w] = (dot(pick[b], call[row, w], 1, 0) * sw[b]).astype(BF)
                return c

            return lax.fori_loop(0, nall.shape[1] // 512, cols, carry)

        lax.fori_loop(0, 4, collect, 0)

        def inner(n, carry):
            w = pl.ds(pl.multiple_of(n * COLS, COLS), COLS)
            gate = dot(xr[...], wg[:, w], 1, 0)
            up = dot(xr[...], wu[:, w], 1, 0)
            hg = dot(pg[...], wd[w, :], 1, 1)
            sig = jax.nn.sigmoid(gate)
            hid[:, w] = (gate * sig * up).astype(BF)
            gg[:, w] = (hg * up * sig * (1.0 + gate * (1.0 - sig))).astype(BF)
            ug[:, w] = (hg * gate * sig).astype(BF)
            return carry

        lax.fori_loop(0, hid.shape[1] // COLS, inner, 0)

        def outer(n, carry):
            w = pl.ds(pl.multiple_of(n * COLS, COLS), COLS)
            eo = dot(hid[...], wd[:, w], 1, 0).astype(BF).astype(F32)
            rg = (dot(gg[...], wg[w, :], 1, 1) + dot(ug[...], wu[w, :], 1, 1)).astype(BF)
            for j in range(4):
                b = place_of(k, j)
                cut = slice(j * SLOTS, (j + 1) * SLOTS)
                weighted = (eo[cut] * sw[b]).astype(BF)
                stage[j, :, w] = dot(pickt[b], weighted, 1, 0).astype(BF)
                part[b, :, w] = dot(pickt[b], rg[cut], 1, 0).astype(BF)
            return carry

        lax.fori_loop(0, xr.shape[1] // COLS, outer, 0)
        sc.far(k)
        if k >= 1:
            sc.near(k - 1)
        if k >= 2:
            sc.along(k - 2)
        saves = [
            pltpu.make_async_copy(a, o.at[k], osem.at[i])
            for i, (a, o) in enumerate([(xr, xr_o), (pg, pg_o), (hid, hid_o), (gg, gg_o), (ug, ug_o)])
        ] + [pltpu.make_async_copy(stage.at[j], p1.at[place_of(k, j)], psem.at[j]) for j in range(4)]
        for c in saves:
            c.start()
    gn.end()
    gc.end()
    sc.near(3)
    sc.along(2)
    sc.along(3)
    sc.end()
    for c in saves:
        c.wait()


def expert(n2, cot, pick, pickt, sw, wg, wu, wd, cid):
    rows, width = n2.shape
    ff = wg.shape[1]
    chunk = 4 * SLOTS
    save = lambda w: jax.ShapeDtypeStruct((4, chunk, w), BF)
    v = lambda *shape: pltpu.VMEM(shape, BF)
    return pl.pallas_call(
        expert_kernel,
        out_shape=[
            jax.ShapeDtypeStruct((rows, width), F32),
            jax.ShapeDtypeStruct((16, rows, width), BF),
            save(width), save(width), save(ff), save(ff), save(ff),
        ],
        in_specs=[ANY, ANY, VM, VM, VM, ANY, ANY, ANY],
        out_specs=[VM] + [ANY] * 6,
        scratch_shapes=[
            v(16 * rows, width), v(16 * rows, width), v(16, rows, width), v(4, rows, width),
            v(width, ff), v(width, ff), v(ff, width),
            v(chunk, width), v(chunk, width), v(chunk, ff), v(chunk, ff), v(chunk, ff),
        ]
        + scatter_bufs(rows, width)
        + [pltpu.SemaphoreType.DMA((3,)), pltpu.SemaphoreType.DMA((5,)), pltpu.SemaphoreType.DMA((4,))]
        + GATHER_SEMS * 2
        + SCATTER_SEMS,
        compiler_params=params(cid, 62),
        name="expert",
    )(n2, cot, pick, pickt, sw, wg, wu, wd)


def rmsnorm(field, gain_row):
    return field * lax.rsqrt(jnp.mean(field * field, -1, keepdims=True) + EPS) * gain_row


def rotate(field, cos_table, sin_table):
    half = field.shape[-1] // 2
    first, second = field[..., :half], field[..., half:]
    return jnp.concatenate(
        [first * cos_table - second * sin_table, second * cos_table + first * sin_table], -1
    )


def rotary_tables(length):
    position = jnp.arange(length).astype(F32)
    freq = THETA ** (-(jnp.arange(HD // 2).astype(F32) * 2.0 / HD))
    angle = position[:, None] * freq[None, :]
    return jnp.cos(angle), jnp.sin(angle)


def dot(a, b, ca, cb):
    return lax.dot_general(a, b, (((ca,), (cb,)), ((), ())), preferred_element_type=F32)


def per_device(
    tokens, segments, routes, route_weight, capacity, norm_gain,
    qkv_weight, out_weight, gate_weight, up_weight, down_weight, cotangent,
):
    rows, width = tokens.shape
    seq = segments.shape[0]
    me = lax.axis_index("dp")
    slots = SLOTS
    stream = tokens.astype(F32)
    normed = rmsnorm(stream, norm_gain[0]).astype(BF)
    meta = jnp.concatenate([routes.astype(F32).T, route_weight.T], 0)
    normed_all, meta_all, w_head = front(normed, meta, qkv_weight)
    projected = dot(normed_all, w_head, 1, 1)
    cos_table, sin_table = rotary_tables(seq)
    q = rotate(projected[:, :HD], cos_table, sin_table).astype(BF)
    k = rotate(projected[:, HD : 2 * HD], cos_table, sin_table).astype(BF)
    v = projected[:, 2 * HD :].astype(BF)
    sq = segments[:, None]
    sk = jnp.where(segments == 0, -1, segments)[None, :]
    ctx_h, lse = attend(q, k, v, sq, sk)
    context = swap(ctx_h.reshape(16, rows, HD), 1).transpose(1, 0, 2).reshape(rows, width)
    dense_out = gather(out_weight, 2)
    attended = dot(context, dense_out, 1, 1)
    middle = stream + attended
    normed2 = rmsnorm(middle, norm_gain[1]).astype(BF)
    mine = meta_all[:, :TOPK] == me.astype(F32)
    member = jnp.sum(mine.astype(F32), 1)
    weight = jnp.sum(jnp.where(mine, meta_all[:, TOPK:], 0.0), 1)
    local = jnp.cumsum(member, 1) - member
    before = jnp.cumsum(jnp.sum(member, 1)) - jnp.sum(member, 1)
    kept = (member > 0) & (local + before[:, None] < capacity[0].astype(F32))
    pick = (jnp.arange(slots, dtype=F32)[None, :, None] == local[:, None, :]) & kept[:, None, :]
    slot_weight = jnp.sum(jnp.where(pick, weight[:, None, :], 0.0), 2)[:, :, None]
    pick = pick.astype(BF)
    n2g, mix_part, xr, pg, hidden, gg, ug = expert(
        normed2, cotangent, pick, pick.transpose(0, 2, 1), slot_weight, gate_weight[0], up_weight[0], down_weight[0], 3
    )
    flat = lambda a: a.reshape(-1, a.shape[2])
    xr, pg, hidden, gg, ug = [flat(a) for a in (xr, pg, hidden, gg, ug)]
    down_g = dot(hidden, pg, 0, 0)
    gate_g = dot(xr, gg, 0, 0)
    up_g = dot(xr, ug, 0, 0)
    mixture = scatter(mix_part.reshape(seq, width), 5)
    layer = middle + mixture
    own_seg = lax.dynamic_slice_in_dim(segments, me * rows, rows)
    valid = (own_seg != 0).astype(F32)
    sums = jnp.stack(
        [
            jnp.sum(valid * jnp.sum(layer * layer, -1)),
            jnp.sum(valid * jnp.sum(attended * attended, -1)),
            jnp.sum(valid * jnp.sum(mixture * mixture, -1)),
            jnp.sum(valid) * width,
        ]
    )
    grad = cotangent.astype(F32)
    mg, gain2 = jax.vjp(rmsnorm, middle, norm_gain[1])[1](n2g)
    middle_grad = grad + mg
    attended_grad = middle_grad.astype(BF)
    context_grad = dot(attended_grad, dense_out, 1, 0).astype(BF)
    cg_h = swap(context_grad.reshape(rows, H, HD).transpose(1, 0, 2), 7).reshape(seq, HD)
    dq, dkt, dvt = attend_back(q, k, v, sq, sk, lse, cg_h)
    pgrad = jnp.concatenate(
        [rotate(dq, cos_table, -sin_table), rotate(dkt.T, cos_table, -sin_table), dvt.T], 1
    ).astype(BF)
    qkv_part = dot(pgrad, normed_all, 0, 0)
    qkv_sum = lax.psum(qkv_part.astype(BF), "grp")
    qkv_total = give_back(qkv_sum.reshape(3, HD, width), 8).reshape(3 * HD, width).astype(F32)
    normed_grad = scatter(dot(pgrad, w_head, 1, 0).astype(BF), 9)
    out_part = scatter(dot(attended_grad, context, 0, 0).astype(BF), 10)
    sg, gain1 = jax.vjp(rmsnorm, stream, norm_gain[0])[1](normed_grad)
    tokens_grad = middle_grad + sg
    seq_sums, gain_dp = lax.psum((sums, jnp.stack([gain1, gain2])), "dp")
    stat_row = jnp.sqrt(seq_sums[:3] / seq_sums[3]).reshape(1, 3)
    over = lambda a: lax.psum(a.astype(BF), "grp").astype(F32)
    return (
        layer.astype(BF),
        tokens_grad,
        qkv_total,
        over(out_part),
        over(gate_g)[None],
        over(up_g)[None],
        over(down_g)[None],
        over(gain_dp),
        stat_row,
    )


def solution(mesh):
    both = ("grp", "dp")
    in_specs = (
        P(both, None), P("grp"), P(both, None), P(both, None), P(), P(),
        P("dp", None), P("dp", None), P("dp", None, None), P("dp", None, None), P("dp", None, None),
        P(both, None),
    )
    out_specs = (
        P(both, None), P(both, None), P("dp", None), P("dp", None),
        P("dp", None, None), P("dp", None, None), P("dp", None, None), P(), P("grp", None),
    )
    return jax.shard_map(per_device, mesh=mesh, in_specs=in_specs, out_specs=out_specs, check_vma=False)
```

```python
import functools

import jax
import jax.numpy as jnp
import numpy as np
from jax import lax
from jax.experimental import pallas as pl
from jax.experimental.pallas import tpu as pltpu
from jax.sharding import PartitionSpec as P

H = 16
HD = 128
TOPK = 8
EPS = 1e-06
THETA = 50000.0
MESH = pl.DeviceIdType.MESH
MIB = 2**20
BF = jnp.bfloat16
F32 = jnp.float32
SCALE = HD**-0.5
LOG2E = 1.4426950408889634


def places():
    me = lax.axis_index("dp")
    z, y, x = me // 4, (me // 2) % 2, me % 2
    xor = [z, z + 1 - 2 * (z % 2), (z + 2) % 4, 3 - z]
    at = lambda k, yy, xx: xor[k] * 4 + yy * 2 + xx
    return dict(
        me=me,
        col=[at(k, y, x) for k in range(4)],
        X=[at(k, y, 1 - x) for k in range(4)],
        Y=[at(k, 1 - y, x) for k in range(4)],
        D=[at(k, 1 - y, 1 - x) for k in range(4)],
    )


def barrier(targets, pair=False):
    sem = pltpu.get_barrier_semaphore()
    for t in targets:
        pl.semaphore_signal(sem, inc=1, device_id={"dp": t}, device_id_type=MESH)
    count = len(targets)
    if pair:
        pl.semaphore_signal(sem, inc=1, device_id={"grp": partner()}, device_id_type=MESH)
        count += 1
    pl.semaphore_wait(sem, count)


def partner():
    g = lax.axis_index("grp")
    return g + 1 - 2 * (g % 2)


def push(src, dst, send, recv, to):
    c = pltpu.make_async_remote_copy(
        src_ref=src, dst_ref=dst, send_sem=send, recv_sem=recv,
        device_id={"dp": to}, device_id_type=MESH,
    )
    c.start()
    return c


def push_pair(src, dst, send, recv):
    c = pltpu.make_async_remote_copy(
        src_ref=src, dst_ref=dst, send_sem=send, recv_sem=recv,
        device_id={"grp": partner()}, device_id_type=MESH,
    )
    c.start()
    return c


GATHER_SEMS = [pltpu.SemaphoreType.DMA((4,))] * 6 + [pltpu.SemaphoreType.DMA((4, 2))] * 2 + [pltpu.SemaphoreType.DMA]


class Gather:
    def __init__(self, src, dst, rows, sems):
        self.src, self.dst, self.rows, self.sems, self.p = src, dst, rows, sems, places()

    def block(self, b):
        return self.dst.at[pl.ds(pl.multiple_of(b * self.rows, self.rows), self.rows)]

    def part(self, b, h):
        half = self.rows // 2
        return self.dst.at[pl.ds(pl.multiple_of(b * self.rows + h * half, half), half)]

    def begin(self):
        zs, zr, xs, xr, ys, yr, _, _, own = self.sems
        p, src = self.p, self.src
        me = p["me"]
        self.mine = pltpu.make_async_copy(src, self.block(me), own)
        self.mine.start()
        self.xc = [push(src, self.block(me), xs.at[0], xr.at[0], p["X"][0])]
        self.yc = [push(src, self.block(me), ys.at[0], yr.at[0], p["Y"][0])]
        self.zc = [push(src, self.block(me), zs.at[k], zr.at[k], p["col"][k]) for k in (1, 2, 3)]
        self.dc = []

    def step(self, k):
        zs, zr, xs, xr, ys, yr, ds, dr, own = self.sems
        p = self.p
        if k < 3:
            self.zc[k].wait_recv()
            b = self.block(p["col"][k + 1])
            self.xc.append(push(b, b, xs.at[k + 1], xr.at[k + 1], p["X"][0]))
            self.yc.append(push(b, b, ys.at[k + 1], yr.at[k + 1], p["Y"][0]))
        b = self.part(p["X"][k], 0)
        self.xc[k].wait_recv()
        self.dc.append(push(b, b, ds.at[k, 0], dr.at[k, 0], p["Y"][0]))
        b = self.part(p["Y"][k], 1)
        self.yc[k].wait_recv()
        self.dc.append(push(b, b, ds.at[k, 1], dr.at[k, 1], p["X"][0]))

    def ready(self, k):
        if k == 0:
            self.mine.wait()
        self.dc[2 * k].wait_recv()
        self.dc[2 * k + 1].wait_recv()

    def end(self):
        for c in self.xc + self.yc + self.zc + self.dc:
            c.wait_send()

    def all(self):
        for k in range(4):
            self.step(k)
        for k in range(4):
            self.ready(k)
        self.end()


def gather_targets():
    p = places()
    return [p["col"][1], p["col"][2], p["col"][3], p["X"][0], p["Y"][0]]


SCATTER_SEMS = [pltpu.SemaphoreType.DMA((4, 2))] * 2 + [pltpu.SemaphoreType.DMA((4,))] * 6


def scatter_bufs(rows, width):
    return [
        pltpu.VMEM((8, rows // 2, width), BF),
        pltpu.VMEM((4, rows, width), BF),
        pltpu.VMEM((4, rows, width), BF),
        pltpu.VMEM((4, rows, width), BF),
    ]


class Scatter:
    def __init__(self, part, out, rows, bufs, sems):
        self.part, self.out, self.half, self.bufs, self.sems, self.p = part, out, rows // 2, bufs, sems, places()
        self.da, self.db, self.xc, self.yc, self.zc = {}, {}, {}, {}, {}

    def far(self, k):
        ds, dr = self.sems[:2]
        rd, h, p = self.bufs[0], self.half, self.p
        b = p["D"][k]
        self.da[k] = push(self.part.at[b, pl.ds(0, h)], rd.at[2 * k], ds.at[k, 0], dr.at[k, 0], p["Y"][0])
        self.db[k] = push(self.part.at[b, pl.ds(h, h)], rd.at[2 * k + 1], ds.at[k, 1], dr.at[k, 1], p["X"][0])

    def near(self, k):
        _, _, xs, xr, ys, yr, _, _ = self.sems
        rd, rx, ry, _ = self.bufs
        part, h, p = self.part, self.half, self.p
        b = p["X"][k]
        self.da[k].wait_recv()
        part[b, pl.ds(0, h)] = (part[b, pl.ds(0, h)].astype(F32) + rd[2 * k].astype(F32)).astype(BF)
        self.xc[k] = push(part.at[b], rx.at[k], xs.at[k], xr.at[k], p["X"][0])
        b = p["Y"][k]
        self.db[k].wait_recv()
        part[b, pl.ds(h, h)] = (part[b, pl.ds(h, h)].astype(F32) + rd[2 * k + 1].astype(F32)).astype(BF)
        self.yc[k] = push(part.at[b], ry.at[k], ys.at[k], yr.at[k], p["Y"][0])

    def along(self, k):
        zs, zr = self.sems[6:]
        _, rx, ry, rz = self.bufs
        part = self.part
        b = self.p["col"][k]
        self.xc[k].wait_recv()
        self.yc[k].wait_recv()
        total = part[b].astype(F32) + rx[k].astype(F32) + ry[k].astype(F32)
        if k:
            part[b] = total.astype(BF)
            self.zc[k] = push(part.at[b], rz.at[k], zs.at[k], zr.at[k], b)
        else:
            self.out[...] = total

    def end(self):
        for k in (1, 2, 3):
            self.zc[k].wait_recv()
            self.out[...] += self.bufs[3][k].astype(F32)
        for group in (self.da, self.db, self.xc, self.yc, self.zc):
            for c in group.values():
                c.wait_send()

    def all(self):
        order = (1, 2, 3, 0)
        for k in order:
            self.far(k)
        for k in order:
            self.near(k)
        for k in order:
            self.along(k)
        self.end()


ANY = pl.BlockSpec(memory_space=pl.ANY)
VM = pl.BlockSpec(memory_space=pltpu.VMEM)


def params(cid, vmem=60):
    return pltpu.CompilerParams(collective_id=cid, has_side_effects=True, vmem_limit_bytes=vmem * MIB)


def front_kernel(n_ref, m_ref, w_ref, nall, mall, wh, *sems):
    g_sems, (ms, mr, mo, ws, wr, ps, pr, wo) = sems[:9], sems[9:]
    me = lax.axis_index("dp")
    core = lax.axis_index("grp") % 2
    barrier([lax.rem(me + d, 16) for d in range(1, 16)], pair=True)
    hr = HD // 2
    g = Gather(n_ref, nall, n_ref.shape[0], g_sems)
    g.begin()
    own = pltpu.make_async_copy(m_ref, mall.at[me], mo)
    own.start()
    mc = []
    for d in range(1, 16):
        to = lax.rem(me + d, 16)
        mc.append(push(m_ref, mall.at[me], ms.at[d], mr.at[d], to))
    off = core * hr
    for l in range(3):
        b = 3 * me + l
        to, slot = lax.rem(b, 16), b // 16
        src = w_ref.at[pl.ds(pl.multiple_of(l * HD + off, hr), hr)]
        dst = wh.at[pl.ds(pl.multiple_of(slot * HD + off, hr), hr)]

        @pl.when(to != me)
        def _():
            push(src, dst, ws.at[l], wr.at[slot], to)

        @pl.when(to == me)
        def _():
            pltpu.make_async_copy(src, dst, wr.at[slot]).start()

    for s in range(3):
        dst = wh.at[pl.ds(pl.multiple_of(s * HD + off, hr), hr)]
        pltpu.make_async_copy(dst, dst, wr.at[s]).wait()
        push_pair(dst, dst, ps.at[s], pr.at[s])
    g.all()
    own.wait()
    for c in mc:
        c.wait()
    for l in range(3):
        b = 3 * me + l
        src = w_ref.at[pl.ds(pl.multiple_of(l * HD + off, hr), hr)]

        @pl.when(lax.rem(b, 16) != me)
        def _():
            pltpu.make_async_copy(src, src, ws.at[l]).wait()

    for s in range(3):
        dst = wh.at[pl.ds(pl.multiple_of(s * HD + off, hr), hr)]
        other = wh.at[pl.ds(pl.multiple_of(s * HD + (hr - off), hr), hr)]
        pltpu.make_async_copy(dst, dst, ps.at[s]).wait()
        pltpu.make_async_copy(other, other, pr.at[s]).wait()


def front(normed, meta, w):
    rows, width = normed.shape
    return pl.pallas_call(
        front_kernel,
        out_shape=[
            jax.ShapeDtypeStruct((16 * rows, width), BF),
            jax.ShapeDtypeStruct((16,) + meta.shape, F32),
            jax.ShapeDtypeStruct((3 * HD, width), BF),
        ],
        in_specs=[ANY] * 3,
        out_specs=[ANY] * 3,
        scratch_shapes=GATHER_SEMS
        + [pltpu.SemaphoreType.DMA((16,)), pltpu.SemaphoreType.DMA((16,)), pltpu.SemaphoreType.DMA]
        + [pltpu.SemaphoreType.DMA((3,))] * 4
        + [pltpu.SemaphoreType.DMA],
        compiler_params=params(0),
        name="front",
    )(normed, meta, w)


def gather_kernel(x_ref, o_ref, *sems):
    barrier(gather_targets())
    g = Gather(x_ref, o_ref, x_ref.shape[0], sems)
    g.begin()
    g.all()


def gather(x, cid):
    rows, width = x.shape
    return pl.pallas_call(
        gather_kernel,
        out_shape=jax.ShapeDtypeStruct((16 * rows, width), x.dtype),
        in_specs=[ANY],
        out_specs=ANY,
        scratch_shapes=GATHER_SEMS,
        compiler_params=params(cid),
        name=f"gather_{cid}",
    )(x)


def swap_kernel(x_ref, o_ref, ss, rs, lo):
    me = lax.axis_index("dp")
    barrier([lax.rem(me + d, 16) for d in range(1, 16)])
    own = pltpu.make_async_copy(x_ref.at[me], o_ref.at[me], lo)
    own.start()
    sent = []
    for d in range(1, 16):
        to = lax.rem(me + d, 16)
        sent.append(push(x_ref.at[to], o_ref.at[me], ss.at[d], rs.at[d], to))
    own.wait()
    for c in sent:
        c.wait()


def swap(x, cid):
    return pl.pallas_call(
        swap_kernel,
        out_shape=jax.ShapeDtypeStruct(x.shape, x.dtype),
        in_specs=[ANY],
        out_specs=ANY,
        scratch_shapes=[pltpu.SemaphoreType.DMA((16,))] * 2 + [pltpu.SemaphoreType.DMA],
        compiler_params=params(cid),
        name=f"swap_{cid}",
    )(x)


QB = 256


def attend_kernel(q, k, v, sq, sk, ctx, lse):
    s = lax.dot_general(q[...], k[...], (((1,), (1,)), ((), ())), preferred_element_type=F32)
    s = jnp.where(sq[...] == sk[...], s, -1e30)
    peak = jnp.maximum(jnp.max(s, -1, keepdims=True), -1e29)
    ex = jnp.exp2((s - peak) * (SCALE * LOG2E))
    total = jnp.maximum(jnp.sum(ex, -1, keepdims=True), 1.0)
    prob = (ex * (1.0 / total)).astype(BF)
    ctx[...] = jnp.dot(prob, v[...], preferred_element_type=F32).astype(BF)
    lse[...] = peak * (SCALE * LOG2E) + jnp.log2(total)


def attend(q, k, v, sq, sk):
    n = q.shape[0]
    row = lambda w: pl.BlockSpec((QB, w), lambda i: (i, 0))
    full = lambda r, w: pl.BlockSpec((r, w), lambda i: (0, 0))
    return pl.pallas_call(
        attend_kernel,
        grid=(n // QB,),
        out_shape=[jax.ShapeDtypeStruct((n, HD), BF), jax.ShapeDtypeStruct((n, 1), F32)],
        in_specs=[row(HD), full(n, HD), full(n, HD), row(1), full(1, n)],
        out_specs=[row(HD), row(1)],
        compiler_params=pltpu.CompilerParams(vmem_limit_bytes=48 * MIB),
        name="attend",
    )(q, k, v, sq, sk)


SLOTS = 80
COLS = 256


def place_of(k, j):
    me = lax.axis_index("dp")
    z, y, x = me // 4, (me // 2) % 2, me % 2
    zk = [z, z + 1 - 2 * (z % 2), (z + 2) % 4, 3 - z][k]
    jy, jx = j // 2, j % 2
    return zk * 4 + (y + jy - 2 * y * jy) * 2 + (x + jx - 2 * x * jx)


def expert_kernel(
    n2, cot, pick, pickt, sw, wg_h, wu_h, wd_h,
    n2g, p1, xr_o, pg_o, hid_o, gg_o, ug_o,
    nall, call, part, stage, wg, wu, wd, xr, pg, hid, gg, ug, rd, rx, ry, rz, wsem, osem, psem, *sems,
):
    rows = n2.shape[0]
    chunk = 4 * SLOTS
    loads = [pltpu.make_async_copy(a, b, wsem.at[i]) for i, (a, b) in enumerate([(wg_h, wg), (wu_h, wu), (wd_h, wd)])]
    for c in loads:
        c.start()
    barrier(gather_targets())
    gn = Gather(n2, nall, rows, sems[:9])
    gc = Gather(cot, call, rows, sems[9:18])
    sc = Scatter(part, n2g, rows, (rd, rx, ry, rz), sems[18:])
    gn.begin()
    gc.begin()
    saves = []
    for k in range(4):
        gn.step(k)
        gc.step(k)
        gn.ready(k)
        gc.ready(k)
        for c in saves:
            c.wait()
        if k == 0:
            for c in loads:
                c.wait()

        def collect(j, carry):
            b = place_of(k, j)
            row = pl.ds(pl.multiple_of(b * rows, rows), rows)
            to = pl.ds(pl.multiple_of(j * SLOTS, SLOTS), SLOTS)

            def cols(n, c):
                w = pl.ds(pl.multiple_of(n * 512, 512), 512)
                xr[to, w] = dot(pick[b], nall[row, w], 1, 0).astype(BF)
                pg[to, w] = (dot(pick[b], call[row, w], 1, 0) * sw[b]).astype(BF)
                return c

            return lax.fori_loop(0, nall.shape[1] // 512, cols, carry)

        lax.fori_loop(0, 4, collect, 0)

        def inner(n, carry):
            w = pl.ds(pl.multiple_of(n * COLS, COLS), COLS)
            gate = dot(xr[...], wg[:, w], 1, 0)
            up = dot(xr[...], wu[:, w], 1, 0)
            hg = dot(pg[...], wd[w, :], 1, 1)
            sig = jax.nn.sigmoid(gate)
            hid[:, w] = (gate * sig * up).astype(BF)
            gg[:, w] = (hg * up * sig * (1.0 + gate * (1.0 - sig))).astype(BF)
            ug[:, w] = (hg * gate * sig).astype(BF)
            return carry

        lax.fori_loop(0, hid.shape[1] // COLS, inner, 0)

        def outer(n, carry):
            w = pl.ds(pl.multiple_of(n * COLS, COLS), COLS)
            eo = dot(hid[...], wd[:, w], 1, 0).astype(BF).astype(F32)
            rg = (dot(gg[...], wg[w, :], 1, 1) + dot(ug[...], wu[w, :], 1, 1)).astype(BF)
            for j in range(4):
                b = place_of(k, j)
                cut = slice(j * SLOTS, (j + 1) * SLOTS)
                weighted = (eo[cut] * sw[b]).astype(BF)
                stage[j, :, w] = dot(pickt[b], weighted, 1, 0).astype(BF)
                part[b, :, w] = dot(pickt[b], rg[cut], 1, 0).astype(BF)
            return carry

        lax.fori_loop(0, xr.shape[1] // COLS, outer, 0)
        sc.far(k)
        if k >= 1:
            sc.near(k - 1)
        if k >= 2:
            sc.along(k - 2)
        saves = [
            pltpu.make_async_copy(a, o.at[k], osem.at[i])
            for i, (a, o) in enumerate([(xr, xr_o), (pg, pg_o), (hid, hid_o), (gg, gg_o), (ug, ug_o)])
        ] + [pltpu.make_async_copy(stage.at[j], p1.at[place_of(k, j)], psem.at[j]) for j in range(4)]
        for c in saves:
            c.start()
    gn.end()
    gc.end()
    sc.near(3)
    sc.along(2)
    sc.along(3)
    sc.end()
    for c in saves:
        c.wait()


def expert(n2, cot, pick, pickt, sw, wg, wu, wd, cid):
    rows, width = n2.shape
    ff = wg.shape[1]
    chunk = 4 * SLOTS
    save = lambda w: jax.ShapeDtypeStruct((4, chunk, w), BF)
    v = lambda *shape: pltpu.VMEM(shape, BF)
    return pl.pallas_call(
        expert_kernel,
        out_shape=[
            jax.ShapeDtypeStruct((rows, width), F32),
            jax.ShapeDtypeStruct((16, rows, width), BF),
            save(width), save(width), save(ff), save(ff), save(ff),
        ],
        in_specs=[ANY, ANY, VM, VM, VM, ANY, ANY, ANY],
        out_specs=[VM] + [ANY] * 6,
        scratch_shapes=[
            v(16 * rows, width), v(16 * rows, width), v(16, rows, width), v(4, rows, width),
            v(width, ff), v(width, ff), v(ff, width),
            v(chunk, width), v(chunk, width), v(chunk, ff), v(chunk, ff), v(chunk, ff),
        ]
        + scatter_bufs(rows, width)
        + [pltpu.SemaphoreType.DMA((3,)), pltpu.SemaphoreType.DMA((5,)), pltpu.SemaphoreType.DMA((4,))]
        + GATHER_SEMS * 2
        + SCATTER_SEMS,
        compiler_params=params(cid, 62),
        name="expert",
    )(n2, cot, pick, pickt, sw, wg, wu, wd)


TILE = (256, 1024)


def weights_kernel(
    p1, xr_h, pg_h, hid_h, gg_h, ug_h,
    mix, gate_o, up_o, down_o,
    part, xr, pg, hid, gg, ug, own, give, got, rd, rx, ry, rz, load, lsem, gs, gr, os_, *sems,
):
    loads = [
        pltpu.make_async_copy(a, b, lsem.at[i])
        for i, (a, b) in enumerate([(p1, part), (xr_h, xr), (gg_h, gg), (ug_h, ug), (hid_h, hid), (pg_h, pg)])
    ]
    for c in loads:
        c.start()
    barrier(gather_targets(), pair=True)
    sc = Scatter(part, mix, part.shape[1], (rd, rx, ry, rz), sems)
    loads[0].wait()
    order = (1, 2, 3, 0)
    for k in order:
        sc.far(k)
    for c in loads[1:]:
        c.wait()
    r, w = TILE

    def product(m, t):
        if m < 2:
            return dot(xr[:, pl.ds(pl.multiple_of(t * r, r), r)], (gg, ug)[m][...], 0, 0)
        i, j = t // 2, t % 2
        return dot(hid[:, pl.ds(pl.multiple_of(i * r, r), r)], pg[:, pl.ds(pl.multiple_of(j * w, w), w)], 0, 0)

    def home(m, t):
        if m < 2:
            return (gate_o, up_o)[m].at[pl.ds(pl.multiple_of(t * r, r), r)]
        i, j = t // 2, t % 2
        return down_o.at[pl.ds(pl.multiple_of(i * r, r), r), pl.ds(pl.multiple_of(j * w, w), w)]

    for m in range(3):

        def sent(t, m=m):
            s = lax.rem(t, 2)
            return pltpu.make_async_remote_copy(
                src_ref=give.at[s], dst_ref=got.at[m, t], send_sem=gs.at[s], recv_sem=gr.at[m, t],
                device_id={"grp": partner()}, device_id_type=MESH,
            )

        def saved(t, m=m):
            s = lax.rem(t, 2)
            return pltpu.make_async_copy(own.at[s], home(m, t), os_.at[s])

        def finish(t, m=m):
            s = lax.rem(t, 2)
            sent(t, m).wait_recv()
            own[s] = own[s] + got[m, t].astype(F32)
            saved(t, m).start()

        def body(t, carry, m=m):
            s = lax.rem(t, 2)

            @pl.when(t >= 2)
            def _():
                sent(t - 2, m).wait_send()
                saved(t - 2, m).wait()

            low = product(m, t).astype(BF)
            give[s] = low
            own[s] = low.astype(F32)
            sent(t, m).start()

            @pl.when(t >= 1)
            def _():
                finish(t - 1, m)

            return carry

        lax.fori_loop(0, 8, body, 0)
        finish(7, m)
        for t in (6, 7):
            sent(t, m).wait_send()
            saved(t, m).wait()
        if m == 0:
            for k in order:
                sc.near(k)
        if m == 1:
            sc.along(1)
            sc.along(2)
    sc.along(3)
    sc.along(0)
    sc.end()


def expert_weights(p1, xr, pg, hid, gg, ug, cid):
    _, rows, width = p1.shape
    n, ff = gg.shape
    r, w = TILE
    v = lambda *shape: pltpu.VMEM(shape, BF)
    return pl.pallas_call(
        weights_kernel,
        out_shape=[
            jax.ShapeDtypeStruct((rows, width), F32),
            jax.ShapeDtypeStruct((width, ff), F32),
            jax.ShapeDtypeStruct((width, ff), F32),
            jax.ShapeDtypeStruct((ff, width), F32),
        ],
        in_specs=[ANY] * 6,
        out_specs=[VM] + [ANY] * 3,
        scratch_shapes=[
            v(16, rows, width), v(n, width), v(n, width), v(n, ff), v(n, ff), v(n, ff),
            pltpu.VMEM((2, r, w), F32), v(2, r, w), v(3, 8, r, w),
        ]
        + scatter_bufs(rows, width)
        + [pltpu.SemaphoreType.DMA, pltpu.SemaphoreType.DMA((6,)), pltpu.SemaphoreType.DMA((2,))]
        + [pltpu.SemaphoreType.DMA((3, 8)), pltpu.SemaphoreType.DMA((2,))]
        + SCATTER_SEMS,
        compiler_params=params(cid, 62),
        name="expert_weights",
    )(p1, xr, pg, hid, gg, ug)


def back_kernel(
    cg, q, k, v, sq, sk, lse, cosf, sinf, wh, nall, ag, ctx,
    ngrad, out_t, qkv_t,
    cgh, dkt, dvt, pgrad, pgt, opart, opair, osum, ostage, ord_, orx, ory, orz,
    part, rd, rx, ry, rz, ntile, qpart, qpair,
    ss, rs, lo, ops, opr, ofs, ofr, nsem, qs, qr, ts, tr, fs, fr, *sems,
):
    me = lax.axis_index("dp")
    core = lax.axis_index("grp") % 2
    hr = HD // 2
    mine, other = pl.multiple_of(core * hr, hr), pl.multiple_of((1 - core) * hr, hr)
    blk = lambda b: pl.ds(pl.multiple_of(b * HD, HD), HD)
    barrier([lax.rem(me + d, 16) for d in range(1, 16)], pair=True)
    hop = lambda d: pltpu.make_async_remote_copy(
        src_ref=cg.at[:, blk(lax.rem(me + d, 16))], dst_ref=cgh.at[blk(me)], send_sem=ss.at[d], recv_sem=rs.at[d],
        device_id={"dp": lax.rem(me + d, 16)}, device_id_type=MESH,
    )
    stay = pltpu.make_async_copy(cg.at[:, blk(me)], cgh.at[blk(me)], lo)
    stay.start()
    for d in range(1, 16):
        hop(d).start()
    tiles = [
        pltpu.make_async_copy(nall.at[:, pl.ds(t * 256, 256)], ntile.at[t % 2], nsem.at[t % 2])
        for t in range(wh.shape[1] // 256)
    ]

    def out_block(b, carry):
        opart[b] = dot(ag[:, blk(b)], ctx[...], 0, 0).astype(BF)
        return carry

    lax.fori_loop(0, 16, out_block, 0)
    pair = push_pair(opart.at[:, pl.ds(other, hr)], opair, ops, opr)
    dkt[...] = jnp.zeros_like(dkt)
    dvt[...] = jnp.zeros_like(dvt)
    so = Scatter(opair, osum, hr, (ord_, orx, ory, orz), sems[:8])
    sn = Scatter(part, ngrad, HD, (rd, rx, ry, rz), sems[8:16])
    pair.wait_recv()

    def out_pair(b, carry):
        opair[b] = (opair[b].astype(F32) + opart[b, pl.ds(mine, hr)].astype(F32)).astype(BF)
        return carry

    lax.fori_loop(0, 16, out_pair, 0)
    stay.wait()
    for d in range(1, 16):
        hop(d).wait_recv()
    order = (1, 2, 3, 0)
    for j in order:
        so.far(j)

    def attend_rows(i, carry):
        row = blk(i)
        s = dot(q[row], k[...], 1, 1)
        prob = jnp.where(sq[row] == sk[...], jnp.exp2(s * (SCALE * LOG2E) - lse[row]), 0.0)
        dp = dot(cgh[row], v[...], 1, 1)
        delta = jnp.sum(prob * dp, -1, keepdims=True)
        ds = (prob * (dp - delta)).astype(BF)
        dq = dot(ds, k[...], 1, 0) * SCALE
        dq = dq * cosf[row] - pltpu.roll(dq, HD // 2, 1) * sinf[row]
        pgrad[row, :HD] = dq.astype(BF)
        pgt[:HD, row] = dq.T.astype(BF)
        dkt[...] += dot(q[row], ds, 0, 0)
        dvt[...] += dot(cgh[row], prob.astype(BF), 0, 0)
        return carry

    n = q.shape[0] // HD
    lax.fori_loop(0, n // 2, attend_rows, 0)
    for j in order:
        so.near(j)
    lax.fori_loop(n // 2, n, attend_rows, 0)
    for j in order:
        so.along(j)

    def turn_back(i, carry):
        row = blk(i)
        dk = dkt[:, row].T * SCALE
        dk = dk * cosf[row] - pltpu.roll(dk, HD // 2, 1) * sinf[row]
        pgrad[row, HD : 2 * HD] = dk.astype(BF)
        pgt[HD : 2 * HD, row] = dk.T.astype(BF)
        dv = dvt[:, row]
        pgrad[row, 2 * HD :] = dv.T.astype(BF)
        pgt[2 * HD :, row] = dv.astype(BF)
        return carry

    lax.fori_loop(0, n, turn_back, 0)
    tiles[0].start()

    def back_block(j, kk):
        b = place_of(kk, j)
        part[b] = dot(pgrad[blk(b)], wh[...], 1, 0).astype(BF)

    for kk in order:
        back_block(3, kk)
        sn.far(kk)
    for t, c in enumerate(tiles):
        if t + 1 < len(tiles):
            tiles[t + 1].start()
        c.wait()
        qpart[:, t * 256 : (t + 1) * 256] = dot(pgt[...], ntile[t % 2], 1, 0).astype(BF)
    qc = [push_pair(qpart.at[pl.ds(s * HD + other, hr)], qpair.at[s], qs.at[s], qr.at[s]) for s in range(3)]
    so.end()
    ostage[...] = osum[...].astype(BF)
    keep = pltpu.make_async_copy(ostage, out_t.at[pl.ds(mine, hr)], lo)
    keep.start()
    give = push_pair(ostage, out_t.at[pl.ds(mine, hr)], ofs, ofr)
    for kk in order:
        back_block(1, kk)
        back_block(2, kk)
        sn.near(kk)
    for s in range(3):
        qc[s].wait_recv()
        qpair[s] = (qpair[s].astype(F32) + qpart[pl.ds(s * HD + mine, hr)].astype(F32)).astype(BF)
        b = 16 * s + me
        to, slot = b // 3, lax.rem(b, 3)
        dst = qkv_t.at[pl.ds(pl.multiple_of(slot * HD + core * hr, hr), hr)]

        @pl.when(to != me)
        def _():
            push(qpair.at[s], dst, ts.at[s], tr.at[slot], to)

        @pl.when(to == me)
        def _():
            pltpu.make_async_copy(qpair.at[s], dst, tr.at[slot]).start()

    for kk in order:
        back_block(0, kk)
    for kk in order:
        sn.along(kk)
    fc = []
    for s in range(3):
        here = qkv_t.at[pl.ds(pl.multiple_of(s * HD + core * hr, hr), hr)]
        pltpu.make_async_copy(here, here, tr.at[s]).wait()
        fc.append(push_pair(here, here, fs.at[s], fr.at[s]))
    sn.end()
    for s in range(3):

        @pl.when((16 * s + me) // 3 != me)
        def _():
            pltpu.make_async_copy(qpair.at[s], qpair.at[s], ts.at[s]).wait()

    keep.wait()
    give.wait()
    pair.wait_send()
    for c in qc:
        c.wait_send()
    for c in fc:
        c.wait()
    for d in range(1, 16):
        hop(d).wait_send()


def back(cg, q, k, v, sq, sk, lse, cosf, sinf, wh, nall, ag, ctx, cid):
    rows, width = cg.shape
    seq = q.shape[0]
    vb = lambda *shape: pltpu.VMEM(shape, BF)
    vf = lambda *shape: pltpu.VMEM(shape, F32)
    sem = lambda *shape: pltpu.SemaphoreType.DMA(shape) if shape else pltpu.SemaphoreType.DMA
    return pl.pallas_call(
        back_kernel,
        out_shape=[
            jax.ShapeDtypeStruct((rows, width), F32),
            jax.ShapeDtypeStruct((rows, width), BF),
            jax.ShapeDtypeStruct((3 * HD, width), BF),
        ],
        in_specs=[ANY] + [VM] * 9 + [ANY, VM, VM],
        out_specs=[VM, ANY, ANY],
        scratch_shapes=[
            vb(seq, HD), vf(HD, seq), vf(HD, seq), vb(seq, 3 * HD), vb(3 * HD, seq),
            vb(16, rows, width), vb(16, rows // 2, width), vf(rows // 2, width), vb(rows // 2, width),
        ]
        + scatter_bufs(rows // 2, width)
        + [vb(16, rows, width)]
        + scatter_bufs(rows, width)
        + [vb(2, seq, 256), vb(3 * HD, width), vb(3, HD // 2, width)]
        + [sem(16), sem(16), sem(), sem(), sem(), sem(), sem(), sem(2), sem(3), sem(3), sem(3), sem(3), sem(3), sem(3)]
        + SCATTER_SEMS * 2,
        compiler_params=params(cid, 62),
        name="back",
    )(cg, q, k, v, sq, sk, lse, cosf, sinf, wh, nall, ag, ctx)


def rmsnorm(field, gain_row):
    return field * lax.rsqrt(jnp.mean(field * field, -1, keepdims=True) + EPS) * gain_row


def rotary_tables(length):
    freq = (THETA ** (-(np.arange(HD // 2) * 2.0 / HD))).astype(np.float32)
    angle = (np.arange(length, dtype=np.float32)[:, None] * freq[None, :]).astype(np.float64)
    cos, sin = np.cos(angle).astype(np.float32), np.sin(angle).astype(np.float32)
    return np.concatenate([cos, cos], 1), np.concatenate([-sin, sin], 1)


def dot(a, b, ca, cb):
    return lax.dot_general(a, b, (((ca,), (cb,)), ((), ())), preferred_element_type=F32)


def per_device(
    tokens, segments, routes, route_weight, capacity, norm_gain,
    qkv_weight, out_weight, gate_weight, up_weight, down_weight, cotangent,
):
    rows, width = tokens.shape
    seq = segments.shape[0]
    me = lax.axis_index("dp")
    slots = SLOTS
    stream = tokens.astype(F32)
    normed = rmsnorm(stream, norm_gain[0]).astype(BF)
    meta = jnp.concatenate([routes.astype(F32).T, route_weight.T], 0)
    normed_all, meta_all, w_head = front(normed, meta, qkv_weight)
    projected = dot(normed_all, w_head, 1, 1)
    cos_table, sin_table = rotary_tables(seq)
    turn = lambda a: a * cos_table + jnp.roll(a, HD // 2, 1) * sin_table
    q = turn(projected[:, :HD]).astype(BF)
    k = turn(projected[:, HD : 2 * HD]).astype(BF)
    v = projected[:, 2 * HD :].astype(BF)
    sq = segments[:, None]
    sk = jnp.where(segments == 0, -1, segments)[None, :]
    ctx_h, lse = attend(q, k, v, sq, sk)
    context = swap(ctx_h.reshape(16, rows, HD), 1).transpose(1, 0, 2).reshape(rows, width)
    dense_out = gather(out_weight, 2)
    attended = dot(context, dense_out, 1, 1)
    middle = stream + attended
    normed2 = rmsnorm(middle, norm_gain[1]).astype(BF)
    mine = meta_all[:, :TOPK] == me.astype(F32)
    member = jnp.sum(mine.astype(F32), 1)
    weight = jnp.sum(jnp.where(mine, meta_all[:, TOPK:], 0.0), 1)
    local = jnp.cumsum(member, 1) - member
    before = jnp.cumsum(jnp.sum(member, 1)) - jnp.sum(member, 1)
    kept = (member > 0) & (local + before[:, None] < capacity[0].astype(F32))
    pick = (jnp.arange(slots, dtype=F32)[None, :, None] == local[:, None, :]) & kept[:, None, :]
    slot_weight = jnp.sum(jnp.where(pick, weight[:, None, :], 0.0), 2)[:, :, None]
    pick = pick.astype(BF)
    n2g, mix_part, xr, pg, hidden, gg, ug = expert(
        normed2, cotangent, pick, pick.transpose(0, 2, 1), slot_weight, gate_weight[0], up_weight[0], down_weight[0], 3
    )
    flat = lambda a: a.reshape(-1, a.shape[2])
    xr, pg, hidden, gg, ug = [flat(a) for a in (xr, pg, hidden, gg, ug)]
    mixture, gate_g, up_g, down_g = expert_weights(mix_part, xr, pg, hidden, gg, ug, 5)
    layer = middle + mixture
    own_seg = lax.dynamic_slice_in_dim(segments, me * rows, rows)
    valid = (own_seg != 0).astype(F32)
    sums = jnp.stack(
        [
            jnp.sum(valid * jnp.sum(layer * layer, -1)),
            jnp.sum(valid * jnp.sum(attended * attended, -1)),
            jnp.sum(valid * jnp.sum(mixture * mixture, -1)),
            jnp.sum(valid) * width,
        ]
    )
    grad = cotangent.astype(F32)
    mg, gain2 = jax.vjp(rmsnorm, middle, norm_gain[1])[1](n2g)
    middle_grad = grad + mg
    attended_grad = middle_grad.astype(BF)
    context_grad = dot(attended_grad, dense_out, 1, 0).astype(BF)
    normed_grad, out_total, qkv_total = back(
        context_grad, q, k, v, sq, sk, lse, cos_table, sin_table, w_head, normed_all, attended_grad, context, 6
    )
    sg, gain1 = jax.vjp(rmsnorm, stream, norm_gain[0])[1](normed_grad)
    tokens_grad = middle_grad + sg
    seq_sums, gain_dp = lax.psum((sums, jnp.stack([gain1, gain2])), "dp")
    stat_row = jnp.sqrt(seq_sums[:3] / seq_sums[3]).reshape(1, 3)
    groups = lax.axis_size("grp")
    over = lambda a: a.astype(F32) if groups == 2 else lax.psum(a.astype(BF), "grp").astype(F32) * 0.5
    return (
        layer.astype(BF),
        tokens_grad,
        over(qkv_total),
        over(out_total),
        over(gate_g)[None],
        over(up_g)[None],
        over(down_g)[None],
        lax.psum(gain_dp.astype(BF), "grp").astype(F32),
        stat_row,
    )


def solution(mesh):
    both = ("grp", "dp")
    in_specs = (
        P(both, None), P("grp"), P(both, None), P(both, None), P(), P(),
        P("dp", None), P("dp", None), P("dp", None, None), P("dp", None, None), P("dp", None, None),
        P(both, None),
    )
    out_specs = (
        P(both, None), P(both, None), P("dp", None), P("dp", None),
        P("dp", None, None), P("dp", None, None), P("dp", None, None), P(), P("grp", None),
    )
    return jax.shard_map(per_device, mesh=mesh, in_specs=in_specs, out_specs=out_specs, check_vma=False)
```

```python
import functools

import jax
import jax.numpy as jnp
import numpy as np
from jax import lax
from jax.experimental import pallas as pl
from jax.experimental.pallas import tpu as pltpu
from jax.sharding import PartitionSpec as P

H = 16
HD = 128
TOPK = 8
EPS = 1e-06
THETA = 50000.0
MESH = pl.DeviceIdType.MESH
MIB = 2**20
BF = jnp.bfloat16
F32 = jnp.float32
SCALE = HD**-0.5
LOG2E = 1.4426950408889634


def places():
    me = lax.axis_index("dp")
    z, y, x = me // 4, (me // 2) % 2, me % 2
    xor = [z, z + 1 - 2 * (z % 2), (z + 2) % 4, 3 - z]
    at = lambda k, yy, xx: xor[k] * 4 + yy * 2 + xx
    return dict(
        me=me,
        col=[at(k, y, x) for k in range(4)],
        X=[at(k, y, 1 - x) for k in range(4)],
        Y=[at(k, 1 - y, x) for k in range(4)],
        D=[at(k, 1 - y, 1 - x) for k in range(4)],
    )


def barrier(targets, pair=False):
    sem = pltpu.get_barrier_semaphore()
    for t in targets:
        pl.semaphore_signal(sem, inc=1, device_id={"dp": t}, device_id_type=MESH)
    count = len(targets)
    if pair:
        pl.semaphore_signal(sem, inc=1, device_id={"grp": partner()}, device_id_type=MESH)
        count += 1
    pl.semaphore_wait(sem, count)


def partner():
    g = lax.axis_index("grp")
    return g + 1 - 2 * (g % 2)


def push(src, dst, send, recv, to):
    c = pltpu.make_async_remote_copy(
        src_ref=src, dst_ref=dst, send_sem=send, recv_sem=recv,
        device_id={"dp": to}, device_id_type=MESH,
    )
    c.start()
    return c


def push_pair(src, dst, send, recv):
    c = pltpu.make_async_remote_copy(
        src_ref=src, dst_ref=dst, send_sem=send, recv_sem=recv,
        device_id={"grp": partner()}, device_id_type=MESH,
    )
    c.start()
    return c


GATHER_SEMS = [pltpu.SemaphoreType.DMA((4,))] * 6 + [pltpu.SemaphoreType.DMA((4, 2))] * 2 + [pltpu.SemaphoreType.DMA]


class Gather:
    def __init__(self, src, dst, rows, sems, first=0):
        self.src, self.dst, self.rows, self.sems, self.first, self.p = src, dst, rows, sems, first, places()

    def block(self, b):
        return self.dst.at[b, pl.ds(self.first, self.rows)]

    def part(self, b, h):
        half = self.rows // 2
        return self.dst.at[b, pl.ds(self.first + h * half, half)]

    def begin(self):
        zs, zr, xs, xr, ys, yr, _, _, own = self.sems
        p, src = self.p, self.src
        me = p["me"]
        self.mine = pltpu.make_async_copy(src, self.block(me), own)
        self.mine.start()
        self.xc = [push(src, self.block(me), xs.at[0], xr.at[0], p["X"][0])]
        self.yc = [push(src, self.block(me), ys.at[0], yr.at[0], p["Y"][0])]
        self.zc = [push(src, self.block(me), zs.at[k], zr.at[k], p["col"][k]) for k in (1, 2, 3)]
        self.dc = []

    def step(self, k):
        zs, zr, xs, xr, ys, yr, ds, dr, own = self.sems
        p = self.p
        if k < 3:
            self.zc[k].wait_recv()
            b = self.block(p["col"][k + 1])
            self.xc.append(push(b, b, xs.at[k + 1], xr.at[k + 1], p["X"][0]))
            self.yc.append(push(b, b, ys.at[k + 1], yr.at[k + 1], p["Y"][0]))
        b = self.part(p["X"][k], 0)
        self.xc[k].wait_recv()
        self.dc.append(push(b, b, ds.at[k, 0], dr.at[k, 0], p["Y"][0]))
        b = self.part(p["Y"][k], 1)
        self.yc[k].wait_recv()
        self.dc.append(push(b, b, ds.at[k, 1], dr.at[k, 1], p["X"][0]))

    def ready(self, k):
        if k == 0:
            self.mine.wait()
        self.dc[2 * k].wait_recv()
        self.dc[2 * k + 1].wait_recv()

    def end(self):
        for c in self.xc + self.yc + self.zc + self.dc:
            c.wait_send()

    def all(self):
        for k in range(4):
            self.step(k)
        for k in range(4):
            self.ready(k)
        self.end()


def gather_targets():
    p = places()
    return [p["col"][1], p["col"][2], p["col"][3], p["X"][0], p["Y"][0]]


SCATTER_SEMS = [pltpu.SemaphoreType.DMA((4, 2))] * 2 + [pltpu.SemaphoreType.DMA((4,))] * 6


def scatter_bufs(rows, width):
    return [
        pltpu.VMEM((8, rows // 2, width), BF),
        pltpu.VMEM((4, rows, width), BF),
        pltpu.VMEM((4, rows, width), BF),
        pltpu.VMEM((4, rows, width), BF),
    ]


class Scatter:
    def __init__(self, part, out, rows, bufs, sems):
        self.part, self.out, self.half, self.bufs, self.sems, self.p = part, out, rows // 2, bufs, sems, places()
        self.da, self.db, self.xc, self.yc, self.zc = {}, {}, {}, {}, {}

    def far(self, k):
        ds, dr = self.sems[:2]
        rd, h, p = self.bufs[0], self.half, self.p
        b = p["D"][k]
        self.da[k] = push(self.part.at[b, pl.ds(0, h)], rd.at[2 * k], ds.at[k, 0], dr.at[k, 0], p["Y"][0])
        self.db[k] = push(self.part.at[b, pl.ds(h, h)], rd.at[2 * k + 1], ds.at[k, 1], dr.at[k, 1], p["X"][0])

    def near(self, k):
        _, _, xs, xr, ys, yr, _, _ = self.sems
        rd, rx, ry, _ = self.bufs
        part, h, p = self.part, self.half, self.p
        b = p["X"][k]
        self.da[k].wait_recv()
        part[b, pl.ds(0, h)] = (part[b, pl.ds(0, h)].astype(F32) + rd[2 * k].astype(F32)).astype(BF)
        self.xc[k] = push(part.at[b], rx.at[k], xs.at[k], xr.at[k], p["X"][0])
        b = p["Y"][k]
        self.db[k].wait_recv()
        part[b, pl.ds(h, h)] = (part[b, pl.ds(h, h)].astype(F32) + rd[2 * k + 1].astype(F32)).astype(BF)
        self.yc[k] = push(part.at[b], ry.at[k], ys.at[k], yr.at[k], p["Y"][0])

    def along(self, k):
        zs, zr = self.sems[6:]
        _, rx, ry, rz = self.bufs
        part = self.part
        b = self.p["col"][k]
        self.xc[k].wait_recv()
        self.yc[k].wait_recv()
        total = part[b].astype(F32) + rx[k].astype(F32) + ry[k].astype(F32)
        if k:
            part[b] = total.astype(BF)
            self.zc[k] = push(part.at[b], rz.at[k], zs.at[k], zr.at[k], b)
        else:
            self.out[...] = total

    def end(self):
        for k in (1, 2, 3):
            self.zc[k].wait_recv()
            self.out[...] += self.bufs[3][k].astype(F32)
        for group in (self.da, self.db, self.xc, self.yc, self.zc):
            for c in group.values():
                c.wait_send()

    def all(self):
        order = (1, 2, 3, 0)
        for k in order:
            self.far(k)
        for k in order:
            self.near(k)
        for k in order:
            self.along(k)
        self.end()


ANY = pl.BlockSpec(memory_space=pl.ANY)
VM = pl.BlockSpec(memory_space=pltpu.VMEM)


def params(cid, vmem=60):
    return pltpu.CompilerParams(collective_id=cid, has_side_effects=True, vmem_limit_bytes=vmem * MIB)


def front_kernel(
    n_ref, m_ref, w_ref, o_ref, cosf, sinf, sq, sk,
    nall_o, mall, wh_o, q, k, v, lse, ctx, oall,
    nall, wh, ctxh, ms, mr, mo, ws, wr, ps, pr, wo, no, cs, cr, co, os_, or_, *sems,
):
    me = lax.axis_index("dp")
    core = lax.axis_index("grp") % 2
    hr = HD // 2
    blk = lambda b: pl.ds(pl.multiple_of(b * HD, HD), HD)
    half = lambda s, c: pl.ds(pl.multiple_of(s * HD + c * hr, hr), hr)
    barrier([lax.rem(me + d, 16) for d in range(1, 16)], pair=True)
    g = Gather(n_ref, nall, n_ref.shape[0], sems[:9])
    go = Gather(o_ref.at[half(0, core)], oall, hr, sems[9:], pl.multiple_of(core * hr, hr))
    g.begin()
    own = pltpu.make_async_copy(m_ref, mall.at[me], mo)
    own.start()
    mc = [push(m_ref, mall.at[me], ms.at[d], mr.at[d], lax.rem(me + d, 16)) for d in range(1, 16)]
    for l in range(3):
        b = 3 * me + l
        to, slot = lax.rem(b, 16), b // 16
        src, dst = w_ref.at[half(l, core)], wh.at[half(slot, core)]

        @pl.when(to != me)
        def _():
            push(src, dst, ws.at[l], wr.at[slot], to)

        @pl.when(to == me)
        def _():
            pltpu.make_async_copy(src, dst, wr.at[slot]).start()

    for c in range(4):
        g.step(c)
        if c == 0:
            pc = []
            for s in range(3):
                dst = wh.at[half(s, core)]
                pltpu.make_async_copy(dst, dst, wr.at[s]).wait()
                pc.append(push_pair(dst, dst, ps.at[s], pr.at[s]))
            for p in pc:
                p.wait_recv()
        if c == 2:
            go.begin()
        g.ready(c)

        def project(j, carry):
            b = place_of(c, j)
            row = blk(b)
            out = dot(nall[b], wh[...], 1, 1)
            turn = lambda a: (a * cosf[row] + pltpu.roll(a, HD // 2, 1) * sinf[row]).astype(BF)
            q[row] = turn(out[:, :HD])
            k[row] = turn(out[:, HD : 2 * HD])
            v[row] = out[:, 2 * HD :].astype(BF)
            return carry

        lax.fori_loop(0, 4, project, 0)
    saves = [pltpu.make_async_copy(nall, nall_o, no), pltpu.make_async_copy(wh, wh_o, wo)]
    for c in saves:
        c.start()

    def hop(d):
        to = lax.rem(me + d, 16)
        return pltpu.make_async_remote_copy(
            src_ref=ctxh.at[blk(to)], dst_ref=ctx.at[:, blk(me)], send_sem=cs.at[d], recv_sem=cr.at[d],
            device_id={"dp": to}, device_id_type=MESH,
        )

    def attend_rows(d, carry):
        row = blk(lax.rem(me + d, 16))
        s = dot(q[row], k[...], 1, 1)
        s = jnp.where(sq[row] == sk[...], s, -1e30)
        peak = jnp.maximum(jnp.max(s, -1, keepdims=True), -1e29)
        ex = jnp.exp2((s - peak) * (SCALE * LOG2E))
        total = jnp.maximum(jnp.sum(ex, -1, keepdims=True), 1.0)
        prob = (ex * (1.0 / total)).astype(BF)
        ctxh[row] = jnp.dot(prob, v[...], preferred_element_type=F32).astype(BF)
        lse[row] = peak * (SCALE * LOG2E) + jnp.log2(total)
        return carry

    def attend_send(d, carry):
        attend_rows(d, carry)
        hop(d).start()
        return carry

    lax.fori_loop(1, 8, attend_send, 0)
    go.step(0)
    lax.fori_loop(8, 16, attend_send, 0)
    attend_rows(0, 0)
    stay = pltpu.make_async_copy(ctxh.at[blk(me)], ctx.at[:, blk(me)], co)
    stay.start()
    for c in (1, 2, 3):
        go.step(c)
    for c in range(4):
        go.ready(c)
    here = oall.at[:, pl.ds(pl.multiple_of(core * hr, hr), hr)]
    oc = push_pair(here, here, os_, or_)
    g.end()
    go.end()
    own.wait()
    for c in mc:
        c.wait()
    for l in range(3):
        src = w_ref.at[half(l, core)]

        @pl.when(lax.rem(3 * me + l, 16) != me)
        def _():
            pltpu.make_async_copy(src, src, ws.at[l]).wait()

    for p in pc:
        p.wait_send()
    for c in saves:
        c.wait()
    stay.wait()
    for d in range(1, 16):
        hop(d).wait()
    oc.wait()


def front(normed, meta, w, wo, cosf, sinf, sq, sk, cid):
    rows, width = normed.shape
    seq = cosf.shape[0]
    sem = lambda *shape: pltpu.SemaphoreType.DMA(shape) if shape else pltpu.SemaphoreType.DMA
    b = lambda *shape: jax.ShapeDtypeStruct(shape, BF)
    f = lambda *shape: jax.ShapeDtypeStruct(shape, F32)
    return pl.pallas_call(
        front_kernel,
        out_shape=[
            b(16, rows, width), f(16, *meta.shape), b(3 * HD, width),
            b(seq, HD), b(seq, HD), b(seq, HD), f(seq, 1), b(rows, width), b(16, rows, width),
        ],
        in_specs=[ANY] * 4 + [VM] * 4,
        out_specs=[ANY] * 3 + [VM] * 4 + [ANY] * 2,
        scratch_shapes=[pltpu.VMEM((16, rows, width), BF), pltpu.VMEM((3 * HD, width), BF), pltpu.VMEM((seq, HD), BF)]
        + [sem(16), sem(16), sem(), sem(3), sem(3), sem(3), sem(3), sem(), sem()]
        + [sem(16), sem(16), sem(), sem(), sem()]
        + GATHER_SEMS * 2,
        compiler_params=params(cid),
        name="front",
    )(normed, meta, w, wo, cosf, sinf, sq, sk)


SLOTS = 80
COLS = 256


def place_of(k, j):
    me = lax.axis_index("dp")
    z, y, x = me // 4, (me // 2) % 2, me % 2
    zk = [z, z + 1 - 2 * (z % 2), (z + 2) % 4, 3 - z][k]
    jy, jx = j // 2, j % 2
    return zk * 4 + (y + jy - 2 * y * jy) * 2 + (x + jx - 2 * x * jx)


def expert_kernel(
    n2, cot, pick, pickt, sw, wg_h, wu_h, wd_h,
    n2g, p1, xr_o, pg_o, hid_o, gg_o, ug_o,
    nall, call, part, stage, wg, wu, wd, xr, pg, hid, gg, ug, rd, rx, ry, rz, wsem, osem, psem, *sems,
):
    rows = n2.shape[0]
    chunk = 4 * SLOTS
    loads = [pltpu.make_async_copy(a, b, wsem.at[i]) for i, (a, b) in enumerate([(wg_h, wg), (wu_h, wu), (wd_h, wd)])]
    for c in loads:
        c.start()
    barrier(gather_targets())
    gn = Gather(n2, nall, rows, sems[:9])
    gc = Gather(cot, call, rows, sems[9:18])
    sc = Scatter(part, n2g, rows, (rd, rx, ry, rz), sems[18:])
    gn.begin()
    gc.begin()
    saves = []
    for k in range(4):
        gn.step(k)
        gc.step(k)
        gn.ready(k)
        gc.ready(k)
        for c in saves:
            c.wait()
        if k == 0:
            for c in loads:
                c.wait()

        def collect(j, carry):
            b = place_of(k, j)
            to = pl.ds(pl.multiple_of(j * SLOTS, SLOTS), SLOTS)

            def cols(n, c):
                w = pl.ds(pl.multiple_of(n * 512, 512), 512)
                xr[to, w] = dot(pick[b], nall[b, :, w], 1, 0).astype(BF)
                pg[to, w] = (dot(pick[b], call[b, :, w], 1, 0) * sw[b]).astype(BF)
                return c

            return lax.fori_loop(0, nall.shape[2] // 512, cols, carry)

        lax.fori_loop(0, 4, collect, 0)

        def inner(n, carry):
            w = pl.ds(pl.multiple_of(n * COLS, COLS), COLS)
            gate = dot(xr[...], wg[:, w], 1, 0)
            up = dot(xr[...], wu[:, w], 1, 0)
            hg = dot(pg[...], wd[w, :], 1, 1)
            sig = jax.nn.sigmoid(gate)
            hid[:, w] = (gate * sig * up).astype(BF)
            gg[:, w] = (hg * up * sig * (1.0 + gate * (1.0 - sig))).astype(BF)
            ug[:, w] = (hg * gate * sig).astype(BF)
            return carry

        lax.fori_loop(0, hid.shape[1] // COLS, inner, 0)

        def outer(n, carry):
            w = pl.ds(pl.multiple_of(n * COLS, COLS), COLS)
            eo = dot(hid[...], wd[:, w], 1, 0).astype(BF).astype(F32)
            rg = (dot(gg[...], wg[w, :], 1, 1) + dot(ug[...], wu[w, :], 1, 1)).astype(BF)
            for j in range(4):
                b = place_of(k, j)
                cut = slice(j * SLOTS, (j + 1) * SLOTS)
                weighted = (eo[cut] * sw[b]).astype(BF)
                stage[j, :, w] = dot(pickt[b], weighted, 1, 0).astype(BF)
                part[b, :, w] = dot(pickt[b], rg[cut], 1, 0).astype(BF)
            return carry

        lax.fori_loop(0, xr.shape[1] // COLS, outer, 0)
        sc.far(k)
        if k >= 1:
            sc.near(k - 1)
        if k >= 2:
            sc.along(k - 2)
        saves = [
            pltpu.make_async_copy(a, o.at[k], osem.at[i])
            for i, (a, o) in enumerate([(xr, xr_o), (pg, pg_o), (hid, hid_o), (gg, gg_o), (ug, ug_o)])
        ] + [pltpu.make_async_copy(stage.at[j], p1.at[place_of(k, j)], psem.at[j]) for j in range(4)]
        for c in saves:
            c.start()
    gn.end()
    gc.end()
    sc.near(3)
    sc.along(2)
    sc.along(3)
    sc.end()
    for c in saves:
        c.wait()


def expert(n2, cot, pick, pickt, sw, wg, wu, wd, cid):
    rows, width = n2.shape
    ff = wg.shape[1]
    chunk = 4 * SLOTS
    save = lambda w: jax.ShapeDtypeStruct((4, chunk, w), BF)
    v = lambda *shape: pltpu.VMEM(shape, BF)
    return pl.pallas_call(
        expert_kernel,
        out_shape=[
            jax.ShapeDtypeStruct((rows, width), F32),
            jax.ShapeDtypeStruct((16, rows, width), BF),
            save(width), save(width), save(ff), save(ff), save(ff),
        ],
        in_specs=[ANY, ANY, VM, VM, VM, ANY, ANY, ANY],
        out_specs=[VM] + [ANY] * 6,
        scratch_shapes=[
            v(16, rows, width), v(16, rows, width), v(16, rows, width), v(4, rows, width),
            v(width, ff), v(width, ff), v(ff, width),
            v(chunk, width), v(chunk, width), v(chunk, ff), v(chunk, ff), v(chunk, ff),
        ]
        + scatter_bufs(rows, width)
        + [pltpu.SemaphoreType.DMA((3,)), pltpu.SemaphoreType.DMA((5,)), pltpu.SemaphoreType.DMA((4,))]
        + GATHER_SEMS * 2
        + SCATTER_SEMS,
        compiler_params=params(cid, 62),
        name="expert",
    )(n2, cot, pick, pickt, sw, wg, wu, wd)


TILE = (256, 1024)


def weights_kernel(
    p1, xr_h, pg_h, hid_h, gg_h, ug_h,
    mix, gate_o, up_o, down_o,
    part, xr, pg, hid, gg, ug, own, give, got, rd, rx, ry, rz, load, lsem, gs, gr, os_, *sems,
):
    loads = [
        pltpu.make_async_copy(a, b, lsem.at[i])
        for i, (a, b) in enumerate([(p1, part), (xr_h, xr), (gg_h, gg), (ug_h, ug), (hid_h, hid), (pg_h, pg)])
    ]
    for c in loads:
        c.start()
    barrier(gather_targets(), pair=True)
    sc = Scatter(part, mix, part.shape[1], (rd, rx, ry, rz), sems)
    loads[0].wait()
    order = (1, 2, 3, 0)
    for k in order:
        sc.far(k)
    for c in loads[1:]:
        c.wait()
    r, w = TILE

    def product(m, t):
        if m < 2:
            return dot(xr[:, pl.ds(pl.multiple_of(t * r, r), r)], (gg, ug)[m][...], 0, 0)
        i, j = t // 2, t % 2
        return dot(hid[:, pl.ds(pl.multiple_of(i * r, r), r)], pg[:, pl.ds(pl.multiple_of(j * w, w), w)], 0, 0)

    def home(m, t):
        if m < 2:
            return (gate_o, up_o)[m].at[pl.ds(pl.multiple_of(t * r, r), r)]
        i, j = t // 2, t % 2
        return down_o.at[pl.ds(pl.multiple_of(i * r, r), r), pl.ds(pl.multiple_of(j * w, w), w)]

    for m in range(3):

        def sent(t, m=m):
            s = lax.rem(t, 2)
            return pltpu.make_async_remote_copy(
                src_ref=give.at[s], dst_ref=got.at[m, t], send_sem=gs.at[s], recv_sem=gr.at[m, t],
                device_id={"grp": partner()}, device_id_type=MESH,
            )

        def saved(t, m=m):
            s = lax.rem(t, 2)
            return pltpu.make_async_copy(own.at[s], home(m, t), os_.at[s])

        def finish(t, m=m):
            s = lax.rem(t, 2)
            sent(t, m).wait_recv()
            own[s] = (own[s].astype(F32) + got[m, t].astype(F32)).astype(BF)
            saved(t, m).start()

        def body(t, carry, m=m):
            s = lax.rem(t, 2)

            @pl.when(t >= 2)
            def _():
                sent(t - 2, m).wait_send()
                saved(t - 2, m).wait()

            low = product(m, t).astype(BF)
            give[s] = low
            own[s] = low
            sent(t, m).start()

            @pl.when(t >= 1)
            def _():
                finish(t - 1, m)

            return carry

        lax.fori_loop(0, 8, body, 0)
        finish(7, m)
        for t in (6, 7):
            sent(t, m).wait_send()
            saved(t, m).wait()
        if m == 0:
            for k in order:
                sc.near(k)
        if m == 1:
            sc.along(1)
            sc.along(2)
    sc.along(3)
    sc.along(0)
    sc.end()


def expert_weights(p1, xr, pg, hid, gg, ug, cid):
    _, rows, width = p1.shape
    n, ff = gg.shape
    r, w = TILE
    v = lambda *shape: pltpu.VMEM(shape, BF)
    return pl.pallas_call(
        weights_kernel,
        out_shape=[
            jax.ShapeDtypeStruct((rows, width), F32),
            jax.ShapeDtypeStruct((width, ff), BF),
            jax.ShapeDtypeStruct((width, ff), BF),
            jax.ShapeDtypeStruct((ff, width), BF),
        ],
        in_specs=[ANY] * 6,
        out_specs=[VM] + [ANY] * 3,
        scratch_shapes=[
            v(16, rows, width), v(n, width), v(n, width), v(n, ff), v(n, ff), v(n, ff),
            v(2, r, w), v(2, r, w), v(3, 8, r, w),
        ]
        + scatter_bufs(rows, width)
        + [pltpu.SemaphoreType.DMA, pltpu.SemaphoreType.DMA((6,)), pltpu.SemaphoreType.DMA((2,))]
        + [pltpu.SemaphoreType.DMA((3, 8)), pltpu.SemaphoreType.DMA((2,))]
        + SCATTER_SEMS,
        compiler_params=params(cid, 62),
        name="expert_weights",
    )(p1, xr, pg, hid, gg, ug)


def back_kernel(
    cg, q, k, v, sq, sk, lse, cosf, sinf, wh, nall, ag, ctx,
    ngrad, out_t, qkv_t,
    cgh, dkt, dvt, pgrad, pgt, opart, opair, osum, ostage, ord_, orx, ory, orz,
    part, rd, rx, ry, rz, ntile, qpart, qpair,
    ss, rs, lo, ops, opr, ofs, ofr, nsem, qs, qr, ts, tr, fs, fr, *sems,
):
    me = lax.axis_index("dp")
    core = lax.axis_index("grp") % 2
    hr = HD // 2
    mine, other = pl.multiple_of(core * hr, hr), pl.multiple_of((1 - core) * hr, hr)
    blk = lambda b: pl.ds(pl.multiple_of(b * HD, HD), HD)
    barrier([lax.rem(me + d, 16) for d in range(1, 16)], pair=True)
    hop = lambda d: pltpu.make_async_remote_copy(
        src_ref=cg.at[:, blk(lax.rem(me + d, 16))], dst_ref=cgh.at[blk(me)], send_sem=ss.at[d], recv_sem=rs.at[d],
        device_id={"dp": lax.rem(me + d, 16)}, device_id_type=MESH,
    )
    stay = pltpu.make_async_copy(cg.at[:, blk(me)], cgh.at[blk(me)], lo)
    stay.start()
    for d in range(1, 16):
        hop(d).start()
    tiles = [
        pltpu.make_async_copy(nall.at[:, pl.ds(t * 256, 256)], ntile.at[t % 2], nsem.at[t % 2])
        for t in range(wh.shape[1] // 256)
    ]

    def out_block(b, carry):
        opart[b] = dot(ag[:, blk(b)], ctx[...], 0, 0).astype(BF)
        return carry

    lax.fori_loop(0, 16, out_block, 0)
    pair = push_pair(opart.at[:, pl.ds(other, hr)], opair, ops, opr)
    dkt[...] = jnp.zeros_like(dkt)
    dvt[...] = jnp.zeros_like(dvt)
    so = Scatter(opair, osum, hr, (ord_, orx, ory, orz), sems[:8])
    sn = Scatter(part, ngrad, HD, (rd, rx, ry, rz), sems[8:16])
    pair.wait_recv()

    def out_pair(b, carry):
        opair[b] = (opair[b].astype(F32) + opart[b, pl.ds(mine, hr)].astype(F32)).astype(BF)
        return carry

    lax.fori_loop(0, 16, out_pair, 0)
    stay.wait()
    for d in range(1, 16):
        hop(d).wait_recv()
    order = (1, 2, 3, 0)
    for j in order:
        so.far(j)

    def attend_rows(i, carry):
        row = blk(i)
        s = dot(q[row], k[...], 1, 1)
        prob = jnp.where(sq[row] == sk[...], jnp.exp2(s * (SCALE * LOG2E) - lse[row]), 0.0)
        dp = dot(cgh[row], v[...], 1, 1)
        delta = jnp.sum(prob * dp, -1, keepdims=True)
        ds = (prob * (dp - delta)).astype(BF)
        dq = dot(ds, k[...], 1, 0) * SCALE
        dq = dq * cosf[row] - pltpu.roll(dq, HD // 2, 1) * sinf[row]
        pgrad[row, :HD] = dq.astype(BF)
        pgt[:HD, row] = dq.T.astype(BF)
        dkt[...] += dot(q[row], ds, 0, 0)
        dvt[...] += dot(cgh[row], prob.astype(BF), 0, 0)
        return carry

    n = q.shape[0] // HD
    lax.fori_loop(0, n // 2, attend_rows, 0)
    for j in order:
        so.near(j)
    lax.fori_loop(n // 2, n, attend_rows, 0)
    for j in order:
        so.along(j)

    def turn_back(i, carry):
        row = blk(i)
        dk = dkt[:, row].T * SCALE
        dk = dk * cosf[row] - pltpu.roll(dk, HD // 2, 1) * sinf[row]
        pgrad[row, HD : 2 * HD] = dk.astype(BF)
        pgt[HD : 2 * HD, row] = dk.T.astype(BF)
        dv = dvt[:, row]
        pgrad[row, 2 * HD :] = dv.T.astype(BF)
        pgt[2 * HD :, row] = dv.astype(BF)
        return carry

    lax.fori_loop(0, n, turn_back, 0)
    tiles[0].start()

    def back_block(j, kk):
        b = place_of(kk, j)
        part[b] = dot(pgrad[blk(b)], wh[...], 1, 0).astype(BF)

    for kk in order:
        back_block(3, kk)
        sn.far(kk)
    for t, c in enumerate(tiles):
        if t + 1 < len(tiles):
            tiles[t + 1].start()
        c.wait()
        qpart[:, t * 256 : (t + 1) * 256] = dot(pgt[...], ntile[t % 2], 1, 0).astype(BF)
    qc = [push_pair(qpart.at[pl.ds(s * HD + other, hr)], qpair.at[s], qs.at[s], qr.at[s]) for s in range(3)]
    so.end()
    ostage[...] = osum[...].astype(BF)
    keep = pltpu.make_async_copy(ostage, out_t.at[pl.ds(mine, hr)], lo)
    keep.start()
    give = push_pair(ostage, out_t.at[pl.ds(mine, hr)], ofs, ofr)
    for kk in order:
        back_block(1, kk)
        back_block(2, kk)
        sn.near(kk)
    for s in range(3):
        qc[s].wait_recv()
        qpair[s] = (qpair[s].astype(F32) + qpart[pl.ds(s * HD + mine, hr)].astype(F32)).astype(BF)
        b = 16 * s + me
        to, slot = b // 3, lax.rem(b, 3)
        dst = qkv_t.at[pl.ds(pl.multiple_of(slot * HD + core * hr, hr), hr)]

        @pl.when(to != me)
        def _():
            push(qpair.at[s], dst, ts.at[s], tr.at[slot], to)

        @pl.when(to == me)
        def _():
            pltpu.make_async_copy(qpair.at[s], dst, tr.at[slot]).start()

    for kk in order:
        back_block(0, kk)
    for kk in order:
        sn.along(kk)
    fc = []
    for s in range(3):
        here = qkv_t.at[pl.ds(pl.multiple_of(s * HD + core * hr, hr), hr)]
        pltpu.make_async_copy(here, here, tr.at[s]).wait()
        fc.append(push_pair(here, here, fs.at[s], fr.at[s]))
    sn.end()
    for s in range(3):

        @pl.when((16 * s + me) // 3 != me)
        def _():
            pltpu.make_async_copy(qpair.at[s], qpair.at[s], ts.at[s]).wait()

    keep.wait()
    give.wait()
    pair.wait_send()
    for c in qc:
        c.wait_send()
    for c in fc:
        c.wait()
    for d in range(1, 16):
        hop(d).wait_send()


def back(cg, q, k, v, sq, sk, lse, cosf, sinf, wh, nall, ag, ctx, cid):
    rows, width = cg.shape
    seq = q.shape[0]
    vb = lambda *shape: pltpu.VMEM(shape, BF)
    vf = lambda *shape: pltpu.VMEM(shape, F32)
    sem = lambda *shape: pltpu.SemaphoreType.DMA(shape) if shape else pltpu.SemaphoreType.DMA
    return pl.pallas_call(
        back_kernel,
        out_shape=[
            jax.ShapeDtypeStruct((rows, width), F32),
            jax.ShapeDtypeStruct((rows, width), BF),
            jax.ShapeDtypeStruct((3 * HD, width), BF),
        ],
        in_specs=[ANY] + [VM] * 9 + [ANY, VM, VM],
        out_specs=[VM, ANY, ANY],
        scratch_shapes=[
            vb(seq, HD), vf(HD, seq), vf(HD, seq), vb(seq, 3 * HD), vb(3 * HD, seq),
            vb(16, rows, width), vb(16, rows // 2, width), vf(rows // 2, width), vb(rows // 2, width),
        ]
        + scatter_bufs(rows // 2, width)
        + [vb(16, rows, width)]
        + scatter_bufs(rows, width)
        + [vb(2, seq, 256), vb(3 * HD, width), vb(3, HD // 2, width)]
        + [sem(16), sem(16), sem(), sem(), sem(), sem(), sem(), sem(2), sem(3), sem(3), sem(3), sem(3), sem(3), sem(3)]
        + SCATTER_SEMS * 2,
        compiler_params=params(cid, 62),
        name="back",
    )(cg, q, k, v, sq, sk, lse, cosf, sinf, wh, nall, ag, ctx)


def total_kernel(x, dp_o, pair_o, got, fromp, ss, rs, ps, pr):
    me = lax.axis_index("dp")
    barrier([lax.rem(me + d, 16) for d in range(1, 16)], pair=True)
    sent = [push(x, got.at[me], ss.at[d], rs.at[d], lax.rem(me + d, 16)) for d in range(1, 16)]
    got[me] = x[...]
    for c in sent:
        c.wait_recv()
    acc = got[0]
    for j in range(1, 16):
        acc = acc + got[j]
    dp_o[...] = acc
    c = push_pair(dp_o, fromp, ps, pr)
    c.wait()
    pair_o[...] = acc + fromp[...]
    for c in sent:
        c.wait_send()


def total(x, cid):
    sem = pltpu.SemaphoreType.DMA
    return pl.pallas_call(
        total_kernel,
        out_shape=[jax.ShapeDtypeStruct(x.shape, F32)] * 2,
        in_specs=[VM],
        out_specs=[VM, VM],
        scratch_shapes=[pltpu.VMEM((16,) + x.shape, F32), pltpu.VMEM(x.shape, F32), sem((16,)), sem((16,)), sem, sem],
        compiler_params=params(cid, 16),
        name="total",
    )(x)


def rmsnorm(field, gain_row):
    return field * lax.rsqrt(jnp.mean(field * field, -1, keepdims=True) + EPS) * gain_row


def rotary_tables(length):
    freq = (THETA ** (-(np.arange(HD // 2) * 2.0 / HD))).astype(np.float32)
    angle = (np.arange(length, dtype=np.float32)[:, None] * freq[None, :]).astype(np.float64)
    cos, sin = np.cos(angle).astype(np.float32), np.sin(angle).astype(np.float32)
    return np.concatenate([cos, cos], 1), np.concatenate([-sin, sin], 1)


def dot(a, b, ca, cb):
    return lax.dot_general(a, b, (((ca,), (cb,)), ((), ())), preferred_element_type=F32)


def per_device(
    tokens, segments, routes, route_weight, capacity, norm_gain,
    qkv_weight, out_weight, gate_weight, up_weight, down_weight, cotangent,
):
    rows, width = tokens.shape
    seq = segments.shape[0]
    me = lax.axis_index("dp")
    slots = SLOTS
    stream = tokens.astype(F32)
    normed = rmsnorm(stream, norm_gain[0]).astype(BF)
    meta = jnp.concatenate([routes.astype(F32).T, route_weight.T], 0)
    sq = segments[:, None]
    sk = jnp.where(segments == 0, -1, segments)[None, :]
    cos_table, sin_table = rotary_tables(seq)
    normed_all, meta_all, w_head, q, k, v, lse, context, dense_out = front(
        normed, meta, qkv_weight, out_weight, cos_table, sin_table, sq, sk, 0
    )
    normed_all = normed_all.reshape(seq, width)
    dense_out = dense_out.reshape(seq, width)
    attended = dot(context, dense_out, 1, 1)
    middle = stream + attended
    normed2 = rmsnorm(middle, norm_gain[1]).astype(BF)
    mine = meta_all[:, :TOPK] == me.astype(F32)
    member = jnp.sum(mine.astype(F32), 1)
    weight = jnp.sum(jnp.where(mine, meta_all[:, TOPK:], 0.0), 1)
    local = jnp.cumsum(member, 1) - member
    before = jnp.cumsum(jnp.sum(member, 1)) - jnp.sum(member, 1)
    kept = (member > 0) & (local + before[:, None] < capacity[0].astype(F32))
    pick = (jnp.arange(slots, dtype=F32)[None, :, None] == local[:, None, :]) & kept[:, None, :]
    slot_weight = jnp.sum(jnp.where(pick, weight[:, None, :], 0.0), 2)[:, :, None]
    pick = pick.astype(BF)
    n2g, mix_part, xr, pg, hidden, gg, ug = expert(
        normed2, cotangent, pick, pick.transpose(0, 2, 1), slot_weight, gate_weight[0], up_weight[0], down_weight[0], 3
    )
    flat = lambda a: a.reshape(-1, a.shape[2])
    xr, pg, hidden, gg, ug = [flat(a) for a in (xr, pg, hidden, gg, ug)]
    mixture, gate_g, up_g, down_g = expert_weights(mix_part, xr, pg, hidden, gg, ug, 5)
    layer = middle + mixture
    own_seg = lax.dynamic_slice_in_dim(segments, me * rows, rows)
    valid = (own_seg != 0).astype(F32)
    sums = jnp.stack(
        [
            jnp.sum(valid * jnp.sum(layer * layer, -1)),
            jnp.sum(valid * jnp.sum(attended * attended, -1)),
            jnp.sum(valid * jnp.sum(mixture * mixture, -1)),
            jnp.sum(valid) * width,
        ]
    )
    grad = cotangent.astype(F32)
    mg, gain2 = jax.vjp(rmsnorm, middle, norm_gain[1])[1](n2g)
    middle_grad = grad + mg
    attended_grad = middle_grad.astype(BF)
    context_grad = dot(attended_grad, dense_out, 1, 0).astype(BF)
    normed_grad, out_total, qkv_total = back(
        context_grad, q, k, v, sq, sk, lse, cos_table, sin_table, w_head, normed_all, attended_grad, context, 6
    )
    sg, gain1 = jax.vjp(rmsnorm, stream, norm_gain[0])[1](normed_grad)
    tokens_grad = middle_grad + sg
    small = jnp.concatenate([gain1, gain2, sums, jnp.zeros((1024 - sums.size,), F32)]).reshape(-1, HD)
    in_group, in_pair = total(small, 4)
    seq_sums = in_group.reshape(-1)[2 * width : 2 * width + 4]
    gain_pair = in_pair.reshape(-1)[: 2 * width].reshape(2, width)
    stat_row = jnp.sqrt(seq_sums[:3] / seq_sums[3]).reshape(1, 3)
    groups = lax.axis_size("grp")
    over = lambda a: a.astype(F32) if groups == 2 else lax.psum(a.astype(BF), "grp").astype(F32) * 0.5
    return (
        layer.astype(BF),
        tokens_grad,
        over(qkv_total),
        over(out_total),
        over(gate_g)[None],
        over(up_g)[None],
        over(down_g)[None],
        gain_pair if groups == 2 else lax.psum(gain_pair, "grp") * 0.5,
        stat_row,
    )


def solution(mesh):
    both = ("grp", "dp")
    in_specs = (
        P(both, None), P("grp"), P(both, None), P(both, None), P(), P(),
        P("dp", None), P("dp", None), P("dp", None, None), P("dp", None, None), P("dp", None, None),
        P(both, None),
    )
    out_specs = (
        P(both, None), P(both, None), P("dp", None), P("dp", None),
        P("dp", None, None), P("dp", None, None), P("dp", None, None), P(), P("grp", None),
    )
    return jax.shard_map(per_device, mesh=mesh, in_specs=in_specs, out_specs=out_specs, check_vma=False)
```

```python
import functools

import jax
import jax.numpy as jnp
import numpy as np
from jax import lax
from jax.experimental import pallas as pl
from jax.experimental.pallas import tpu as pltpu
from jax.sharding import PartitionSpec as P

H = 16
HD = 128
TOPK = 8
EPS = 1e-06
THETA = 50000.0
MESH = pl.DeviceIdType.MESH
MIB = 2**20
BF = jnp.bfloat16
F32 = jnp.float32
SCALE = HD**-0.5
LOG2E = 1.4426950408889634


def places():
    me = lax.axis_index("dp")
    z, y, x = me // 4, (me // 2) % 2, me % 2
    xor = [z, z + 1 - 2 * (z % 2), (z + 2) % 4, 3 - z]
    at = lambda k, yy, xx: xor[k] * 4 + yy * 2 + xx
    return dict(
        me=me,
        col=[at(k, y, x) for k in range(4)],
        X=[at(k, y, 1 - x) for k in range(4)],
        Y=[at(k, 1 - y, x) for k in range(4)],
        D=[at(k, 1 - y, 1 - x) for k in range(4)],
    )


def barrier(targets, pair=False):
    sem = pltpu.get_barrier_semaphore()
    for t in targets:
        pl.semaphore_signal(sem, inc=1, device_id={"dp": t}, device_id_type=MESH)
    count = len(targets)
    if pair:
        pl.semaphore_signal(sem, inc=1, device_id={"grp": partner()}, device_id_type=MESH)
        count += 1
    pl.semaphore_wait(sem, count)


def partner():
    g = lax.axis_index("grp")
    return g + 1 - 2 * (g % 2)


def push(src, dst, send, recv, to):
    c = pltpu.make_async_remote_copy(
        src_ref=src, dst_ref=dst, send_sem=send, recv_sem=recv,
        device_id={"dp": to}, device_id_type=MESH,
    )
    c.start()
    return c


def push_pair(src, dst, send, recv):
    c = pltpu.make_async_remote_copy(
        src_ref=src, dst_ref=dst, send_sem=send, recv_sem=recv,
        device_id={"grp": partner()}, device_id_type=MESH,
    )
    c.start()
    return c


GATHER_SEMS = [pltpu.SemaphoreType.DMA((4,))] * 6 + [pltpu.SemaphoreType.DMA((4, 2))] * 2 + [pltpu.SemaphoreType.DMA]


class Gather:
    def __init__(self, src, dst, rows, sems, first=0):
        self.src, self.dst, self.rows, self.sems, self.first, self.p = src, dst, rows, sems, first, places()

    def block(self, b):
        return self.dst.at[b, pl.ds(self.first, self.rows)]

    def part(self, b, h):
        half = self.rows // 2
        return self.dst.at[b, pl.ds(self.first + h * half, half)]

    def begin(self):
        zs, zr, xs, xr, ys, yr, _, _, own = self.sems
        p, src = self.p, self.src
        me = p["me"]
        self.mine = pltpu.make_async_copy(src, self.block(me), own)
        self.mine.start()
        self.xc = [push(src, self.block(me), xs.at[0], xr.at[0], p["X"][0])]
        self.yc = [push(src, self.block(me), ys.at[0], yr.at[0], p["Y"][0])]
        self.zc = [push(src, self.block(me), zs.at[k], zr.at[k], p["col"][k]) for k in (1, 2, 3)]
        self.dc = []

    def near(self, k):
        _, _, xs, xr, ys, yr, _, _, _ = self.sems
        p = self.p
        self.zc[k - 1].wait_recv()
        b = self.block(p["col"][k])
        self.xc.append(push(b, b, xs.at[k], xr.at[k], p["X"][0]))
        self.yc.append(push(b, b, ys.at[k], yr.at[k], p["Y"][0]))

    def far(self, k):
        ds, dr = self.sems[6:8]
        p = self.p
        b = self.part(p["X"][k], 0)
        self.xc[k].wait_recv()
        self.dc.append(push(b, b, ds.at[k, 0], dr.at[k, 0], p["Y"][0]))
        b = self.part(p["Y"][k], 1)
        self.yc[k].wait_recv()
        self.dc.append(push(b, b, ds.at[k, 1], dr.at[k, 1], p["X"][0]))

    def step(self, k):
        self.far(k)
        if k < 3:
            self.near(k + 1)

    def ready(self, k):
        if k == 0:
            self.mine.wait()
        self.dc[2 * k].wait_recv()
        self.dc[2 * k + 1].wait_recv()

    def end(self):
        for c in self.xc + self.yc + self.zc + self.dc:
            c.wait_send()

    def all(self):
        for k in range(4):
            self.step(k)
        for k in range(4):
            self.ready(k)
        self.end()


def gather_targets():
    p = places()
    return [p["col"][1], p["col"][2], p["col"][3], p["X"][0], p["Y"][0]]


SCATTER_SEMS = [pltpu.SemaphoreType.DMA((4, 2))] * 2 + [pltpu.SemaphoreType.DMA((4,))] * 6


def scatter_bufs(rows, width):
    return [
        pltpu.VMEM((8, rows // 2, width), BF),
        pltpu.VMEM((4, rows, width), BF),
        pltpu.VMEM((4, rows, width), BF),
        pltpu.VMEM((4, rows, width), BF),
    ]


class Scatter:
    def __init__(self, part, out, rows, bufs, sems):
        self.part, self.out, self.half, self.bufs, self.sems, self.p = part, out, rows // 2, bufs, sems, places()
        self.da, self.db, self.xc, self.yc, self.zc = {}, {}, {}, {}, {}

    def far(self, k):
        ds, dr = self.sems[:2]
        rd, h, p = self.bufs[0], self.half, self.p
        b = p["D"][k]
        self.da[k] = push(self.part.at[b, pl.ds(0, h)], rd.at[2 * k], ds.at[k, 0], dr.at[k, 0], p["Y"][0])
        self.db[k] = push(self.part.at[b, pl.ds(h, h)], rd.at[2 * k + 1], ds.at[k, 1], dr.at[k, 1], p["X"][0])

    def near(self, k):
        _, _, xs, xr, ys, yr, _, _ = self.sems
        rd, rx, ry, _ = self.bufs
        part, h, p = self.part, self.half, self.p
        b = p["X"][k]
        self.da[k].wait_recv()
        part[b, pl.ds(0, h)] = (part[b, pl.ds(0, h)].astype(F32) + rd[2 * k].astype(F32)).astype(BF)
        self.xc[k] = push(part.at[b], rx.at[k], xs.at[k], xr.at[k], p["X"][0])
        b = p["Y"][k]
        self.db[k].wait_recv()
        part[b, pl.ds(h, h)] = (part[b, pl.ds(h, h)].astype(F32) + rd[2 * k + 1].astype(F32)).astype(BF)
        self.yc[k] = push(part.at[b], ry.at[k], ys.at[k], yr.at[k], p["Y"][0])

    def along(self, k):
        zs, zr = self.sems[6:]
        _, rx, ry, rz = self.bufs
        part = self.part
        b = self.p["col"][k]
        self.xc[k].wait_recv()
        self.yc[k].wait_recv()
        total = part[b].astype(F32) + rx[k].astype(F32) + ry[k].astype(F32)
        if k:
            part[b] = total.astype(BF)
            self.zc[k] = push(part.at[b], rz.at[k], zs.at[k], zr.at[k], b)
        else:
            self.out[...] = total

    def end(self):
        for k in (1, 2, 3):
            self.zc[k].wait_recv()
            self.out[...] += self.bufs[3][k].astype(F32)
        for group in (self.da, self.db, self.xc, self.yc, self.zc):
            for c in group.values():
                c.wait_send()

    def all(self):
        order = (1, 2, 3, 0)
        for k in order:
            self.far(k)
        for k in order:
            self.near(k)
        for k in order:
            self.along(k)
        self.end()


ANY = pl.BlockSpec(memory_space=pl.ANY)
VM = pl.BlockSpec(memory_space=pltpu.VMEM)


def params(cid, vmem=60):
    return pltpu.CompilerParams(collective_id=cid, has_side_effects=True, vmem_limit_bytes=vmem * MIB)


def front_kernel(
    n_ref, m_ref, w_ref, o_ref, cosf, sinf, sq, sk,
    nall_o, mall, wh_o, q, k, v, lse, ctx, oall,
    nall, wh, ctxh, ms, mr, mo, ws, wr, ps, pr, wo, no, cs, cr, co, os_, or_, *sems,
):
    me = lax.axis_index("dp")
    core = lax.axis_index("grp") % 2
    hr = HD // 2
    blk = lambda b: pl.ds(pl.multiple_of(b * HD, HD), HD)
    half = lambda s, c: pl.ds(pl.multiple_of(s * HD + c * hr, hr), hr)
    barrier([lax.rem(me + d, 16) for d in range(1, 16)], pair=True)
    g = Gather(n_ref, nall, n_ref.shape[0], sems[:9])
    go = Gather(o_ref.at[half(0, core)], oall, hr, sems[9:], pl.multiple_of(core * hr, hr))
    g.begin()
    own = pltpu.make_async_copy(m_ref, mall.at[me], mo)
    own.start()
    mc = [push(m_ref, mall.at[me], ms.at[d], mr.at[d], lax.rem(me + d, 16)) for d in range(1, 16)]
    for l in range(3):
        b = 3 * me + l
        to, slot = lax.rem(b, 16), b // 16
        src, dst = w_ref.at[half(l, core)], wh.at[half(slot, core)]

        @pl.when(to != me)
        def _():
            push(src, dst, ws.at[l], wr.at[slot], to)

        @pl.when(to == me)
        def _():
            pltpu.make_async_copy(src, dst, wr.at[slot]).start()

    def project(b, carry):
        row = blk(b)
        out = dot(nall[b], wh[...], 1, 1)
        turn = lambda a: (a * cosf[row] + pltpu.roll(a, HD // 2, 1) * sinf[row]).astype(BF)
        q[row] = turn(out[:, :HD])
        k[row] = turn(out[:, HD : 2 * HD])
        v[row] = out[:, 2 * HD :].astype(BF)
        return carry

    def project_plane(c):
        lax.fori_loop(0, 4, lambda j, carry: project(place_of(c, j), carry), 0)

    for c in range(4):
        g.step(c)
        if c == WAIT_AT:
            pc = []
            for s in range(3):
                dst = wh.at[half(s, core)]
                pltpu.make_async_copy(dst, dst, wr.at[s]).wait()
                pc.append(push_pair(dst, dst, ps.at[s], pr.at[s]))
        if c == BEGIN_AT:
            go.begin()
        if c == WAIT_AT:
            for p in pc:
                p.wait_recv()
        g.ready(c)
        if c == WAIT_AT:
            for e in range(c):
                project_plane(e)
        if c >= WAIT_AT:
            project_plane(c)
    saves = [pltpu.make_async_copy(nall, nall_o, no), pltpu.make_async_copy(wh, wh_o, wo)]
    for c in saves:
        c.start()

    def hop(d):
        to = lax.rem(me + d, 16)
        return pltpu.make_async_remote_copy(
            src_ref=ctxh.at[blk(to)], dst_ref=ctx.at[:, blk(me)], send_sem=cs.at[d], recv_sem=cr.at[d],
            device_id={"dp": to}, device_id_type=MESH,
        )

    def attend_rows(d, carry):
        row = blk(lax.rem(me + d, 16))
        s = dot(q[row], k[...], 1, 1)
        s = jnp.where(sq[row] == sk[...], s, -1e30)
        peak = jnp.maximum(jnp.max(s, -1, keepdims=True), -1e29)
        ex = jnp.exp2((s - peak) * (SCALE * LOG2E))
        total = jnp.maximum(jnp.sum(ex, -1, keepdims=True), 1.0)
        prob = (ex * (1.0 / total)).astype(BF)
        ctxh[row] = jnp.dot(prob, v[...], preferred_element_type=F32).astype(BF)
        lse[row] = peak * (SCALE * LOG2E) + jnp.log2(total)
        return carry

    def attend_send(d, carry):
        attend_rows(d, carry)
        hop(d).start()
        return carry

    lax.fori_loop(1, 8, attend_send, 0)
    go.step(0)
    lax.fori_loop(8, 16, attend_send, 0)
    attend_rows(0, 0)
    stay = pltpu.make_async_copy(ctxh.at[blk(me)], ctx.at[:, blk(me)], co)
    stay.start()
    for c in (1, 2, 3):
        go.step(c)
    for c in range(4):
        go.ready(c)
    here = oall.at[:, pl.ds(pl.multiple_of(core * hr, hr), hr)]
    oc = push_pair(here, here, os_, or_)
    g.end()
    go.end()
    own.wait()
    for c in mc:
        c.wait()
    for l in range(3):
        src = w_ref.at[half(l, core)]

        @pl.when(lax.rem(3 * me + l, 16) != me)
        def _():
            pltpu.make_async_copy(src, src, ws.at[l]).wait()

    for p in pc:
        p.wait_send()
    for c in saves:
        c.wait()
    stay.wait()
    for d in range(1, 16):
        hop(d).wait()
    oc.wait()


def front(normed, meta, w, wo, cosf, sinf, sq, sk, cid):
    rows, width = normed.shape
    seq = cosf.shape[0]
    sem = lambda *shape: pltpu.SemaphoreType.DMA(shape) if shape else pltpu.SemaphoreType.DMA
    b = lambda *shape: jax.ShapeDtypeStruct(shape, BF)
    f = lambda *shape: jax.ShapeDtypeStruct(shape, F32)
    return pl.pallas_call(
        front_kernel,
        out_shape=[
            b(16, rows, width), f(16, *meta.shape), b(3 * HD, width),
            b(seq, HD), b(seq, HD), b(seq, HD), f(seq, 1), b(rows, width), b(16, rows, width),
        ],
        in_specs=[ANY] * 4 + [VM] * 4,
        out_specs=[ANY] * 3 + [VM] * 4 + [ANY] * 2,
        scratch_shapes=[pltpu.VMEM((16, rows, width), BF), pltpu.VMEM((3 * HD, width), BF), pltpu.VMEM((seq, HD), BF)]
        + [sem(16), sem(16), sem(), sem(3), sem(3), sem(3), sem(3), sem(), sem()]
        + [sem(16), sem(16), sem(), sem(), sem()]
        + GATHER_SEMS * 2,
        compiler_params=params(cid),
        name="front",
    )(normed, meta, w, wo, cosf, sinf, sq, sk)


SLOTS = 80
WAIT_AT = 2
BEGIN_AT = 2
COLS = 256


def place_of(k, j):
    me = lax.axis_index("dp")
    z, y, x = me // 4, (me // 2) % 2, me % 2
    zk = [z, z + 1 - 2 * (z % 2), (z + 2) % 4, 3 - z][k]
    jy, jx = j // 2, j % 2
    return zk * 4 + (y + jy - 2 * y * jy) * 2 + (x + jx - 2 * x * jx)


def expert_kernel(
    n2, cot, pick, pickt, sw, wg_h, wu_h, wd_h,
    n2g, p1, xr_o, pg_o, hid_o, gg_o, ug_o,
    nall, call, part, stage, wg, wu, wd, xr, pg, hid, gg, ug, rd, rx, ry, rz, wsem, osem, psem, *sems,
):
    rows = n2.shape[0]
    chunk = 4 * SLOTS
    loads = [pltpu.make_async_copy(a, b, wsem.at[i]) for i, (a, b) in enumerate([(wg_h, wg), (wu_h, wu), (wd_h, wd)])]
    for c in loads:
        c.start()
    barrier(gather_targets())
    gn = Gather(n2, nall, rows, sems[:9])
    gc = Gather(cot, call, rows, sems[9:18])
    sc = Scatter(part, n2g, rows, (rd, rx, ry, rz), sems[18:])
    gn.begin()
    gc.begin()
    saves = []
    for k in range(4):
        gn.step(k)
        gc.step(k)
        gn.ready(k)
        gc.ready(k)
        for c in saves:
            c.wait()
        if k == 0:
            for c in loads:
                c.wait()

        def collect(j, carry):
            b = place_of(k, j)
            to = pl.ds(pl.multiple_of(j * SLOTS, SLOTS), SLOTS)

            def cols(n, c):
                w = pl.ds(pl.multiple_of(n * 512, 512), 512)
                xr[to, w] = dot(pick[b], nall[b, :, w], 1, 0).astype(BF)
                pg[to, w] = (dot(pick[b], call[b, :, w], 1, 0) * sw[b]).astype(BF)
                return c

            return lax.fori_loop(0, nall.shape[2] // 512, cols, carry)

        lax.fori_loop(0, 4, collect, 0)

        def inner(n, carry):
            w = pl.ds(pl.multiple_of(n * COLS, COLS), COLS)
            gate = dot(xr[...], wg[:, w], 1, 0)
            up = dot(xr[...], wu[:, w], 1, 0)
            hg = dot(pg[...], wd[w, :], 1, 1)
            sig = jax.nn.sigmoid(gate)
            hid[:, w] = (gate * sig * up).astype(BF)
            gg[:, w] = (hg * up * sig * (1.0 + gate * (1.0 - sig))).astype(BF)
            ug[:, w] = (hg * gate * sig).astype(BF)
            return carry

        lax.fori_loop(0, hid.shape[1] // COLS, inner, 0)

        def outer(n, carry):
            w = pl.ds(pl.multiple_of(n * COLS, COLS), COLS)
            eo = dot(hid[...], wd[:, w], 1, 0).astype(BF).astype(F32)
            rg = (dot(gg[...], wg[w, :], 1, 1) + dot(ug[...], wu[w, :], 1, 1)).astype(BF)
            for j in range(4):
                b = place_of(k, j)
                cut = slice(j * SLOTS, (j + 1) * SLOTS)
                weighted = (eo[cut] * sw[b]).astype(BF)
                stage[j, :, w] = dot(pickt[b], weighted, 1, 0).astype(BF)
                part[b, :, w] = dot(pickt[b], rg[cut], 1, 0).astype(BF)
            return carry

        lax.fori_loop(0, xr.shape[1] // COLS, outer, 0)
        sc.far(k)
        if k >= 1:
            sc.near(k - 1)
        if k >= 2:
            sc.along(k - 2)
        saves = [
            pltpu.make_async_copy(a, o.at[k], osem.at[i])
            for i, (a, o) in enumerate([(xr, xr_o), (pg, pg_o), (hid, hid_o), (gg, gg_o), (ug, ug_o)])
        ] + [pltpu.make_async_copy(stage.at[j], p1.at[place_of(k, j)], psem.at[j]) for j in range(4)]
        for c in saves:
            c.start()
    gn.end()
    gc.end()
    sc.near(3)
    sc.along(2)
    sc.along(3)
    sc.end()
    for c in saves:
        c.wait()


def expert(n2, cot, pick, pickt, sw, wg, wu, wd, cid):
    rows, width = n2.shape
    ff = wg.shape[1]
    chunk = 4 * SLOTS
    save = lambda w: jax.ShapeDtypeStruct((4, chunk, w), BF)
    v = lambda *shape: pltpu.VMEM(shape, BF)
    return pl.pallas_call(
        expert_kernel,
        out_shape=[
            jax.ShapeDtypeStruct((rows, width), F32),
            jax.ShapeDtypeStruct((16, rows, width), BF),
            save(width), save(width), save(ff), save(ff), save(ff),
        ],
        in_specs=[ANY, ANY, VM, VM, VM, ANY, ANY, ANY],
        out_specs=[VM] + [ANY] * 6,
        scratch_shapes=[
            v(16, rows, width), v(16, rows, width), v(16, rows, width), v(4, rows, width),
            v(width, ff), v(width, ff), v(ff, width),
            v(chunk, width), v(chunk, width), v(chunk, ff), v(chunk, ff), v(chunk, ff),
        ]
        + scatter_bufs(rows, width)
        + [pltpu.SemaphoreType.DMA((3,)), pltpu.SemaphoreType.DMA((5,)), pltpu.SemaphoreType.DMA((4,))]
        + GATHER_SEMS * 2
        + SCATTER_SEMS,
        compiler_params=params(cid, 62),
        name="expert",
    )(n2, cot, pick, pickt, sw, wg, wu, wd)


TILE = (256, 1024)


def weights_kernel(
    p1, xr_h, pg_h, hid_h, gg_h, ug_h,
    mix, gate_o, up_o, down_o,
    part, xr, pg, hid, gg, ug, own, give, got, rd, rx, ry, rz, load, lsem, gs, gr, os_, *sems,
):
    loads = [
        pltpu.make_async_copy(a, b, lsem.at[i])
        for i, (a, b) in enumerate([(p1, part), (xr_h, xr), (gg_h, gg), (ug_h, ug), (hid_h, hid), (pg_h, pg)])
    ]
    for c in loads:
        c.start()
    barrier(gather_targets(), pair=True)
    sc = Scatter(part, mix, part.shape[1], (rd, rx, ry, rz), sems)
    loads[0].wait()
    order = (1, 2, 3, 0)
    for k in order:
        sc.far(k)
    for c in loads[1:]:
        c.wait()
    r, w = TILE

    def product(m, t):
        if m < 2:
            return dot(xr[:, pl.ds(pl.multiple_of(t * r, r), r)], (gg, ug)[m][...], 0, 0)
        i, j = t // 2, t % 2
        return dot(hid[:, pl.ds(pl.multiple_of(i * r, r), r)], pg[:, pl.ds(pl.multiple_of(j * w, w), w)], 0, 0)

    def home(m, t):
        if m < 2:
            return (gate_o, up_o)[m].at[pl.ds(pl.multiple_of(t * r, r), r)]
        i, j = t // 2, t % 2
        return down_o.at[pl.ds(pl.multiple_of(i * r, r), r), pl.ds(pl.multiple_of(j * w, w), w)]

    for m in range(3):

        def sent(t, m=m):
            s = lax.rem(t, 2)
            return pltpu.make_async_remote_copy(
                src_ref=give.at[s], dst_ref=got.at[m, t], send_sem=gs.at[s], recv_sem=gr.at[m, t],
                device_id={"grp": partner()}, device_id_type=MESH,
            )

        def saved(t, m=m):
            s = lax.rem(t, 2)
            return pltpu.make_async_copy(own.at[s], home(m, t), os_.at[s])

        def finish(t, m=m):
            s = lax.rem(t, 2)
            sent(t, m).wait_recv()
            own[s] = (own[s].astype(F32) + got[m, t].astype(F32)).astype(BF)
            saved(t, m).start()

        def body(t, carry, m=m):
            s = lax.rem(t, 2)

            @pl.when(t >= 2)
            def _():
                sent(t - 2, m).wait_send()
                saved(t - 2, m).wait()

            low = product(m, t).astype(BF)
            give[s] = low
            own[s] = low
            sent(t, m).start()

            @pl.when(t >= 1)
            def _():
                finish(t - 1, m)

            return carry

        lax.fori_loop(0, 8, body, 0)
        finish(7, m)
        for t in (6, 7):
            sent(t, m).wait_send()
            saved(t, m).wait()
        if m == 0:
            for k in order:
                sc.near(k)
        if m == 1:
            sc.along(1)
            sc.along(2)
    sc.along(3)
    sc.along(0)
    sc.end()


def expert_weights(p1, xr, pg, hid, gg, ug, cid):
    _, rows, width = p1.shape
    n, ff = gg.shape
    r, w = TILE
    v = lambda *shape: pltpu.VMEM(shape, BF)
    return pl.pallas_call(
        weights_kernel,
        out_shape=[
            jax.ShapeDtypeStruct((rows, width), F32),
            jax.ShapeDtypeStruct((width, ff), BF),
            jax.ShapeDtypeStruct((width, ff), BF),
            jax.ShapeDtypeStruct((ff, width), BF),
        ],
        in_specs=[ANY] * 6,
        out_specs=[VM] + [ANY] * 3,
        scratch_shapes=[
            v(16, rows, width), v(n, width), v(n, width), v(n, ff), v(n, ff), v(n, ff),
            v(2, r, w), v(2, r, w), v(3, 8, r, w),
        ]
        + scatter_bufs(rows, width)
        + [pltpu.SemaphoreType.DMA, pltpu.SemaphoreType.DMA((6,)), pltpu.SemaphoreType.DMA((2,))]
        + [pltpu.SemaphoreType.DMA((3, 8)), pltpu.SemaphoreType.DMA((2,))]
        + SCATTER_SEMS,
        compiler_params=params(cid, 62),
        name="expert_weights",
    )(p1, xr, pg, hid, gg, ug)


def back_kernel(
    cg, q, k, v, sq, sk, lse, cosf, sinf, wh, nall, ag, ctx,
    ngrad, out_t, qkv_t,
    cgh, dkt, dvt, pgrad, pgt, opart, opair, osum, ostage, ord_, orx, ory, orz,
    part, rd, rx, ry, rz, ntile, qpart, qpair,
    ss, rs, lo, ops, opr, ofs, ofr, nsem, qs, qr, ts, tr, fs, fr, *sems,
):
    me = lax.axis_index("dp")
    core = lax.axis_index("grp") % 2
    hr = HD // 2
    mine, other = pl.multiple_of(core * hr, hr), pl.multiple_of((1 - core) * hr, hr)
    blk = lambda b: pl.ds(pl.multiple_of(b * HD, HD), HD)
    barrier([lax.rem(me + d, 16) for d in range(1, 16)], pair=True)
    hop = lambda d: pltpu.make_async_remote_copy(
        src_ref=cg.at[:, blk(lax.rem(me + d, 16))], dst_ref=cgh.at[blk(me)], send_sem=ss.at[d], recv_sem=rs.at[d],
        device_id={"dp": lax.rem(me + d, 16)}, device_id_type=MESH,
    )
    stay = pltpu.make_async_copy(cg.at[:, blk(me)], cgh.at[blk(me)], lo)
    stay.start()
    for d in range(1, 16):
        hop(d).start()
    tiles = [
        pltpu.make_async_copy(nall.at[:, pl.ds(t * 256, 256)], ntile.at[t % 2], nsem.at[t % 2])
        for t in range(wh.shape[1] // 256)
    ]

    def out_block(b, carry):
        opart[b] = dot(ag[:, blk(b)], ctx[...], 0, 0).astype(BF)
        return carry

    lax.fori_loop(0, 16, out_block, 0)
    pair = push_pair(opart.at[:, pl.ds(other, hr)], opair, ops, opr)
    dkt[...] = jnp.zeros_like(dkt)
    dvt[...] = jnp.zeros_like(dvt)
    so = Scatter(opair, osum, hr, (ord_, orx, ory, orz), sems[:8])
    sn = Scatter(part, ngrad, HD, (rd, rx, ry, rz), sems[8:16])
    pair.wait_recv()

    def out_pair(b, carry):
        opair[b] = (opair[b].astype(F32) + opart[b, pl.ds(mine, hr)].astype(F32)).astype(BF)
        return carry

    lax.fori_loop(0, 16, out_pair, 0)
    stay.wait()
    for d in range(1, 16):
        hop(d).wait_recv()
    order = (1, 2, 3, 0)
    for j in order:
        so.far(j)

    def attend_rows(i, carry):
        row = blk(i)
        s = dot(q[row], k[...], 1, 1)
        prob = jnp.where(sq[row] == sk[...], jnp.exp2(s * (SCALE * LOG2E) - lse[row]), 0.0)
        dp = dot(cgh[row], v[...], 1, 1)
        delta = jnp.sum(prob * dp, -1, keepdims=True)
        ds = (prob * (dp - delta)).astype(BF)
        dq = dot(ds, k[...], 1, 0) * SCALE
        dq = dq * cosf[row] - pltpu.roll(dq, HD // 2, 1) * sinf[row]
        pgrad[row, :HD] = dq.astype(BF)
        pgt[:HD, row] = dq.T.astype(BF)
        dkt[...] += dot(q[row], ds, 0, 0)
        dvt[...] += dot(cgh[row], prob.astype(BF), 0, 0)
        return carry

    n = q.shape[0] // HD
    lax.fori_loop(0, n // 2, attend_rows, 0)
    for j in order:
        so.near(j)
    lax.fori_loop(n // 2, n, attend_rows, 0)
    for j in order:
        so.along(j)

    def turn_back(i, carry):
        row = blk(i)
        dk = dkt[:, row].T * SCALE
        dk = dk * cosf[row] - pltpu.roll(dk, HD // 2, 1) * sinf[row]
        pgrad[row, HD : 2 * HD] = dk.astype(BF)
        pgt[HD : 2 * HD, row] = dk.T.astype(BF)
        dv = dvt[:, row]
        pgrad[row, 2 * HD :] = dv.T.astype(BF)
        pgt[2 * HD :, row] = dv.astype(BF)
        return carry

    lax.fori_loop(0, n, turn_back, 0)
    tiles[0].start()

    def back_block(j, kk):
        b = place_of(kk, j)
        part[b] = dot(pgrad[blk(b)], wh[...], 1, 0).astype(BF)

    for kk in order:
        back_block(3, kk)
        sn.far(kk)
    for t, c in enumerate(tiles):
        if t + 1 < len(tiles):
            tiles[t + 1].start()
        c.wait()
        qpart[:, t * 256 : (t + 1) * 256] = dot(pgt[...], ntile[t % 2], 1, 0).astype(BF)
    qc = [push_pair(qpart.at[pl.ds(s * HD + other, hr)], qpair.at[s], qs.at[s], qr.at[s]) for s in range(3)]
    so.end()
    ostage[...] = osum[...].astype(BF)
    keep = pltpu.make_async_copy(ostage, out_t.at[pl.ds(mine, hr)], lo)
    keep.start()
    give = push_pair(ostage, out_t.at[pl.ds(mine, hr)], ofs, ofr)
    for kk in order:
        back_block(1, kk)
        back_block(2, kk)
        sn.near(kk)
    for s in range(3):
        qc[s].wait_recv()
        qpair[s] = (qpair[s].astype(F32) + qpart[pl.ds(s * HD + mine, hr)].astype(F32)).astype(BF)
        b = 16 * s + me
        to, slot = b // 3, lax.rem(b, 3)
        dst = qkv_t.at[pl.ds(pl.multiple_of(slot * HD + core * hr, hr), hr)]

        @pl.when(to != me)
        def _():
            push(qpair.at[s], dst, ts.at[s], tr.at[slot], to)

        @pl.when(to == me)
        def _():
            pltpu.make_async_copy(qpair.at[s], dst, tr.at[slot]).start()

    for kk in order:
        back_block(0, kk)
    for kk in order:
        sn.along(kk)
    fc = []
    for s in range(3):
        here = qkv_t.at[pl.ds(pl.multiple_of(s * HD + core * hr, hr), hr)]
        pltpu.make_async_copy(here, here, tr.at[s]).wait()
        fc.append(push_pair(here, here, fs.at[s], fr.at[s]))
    sn.end()
    for s in range(3):

        @pl.when((16 * s + me) // 3 != me)
        def _():
            pltpu.make_async_copy(qpair.at[s], qpair.at[s], ts.at[s]).wait()

    keep.wait()
    give.wait()
    pair.wait_send()
    for c in qc:
        c.wait_send()
    for c in fc:
        c.wait()
    for d in range(1, 16):
        hop(d).wait_send()


def back(cg, q, k, v, sq, sk, lse, cosf, sinf, wh, nall, ag, ctx, cid):
    rows, width = cg.shape
    seq = q.shape[0]
    vb = lambda *shape: pltpu.VMEM(shape, BF)
    vf = lambda *shape: pltpu.VMEM(shape, F32)
    sem = lambda *shape: pltpu.SemaphoreType.DMA(shape) if shape else pltpu.SemaphoreType.DMA
    return pl.pallas_call(
        back_kernel,
        out_shape=[
            jax.ShapeDtypeStruct((rows, width), F32),
            jax.ShapeDtypeStruct((rows, width), BF),
            jax.ShapeDtypeStruct((3 * HD, width), BF),
        ],
        in_specs=[ANY] + [VM] * 9 + [ANY, VM, VM],
        out_specs=[VM, ANY, ANY],
        scratch_shapes=[
            vb(seq, HD), vf(HD, seq), vf(HD, seq), vb(seq, 3 * HD), vb(3 * HD, seq),
            vb(16, rows, width), vb(16, rows // 2, width), vf(rows // 2, width), vb(rows // 2, width),
        ]
        + scatter_bufs(rows // 2, width)
        + [vb(16, rows, width)]
        + scatter_bufs(rows, width)
        + [vb(2, seq, 256), vb(3 * HD, width), vb(3, HD // 2, width)]
        + [sem(16), sem(16), sem(), sem(), sem(), sem(), sem(), sem(2), sem(3), sem(3), sem(3), sem(3), sem(3), sem(3)]
        + SCATTER_SEMS * 2,
        compiler_params=params(cid, 62),
        name="back",
    )(cg, q, k, v, sq, sk, lse, cosf, sinf, wh, nall, ag, ctx)


def total_kernel(x, dp_o, pair_o, got, fromp, ss, rs, ps, pr):
    me = lax.axis_index("dp")
    barrier([lax.rem(me + d, 16) for d in range(1, 16)], pair=True)
    sent = [push(x, got.at[me], ss.at[d], rs.at[d], lax.rem(me + d, 16)) for d in range(1, 16)]
    got[me] = x[...]
    for c in sent:
        c.wait_recv()
    acc = got[0]
    for j in range(1, 16):
        acc = acc + got[j]
    dp_o[...] = acc
    c = push_pair(dp_o, fromp, ps, pr)
    c.wait()
    pair_o[...] = acc + fromp[...]
    for c in sent:
        c.wait_send()


def total(x, cid):
    sem = pltpu.SemaphoreType.DMA
    return pl.pallas_call(
        total_kernel,
        out_shape=[jax.ShapeDtypeStruct(x.shape, F32)] * 2,
        in_specs=[VM],
        out_specs=[VM, VM],
        scratch_shapes=[pltpu.VMEM((16,) + x.shape, F32), pltpu.VMEM(x.shape, F32), sem((16,)), sem((16,)), sem, sem],
        compiler_params=params(cid, 16),
        name="total",
    )(x)


def rmsnorm(field, gain_row):
    return field * lax.rsqrt(jnp.mean(field * field, -1, keepdims=True) + EPS) * gain_row


def rotary_tables(length):
    freq = (THETA ** (-(np.arange(HD // 2) * 2.0 / HD))).astype(np.float32)
    angle = (np.arange(length, dtype=np.float32)[:, None] * freq[None, :]).astype(np.float64)
    cos, sin = np.cos(angle).astype(np.float32), np.sin(angle).astype(np.float32)
    return np.concatenate([cos, cos], 1), np.concatenate([-sin, sin], 1)


def dot(a, b, ca, cb):
    return lax.dot_general(a, b, (((ca,), (cb,)), ((), ())), preferred_element_type=F32)


def per_device(
    tokens, segments, routes, route_weight, capacity, norm_gain,
    qkv_weight, out_weight, gate_weight, up_weight, down_weight, cotangent,
):
    rows, width = tokens.shape
    seq = segments.shape[0]
    me = lax.axis_index("dp")
    slots = SLOTS
    stream = tokens.astype(F32)
    normed = rmsnorm(stream, norm_gain[0]).astype(BF)
    meta = jnp.concatenate([routes.astype(F32).T, route_weight.T], 0)
    sq = segments[:, None]
    sk = jnp.where(segments == 0, -1, segments)[None, :]
    cos_table, sin_table = rotary_tables(seq)
    normed_all, meta_all, w_head, q, k, v, lse, context, dense_out = front(
        normed, meta, qkv_weight, out_weight, cos_table, sin_table, sq, sk, 0
    )
    normed_all = normed_all.reshape(seq, width)
    dense_out = dense_out.reshape(seq, width)
    attended = dot(context, dense_out, 1, 1)
    middle = stream + attended
    normed2 = rmsnorm(middle, norm_gain[1]).astype(BF)
    mine = meta_all[:, :TOPK] == me.astype(F32)
    member = jnp.sum(mine.astype(F32), 1)
    weight = jnp.sum(jnp.where(mine, meta_all[:, TOPK:], 0.0), 1)
    local = jnp.cumsum(member, 1) - member
    before = jnp.cumsum(jnp.sum(member, 1)) - jnp.sum(member, 1)
    kept = (member > 0) & (local + before[:, None] < capacity[0].astype(F32))
    pick = (jnp.arange(slots, dtype=F32)[None, :, None] == local[:, None, :]) & kept[:, None, :]
    slot_weight = jnp.sum(jnp.where(pick, weight[:, None, :], 0.0), 2)[:, :, None]
    pick = pick.astype(BF)
    n2g, mix_part, xr, pg, hidden, gg, ug = expert(
        normed2, cotangent, pick, pick.transpose(0, 2, 1), slot_weight, gate_weight[0], up_weight[0], down_weight[0], 3
    )
    flat = lambda a: a.reshape(-1, a.shape[2])
    xr, pg, hidden, gg, ug = [flat(a) for a in (xr, pg, hidden, gg, ug)]
    mixture, gate_g, up_g, down_g = expert_weights(mix_part, xr, pg, hidden, gg, ug, 5)
    layer = middle + mixture
    own_seg = lax.dynamic_slice_in_dim(segments, me * rows, rows)
    valid = (own_seg != 0).astype(F32)
    sums = jnp.stack(
        [
            jnp.sum(valid * jnp.sum(layer * layer, -1)),
            jnp.sum(valid * jnp.sum(attended * attended, -1)),
            jnp.sum(valid * jnp.sum(mixture * mixture, -1)),
            jnp.sum(valid) * width,
        ]
    )
    grad = cotangent.astype(F32)
    mg, gain2 = jax.vjp(rmsnorm, middle, norm_gain[1])[1](n2g)
    middle_grad = grad + mg
    attended_grad = middle_grad.astype(BF)
    context_grad = dot(attended_grad, dense_out, 1, 0).astype(BF)
    normed_grad, out_total, qkv_total = back(
        context_grad, q, k, v, sq, sk, lse, cos_table, sin_table, w_head, normed_all, attended_grad, context, 6
    )
    sg, gain1 = jax.vjp(rmsnorm, stream, norm_gain[0])[1](normed_grad)
    tokens_grad = middle_grad + sg
    small = jnp.concatenate([gain1, gain2, sums, jnp.zeros((1024 - sums.size,), F32)]).reshape(-1, HD)
    in_group, in_pair = total(small, 4)
    seq_sums = in_group.reshape(-1)[2 * width : 2 * width + 4]
    gain_pair = in_pair.reshape(-1)[: 2 * width].reshape(2, width)
    stat_row = jnp.sqrt(seq_sums[:3] / seq_sums[3]).reshape(1, 3)
    groups = lax.axis_size("grp")
    over = lambda a: a.astype(F32) if groups == 2 else lax.psum(a.astype(BF), "grp").astype(F32) * 0.5
    return (
        layer.astype(BF),
        tokens_grad,
        over(qkv_total),
        over(out_total),
        over(gate_g)[None],
        over(up_g)[None],
        over(down_g)[None],
        gain_pair if groups == 2 else lax.psum(gain_pair, "grp") * 0.5,
        stat_row,
    )


def solution(mesh):
    both = ("grp", "dp")
    in_specs = (
        P(both, None), P("grp"), P(both, None), P(both, None), P(), P(),
        P("dp", None), P("dp", None), P("dp", None, None), P("dp", None, None), P("dp", None, None),
        P(both, None),
    )
    out_specs = (
        P(both, None), P(both, None), P("dp", None), P("dp", None),
        P("dp", None, None), P("dp", None, None), P("dp", None, None), P(), P("grp", None),
    )
    return jax.shard_map(per_device, mesh=mesh, in_specs=in_specs, out_specs=out_specs, check_vma=False)
```

```python
import functools

import jax
import jax.numpy as jnp
import numpy as np
from jax import lax
from jax.experimental import pallas as pl
from jax.experimental.pallas import tpu as pltpu
from jax.sharding import PartitionSpec as P

H = 16
HD = 128
TOPK = 8
EPS = 1e-06
THETA = 50000.0
MESH = pl.DeviceIdType.MESH
MIB = 2**20
BF = jnp.bfloat16
F32 = jnp.float32
SCALE = HD**-0.5
LOG2E = 1.4426950408889634


def places():
    me = lax.axis_index("dp")
    z, y, x = me // 4, (me // 2) % 2, me % 2
    xor = [z, z + 1 - 2 * (z % 2), (z + 2) % 4, 3 - z]
    at = lambda k, yy, xx: xor[k] * 4 + yy * 2 + xx
    return dict(
        me=me,
        col=[at(k, y, x) for k in range(4)],
        X=[at(k, y, 1 - x) for k in range(4)],
        Y=[at(k, 1 - y, x) for k in range(4)],
        D=[at(k, 1 - y, 1 - x) for k in range(4)],
    )


def barrier(targets, pair=False):
    sem = pltpu.get_barrier_semaphore()
    for t in targets:
        pl.semaphore_signal(sem, inc=1, device_id={"dp": t}, device_id_type=MESH)
    count = len(targets)
    if pair:
        pl.semaphore_signal(sem, inc=1, device_id={"grp": partner()}, device_id_type=MESH)
        count += 1
    pl.semaphore_wait(sem, count)


def partner():
    g = lax.axis_index("grp")
    return g + 1 - 2 * (g % 2)


def push(src, dst, send, recv, to):
    c = pltpu.make_async_remote_copy(
        src_ref=src, dst_ref=dst, send_sem=send, recv_sem=recv,
        device_id={"dp": to}, device_id_type=MESH,
    )
    c.start()
    return c


def push_pair(src, dst, send, recv):
    c = pltpu.make_async_remote_copy(
        src_ref=src, dst_ref=dst, send_sem=send, recv_sem=recv,
        device_id={"grp": partner()}, device_id_type=MESH,
    )
    c.start()
    return c


GATHER_SEMS = [pltpu.SemaphoreType.DMA((4,))] * 6 + [pltpu.SemaphoreType.DMA((4, 2))] * 2 + [pltpu.SemaphoreType.DMA]


class Gather:
    def __init__(self, src, dst, rows, sems, first=0):
        self.src, self.dst, self.rows, self.sems, self.first, self.p = src, dst, rows, sems, first, places()

    def block(self, b):
        return self.dst.at[b, pl.ds(self.first, self.rows)]

    def part(self, b, h):
        half = self.rows // 2
        return self.dst.at[b, pl.ds(self.first + h * half, half)]

    def begin(self):
        zs, zr, xs, xr, ys, yr, _, _, own = self.sems
        p, src = self.p, self.src
        me = p["me"]
        self.mine = pltpu.make_async_copy(src, self.block(me), own)
        self.mine.start()
        self.xc = {0: push(src, self.block(me), xs.at[0], xr.at[0], p["X"][0])}
        self.yc = {0: push(src, self.block(me), ys.at[0], yr.at[0], p["Y"][0])}
        self.zc = {k: push(src, self.block(me), zs.at[k], zr.at[k], p["col"][k]) for k in (1, 2, 3)}
        self.dc = {}

    def near(self, k):
        _, _, xs, xr, ys, yr, _, _, _ = self.sems
        p = self.p
        self.zc[k].wait_recv()
        b = self.block(p["col"][k])
        self.xc[k] = push(b, b, xs.at[k], xr.at[k], p["X"][0])
        self.yc[k] = push(b, b, ys.at[k], yr.at[k], p["Y"][0])

    def far(self, k):
        ds, dr = self.sems[6:8]
        p = self.p
        b = self.part(p["X"][k], 0)
        self.xc[k].wait_recv()
        self.dc[k, 0] = push(b, b, ds.at[k, 0], dr.at[k, 0], p["Y"][0])
        b = self.part(p["Y"][k], 1)
        self.yc[k].wait_recv()
        self.dc[k, 1] = push(b, b, ds.at[k, 1], dr.at[k, 1], p["X"][0])

    def step(self, k):
        self.far(k)
        if k < 3:
            self.near(k + 1)

    def ready(self, k):
        if k == 0:
            self.mine.wait()
        self.dc[k, 0].wait_recv()
        self.dc[k, 1].wait_recv()

    def end(self):
        for group in (self.xc, self.yc, self.zc, self.dc):
            for c in group.values():
                c.wait_send()

    def all(self):
        for k in range(4):
            self.step(k)
        for k in range(4):
            self.ready(k)
        self.end()


def gather_targets():
    p = places()
    return [p["col"][1], p["col"][2], p["col"][3], p["X"][0], p["Y"][0]]


SCATTER_SEMS = [pltpu.SemaphoreType.DMA((4, 2))] * 2 + [pltpu.SemaphoreType.DMA((4,))] * 6


def scatter_bufs(rows, width):
    return [
        pltpu.VMEM((8, rows // 2, width), BF),
        pltpu.VMEM((4, rows, width), BF),
        pltpu.VMEM((4, rows, width), BF),
        pltpu.VMEM((4, rows, width), BF),
    ]


class Scatter:
    def __init__(self, part, out, rows, bufs, sems):
        self.part, self.out, self.half, self.bufs, self.sems, self.p = part, out, rows // 2, bufs, sems, places()
        self.da, self.db, self.xc, self.yc, self.zc = {}, {}, {}, {}, {}

    def far(self, k):
        ds, dr = self.sems[:2]
        rd, h, p = self.bufs[0], self.half, self.p
        b = p["D"][k]
        self.da[k] = push(self.part.at[b, pl.ds(0, h)], rd.at[2 * k], ds.at[k, 0], dr.at[k, 0], p["Y"][0])
        self.db[k] = push(self.part.at[b, pl.ds(h, h)], rd.at[2 * k + 1], ds.at[k, 1], dr.at[k, 1], p["X"][0])

    def near(self, k):
        _, _, xs, xr, ys, yr, _, _ = self.sems
        rd, rx, ry, _ = self.bufs
        part, h, p = self.part, self.half, self.p
        b = p["X"][k]
        if k in self.da:
            self.da[k].wait_recv()
        part[b, pl.ds(0, h)] = (part[b, pl.ds(0, h)].astype(F32) + rd[2 * k].astype(F32)).astype(BF)
        self.xc[k] = push(part.at[b], rx.at[k], xs.at[k], xr.at[k], p["X"][0])
        b = p["Y"][k]
        if k in self.db:
            self.db[k].wait_recv()
        part[b, pl.ds(h, h)] = (part[b, pl.ds(h, h)].astype(F32) + rd[2 * k + 1].astype(F32)).astype(BF)
        self.yc[k] = push(part.at[b], ry.at[k], ys.at[k], yr.at[k], p["Y"][0])

    def along(self, k):
        zs, zr = self.sems[6:]
        _, rx, ry, rz = self.bufs
        part = self.part
        b = self.p["col"][k]
        self.xc[k].wait_recv()
        self.yc[k].wait_recv()
        total = part[b].astype(F32) + rx[k].astype(F32) + ry[k].astype(F32)
        if k:
            part[b] = total.astype(BF)
            self.zc[k] = push(part.at[b], rz.at[k], zs.at[k], zr.at[k], b)
        else:
            self.out[...] = total

    def end(self):
        for k in (1, 2, 3):
            self.zc[k].wait_recv()
            self.out[...] += self.bufs[3][k].astype(F32)
        for group in (self.da, self.db, self.xc, self.yc, self.zc):
            for c in group.values():
                c.wait_send()

    def all(self):
        order = (1, 2, 3, 0)
        for k in order:
            self.far(k)
        for k in order:
            self.near(k)
        for k in order:
            self.along(k)
        self.end()


ANY = pl.BlockSpec(memory_space=pl.ANY)
VM = pl.BlockSpec(memory_space=pltpu.VMEM)


def params(cid, vmem=60):
    return pltpu.CompilerParams(collective_id=cid, has_side_effects=True, vmem_limit_bytes=vmem * MIB)


def rmsnorm(field, gain_row):
    return field * lax.rsqrt(jnp.mean(field * field, -1, keepdims=True) + EPS) * gain_row


def rmsnorm_pull(field, gain_row, grad):
    r = lax.rsqrt(jnp.mean(field * field, -1, keepdims=True) + EPS)
    scaled = grad * gain_row
    back = r * scaled - field * (r * r * r * jnp.mean(scaled * field, -1, keepdims=True))
    return back, grad * field * r


def column(rows, b):
    return jnp.broadcast_to(rows[pl.ds(b, 1), :], (8, rows.shape[1])).T[:, :1]


def dot(a, b, ca, cb):
    return lax.dot_general(a, b, (((ca,), (cb,)), ((), ())), preferred_element_type=F32)


def front_kernel(
    tok, gain, m_ref, w_ref, o_ref, cosf, sinf, seg, sk,
    nall_o, mall, wh_o, q, k, v, lse, ctx, oall,
    n_ref, nall, wh, ctxh, ms, mr, mo, ws, wr, ps, pr, wo, no, cs, cr, co, os_, or_, *sems,
):
    me = lax.axis_index("dp")
    core = lax.axis_index("grp") % 2
    hr = HD // 2
    blk = lambda b: pl.ds(pl.multiple_of(b * HD, HD), HD)
    half = lambda s, c: pl.ds(pl.multiple_of(s * HD + c * hr, hr), hr)
    n_ref[...] = rmsnorm(tok[...].astype(F32), gain[...]).astype(BF)
    barrier([lax.rem(me + d, 16) for d in range(1, 16)], pair=True)
    g = Gather(n_ref, nall, n_ref.shape[0], sems[:9])
    go = Gather(o_ref.at[half(0, core)], oall, hr, sems[9:], pl.multiple_of(core * hr, hr))
    g.begin()
    own = pltpu.make_async_copy(m_ref, mall.at[me], mo)
    own.start()
    mc = [push(m_ref, mall.at[me], ms.at[d], mr.at[d], lax.rem(me + d, 16)) for d in range(1, 16)]
    for l in range(3):
        b = 3 * me + l
        to, slot = lax.rem(b, 16), b // 16
        src, dst = w_ref.at[half(l, core)], wh.at[half(slot, core)]

        @pl.when(to != me)
        def _():
            push(src, dst, ws.at[l], wr.at[slot], to)

        @pl.when(to == me)
        def _():
            pltpu.make_async_copy(src, dst, wr.at[slot]).start()

    def project(b, carry):
        row = blk(b)
        out = dot(nall[b], wh[...], 1, 1)
        turn = lambda a: (a * cosf[row] + pltpu.roll(a, HD // 2, 1) * sinf[row]).astype(BF)
        q[row] = turn(out[:, :HD])
        k[row] = turn(out[:, HD : 2 * HD])
        v[row] = out[:, 2 * HD :].astype(BF)
        return carry

    def project_plane(c):
        lax.fori_loop(0, 4, lambda j, carry: project(place_of(c, j), carry), 0)

    for c in range(4):
        g.step(c)
        if c == WAIT_AT:
            pc = []
            for s in range(3):
                dst = wh.at[half(s, core)]
                pltpu.make_async_copy(dst, dst, wr.at[s]).wait()
                pc.append(push_pair(dst, dst, ps.at[s], pr.at[s]))
        if c == BEGIN_AT:
            go.begin()
        if c == WAIT_AT:
            for p in pc:
                p.wait_recv()
        g.ready(c)
        if c == WAIT_AT:
            for e in range(c):
                project_plane(e)
        if c >= WAIT_AT:
            project_plane(c)
    saves = [pltpu.make_async_copy(nall, nall_o, no), pltpu.make_async_copy(wh, wh_o, wo)]
    for c in saves:
        c.start()

    def hop(d):
        to = lax.rem(me + d, 16)
        return pltpu.make_async_remote_copy(
            src_ref=ctxh.at[blk(to)], dst_ref=ctx.at[:, blk(me)], send_sem=cs.at[d], recv_sem=cr.at[d],
            device_id={"dp": to}, device_id_type=MESH,
        )

    def attend_rows(d, carry):
        b = lax.rem(me + d, 16)
        row = blk(b)
        s = dot(q[row], k[...], 1, 1)
        s = jnp.where(column(seg, b) == sk[...], s, -1e30)
        peak = jnp.maximum(jnp.max(s, -1, keepdims=True), -1e29)
        ex = jnp.exp2((s - peak) * (SCALE * LOG2E))
        total = jnp.maximum(jnp.sum(ex, -1, keepdims=True), 1.0)
        prob = (ex * (1.0 / total)).astype(BF)
        ctxh[row] = jnp.dot(prob, v[...], preferred_element_type=F32).astype(BF)
        lse[row] = peak * (SCALE * LOG2E) + jnp.log2(total)
        return carry

    def attend_send(d, carry):
        attend_rows(d, carry)
        hop(d).start()
        return carry

    lax.fori_loop(1, 8, attend_send, 0)
    go.step(0)
    lax.fori_loop(8, 16, attend_send, 0)
    attend_rows(0, 0)
    stay = pltpu.make_async_copy(ctxh.at[blk(me)], ctx.at[:, blk(me)], co)
    stay.start()
    for c in (1, 2, 3):
        go.step(c)
    for c in range(4):
        go.ready(c)
    here = oall.at[:, pl.ds(pl.multiple_of(core * hr, hr), hr)]
    oc = push_pair(here, here, os_, or_)
    g.end()
    go.end()
    own.wait()
    for c in mc:
        c.wait()
    for l in range(3):
        src = w_ref.at[half(l, core)]

        @pl.when(lax.rem(3 * me + l, 16) != me)
        def _():
            pltpu.make_async_copy(src, src, ws.at[l]).wait()

    for p in pc:
        p.wait_send()
    for c in saves:
        c.wait()
    stay.wait()
    for d in range(1, 16):
        hop(d).wait()
    oc.wait()


def front(tokens, gain, meta, w, wo, cosf, sinf, seg, sk, cid):
    rows, width = tokens.shape
    seq = cosf.shape[0]
    sem = lambda *shape: pltpu.SemaphoreType.DMA(shape) if shape else pltpu.SemaphoreType.DMA
    b = lambda *shape: jax.ShapeDtypeStruct(shape, BF)
    f = lambda *shape: jax.ShapeDtypeStruct(shape, F32)
    v = lambda *shape: pltpu.VMEM(shape, BF)
    return pl.pallas_call(
        front_kernel,
        out_shape=[
            b(16, rows, width), f(16, *meta.shape), b(3 * HD, width),
            b(seq, HD), b(seq, HD), b(seq, HD), f(seq, 1), b(rows, width), b(16, rows, width),
        ],
        in_specs=[VM, VM] + [ANY] * 3 + [VM] * 4,
        out_specs=[ANY] * 3 + [VM] * 4 + [ANY] * 2,
        scratch_shapes=[v(rows, width), v(16, rows, width), v(3 * HD, width), v(seq, HD)]
        + [sem(16), sem(16), sem(), sem(3), sem(3), sem(3), sem(3), sem(), sem()]
        + [sem(16), sem(16), sem(), sem(), sem()]
        + GATHER_SEMS * 2,
        compiler_params=params(cid),
        name="front",
    )(tokens, gain, meta, w, wo, cosf, sinf, seg, sk)


SLOTS = 80
WAIT_AT = 2
BEGIN_AT = 2
COLS = 512


def place_of(k, j):
    me = lax.axis_index("dp")
    z, y, x = me // 4, (me // 2) % 2, me % 2
    zk = [z, z + 1 - 2 * (z % 2), (z + 2) % 4, 3 - z][k]
    jy, jx = j // 2, j % 2
    return zk * 4 + (y + jy - 2 * y * jy) * 2 + (x + jx - 2 * x * jx)


def expert_kernel(
    ctx, wout, tok, gain, cot, meta, cap, wg_h, wu_h, wd_h,
    att, n2g, p1, rdm, xr_o, pg_o, hid_o, gg_o, ug_o,
    n2, rank, coef, pick, sw, nall, call, part, stage, wg, wu, wd, xr, pg, hid, gg, ug, rd, rx, ry, rz,
    wosem, wsem, osem, psem, ms, mr, *sems,
):
    rows, width = ctx.shape
    wload = pltpu.make_async_copy(wout, part, wosem)
    wload.start()
    barrier(gather_targets())
    gn = Gather(n2, nall, rows, sems[:9])
    gc = Gather(cot, call, rows, sems[9:18])
    sc = Scatter(part, n2g, rows, (rd, rx, ry, rz), sems[18:])
    sm = Scatter(p1, None, rows, (rdm, None, None, None), (ms, mr))
    gc.begin()
    loads = [pltpu.make_async_copy(a, b, wsem.at[i]) for i, (a, b) in enumerate([(wg_h, wg), (wu_h, wu), (wd_h, wd)])]
    me = lax.axis_index("dp").astype(F32)
    hits = [meta[:, r, :] == me for r in range(TOPK)]
    member = sum(h.astype(F32) for h in hits)
    coef[...] = sum(jnp.where(h, meta[:, TOPK + r, :], 0.0) for r, h in enumerate(hits))
    i0, i1 = lax.broadcasted_iota(jnp.int32, (HD, HD), 0), lax.broadcasted_iota(jnp.int32, (HD, HD), 1)
    local = dot(member.astype(BF), (i0 < i1).astype(BF), 1, 0)
    count = jnp.broadcast_to(jnp.sum(member, 1, keepdims=True), member.shape).astype(BF)
    j0, j1 = lax.broadcasted_iota(jnp.int32, (16, 16), 0), lax.broadcasted_iota(jnp.int32, (16, 16), 1)
    before = dot((j1 < j0).astype(BF), count, 1, 0)
    kept = (member > 0.0) & (local + before < cap[0].astype(F32))
    rank[...] = jnp.where(kept, local, -1.0)
    wload.wait()

    def attend_cols(t, carry):
        w = part[pl.ds(2 * t, 2)].reshape(2 * rows, width)
        att[:, pl.ds(pl.multiple_of(t * 2 * rows, 2 * rows), 2 * rows)] = dot(ctx[...], w, 1, 1)
        return carry

    lax.fori_loop(0, 8, attend_cols, 0)
    n2[...] = rmsnorm(tok[...].astype(F32) + att[...], gain[...]).astype(BF)
    gn.begin()
    for c in loads:
        c.start()
    saves = []
    gc.near(1)
    gn.near(1)
    order = (1, 2, 3, 0)
    for i, k in enumerate(order):
        for g in (gn, gc):
            if i < 3:
                g.far(k)
            if i < 2:
                g.near(order[i + 1])
            if i == 2:
                g.far(0)
        gn.ready(k)
        gc.ready(k)
        if i >= 1:
            sc.near(order[i - 1])
        if i >= 2:
            sc.along(order[i - 2])
        for c in saves:
            c.wait()
        if i == 0:
            for c in loads:
                c.wait()
        if i == 3:
            sm.far(1)
            sm.far(2)

        def collect(j, carry):
            b = place_of(k, j)
            to = pl.ds(pl.multiple_of(j * SLOTS, SLOTS), SLOTS)
            s0 = lax.broadcasted_iota(jnp.int32, (SLOTS, rows), 0).astype(F32)
            mine = s0 == rank[pl.ds(b, 1), :]
            sw[to, :] = jnp.sum(jnp.where(mine, coef[pl.ds(b, 1), :], 0.0), 1, keepdims=True)
            pick[to, :] = mine.astype(BF)

            def cols(n, c):
                w = pl.ds(pl.multiple_of(n * 512, 512), 512)
                xr[to, w] = dot(pick[to, :], nall[b, :, w], 1, 0).astype(BF)
                pg[to, w] = (dot(pick[to, :], call[b, :, w], 1, 0) * sw[to, :]).astype(BF)
                return c

            return lax.fori_loop(0, width // 512, cols, carry)

        lax.fori_loop(0, 4, collect, 0)

        def inner(n, carry):
            w = pl.ds(pl.multiple_of(n * COLS, COLS), COLS)
            gate = dot(xr[...], wg[:, w], 1, 0)
            up = dot(xr[...], wu[:, w], 1, 0)
            hg = dot(pg[...], wd[w, :], 1, 1)
            sig = jax.nn.sigmoid(gate)
            hid[:, w] = (gate * sig * up).astype(BF)
            gg[:, w] = (hg * up * sig * (1.0 + gate * (1.0 - sig))).astype(BF)
            ug[:, w] = (hg * gate * sig).astype(BF)
            return carry

        lax.fori_loop(0, hid.shape[1] // COLS, inner, 0)

        def outer(n, carry):
            w = pl.ds(pl.multiple_of(n * COLS, COLS), COLS)
            eo = dot(hid[...], wd[:, w], 1, 0).astype(BF).astype(F32)
            rg = (dot(gg[...], wg[w, :], 1, 1) + dot(ug[...], wu[w, :], 1, 1)).astype(BF)
            for j in range(4):
                b = place_of(k, j)
                cut = slice(j * SLOTS, (j + 1) * SLOTS)
                weighted = (eo[cut] * sw[cut]).astype(BF)
                stage[j, :, w] = dot(pick[cut], weighted, 0, 0).astype(BF)
                part[b, :, w] = dot(pick[cut], rg[cut], 0, 0).astype(BF)
            return carry

        lax.fori_loop(0, xr.shape[1] // COLS, outer, 0)
        sc.far(k)
        saves = [
            pltpu.make_async_copy(a, o.at[k], osem.at[i])
            for i, (a, o) in enumerate([(xr, xr_o), (pg, pg_o), (hid, hid_o), (gg, gg_o), (ug, ug_o)])
        ] + [pltpu.make_async_copy(stage.at[j], p1.at[place_of(k, j)], psem.at[j]) for j in range(4)]
        for c in saves:
            c.start()
    gn.end()
    gc.end()
    sc.along(3)
    sc.near(0)
    for c in saves:
        c.wait()
    sm.far(3)
    sm.far(0)
    sc.along(0)
    sc.end()
    for c in list(sm.da.values()) + list(sm.db.values()):
        c.wait()


def expert(ctx, wout, tokens, gain, cot, meta, cap, wg, wu, wd, cid):
    rows, width = ctx.shape
    ff = wg.shape[1]
    chunk = 4 * SLOTS
    save = lambda w: jax.ShapeDtypeStruct((4, chunk, w), BF)
    v = lambda *shape: pltpu.VMEM(shape, BF)
    f = lambda *shape: pltpu.VMEM(shape, F32)
    return pl.pallas_call(
        expert_kernel,
        out_shape=[
            jax.ShapeDtypeStruct((rows, width), F32),
            jax.ShapeDtypeStruct((rows, width), F32),
            jax.ShapeDtypeStruct((16, rows, width), BF),
            jax.ShapeDtypeStruct((8, rows // 2, width), BF),
            save(width), save(width), save(ff), save(ff), save(ff),
        ],
        in_specs=[VM, ANY, VM, VM, ANY, VM, pl.BlockSpec(memory_space=pltpu.SMEM), ANY, ANY, ANY],
        out_specs=[VM, VM] + [ANY] * 7,
        scratch_shapes=[
            v(rows, width), f(16, rows), f(16, rows), v(chunk, rows), f(chunk, 1),
            v(16, rows, width), v(16, rows, width), v(16, rows, width), v(4, rows, width),
            v(width, ff), v(width, ff), v(ff, width),
            v(chunk, width), v(chunk, width), v(chunk, ff), v(chunk, ff), v(chunk, ff),
        ]
        + scatter_bufs(rows, width)
        + [pltpu.SemaphoreType.DMA, pltpu.SemaphoreType.DMA((3,)), pltpu.SemaphoreType.DMA((5,)), pltpu.SemaphoreType.DMA((4,))]
        + [pltpu.SemaphoreType.DMA((4, 2))] * 2
        + GATHER_SEMS * 2
        + SCATTER_SEMS,
        compiler_params=params(cid, 62),
        name="expert",
    )(ctx, wout, tokens, gain, cot, meta, cap, wg, wu, wd)


TILE = (256, 1024)


def weights_kernel(
    p1, rdm, xr_h, pg_h, hid_h, gg_h, ug_h, wout, n2g, tok, att, cot, gain,
    mix, gate_o, up_o, down_o, ag, mg, gain_g, cgh,
    part, wo, cg, xr, pg, hid, gg, ug, own, give, got, rd, rx, ry, rz, lsem, wsem, gs, gr, os_, cs, cr, co, *sems,
):
    me = lax.axis_index("dp")
    blk = lambda b: pl.ds(pl.multiple_of(b * HD, HD), HD)
    loads = [
        pltpu.make_async_copy(a, b, lsem.at[i])
        for i, (a, b) in enumerate(
            [(p1, part), (rdm, rd), (xr_h, xr), (gg_h, gg), (ug_h, ug), (hid_h, hid), (pg_h, pg)]
        )
    ]
    column_load = lambda t: pltpu.make_async_copy(
        wout.at[:, pl.ds(pl.multiple_of(t * 256, 256), 256)], wo.at[lax.rem(t, 2)], wsem.at[lax.rem(t, 2)]
    )
    column_load(0).start()
    for c in loads:
        c.start()
    back, gains = rmsnorm_pull(tok[...].astype(F32) + att[...], gain[...], n2g[...])
    gain_g[...] = jnp.sum(gains, 0, keepdims=True)
    mg[...] = cot[...].astype(F32) + back
    ag[...] = mg[...].astype(BF)
    barrier([lax.rem(me + d, 16) for d in range(1, 16)], pair=True)
    sc = Scatter(part, mix, part.shape[1], (rd, rx, ry, rz), sems)
    tiles = cg.shape[1] // 256

    def context_cols(t, carry):
        @pl.when(t + 1 < tiles)
        def _():
            column_load(t + 1).start()

        column_load(t).wait()
        cols = pl.ds(pl.multiple_of(t * 256, 256), 256)
        cg[:, cols] = dot(ag[...], wo[lax.rem(t, 2)], 1, 0).astype(BF)
        return carry

    lax.fori_loop(0, tiles, context_cols, 0)

    def hop(d):
        to = lax.rem(me + d, 16)
        return pltpu.make_async_remote_copy(
            src_ref=cg.at[:, blk(to)], dst_ref=cgh.at[blk(me)], send_sem=cs.at[d], recv_sem=cr.at[d],
            device_id={"dp": to}, device_id_type=MESH,
        )

    for d in range(1, 16):
        hop(d).start()
    stay = pltpu.make_async_copy(cg.at[:, blk(me)], cgh.at[blk(me)], co)
    stay.start()
    loads[0].wait()
    loads[1].wait()
    order = (1, 2, 3, 0)
    for k in order:
        sc.near(k)
    for c in loads[2:]:
        c.wait()
    r, w = TILE

    def product(m, t):
        if m < 2:
            return dot(xr[:, pl.ds(pl.multiple_of(t * r, r), r)], (gg, ug)[m][...], 0, 0)
        i, j = t // 2, t % 2
        return dot(hid[:, pl.ds(pl.multiple_of(i * r, r), r)], pg[:, pl.ds(pl.multiple_of(j * w, w), w)], 0, 0)

    def home(m, t):
        if m < 2:
            return (gate_o, up_o)[m].at[pl.ds(pl.multiple_of(t * r, r), r)]
        i, j = t // 2, t % 2
        return down_o.at[pl.ds(pl.multiple_of(i * r, r), r), pl.ds(pl.multiple_of(j * w, w), w)]

    for m in range(3):

        def sent(t, m=m):
            s = lax.rem(t, 2)
            return pltpu.make_async_remote_copy(
                src_ref=give.at[s], dst_ref=got.at[m, t], send_sem=gs.at[s], recv_sem=gr.at[m, t],
                device_id={"grp": partner()}, device_id_type=MESH,
            )

        def saved(t, m=m):
            s = lax.rem(t, 2)
            return pltpu.make_async_copy(own.at[s], home(m, t), os_.at[s])

        def finish(t, m=m):
            s = lax.rem(t, 2)
            sent(t, m).wait_recv()
            own[s] = (own[s].astype(F32) + got[m, t].astype(F32)).astype(BF)
            saved(t, m).start()

        def body(t, carry, m=m):
            s = lax.rem(t, 2)

            @pl.when(t >= 2)
            def _():
                sent(t - 2, m).wait_send()
                saved(t - 2, m).wait()

            low = product(m, t).astype(BF)
            give[s] = low
            own[s] = low
            sent(t, m).start()

            @pl.when(t >= 1)
            def _():
                finish(t - 1, m)

            return carry

        lax.fori_loop(0, 8, body, 0)
        finish(7, m)
        for t in (6, 7):
            sent(t, m).wait_send()
            saved(t, m).wait()
        if m == 0:
            sc.along(1)
        if m == 1:
            sc.along(2)
            sc.along(3)
    sc.along(0)
    sc.end()
    stay.wait()
    for d in range(1, 16):
        hop(d).wait()


def expert_weights(p1, rdm, xr, pg, hid, gg, ug, wout, n2g, tokens, att, cot, gain, cid):
    _, rows, width = p1.shape
    n, ff = gg.shape
    seq = wout.shape[0]
    r, w = TILE
    v = lambda *shape: pltpu.VMEM(shape, BF)
    sem = lambda *shape: pltpu.SemaphoreType.DMA(shape) if shape else pltpu.SemaphoreType.DMA
    b = lambda *shape: jax.ShapeDtypeStruct(shape, BF)
    f = lambda *shape: jax.ShapeDtypeStruct(shape, F32)
    return pl.pallas_call(
        weights_kernel,
        out_shape=[
            f(rows, width), b(width, ff), b(width, ff), b(ff, width), b(rows, width), f(rows, width), f(1, width),
            b(16 * rows, HD),
        ],
        in_specs=[ANY] * 8 + [VM] * 5,
        out_specs=[VM] + [ANY] * 3 + [VM] * 3 + [ANY],
        scratch_shapes=[
            v(16, rows, width), v(2, seq, 256), v(rows, width),
            v(n, width), v(n, width), v(n, ff), v(n, ff), v(n, ff), v(2, r, w), v(2, r, w), v(3, 8, r, w),
        ]
        + scatter_bufs(rows, width)
        + [sem(7), sem(2), sem(2), sem(3, 8), sem(2), sem(16), sem(16), sem()]
        + SCATTER_SEMS,
        compiler_params=params(cid, 63),
        name="expert_weights",
    )(p1, rdm, xr, pg, hid, gg, ug, wout, n2g, tokens, att, cot, gain)


def back_kernel(
    cgh, q, k, v, seg, sk, lse, cosf, sinf, wh, nall, ag, ctx,
    ngrad, out_t, qkv_t,
    dkt, dvt, pgrad, pgt, opart, opair, osum, ostage, ord_, orx, ory, orz,
    part, rd, rx, ry, rz, ntile, qpart, qpair,
    lo, ops, opr, ofs, ofr, nsem, qs, qr, ts, tr, fs, fr, *sems,
):
    me = lax.axis_index("dp")
    core = lax.axis_index("grp") % 2
    hr = HD // 2
    mine, other = pl.multiple_of(core * hr, hr), pl.multiple_of((1 - core) * hr, hr)
    blk = lambda b: pl.ds(pl.multiple_of(b * HD, HD), HD)
    barrier([lax.rem(me + d, 16) for d in range(1, 16)], pair=True)
    tiles = [
        pltpu.make_async_copy(nall.at[:, pl.ds(t * 256, 256)], ntile.at[t % 2], nsem.at[t % 2])
        for t in range(wh.shape[1] // 256)
    ]

    def out_block(b, carry):
        opart[b] = dot(ag[:, blk(b)], ctx[...], 0, 0).astype(BF)
        return carry

    lax.fori_loop(0, 16, out_block, 0)
    pair = push_pair(opart.at[:, pl.ds(other, hr)], opair, ops, opr)
    dkt[...] = jnp.zeros_like(dkt)
    dvt[...] = jnp.zeros_like(dvt)
    so = Scatter(opair, osum, hr, (ord_, orx, ory, orz), sems[:8])
    sn = Scatter(part, ngrad, HD, (rd, rx, ry, rz), sems[8:16])
    pair.wait_recv()

    def out_pair(b, carry):
        opair[b] = (opair[b].astype(F32) + opart[b, pl.ds(mine, hr)].astype(F32)).astype(BF)
        return carry

    lax.fori_loop(0, 16, out_pair, 0)
    order = (1, 2, 3, 0)
    for j in order:
        so.far(j)

    def attend_rows(i, carry):
        row = blk(i)
        s = dot(q[row], k[...], 1, 1)
        prob = jnp.where(column(seg, i) == sk[...], jnp.exp2(s * (SCALE * LOG2E) - lse[row]), 0.0)
        dp = dot(cgh[row], v[...], 1, 1)
        delta = jnp.sum(prob * dp, -1, keepdims=True)
        ds = (prob * (dp - delta)).astype(BF)
        dq = dot(ds, k[...], 1, 0) * SCALE
        dq = dq * cosf[row] - pltpu.roll(dq, HD // 2, 1) * sinf[row]
        pgrad[row, :HD] = dq.astype(BF)
        pgt[:HD, row] = dq.T.astype(BF)
        dkt[...] += dot(q[row], ds, 0, 0)
        dvt[...] += dot(cgh[row], prob.astype(BF), 0, 0)
        return carry

    n = q.shape[0] // HD
    lax.fori_loop(0, n // 2, attend_rows, 0)
    for j in order:
        so.near(j)
    lax.fori_loop(n // 2, n, attend_rows, 0)
    for j in order:
        so.along(j)

    def turn_back(i, carry):
        row = blk(i)
        dk = dkt[:, row].T * SCALE
        dk = dk * cosf[row] - pltpu.roll(dk, HD // 2, 1) * sinf[row]
        pgrad[row, HD : 2 * HD] = dk.astype(BF)
        pgt[HD : 2 * HD, row] = dk.T.astype(BF)
        dv = dvt[:, row]
        pgrad[row, 2 * HD :] = dv.T.astype(BF)
        pgt[2 * HD :, row] = dv.astype(BF)
        return carry

    lax.fori_loop(0, n, turn_back, 0)
    tiles[0].start()

    def back_block(j, kk):
        b = place_of(kk, j)
        part[b] = dot(pgrad[blk(b)], wh[...], 1, 0).astype(BF)

    for kk in order:
        back_block(3, kk)
        sn.far(kk)
    for t, c in enumerate(tiles):
        if t + 1 < len(tiles):
            tiles[t + 1].start()
        c.wait()
        qpart[:, t * 256 : (t + 1) * 256] = dot(pgt[...], ntile[t % 2], 1, 0).astype(BF)
    qc = [push_pair(qpart.at[pl.ds(s * HD + other, hr)], qpair.at[s], qs.at[s], qr.at[s]) for s in range(3)]
    so.end()
    ostage[...] = osum[...].astype(BF)
    keep = pltpu.make_async_copy(ostage, out_t.at[pl.ds(mine, hr)], lo)
    keep.start()
    give = push_pair(ostage, out_t.at[pl.ds(mine, hr)], ofs, ofr)
    for kk in order:
        back_block(1, kk)
        back_block(2, kk)
        sn.near(kk)
    for s in range(3):
        qc[s].wait_recv()
        qpair[s] = (qpair[s].astype(F32) + qpart[pl.ds(s * HD + mine, hr)].astype(F32)).astype(BF)
        b = 16 * s + me
        to, slot = b // 3, lax.rem(b, 3)
        dst = qkv_t.at[pl.ds(pl.multiple_of(slot * HD + core * hr, hr), hr)]

        @pl.when(to != me)
        def _():
            push(qpair.at[s], dst, ts.at[s], tr.at[slot], to)

        @pl.when(to == me)
        def _():
            pltpu.make_async_copy(qpair.at[s], dst, tr.at[slot]).start()

    for kk in order:
        back_block(0, kk)
    for kk in order:
        sn.along(kk)
    fc = []
    for s in range(3):
        here = qkv_t.at[pl.ds(pl.multiple_of(s * HD + core * hr, hr), hr)]
        pltpu.make_async_copy(here, here, tr.at[s]).wait()
        fc.append(push_pair(here, here, fs.at[s], fr.at[s]))
    sn.end()
    for s in range(3):

        @pl.when((16 * s + me) // 3 != me)
        def _():
            pltpu.make_async_copy(qpair.at[s], qpair.at[s], ts.at[s]).wait()

    keep.wait()
    give.wait()
    pair.wait_send()
    for c in qc:
        c.wait_send()
    for c in fc:
        c.wait()


def back(cgh, q, k, v, seg, sk, lse, cosf, sinf, wh, nall, ag, ctx, cid):
    rows, width = ag.shape
    seq = q.shape[0]
    vb = lambda *shape: pltpu.VMEM(shape, BF)
    vf = lambda *shape: pltpu.VMEM(shape, F32)
    sem = lambda *shape: pltpu.SemaphoreType.DMA(shape) if shape else pltpu.SemaphoreType.DMA
    return pl.pallas_call(
        back_kernel,
        out_shape=[
            jax.ShapeDtypeStruct((rows, width), F32),
            jax.ShapeDtypeStruct((rows, width), BF),
            jax.ShapeDtypeStruct((3 * HD, width), BF),
        ],
        in_specs=[VM] * 10 + [ANY, VM, VM],
        out_specs=[VM, ANY, ANY],
        scratch_shapes=[
            vf(HD, seq), vf(HD, seq), vb(seq, 3 * HD), vb(3 * HD, seq),
            vb(16, rows, width), vb(16, rows // 2, width), vf(rows // 2, width), vb(rows // 2, width),
        ]
        + scatter_bufs(rows // 2, width)
        + [vb(16, rows, width)]
        + scatter_bufs(rows, width)
        + [vb(2, seq, 256), vb(3 * HD, width), vb(3, HD // 2, width)]
        + [sem(), sem(), sem(), sem(), sem(), sem(2), sem(3), sem(3), sem(3), sem(3), sem(3), sem(3)]
        + SCATTER_SEMS * 2,
        compiler_params=params(cid, 62),
        name="back",
    )(cgh, q, k, v, seg, sk, lse, cosf, sinf, wh, nall, ag, ctx)


def total_kernel(x, dp_o, pair_o, got, fromp, ss, rs, ps, pr):
    me = lax.axis_index("dp")
    barrier([lax.rem(me + d, 16) for d in range(1, 16)], pair=True)
    sent = [push(x, got.at[me], ss.at[d], rs.at[d], lax.rem(me + d, 16)) for d in range(1, 16)]
    got[me] = x[...]
    for c in sent:
        c.wait_recv()
    acc = got[0]
    for j in range(1, 16):
        acc = acc + got[j]
    dp_o[...] = acc
    c = push_pair(dp_o, fromp, ps, pr)
    c.wait()
    pair_o[...] = acc + fromp[...]
    for c in sent:
        c.wait_send()


def total(x, cid):
    sem = pltpu.SemaphoreType.DMA
    return pl.pallas_call(
        total_kernel,
        out_shape=[jax.ShapeDtypeStruct(x.shape, F32)] * 2,
        in_specs=[VM],
        out_specs=[VM, VM],
        scratch_shapes=[pltpu.VMEM((16,) + x.shape, F32), pltpu.VMEM(x.shape, F32), sem((16,)), sem((16,)), sem, sem],
        compiler_params=params(cid, 16),
        name="total",
    )(x)


def rotary_tables(length):
    freq = (THETA ** (-(np.arange(HD // 2) * 2.0 / HD))).astype(np.float32)
    angle = (np.arange(length, dtype=np.float32)[:, None] * freq[None, :]).astype(np.float64)
    cos, sin = np.cos(angle).astype(np.float32), np.sin(angle).astype(np.float32)
    return np.concatenate([cos, cos], 1), np.concatenate([-sin, sin], 1)


def per_device(
    tokens, segments, routes, route_weight, capacity, norm_gain,
    qkv_weight, out_weight, gate_weight, up_weight, down_weight, cotangent,
):
    rows, width = tokens.shape
    seq = segments.shape[0]
    me = lax.axis_index("dp")
    gain1_row, gain2_row = norm_gain[:1], norm_gain[1:]
    stream = tokens.astype(F32)
    meta = jnp.concatenate([routes.astype(F32).T, route_weight.T], 0)
    seg = segments.astype(F32).reshape(16, rows)
    sk = jnp.where(segments == 0, -1.0, segments.astype(F32))[None, :]
    cos_table, sin_table = rotary_tables(seq)
    normed_all, meta_all, w_head, q, k, v, lse, context, dense_out = front(
        tokens, gain1_row, meta, qkv_weight, out_weight, cos_table, sin_table, seg, sk, 0
    )
    attended, n2g, mix_part, mix_far, xr, pg, hidden, gg, ug = expert(
        context, dense_out, tokens, gain2_row, cotangent, meta_all, capacity,
        gate_weight[0], up_weight[0], down_weight[0], 3,
    )
    flat = lambda a: a.reshape(-1, a.shape[2])
    mixture, gate_g, up_g, down_g, attended_grad, middle_grad, gain2, cgh = expert_weights(
        mix_part, mix_far, flat(xr), flat(pg), flat(hidden), flat(gg), flat(ug), flat(dense_out),
        n2g, tokens, attended, cotangent, gain2_row, 5,
    )
    layer = stream + attended + mixture
    own_seg = lax.dynamic_slice_in_dim(segments, me * rows, rows)
    valid = (own_seg != 0).astype(F32)
    sums = jnp.stack(
        [
            jnp.sum(valid * jnp.sum(layer * layer, -1)),
            jnp.sum(valid * jnp.sum(attended * attended, -1)),
            jnp.sum(valid * jnp.sum(mixture * mixture, -1)),
            jnp.sum(valid) * width,
        ]
    )
    normed_grad, out_total, qkv_total = back(
        cgh, q, k, v, seg, sk, lse, cos_table, sin_table, w_head, flat(normed_all), attended_grad, context, 6
    )
    sg, gain1 = rmsnorm_pull(stream, gain1_row, normed_grad)
    tokens_grad = middle_grad + sg
    small = jnp.concatenate([jnp.sum(gain1, 0), gain2[0], sums, jnp.zeros((1024 - sums.size,), F32)]).reshape(-1, HD)
    in_group, in_pair = total(small, 4)
    seq_sums = in_group.reshape(-1)[2 * width : 2 * width + 4]
    gain_pair = in_pair.reshape(-1)[: 2 * width].reshape(2, width)
    stat_row = jnp.sqrt(seq_sums[:3] / seq_sums[3]).reshape(1, 3)
    groups = lax.axis_size("grp")
    over = lambda a: a.astype(F32) if groups == 2 else lax.psum(a.astype(BF), "grp").astype(F32) * 0.5
    return (
        layer.astype(BF),
        tokens_grad,
        over(qkv_total),
        over(out_total),
        over(gate_g)[None],
        over(up_g)[None],
        over(down_g)[None],
        gain_pair if groups == 2 else lax.psum(gain_pair, "grp") * 0.5,
        stat_row,
    )


def solution(mesh):
    both = ("grp", "dp")
    in_specs = (
        P(both, None), P("grp"), P(both, None), P(both, None), P(), P(),
        P("dp", None), P("dp", None), P("dp", None, None), P("dp", None, None), P("dp", None, None),
        P(both, None),
    )
    out_specs = (
        P(both, None), P(both, None), P("dp", None), P("dp", None),
        P("dp", None, None), P("dp", None, None), P("dp", None, None), P(), P("grp", None),
    )
    return jax.shard_map(per_device, mesh=mesh, in_specs=in_specs, out_specs=out_specs, check_vma=False)
```

```python
import functools

import jax
import jax.numpy as jnp
import numpy as np
from jax import lax
from jax.experimental import pallas as pl
from jax.experimental.pallas import tpu as pltpu
from jax.sharding import PartitionSpec as P

H = 16
HD = 128
TOPK = 8
EPS = 1e-06
THETA = 50000.0
MESH = pl.DeviceIdType.MESH
MIB = 2**20
BF = jnp.bfloat16
F32 = jnp.float32
SCALE = HD**-0.5
LOG2E = 1.4426950408889634


def places():
    me = lax.axis_index("dp")
    z, y, x = me // 4, (me // 2) % 2, me % 2
    xor = [z, z + 1 - 2 * (z % 2), (z + 2) % 4, 3 - z]
    at = lambda k, yy, xx: xor[k] * 4 + yy * 2 + xx
    return dict(
        me=me,
        col=[at(k, y, x) for k in range(4)],
        X=[at(k, y, 1 - x) for k in range(4)],
        Y=[at(k, 1 - y, x) for k in range(4)],
        D=[at(k, 1 - y, 1 - x) for k in range(4)],
    )


def barrier(targets, pair=False):
    sem = pltpu.get_barrier_semaphore()
    for t in targets:
        pl.semaphore_signal(sem, inc=1, device_id={"dp": t}, device_id_type=MESH)
    count = len(targets)
    if pair:
        pl.semaphore_signal(sem, inc=1, device_id={"grp": partner()}, device_id_type=MESH)
        count += 1
    pl.semaphore_wait(sem, count)


def partner():
    g = lax.axis_index("grp")
    return g + 1 - 2 * (g % 2)


def push(src, dst, send, recv, to):
    c = pltpu.make_async_remote_copy(
        src_ref=src, dst_ref=dst, send_sem=send, recv_sem=recv,
        device_id={"dp": to}, device_id_type=MESH,
    )
    c.start()
    return c


def push_pair(src, dst, send, recv):
    c = pltpu.make_async_remote_copy(
        src_ref=src, dst_ref=dst, send_sem=send, recv_sem=recv,
        device_id={"grp": partner()}, device_id_type=MESH,
    )
    c.start()
    return c


ORDER = (1, 0, 3, 2)
GATHER_SEMS = (
    [pltpu.SemaphoreType.DMA((4,))] * 6 + [pltpu.SemaphoreType.DMA((4, 2))] * 2 + [pltpu.SemaphoreType.DMA]
    + [pltpu.SemaphoreType.DMA((4,))] * 2
)


class Gather:
    def __init__(self, src, dst, rows, sems, first=0):
        self.src, self.dst, self.rows, self.sems, self.first, self.p = src, dst, rows, sems, first, places()

    def block(self, b):
        return self.dst.at[b, pl.ds(self.first, self.rows)]

    def part(self, b, h):
        half = self.rows // 2
        return self.dst.at[b, pl.ds(self.first + h * half, half)]

    def begin(self):
        zs, zr, xs, xr, ys, yr, _, _, own, _, _ = self.sems
        p, src = self.p, self.src
        me = p["me"]
        self.mine = pltpu.make_async_copy(src, self.block(me), own)
        self.mine.start()
        self.xc = {0: push(src, self.block(me), xs.at[0], xr.at[0], p["X"][0])}
        self.yc = {0: push(src, self.block(me), ys.at[0], yr.at[0], p["Y"][0])}
        self.zc = {k: push(src, self.block(me), zs.at[k], zr.at[k], p["col"][k]) for k in (1, 2, 3)}
        self.dc, self.vc = {}, {}

    def near(self, k):
        _, _, xs, xr, ys, yr = self.sems[:6]
        p = self.p
        self.zc[k].wait_recv()
        b = self.block(p["col"][k])
        self.xc[k] = push(b, b, xs.at[k], xr.at[k], p["X"][0])
        self.yc[k] = push(b, b, ys.at[k], yr.at[k], p["Y"][0])

    def far(self, k):
        ds, dr = self.sems[6:8]
        p = self.p
        b = self.part(p["X"][k], 0)
        self.xc[k].wait_recv()
        self.dc[k, 0] = push(b, b, ds.at[k, 0], dr.at[k, 0], p["Y"][0])
        b = self.part(p["Y"][k], 1)
        self.yc[k].wait_recv()
        self.dc[k, 1] = push(b, b, ds.at[k, 1], dr.at[k, 1], p["X"][0])

    def over(self, k):
        vs, vr = self.sems[9:11]
        self.dc[k, 0].wait_recv()
        self.dc[k, 1].wait_recv()
        b = self.block(self.p["D"][k])
        self.vc[k] = push(b, b, vs.at[k], vr.at[k], self.p["col"][1])

    def ready(self, k):
        if k == 0:
            self.mine.wait()
        if k % 2:
            self.xc[k].wait_recv()
            self.yc[k].wait_recv()
            self.vc[k - 1].wait_recv()

    def end(self):
        for group in (self.xc, self.yc, self.zc, self.dc, self.vc):
            for c in group.values():
                c.wait_send()


def gather_targets():
    p = places()
    return [p["col"][1], p["col"][2], p["col"][3], p["X"][0], p["Y"][0]]


SCATTER_SEMS = [pltpu.SemaphoreType.DMA((4, 2))] * 2 + [pltpu.SemaphoreType.DMA((4,))] * 8


def scatter_bufs(rows, width):
    return [
        pltpu.VMEM((4, rows // 2, width), BF),
        pltpu.VMEM((4, rows, width), BF),
        pltpu.VMEM((4, rows, width), BF),
        pltpu.VMEM((4, rows, width), BF),
        pltpu.VMEM((2, rows, width), BF),
    ]


class Scatter:
    def __init__(self, part, out, rows, bufs, sems):
        self.part, self.out, self.half, self.bufs, self.sems, self.p = part, out, rows // 2, bufs, sems, places()
        self.da, self.db, self.xc, self.yc, self.zc, self.vc = {}, {}, {}, {}, {}, {}

    def lift(self, k):
        vs, vr = self.sems[8:]
        self.vc[k] = push(self.part.at[self.p["D"][k]], self.bufs[4].at[k // 2], vs.at[k], vr.at[k], self.p["col"][1])

    def far(self, k):
        ds, dr = self.sems[:2]
        rd, h, p, part = self.bufs[0], self.half, self.p, self.part
        b = p["D"][k]
        self.vc[k + 1].wait_recv()
        part[b] = (part[b].astype(F32) + self.bufs[4][k // 2].astype(F32)).astype(BF)
        self.da[k] = push(part.at[b, pl.ds(0, h)], rd.at[k], ds.at[k, 0], dr.at[k, 0], p["Y"][0])
        self.db[k] = push(part.at[b, pl.ds(h, h)], rd.at[k + 1], ds.at[k, 1], dr.at[k, 1], p["X"][0])

    def near(self, k):
        xs, xr, ys, yr = self.sems[2:6]
        rd, rx, ry = self.bufs[:3]
        part, h, p = self.part, self.half, self.p
        b = p["X"][k]
        if k % 2 == 0:
            self.da[k].wait_recv()
            part[b, pl.ds(0, h)] = (part[b, pl.ds(0, h)].astype(F32) + rd[k].astype(F32)).astype(BF)
        self.xc[k] = push(part.at[b], rx.at[k], xs.at[k], xr.at[k], p["X"][0])
        b = p["Y"][k]
        if k % 2 == 0:
            self.db[k].wait_recv()
            part[b, pl.ds(h, h)] = (part[b, pl.ds(h, h)].astype(F32) + rd[k + 1].astype(F32)).astype(BF)
        self.yc[k] = push(part.at[b], ry.at[k], ys.at[k], yr.at[k], p["Y"][0])

    def along(self, k):
        zs, zr = self.sems[6:8]
        rx, ry, rz = self.bufs[1:4]
        part = self.part
        b = self.p["col"][k]
        self.xc[k].wait_recv()
        self.yc[k].wait_recv()
        total = part[b].astype(F32) + rx[k].astype(F32) + ry[k].astype(F32)
        if k:
            part[b] = total.astype(BF)
            self.zc[k] = push(part.at[b], rz.at[k], zs.at[k], zr.at[k], b)
        else:
            self.out[...] = total

    def end(self):
        for k in (1, 2, 3):
            self.zc[k].wait_recv()
            self.out[...] += self.bufs[3][k].astype(F32)
        for group in (self.da, self.db, self.xc, self.yc, self.zc, self.vc):
            for c in group.values():
                c.wait_send()


class PlainScatter(Scatter):
    def far(self, k):
        ds, dr = self.sems[:2]
        rd, h, p = self.bufs[0], self.half, self.p
        b = p["D"][k]
        self.da[k] = push(self.part.at[b, pl.ds(0, h)], rd.at[2 * k], ds.at[k, 0], dr.at[k, 0], p["Y"][0])
        self.db[k] = push(self.part.at[b, pl.ds(h, h)], rd.at[2 * k + 1], ds.at[k, 1], dr.at[k, 1], p["X"][0])

    def near(self, k):
        xs, xr, ys, yr = self.sems[2:6]
        rd, rx, ry = self.bufs[:3]
        part, h, p = self.part, self.half, self.p
        b = p["X"][k]
        self.da[k].wait_recv()
        part[b, pl.ds(0, h)] = (part[b, pl.ds(0, h)].astype(F32) + rd[2 * k].astype(F32)).astype(BF)
        self.xc[k] = push(part.at[b], rx.at[k], xs.at[k], xr.at[k], p["X"][0])
        b = p["Y"][k]
        self.db[k].wait_recv()
        part[b, pl.ds(h, h)] = (part[b, pl.ds(h, h)].astype(F32) + rd[2 * k + 1].astype(F32)).astype(BF)
        self.yc[k] = push(part.at[b], ry.at[k], ys.at[k], yr.at[k], p["Y"][0])


def plain_bufs(rows, width):
    return [pltpu.VMEM((8, rows // 2, width), BF)] + scatter_bufs(rows, width)[1:4]


FAR_FIRST = (3, 2, 1, 0)


ANY = pl.BlockSpec(memory_space=pl.ANY)
VM = pl.BlockSpec(memory_space=pltpu.VMEM)


def params(cid, vmem=60):
    return pltpu.CompilerParams(collective_id=cid, has_side_effects=True, vmem_limit_bytes=vmem * MIB)


def rmsnorm(field, gain_row):
    return field * lax.rsqrt(jnp.mean(field * field, -1, keepdims=True) + EPS) * gain_row


def rmsnorm_pull(field, gain_row, grad):
    r = lax.rsqrt(jnp.mean(field * field, -1, keepdims=True) + EPS)
    scaled = grad * gain_row
    back = r * scaled - field * (r * r * r * jnp.mean(scaled * field, -1, keepdims=True))
    return back, grad * field * r


def column(rows, b):
    return jnp.broadcast_to(rows[pl.ds(b, 1), :], (8, rows.shape[1])).T[:, :1]


def dot(a, b, ca, cb):
    return lax.dot_general(a, b, (((ca,), (cb,)), ((), ())), preferred_element_type=F32)


def front_kernel(
    tok, gain, m_ref, w_ref, o_ref, cosf, sinf, seg, sk,
    nall_o, mall, wh_o, q, k, v, lse, ctx, oall,
    n_ref, nall, wh, ctxh, ms, mr, mo, ws, wr, ps, pr, wo, no, cs, cr, co, os_, or_, *sems,
):
    me = lax.axis_index("dp")
    core = lax.axis_index("grp") % 2
    hr = HD // 2
    blk = lambda b: pl.ds(pl.multiple_of(b * HD, HD), HD)
    half = lambda s, c: pl.ds(pl.multiple_of(s * HD + c * hr, hr), hr)
    n_ref[...] = rmsnorm(tok[...].astype(F32), gain[...]).astype(BF)
    barrier([lax.rem(me + d, 16) for d in range(1, 16)], pair=True)
    g = Gather(n_ref, nall, n_ref.shape[0], sems[:11])
    go = Gather(o_ref.at[half(0, core)], oall, hr, sems[11:], pl.multiple_of(core * hr, hr))
    g.begin()
    own = pltpu.make_async_copy(m_ref, mall.at[me], mo)
    own.start()
    mc = [push(m_ref, mall.at[me], ms.at[d], mr.at[d], lax.rem(me + d, 16)) for d in range(1, 16)]
    for l in range(3):
        b = 3 * me + l
        to, slot = lax.rem(b, 16), b // 16
        src, dst = w_ref.at[half(l, core)], wh.at[half(slot, core)]

        @pl.when(to != me)
        def _():
            push(src, dst, ws.at[l], wr.at[slot], to)

        @pl.when(to == me)
        def _():
            pltpu.make_async_copy(src, dst, wr.at[slot]).start()

    def project(b, carry):
        row = blk(b)
        out = dot(nall[b], wh[...], 1, 1)
        turn = lambda a: (a * cosf[row] + pltpu.roll(a, HD // 2, 1) * sinf[row]).astype(BF)
        q[row] = turn(out[:, :HD])
        k[row] = turn(out[:, HD : 2 * HD])
        v[row] = out[:, 2 * HD :].astype(BF)
        return carry

    def project_plane(c):
        lax.fori_loop(0, 4, lambda j, carry: project(place_of(c, j), carry), 0)

    g.near(1)
    g.far(0)
    g.near(2)
    g.over(0)
    g.far(2)
    g.near(3)
    pc = []
    for s in range(3):
        dst = wh.at[half(s, core)]
        pltpu.make_async_copy(dst, dst, wr.at[s]).wait()
        pc.append(push_pair(dst, dst, ps.at[s], pr.at[s]))
    go.begin()
    for p in pc:
        p.wait_recv()
    g.ready(0)
    project_plane(0)
    g.ready(1)
    project_plane(1)
    g.over(2)
    g.ready(2)
    project_plane(2)
    g.ready(3)
    project_plane(3)
    saves = [pltpu.make_async_copy(nall, nall_o, no), pltpu.make_async_copy(wh, wh_o, wo)]
    for c in saves:
        c.start()

    def hop(d):
        to = lax.rem(me + d, 16)
        return pltpu.make_async_remote_copy(
            src_ref=ctxh.at[blk(to)], dst_ref=ctx.at[:, blk(me)], send_sem=cs.at[d], recv_sem=cr.at[d],
            device_id={"dp": to}, device_id_type=MESH,
        )

    def attend_rows(d, carry):
        b = lax.rem(me + d, 16)
        row = blk(b)
        s = dot(q[row], k[...], 1, 1)
        s = jnp.where(column(seg, b) == sk[...], s, -1e30)
        peak = jnp.maximum(jnp.max(s, -1, keepdims=True), -1e29)
        ex = jnp.exp2((s - peak) * (SCALE * LOG2E))
        total = jnp.maximum(jnp.sum(ex, -1, keepdims=True), 1.0)
        prob = (ex * (1.0 / total)).astype(BF)
        ctxh[row] = jnp.dot(prob, v[...], preferred_element_type=F32).astype(BF)
        lse[row] = peak * (SCALE * LOG2E) + jnp.log2(total)
        return carry

    def attend_send(d, carry):
        attend_rows(d, carry)
        hop(d).start()
        return carry

    lax.fori_loop(1, 8, attend_send, 0)
    go.near(1)
    go.far(0)
    go.near(2)
    lax.fori_loop(8, 16, attend_send, 0)
    attend_rows(0, 0)
    stay = pltpu.make_async_copy(ctxh.at[blk(me)], ctx.at[:, blk(me)], co)
    stay.start()
    oc = []

    def swap_plane(c):
        go.ready(c)
        z = place_of(c, 0) // 4
        here = oall.at[pl.ds(4 * z, 4), pl.ds(pl.multiple_of(core * hr, hr), hr)]
        oc.append(push_pair(here, here, os_.at[c], or_.at[c]))

    go.over(0)
    go.far(2)
    go.near(3)
    swap_plane(0)
    swap_plane(1)
    go.over(2)
    swap_plane(2)
    swap_plane(3)
    g.end()
    go.end()
    own.wait()
    for c in mc:
        c.wait()
    for l in range(3):
        src = w_ref.at[half(l, core)]

        @pl.when(lax.rem(3 * me + l, 16) != me)
        def _():
            pltpu.make_async_copy(src, src, ws.at[l]).wait()

    for p in pc:
        p.wait_send()
    for c in saves:
        c.wait()
    stay.wait()
    for d in range(1, 16):
        hop(d).wait()
    for c in oc:
        c.wait()


def front(tokens, gain, meta, w, wo, cosf, sinf, seg, sk, cid):
    rows, width = tokens.shape
    seq = cosf.shape[0]
    sem = lambda *shape: pltpu.SemaphoreType.DMA(shape) if shape else pltpu.SemaphoreType.DMA
    b = lambda *shape: jax.ShapeDtypeStruct(shape, BF)
    f = lambda *shape: jax.ShapeDtypeStruct(shape, F32)
    v = lambda *shape: pltpu.VMEM(shape, BF)
    return pl.pallas_call(
        front_kernel,
        out_shape=[
            b(16, rows, width), f(16, *meta.shape), b(3 * HD, width),
            b(seq, HD), b(seq, HD), b(seq, HD), f(seq, 1), b(rows, width), b(16, rows, width),
        ],
        in_specs=[VM, VM] + [ANY] * 3 + [VM] * 4,
        out_specs=[ANY] * 3 + [VM] * 4 + [ANY] * 2,
        scratch_shapes=[v(rows, width), v(16, rows, width), v(3 * HD, width), v(seq, HD)]
        + [sem(16), sem(16), sem(), sem(3), sem(3), sem(3), sem(3), sem(), sem()]
        + [sem(16), sem(16), sem(), sem(4), sem(4)]
        + GATHER_SEMS * 2,
        compiler_params=params(cid),
        name="front",
    )(tokens, gain, meta, w, wo, cosf, sinf, seg, sk)


SLOTS = 80
COLS = 512


def place_of(k, j):
    me = lax.axis_index("dp")
    z, y, x = me // 4, (me // 2) % 2, me % 2
    zk = [z, z + 1 - 2 * (z % 2), (z + 2) % 4, 3 - z][k]
    jy, jx = j // 2, j % 2
    return zk * 4 + (y + jy - 2 * y * jy) * 2 + (x + jx - 2 * x * jx)


def expert_kernel(
    ctx, wout, tok, gain, cot, meta, cap, wg_h, wu_h, wd_h,
    att, n2g, p1, xr_o, pg_o, hid_o, gg_o, ug_o,
    n2, rank, coef, pick, sw, nall, call, part, stage, wg, wu, wd, xr, pg, hid, gg, ug, rd, rx, ry, rz, rv,
    wosem, wsem, osem, psem, *sems,
):
    rows, width = ctx.shape
    wload = pltpu.make_async_copy(wout, part, wosem)
    wload.start()
    barrier(gather_targets())
    gn = Gather(n2, nall, rows, sems[:11])
    gc = Gather(cot, call, rows, sems[11:22])
    sc = Scatter(part, n2g, rows, (rd, rx, ry, rz, rv), sems[22:])
    gc.begin()
    loads = [pltpu.make_async_copy(a, b, wsem.at[i]) for i, (a, b) in enumerate([(wg_h, wg), (wu_h, wu), (wd_h, wd)])]
    me = lax.axis_index("dp").astype(F32)
    hits = [meta[:, r, :] == me for r in range(TOPK)]
    member = sum(h.astype(F32) for h in hits)
    coef[...] = sum(jnp.where(h, meta[:, TOPK + r, :], 0.0) for r, h in enumerate(hits))
    i0, i1 = lax.broadcasted_iota(jnp.int32, (HD, HD), 0), lax.broadcasted_iota(jnp.int32, (HD, HD), 1)
    local = dot(member.astype(BF), (i0 < i1).astype(BF), 1, 0)
    count = jnp.broadcast_to(jnp.sum(member, 1, keepdims=True), member.shape).astype(BF)
    j0, j1 = lax.broadcasted_iota(jnp.int32, (16, 16), 0), lax.broadcasted_iota(jnp.int32, (16, 16), 1)
    before = dot((j1 < j0).astype(BF), count, 1, 0)
    kept = (member > 0.0) & (local + before < cap[0].astype(F32))
    rank[...] = jnp.where(kept, local, -1.0)
    wload.wait()

    def attend_cols(t, carry):
        w = part[pl.ds(2 * t, 2)].reshape(2 * rows, width)
        att[:, pl.ds(pl.multiple_of(t * 2 * rows, 2 * rows), 2 * rows)] = dot(ctx[...], w, 1, 1)
        return carry

    lax.fori_loop(0, 8, attend_cols, 0)
    n2[...] = rmsnorm(tok[...].astype(F32) + att[...], gain[...]).astype(BF)
    gn.begin()
    for c in loads:
        c.start()
    saves = []
    both = lambda name, k: [getattr(g, name)(k) for g in (gn, gc)]
    both("near", 1)
    both("far", 0)
    both("near", 2)
    both("over", 0)
    for i, k in enumerate(ORDER):
        both("ready", k)
        if k == 1:
            both("far", 2)
            both("near", 3)
        if k == 0:
            sc.near(1)
            both("over", 2)
        if k == 3:
            sc.near(0)
            sc.along(1)
        if k == 2:
            sc.near(3)
            sc.along(0)
        for c in saves:
            c.wait()
        if i == 0:
            for c in loads:
                c.wait()

        def collect(j, carry):
            b = place_of(k, j)
            to = pl.ds(pl.multiple_of(j * SLOTS, SLOTS), SLOTS)
            s0 = lax.broadcasted_iota(jnp.int32, (SLOTS, rows), 0).astype(F32)
            mine = s0 == rank[pl.ds(b, 1), :]
            sw[to, :] = jnp.sum(jnp.where(mine, coef[pl.ds(b, 1), :], 0.0), 1, keepdims=True)
            pick[to, :] = mine.astype(BF)

            def cols(n, c):
                w = pl.ds(pl.multiple_of(n * 512, 512), 512)
                xr[to, w] = dot(pick[to, :], nall[b, :, w], 1, 0).astype(BF)
                pg[to, w] = (dot(pick[to, :], call[b, :, w], 1, 0) * sw[to, :]).astype(BF)
                return c

            return lax.fori_loop(0, width // 512, cols, carry)

        lax.fori_loop(0, 4, collect, 0)

        def inner(n, carry):
            w = pl.ds(pl.multiple_of(n * COLS, COLS), COLS)
            gate = dot(xr[...], wg[:, w], 1, 0)
            up = dot(xr[...], wu[:, w], 1, 0)
            hg = dot(pg[...], wd[w, :], 1, 1)
            sig = jax.nn.sigmoid(gate)
            hid[:, w] = (gate * sig * up).astype(BF)
            gg[:, w] = (hg * up * sig * (1.0 + gate * (1.0 - sig))).astype(BF)
            ug[:, w] = (hg * gate * sig).astype(BF)
            return carry

        lax.fori_loop(0, hid.shape[1] // COLS, inner, 0)

        def outer(n, carry):
            w = pl.ds(pl.multiple_of(n * COLS, COLS), COLS)
            eo = dot(hid[...], wd[:, w], 1, 0).astype(BF).astype(F32)
            rg = (dot(gg[...], wg[w, :], 1, 1) + dot(ug[...], wu[w, :], 1, 1)).astype(BF)
            for j in range(4):
                b = place_of(k, j)
                cut = slice(j * SLOTS, (j + 1) * SLOTS)
                weighted = (eo[cut] * sw[cut]).astype(BF)
                stage[j, :, w] = dot(pick[cut], weighted, 0, 0).astype(BF)
                part[b, :, w] = dot(pick[cut], rg[cut], 0, 0).astype(BF)
            return carry

        lax.fori_loop(0, xr.shape[1] // COLS, outer, 0)
        if k % 2:
            sc.lift(k)
        else:
            sc.far(k)
        saves = [
            pltpu.make_async_copy(a, o.at[k], osem.at[i])
            for i, (a, o) in enumerate([(xr, xr_o), (pg, pg_o), (hid, hid_o), (gg, gg_o), (ug, ug_o)])
        ] + [pltpu.make_async_copy(stage.at[j], p1.at[place_of(k, j)], psem.at[j]) for j in range(4)]
        for c in saves:
            c.start()
    gn.end()
    gc.end()
    sc.near(2)
    sc.along(3)
    sc.along(2)
    sc.end()
    for c in saves:
        c.wait()


def expert(ctx, wout, tokens, gain, cot, meta, cap, wg, wu, wd, cid):
    rows, width = ctx.shape
    ff = wg.shape[1]
    chunk = 4 * SLOTS
    save = lambda w: jax.ShapeDtypeStruct((4, chunk, w), BF)
    v = lambda *shape: pltpu.VMEM(shape, BF)
    f = lambda *shape: pltpu.VMEM(shape, F32)
    return pl.pallas_call(
        expert_kernel,
        out_shape=[
            jax.ShapeDtypeStruct((rows, width), F32),
            jax.ShapeDtypeStruct((rows, width), F32),
            jax.ShapeDtypeStruct((16, rows, width), BF),
            save(width), save(width), save(ff), save(ff), save(ff),
        ],
        in_specs=[VM, ANY, VM, VM, ANY, VM, pl.BlockSpec(memory_space=pltpu.SMEM), ANY, ANY, ANY],
        out_specs=[VM, VM] + [ANY] * 6,
        scratch_shapes=[
            v(rows, width), f(16, rows), f(16, rows), v(chunk, rows), f(chunk, 1),
            v(16, rows, width), v(16, rows, width), v(16, rows, width), v(4, rows, width),
            v(width, ff), v(width, ff), v(ff, width),
            v(chunk, width), v(chunk, width), v(chunk, ff), v(chunk, ff), v(chunk, ff),
        ]
        + scatter_bufs(rows, width)
        + [pltpu.SemaphoreType.DMA, pltpu.SemaphoreType.DMA((3,)), pltpu.SemaphoreType.DMA((5,)), pltpu.SemaphoreType.DMA((4,))]
        + GATHER_SEMS * 2
        + SCATTER_SEMS,
        compiler_params=params(cid, 62),
        name="expert",
    )(ctx, wout, tokens, gain, cot, meta, cap, wg, wu, wd)


TILE = (256, 1024)


def weights_kernel(
    p1, xr_h, pg_h, hid_h, gg_h, ug_h, wout, n2g, tok, att, cot, gain,
    mix, gate_o, up_o, down_o, ag, mg, gain_g, cgh,
    part, wo, cg, xr, pg, hid, gg, ug, give, got, rd, rx, ry, rz, rv, lsem, wsem, gs, gr, os_, cs, cr, co, *sems,
):
    me = lax.axis_index("dp")
    blk = lambda b: pl.ds(pl.multiple_of(b * HD, HD), HD)
    loads = [
        pltpu.make_async_copy(a, b, lsem.at[i])
        for i, (a, b) in enumerate(
            [(p1, part), (xr_h, xr), (gg_h, gg), (ug_h, ug), (hid_h, hid), (pg_h, pg)]
        )
    ]
    column_load = lambda t: pltpu.make_async_copy(
        wout.at[:, pl.ds(pl.multiple_of(t * HD, HD), HD)], wo.at[lax.rem(t, 2)], wsem.at[lax.rem(t, 2)]
    )
    column_load(0).start()
    for c in loads:
        c.start()
    gain_g[...] = jnp.zeros_like(gain_g)

    def middle_rows(i, carry):
        rows = pl.ds(pl.multiple_of(i * 16, 16), 16)
        back, gains = rmsnorm_pull(tok[rows].astype(F32) + att[rows], gain[...], n2g[rows])
        gain_g[...] += jnp.sum(gains, 0, keepdims=True)
        grad = cot[rows].astype(F32) + back
        mg[rows] = grad
        ag[rows] = grad.astype(BF)
        return carry

    lax.fori_loop(0, tok.shape[0] // 16, middle_rows, 0)
    barrier([lax.rem(me + d, 16) for d in range(1, 16)], pair=True)
    sc = Scatter(part, mix, part.shape[1], (rd, rx, ry, rz, rv), sems)
    loads[0].wait()
    sc.lift(1)
    sc.lift(3)
    sc.near(3)
    sc.near(1)
    tiles = cg.shape[1] // HD

    def context_cols(t, carry):
        @pl.when(t + 1 < tiles)
        def _():
            column_load(t + 1).start()

        column_load(t).wait()
        cols = pl.ds(pl.multiple_of(t * HD, HD), HD)
        cg[:, cols] = dot(ag[...], wo[lax.rem(t, 2)], 1, 0).astype(BF)
        return carry

    lax.fori_loop(0, tiles, context_cols, 0)

    def hop(d):
        to = lax.rem(me + d, 16)
        return pltpu.make_async_remote_copy(
            src_ref=cg.at[:, blk(to)], dst_ref=cgh.at[blk(me)], send_sem=cs.at[d], recv_sem=cr.at[d],
            device_id={"dp": to}, device_id_type=MESH,
        )

    for d in range(1, 16):
        hop(d).start()
    stay = pltpu.make_async_copy(cg.at[:, blk(me)], cgh.at[blk(me)], co)
    stay.start()
    sc.far(2)
    sc.far(0)
    for c in loads[1:]:
        c.wait()
    r, w = TILE
    strip = lambda a, t, size: a[:, pl.ds(pl.multiple_of(t * size, size), size)]

    def product(m, t):
        left = strip((xr, hid)[m], t, r).T
        for e in range(2):
            yield dot(left, (gg, ug)[e][...] if m == 0 else pg[:, e * w : (e + 1) * w], 1, 0)

    def home(m, t, e):
        rows = pl.ds(pl.multiple_of(t * r, r), r)
        return (gate_o, up_o)[e].at[rows] if m == 0 else down_o.at[rows, pl.ds(e * w, w)]

    def sent(m, t):
        s = lax.rem(t, 2)
        return pltpu.make_async_remote_copy(
            src_ref=give.at[s], dst_ref=got.at[8 * m + t], send_sem=gs.at[s], recv_sem=gr.at[8 * m + t],
            device_id={"grp": partner()}, device_id_type=MESH,
        )

    def saved(m, t):
        s = lax.rem(t, 2)
        return [pltpu.make_async_copy(got.at[8 * m + t, e], home(m, t, e), os_.at[s, e]) for e in range(2)]

    def finish(m, t):
        s = lax.rem(t, 2)
        sent(m, t).wait_recv()
        got[8 * m + t] = (give[s].astype(F32) + got[8 * m + t].astype(F32)).astype(BF)
        for c in saved(m, t):
            c.start()

    def free(m, t):
        sent(m, t).wait_send()
        for c in saved(m, t):
            c.wait()

    def body(m, start):
        def step(t, carry):
            s = lax.rem(t, 2)

            @pl.when(t >= start + 2)
            def _():
                free(m, t - 2)

            for e, tile in enumerate(product(m, t)):
                give[s, e] = tile.astype(BF)
            sent(m, t).start()

            @pl.when(t >= start + 1)
            def _():
                finish(m, t - 1)

            return carry

        return step

    for i, (m, start) in enumerate(((0, 0), (0, 4), (1, 0))):
        lax.fori_loop(start, start + 4, body(m, start), 0)
        finish(m, start + 3)
        free(m, start + 2)
        free(m, start + 3)
        if i == 0:
            sc.near(2)
            sc.near(0)
            sc.along(3)
        if i == 1:
            sc.along(1)
            sc.along(2)
    sc.along(0)
    sc.end()
    stay.wait()
    for d in range(1, 16):
        hop(d).wait()


def expert_weights(p1, xr, pg, hid, gg, ug, wout, n2g, tokens, att, cot, gain, cid):
    _, rows, width = p1.shape
    n, ff = gg.shape
    seq = wout.shape[0]
    r, w = TILE
    v = lambda *shape: pltpu.VMEM(shape, BF)
    sem = lambda *shape: pltpu.SemaphoreType.DMA(shape) if shape else pltpu.SemaphoreType.DMA
    b = lambda *shape: jax.ShapeDtypeStruct(shape, BF)
    f = lambda *shape: jax.ShapeDtypeStruct(shape, F32)
    return pl.pallas_call(
        weights_kernel,
        out_shape=[
            f(rows, width), b(width, ff), b(width, ff), b(ff, width), b(rows, width), f(rows, width), f(1, width),
            b(16 * rows, HD),
        ],
        in_specs=[ANY] * 7 + [VM] * 5,
        out_specs=[VM] + [ANY] * 3 + [VM] * 3 + [ANY],
        scratch_shapes=[
            v(16, rows, width), v(2, seq, HD), v(rows, width),
            v(n, width), v(n, width), v(n, ff), v(n, ff), v(n, ff), v(2, 2, r, w), v(12, 2, r, w),
        ]
        + scatter_bufs(rows, width)
        + [sem(6), sem(2), sem(2), sem(12), sem(2, 2), sem(16), sem(16), sem()]
        + SCATTER_SEMS,
        compiler_params=params(cid, 63),
        name="expert_weights",
    )(p1, xr, pg, hid, gg, ug, wout, n2g, tokens, att, cot, gain)


def back_kernel(
    cgh, q, k, v, seg, sk, lse, cosf, sinf, wh, nall, ag, ctx,
    ngrad, out_t, qkv_t,
    dkt, dvt, pgrad, pgt, opart, opair, osum, ostage, ord_, orx, ory, orz,
    part, rd, rx, ry, rz, ntile, qpart, qpair,
    lo, ops, opr, ofs, ofr, nsem, qs, qr, ts, tr, fs, fr, *sems,
):
    me = lax.axis_index("dp")
    core = lax.axis_index("grp") % 2
    hr = HD // 2
    mine, other = pl.multiple_of(core * hr, hr), pl.multiple_of((1 - core) * hr, hr)
    blk = lambda b: pl.ds(pl.multiple_of(b * HD, HD), HD)
    barrier([lax.rem(me + d, 16) for d in range(1, 16)], pair=True)
    tiles = [
        pltpu.make_async_copy(nall.at[:, pl.ds(t * 256, 256)], ntile.at[t % 2], nsem.at[t % 2])
        for t in range(wh.shape[1] // 256)
    ]

    def out_block(b, carry):
        opart[b] = dot(ag[:, blk(b)], ctx[...], 0, 0).astype(BF)
        return carry

    lax.fori_loop(0, 16, out_block, 0)
    pair = push_pair(opart.at[:, pl.ds(other, hr)], opair, ops, opr)
    dkt[...] = jnp.zeros_like(dkt)
    dvt[...] = jnp.zeros_like(dvt)
    so = PlainScatter(opair, osum, hr, (ord_, orx, ory, orz), sems[:10])
    sn = PlainScatter(part, ngrad, HD, (rd, rx, ry, rz), sems[10:20])
    def out_pair(b, carry):
        opair[b] = (opair[b].astype(F32) + opart[b, pl.ds(mine, hr)].astype(F32)).astype(BF)
        return carry

    def attend_rows(i, carry):
        row = blk(i)
        s = dot(q[row], k[...], 1, 1)
        prob = jnp.where(column(seg, i) == sk[...], jnp.exp2(s * (SCALE * LOG2E) - lse[row]), 0.0)
        dp = dot(cgh[row], v[...], 1, 1)
        delta = jnp.sum(prob * dp, -1, keepdims=True)
        ds = (prob * (dp - delta)).astype(BF)
        dq = dot(ds, k[...], 1, 0) * SCALE
        dq = dq * cosf[row] - pltpu.roll(dq, HD // 2, 1) * sinf[row]
        pgrad[row, :HD] = dq.astype(BF)
        pgt[:HD, row] = dq.T.astype(BF)
        dkt[...] += dot(q[row], ds, 0, 0)
        dvt[...] += dot(cgh[row], prob.astype(BF), 0, 0)
        return carry

    n = q.shape[0] // HD
    lax.fori_loop(0, n // 2, attend_rows, 0)
    pair.wait_recv()
    lax.fori_loop(0, 16, out_pair, 0)
    for j in FAR_FIRST:
        so.far(j)
    lax.fori_loop(n // 2, n, attend_rows, 0)
    for j in FAR_FIRST:
        so.near(j)

    def turn_back(i, carry):
        row = blk(i)
        dk = dkt[:, row].T * SCALE
        dk = dk * cosf[row] - pltpu.roll(dk, HD // 2, 1) * sinf[row]
        pgrad[row, HD : 2 * HD] = dk.astype(BF)
        pgt[HD : 2 * HD, row] = dk.T.astype(BF)
        dv = dvt[:, row]
        pgrad[row, 2 * HD :] = dv.T.astype(BF)
        pgt[2 * HD :, row] = dv.astype(BF)
        return carry

    lax.fori_loop(0, n, turn_back, 0)
    tiles[0].start()

    def back_block(j, kk):
        b = place_of(kk, j)
        part[b] = dot(pgrad[blk(b)], wh[...], 1, 0).astype(BF)

    for kk in FAR_FIRST:
        back_block(3, kk)
        sn.far(kk)
    for j in FAR_FIRST:
        so.along(j)
    for t, c in enumerate(tiles):
        if t + 1 < len(tiles):
            tiles[t + 1].start()
        c.wait()
        qpart[:, t * 256 : (t + 1) * 256] = dot(pgt[...], ntile[t % 2], 1, 0).astype(BF)
    qc = [push_pair(qpart.at[pl.ds(s * HD + other, hr)], qpair.at[s], qs.at[s], qr.at[s]) for s in range(3)]
    so.end()
    ostage[...] = osum[...].astype(BF)
    keep = pltpu.make_async_copy(ostage, out_t.at[pl.ds(mine, hr)], lo)
    keep.start()
    give = push_pair(ostage, out_t.at[pl.ds(mine, hr)], ofs, ofr)
    for kk in FAR_FIRST:
        back_block(1, kk)
        back_block(2, kk)
        sn.near(kk)
    for s in range(3):
        qc[s].wait_recv()
        qpair[s] = (qpair[s].astype(F32) + qpart[pl.ds(s * HD + mine, hr)].astype(F32)).astype(BF)
        b = 16 * s + me
        to, slot = b // 3, lax.rem(b, 3)
        dst = qkv_t.at[pl.ds(pl.multiple_of(slot * HD + core * hr, hr), hr)]

        @pl.when(to != me)
        def _():
            push(qpair.at[s], dst, ts.at[s], tr.at[slot], to)

        @pl.when(to == me)
        def _():
            pltpu.make_async_copy(qpair.at[s], dst, tr.at[slot]).start()

    for kk in FAR_FIRST:
        back_block(0, kk)
    for kk in FAR_FIRST:
        sn.along(kk)
    fc = []
    for s in range(3):
        here = qkv_t.at[pl.ds(pl.multiple_of(s * HD + core * hr, hr), hr)]
        pltpu.make_async_copy(here, here, tr.at[s]).wait()
        fc.append(push_pair(here, here, fs.at[s], fr.at[s]))
    sn.end()
    for s in range(3):

        @pl.when((16 * s + me) // 3 != me)
        def _():
            pltpu.make_async_copy(qpair.at[s], qpair.at[s], ts.at[s]).wait()

    keep.wait()
    give.wait()
    pair.wait_send()
    for c in qc:
        c.wait_send()
    for c in fc:
        c.wait()


def back(cgh, q, k, v, seg, sk, lse, cosf, sinf, wh, nall, ag, ctx, cid):
    rows, width = ag.shape
    seq = q.shape[0]
    vb = lambda *shape: pltpu.VMEM(shape, BF)
    vf = lambda *shape: pltpu.VMEM(shape, F32)
    sem = lambda *shape: pltpu.SemaphoreType.DMA(shape) if shape else pltpu.SemaphoreType.DMA
    return pl.pallas_call(
        back_kernel,
        out_shape=[
            jax.ShapeDtypeStruct((rows, width), F32),
            jax.ShapeDtypeStruct((rows, width), BF),
            jax.ShapeDtypeStruct((3 * HD, width), BF),
        ],
        in_specs=[VM] * 10 + [ANY, VM, VM],
        out_specs=[VM, ANY, ANY],
        scratch_shapes=[
            vf(HD, seq), vf(HD, seq), vb(seq, 3 * HD), vb(3 * HD, seq),
            vb(16, rows, width), vb(16, rows // 2, width), vf(rows // 2, width), vb(rows // 2, width),
        ]
        + plain_bufs(rows // 2, width)
        + [vb(16, rows, width)]
        + plain_bufs(rows, width)
        + [vb(2, seq, 256), vb(3 * HD, width), vb(3, HD // 2, width)]
        + [sem(), sem(), sem(), sem(), sem(), sem(2), sem(3), sem(3), sem(3), sem(3), sem(3), sem(3)]
        + SCATTER_SEMS * 2,
        compiler_params=params(cid, 62),
        name="back",
    )(cgh, q, k, v, seg, sk, lse, cosf, sinf, wh, nall, ag, ctx)


def total_kernel(x, dp_o, pair_o, got, fromp, ss, rs, ps, pr):
    me = lax.axis_index("dp")
    barrier([lax.rem(me + d, 16) for d in range(1, 16)], pair=True)
    sent = [push(x, got.at[me], ss.at[d], rs.at[d], lax.rem(me + d, 16)) for d in range(1, 16)]
    got[me] = x[...]
    for c in sent:
        c.wait_recv()
    acc = got[0]
    for j in range(1, 16):
        acc = acc + got[j]
    dp_o[...] = acc
    c = push_pair(dp_o, fromp, ps, pr)
    c.wait()
    pair_o[...] = acc + fromp[...]
    for c in sent:
        c.wait_send()


def total(x, cid):
    sem = pltpu.SemaphoreType.DMA
    return pl.pallas_call(
        total_kernel,
        out_shape=[jax.ShapeDtypeStruct(x.shape, F32)] * 2,
        in_specs=[VM],
        out_specs=[VM, VM],
        scratch_shapes=[pltpu.VMEM((16,) + x.shape, F32), pltpu.VMEM(x.shape, F32), sem((16,)), sem((16,)), sem, sem],
        compiler_params=params(cid, 16),
        name="total",
    )(x)


def rotary_tables(length):
    freq = (THETA ** (-(np.arange(HD // 2) * 2.0 / HD))).astype(np.float32)
    angle = (np.arange(length, dtype=np.float32)[:, None] * freq[None, :]).astype(np.float64)
    cos, sin = np.cos(angle).astype(np.float32), np.sin(angle).astype(np.float32)
    return np.concatenate([cos, cos], 1), np.concatenate([-sin, sin], 1)


def per_device(
    tokens, segments, routes, route_weight, capacity, norm_gain,
    qkv_weight, out_weight, gate_weight, up_weight, down_weight, cotangent,
):
    rows, width = tokens.shape
    seq = segments.shape[0]
    me = lax.axis_index("dp")
    gain1_row, gain2_row = norm_gain[:1], norm_gain[1:]
    stream = tokens.astype(F32)
    meta = jnp.concatenate([routes.astype(F32).T, route_weight.T], 0)
    seg = segments.astype(F32).reshape(16, rows)
    sk = jnp.where(segments == 0, -1.0, segments.astype(F32))[None, :]
    cos_table, sin_table = rotary_tables(seq)
    normed_all, meta_all, w_head, q, k, v, lse, context, dense_out = front(
        tokens, gain1_row, meta, qkv_weight, out_weight, cos_table, sin_table, seg, sk, 0
    )
    attended, n2g, mix_part, xr, pg, hidden, gg, ug = expert(
        context, dense_out, tokens, gain2_row, cotangent, meta_all, capacity,
        gate_weight[0], up_weight[0], down_weight[0], 3,
    )
    flat = lambda a: a.reshape(-1, a.shape[2])
    mixture, gate_g, up_g, down_g, attended_grad, middle_grad, gain2, cgh = expert_weights(
        mix_part, flat(xr), flat(pg), flat(hidden), flat(gg), flat(ug), flat(dense_out),
        n2g, tokens, attended, cotangent, gain2_row, 5,
    )
    layer = stream + attended + mixture
    own_seg = lax.dynamic_slice_in_dim(segments, me * rows, rows)
    valid = (own_seg != 0).astype(F32)
    sums = jnp.stack(
        [
            jnp.sum(valid * jnp.sum(layer * layer, -1)),
            jnp.sum(valid * jnp.sum(attended * attended, -1)),
            jnp.sum(valid * jnp.sum(mixture * mixture, -1)),
            jnp.sum(valid) * width,
        ]
    )
    normed_grad, out_total, qkv_total = back(
        cgh, q, k, v, seg, sk, lse, cos_table, sin_table, w_head, flat(normed_all), attended_grad, context, 6
    )
    sg, gain1 = rmsnorm_pull(stream, gain1_row, normed_grad)
    tokens_grad = middle_grad + sg
    small = jnp.concatenate([jnp.sum(gain1, 0), gain2[0], sums, jnp.zeros((1024 - sums.size,), F32)]).reshape(-1, HD)
    in_group, in_pair = total(small, 4)
    seq_sums = in_group.reshape(-1)[2 * width : 2 * width + 4]
    gain_pair = in_pair.reshape(-1)[: 2 * width].reshape(2, width)
    stat_row = jnp.sqrt(seq_sums[:3] / seq_sums[3]).reshape(1, 3)
    groups = lax.axis_size("grp")
    over = lambda a: a.astype(F32) if groups == 2 else lax.psum(a.astype(BF), "grp").astype(F32) * 0.5
    return (
        layer.astype(BF),
        tokens_grad,
        over(qkv_total),
        over(out_total),
        over(gate_g)[None],
        over(up_g)[None],
        over(down_g)[None],
        gain_pair if groups == 2 else lax.psum(gain_pair, "grp") * 0.5,
        stat_row,
    )


def solution(mesh):
    both = ("grp", "dp")
    in_specs = (
        P(both, None), P("grp"), P(both, None), P(both, None), P(), P(),
        P("dp", None), P("dp", None), P("dp", None, None), P("dp", None, None), P("dp", None, None),
        P(both, None),
    )
    out_specs = (
        P(both, None), P(both, None), P("dp", None), P("dp", None),
        P("dp", None, None), P("dp", None, None), P("dp", None, None), P(), P("grp", None),
    )
    return jax.shard_map(per_device, mesh=mesh, in_specs=in_specs, out_specs=out_specs, check_vma=False)
```

```python
import functools

import jax
import jax.numpy as jnp
import numpy as np
from jax import lax
from jax.experimental import pallas as pl
from jax.experimental.pallas import tpu as pltpu
from jax.sharding import PartitionSpec as P

H = 16
HD = 128
TOPK = 8
EPS = 1e-06
THETA = 50000.0
MESH = pl.DeviceIdType.MESH
MIB = 2**20
BF = jnp.bfloat16
F32 = jnp.float32
SCALE = HD**-0.5
LOG2E = 1.4426950408889634


def places():
    me = lax.axis_index("dp")
    z, y, x = me // 4, (me // 2) % 2, me % 2
    xor = [z, z + 1 - 2 * (z % 2), (z + 2) % 4, 3 - z]
    at = lambda k, yy, xx: xor[k] * 4 + yy * 2 + xx
    return dict(
        me=me,
        col=[at(k, y, x) for k in range(4)],
        X=[at(k, y, 1 - x) for k in range(4)],
        Y=[at(k, 1 - y, x) for k in range(4)],
        D=[at(k, 1 - y, 1 - x) for k in range(4)],
    )


def barrier(targets, pair=False):
    sem = pltpu.get_barrier_semaphore()
    for t in targets:
        pl.semaphore_signal(sem, inc=1, device_id={"dp": t}, device_id_type=MESH)
    count = len(targets)
    if pair:
        pl.semaphore_signal(sem, inc=1, device_id={"grp": partner()}, device_id_type=MESH)
        count += 1
    pl.semaphore_wait(sem, count)


def partner():
    g = lax.axis_index("grp")
    return g + 1 - 2 * (g % 2)


def push(src, dst, send, recv, to):
    c = pltpu.make_async_remote_copy(
        src_ref=src, dst_ref=dst, send_sem=send, recv_sem=recv,
        device_id={"dp": to}, device_id_type=MESH,
    )
    c.start()
    return c


def push_pair(src, dst, send, recv):
    c = pltpu.make_async_remote_copy(
        src_ref=src, dst_ref=dst, send_sem=send, recv_sem=recv,
        device_id={"grp": partner()}, device_id_type=MESH,
    )
    c.start()
    return c


ORDER = (1, 0, 3, 2)
GATHER_SEMS = (
    [pltpu.SemaphoreType.DMA((4,))] * 6 + [pltpu.SemaphoreType.DMA((4, 2))] * 2 + [pltpu.SemaphoreType.DMA]
    + [pltpu.SemaphoreType.DMA((4,))] * 2
)


class Gather:
    def __init__(self, src, dst, rows, sems, first=0):
        self.src, self.dst, self.rows, self.sems, self.first, self.p = src, dst, rows, sems, first, places()

    def block(self, b):
        return self.dst.at[b, pl.ds(self.first, self.rows)]

    def part(self, b, h):
        half = self.rows // 2
        return self.dst.at[b, pl.ds(self.first + h * half, half)]

    def begin(self):
        zs, zr, xs, xr, ys, yr, _, _, own, _, _ = self.sems
        p, src = self.p, self.src
        me = p["me"]
        self.mine = pltpu.make_async_copy(src, self.block(me), own)
        self.mine.start()
        self.xc = {0: push(src, self.block(me), xs.at[0], xr.at[0], p["X"][0])}
        self.yc = {0: push(src, self.block(me), ys.at[0], yr.at[0], p["Y"][0])}
        self.zc = {k: push(src, self.block(me), zs.at[k], zr.at[k], p["col"][k]) for k in (1, 2, 3)}
        self.dc, self.vc = {}, {}

    def near(self, k):
        _, _, xs, xr, ys, yr = self.sems[:6]
        p = self.p
        self.zc[k].wait_recv()
        b = self.block(p["col"][k])
        self.xc[k] = push(b, b, xs.at[k], xr.at[k], p["X"][0])
        self.yc[k] = push(b, b, ys.at[k], yr.at[k], p["Y"][0])

    def far(self, k):
        ds, dr = self.sems[6:8]
        p = self.p
        b = self.part(p["X"][k], 0)
        self.xc[k].wait_recv()
        self.dc[k, 0] = push(b, b, ds.at[k, 0], dr.at[k, 0], p["Y"][0])
        b = self.part(p["Y"][k], 1)
        self.yc[k].wait_recv()
        self.dc[k, 1] = push(b, b, ds.at[k, 1], dr.at[k, 1], p["X"][0])

    def over(self, k):
        vs, vr = self.sems[9:11]
        self.dc[k, 0].wait_recv()
        self.dc[k, 1].wait_recv()
        b = self.block(self.p["D"][k])
        self.vc[k] = push(b, b, vs.at[k], vr.at[k], self.p["col"][1])

    def ready(self, k):
        if k == 0:
            self.mine.wait()
        if k % 2:
            self.xc[k].wait_recv()
            self.yc[k].wait_recv()
            self.vc[k - 1].wait_recv()

    def end(self):
        for group in (self.xc, self.yc, self.zc, self.dc, self.vc):
            for c in group.values():
                c.wait_send()


def gather_targets():
    p = places()
    return [p["col"][1], p["col"][2], p["col"][3], p["X"][0], p["Y"][0]]


SCATTER_SEMS = [pltpu.SemaphoreType.DMA((4, 2))] * 2 + [pltpu.SemaphoreType.DMA((4,))] * 8


def scatter_bufs(rows, width):
    return [
        pltpu.VMEM((4, rows // 2, width), BF),
        pltpu.VMEM((4, rows, width), BF),
        pltpu.VMEM((4, rows, width), BF),
        pltpu.VMEM((4, rows, width), BF),
        pltpu.VMEM((2, rows, width), BF),
    ]


class Scatter:
    def __init__(self, part, out, rows, bufs, sems):
        self.part, self.out, self.half, self.bufs, self.sems, self.p = part, out, rows // 2, bufs, sems, places()
        self.at = self.p
        self.da, self.db, self.xc, self.yc, self.zc, self.vc = {}, {}, {}, {}, {}, {}

    def lift(self, k):
        vs, vr = self.sems[8:]
        self.vc[k] = push(self.part.at[self.p["D"][k]], self.bufs[4].at[k // 2], vs.at[k], vr.at[k], self.p["col"][1])

    def far(self, k):
        ds, dr = self.sems[:2]
        rd, h, p, part = self.bufs[0], self.half, self.p, self.part
        b = p["D"][k]
        self.vc[k + 1].wait_recv()
        part[b] = (part[b].astype(F32) + self.bufs[4][k // 2].astype(F32)).astype(BF)
        self.da[k] = push(part.at[b, pl.ds(0, h)], rd.at[k], ds.at[k, 0], dr.at[k, 0], p["Y"][0])
        self.db[k] = push(part.at[b, pl.ds(h, h)], rd.at[k + 1], ds.at[k, 1], dr.at[k, 1], p["X"][0])

    def near(self, k):
        xs, xr, ys, yr = self.sems[2:6]
        rd, rx, ry = self.bufs[:3]
        part, h, p = self.part, self.half, self.p
        b = p["X"][k]
        if k % 2 == 0:
            self.da[k].wait_recv()
            part[b, pl.ds(0, h)] = (part[b, pl.ds(0, h)].astype(F32) + rd[k].astype(F32)).astype(BF)
        self.xc[k] = push(part.at[b], rx.at[k], xs.at[k], xr.at[k], p["X"][0])
        b = p["Y"][k]
        if k % 2 == 0:
            self.db[k].wait_recv()
            part[b, pl.ds(h, h)] = (part[b, pl.ds(h, h)].astype(F32) + rd[k + 1].astype(F32)).astype(BF)
        self.yc[k] = push(part.at[b], ry.at[k], ys.at[k], yr.at[k], p["Y"][0])

    def along(self, k):
        zs, zr = self.sems[6:8]
        rx, ry, rz = self.bufs[1:4]
        part = self.part
        b = self.p["col"][k]
        self.xc[k].wait_recv()
        self.yc[k].wait_recv()
        total = part[b].astype(F32) + rx[k].astype(F32) + ry[k].astype(F32)
        if k:
            part[b] = total.astype(BF)
            self.zc[k] = push(part.at[b], rz.at[k], zs.at[k], zr.at[k], b)
        else:
            self.out[...] = total

    def end(self):
        for k in (1, 2, 3):
            self.zc[k].wait_recv()
            self.out[...] += self.bufs[3][k].astype(F32)
        for group in (self.da, self.db, self.xc, self.yc, self.zc, self.vc):
            for c in group.values():
                c.wait_send()


class PlainScatter(Scatter):
    def far(self, k):
        ds, dr = self.sems[:2]
        rd, h, p = self.bufs[0], self.half, self.p
        b = self.at["D"][k]
        self.da[k] = push(self.part.at[b, pl.ds(0, h)], rd.at[2 * k], ds.at[k, 0], dr.at[k, 0], p["Y"][0])
        self.db[k] = push(self.part.at[b, pl.ds(h, h)], rd.at[2 * k + 1], ds.at[k, 1], dr.at[k, 1], p["X"][0])

    def near(self, k):
        xs, xr, ys, yr = self.sems[2:6]
        rd, rx, ry = self.bufs[:3]
        part, h, p = self.part, self.half, self.p
        b = self.at["X"][k]
        self.da[k].wait_recv()
        part[b, pl.ds(0, h)] = (part[b, pl.ds(0, h)].astype(F32) + rd[2 * k].astype(F32)).astype(BF)
        self.xc[k] = push(part.at[b], rx.at[k], xs.at[k], xr.at[k], p["X"][0])
        b = self.at["Y"][k]
        self.db[k].wait_recv()
        part[b, pl.ds(h, h)] = (part[b, pl.ds(h, h)].astype(F32) + rd[2 * k + 1].astype(F32)).astype(BF)
        self.yc[k] = push(part.at[b], ry.at[k], ys.at[k], yr.at[k], p["Y"][0])

    def along(self, k):
        zs, zr = self.sems[6:8]
        rx, ry, rz = self.bufs[1:4]
        part, b = self.part, self.at["col"][k]
        self.xc[k].wait_recv()
        self.yc[k].wait_recv()
        total = part[b].astype(F32) + rx[k].astype(F32) + ry[k].astype(F32)
        if k:
            part[b] = total.astype(BF)
            self.zc[k] = push(part.at[b], rz.at[k], zs.at[k], zr.at[k], self.p["col"][k])
        else:
            self.out[...] = total


def plain_bufs(rows, width):
    return [pltpu.VMEM((8, rows // 2, width), BF)] + scatter_bufs(rows, width)[1:4]


FAR_FIRST = (3, 2, 1, 0)


ANY = pl.BlockSpec(memory_space=pl.ANY)
VM = pl.BlockSpec(memory_space=pltpu.VMEM)


def params(cid, vmem=60):
    return pltpu.CompilerParams(collective_id=cid, has_side_effects=True, vmem_limit_bytes=vmem * MIB)


def rmsnorm(field, gain_row):
    return field * lax.rsqrt(jnp.mean(field * field, -1, keepdims=True) + EPS) * gain_row


def rmsnorm_pull(field, gain_row, grad):
    r = lax.rsqrt(jnp.mean(field * field, -1, keepdims=True) + EPS)
    scaled = grad * gain_row
    back = r * scaled - field * (r * r * r * jnp.mean(scaled * field, -1, keepdims=True))
    return back, grad * field * r


def column(rows, b):
    return jnp.broadcast_to(rows[pl.ds(b, 1), :], (8, rows.shape[1])).T[:, :1]


def dot(a, b, ca, cb):
    return lax.dot_general(a, b, (((ca,), (cb,)), ((), ())), preferred_element_type=F32)


def front_kernel(
    tok, gain, m_ref, w_ref, o_ref, cosf, sinf, seg, sk,
    nall_o, mall, wh_o, q, k, v, lse, ctx, oall,
    n_ref, nall, wh, ctxh, ms, mr, mo, ws, wr, ps, pr, wo, no, cs, cr, co, os_, or_, *sems,
):
    me = lax.axis_index("dp")
    core = lax.axis_index("grp") % 2
    hr = HD // 2
    blk = lambda b: pl.ds(pl.multiple_of(b * HD, HD), HD)
    half = lambda s, c: pl.ds(pl.multiple_of(s * HD + c * hr, hr), hr)
    n_ref[...] = rmsnorm(tok[...].astype(F32), gain[...]).astype(BF)
    barrier([lax.rem(me + d, 16) for d in range(1, 16)], pair=True)
    g = Gather(n_ref, nall, n_ref.shape[0], sems[:11])
    go = Gather(o_ref.at[half(0, core)], oall, hr, sems[11:], pl.multiple_of(core * hr, hr))
    g.begin()
    own = pltpu.make_async_copy(m_ref, mall.at[me], mo)
    own.start()
    mc = [push(m_ref, mall.at[me], ms.at[d], mr.at[d], lax.rem(me + d, 16)) for d in range(1, 16)]
    for l in range(3):
        b = 3 * me + l
        to, slot = lax.rem(b, 16), b // 16
        src, dst = w_ref.at[half(l, core)], wh.at[half(slot, core)]

        @pl.when(to != me)
        def _():
            push(src, dst, ws.at[l], wr.at[slot], to)

        @pl.when(to == me)
        def _():
            pltpu.make_async_copy(src, dst, wr.at[slot]).start()

    def project(b, carry):
        row = blk(b)
        out = dot(nall[b], wh[...], 1, 1)
        turn = lambda a: (a * cosf[row] + pltpu.roll(a, HD // 2, 1) * sinf[row]).astype(BF)
        q[row] = turn(out[:, :HD])
        k[row] = turn(out[:, HD : 2 * HD])
        v[row] = out[:, 2 * HD :].astype(BF)
        return carry

    def project_plane(c):
        lax.fori_loop(0, 4, lambda j, carry: project(place_of(c, j), carry), 0)

    g.near(1)
    g.far(0)
    g.near(2)
    g.over(0)
    g.far(2)
    g.near(3)
    go.begin()
    g.over(2)
    pc = []
    for s in range(3):
        dst = wh.at[half(s, core)]
        pltpu.make_async_copy(dst, dst, wr.at[s]).wait()
        pc.append(push_pair(dst, dst, ps.at[s], pr.at[s]))
    go.near(1)
    for p in pc:
        p.wait_recv()
    g.ready(0)
    project_plane(0)
    g.ready(1)
    project_plane(1)
    g.ready(2)
    project_plane(2)
    go.far(0)
    go.near(2)
    g.ready(3)
    project_plane(3)
    saves = [pltpu.make_async_copy(nall, nall_o, no), pltpu.make_async_copy(wh, wh_o, wo)]
    for c in saves:
        c.start()

    def hop(d):
        to = lax.rem(me + d, 16)
        return pltpu.make_async_remote_copy(
            src_ref=ctxh.at[blk(to)], dst_ref=ctx.at[:, blk(me)], send_sem=cs.at[d], recv_sem=cr.at[d],
            device_id={"dp": to}, device_id_type=MESH,
        )

    def attend_rows(d, carry):
        b = lax.rem(me + d, 16)
        row = blk(b)
        s = dot(q[row], k[...], 1, 1)
        s = jnp.where(column(seg, b) == sk[...], s, -1e30)
        peak = jnp.maximum(jnp.max(s, -1, keepdims=True), -1e29)
        ex = jnp.exp2((s - peak) * (SCALE * LOG2E))
        total = jnp.maximum(jnp.sum(ex, -1, keepdims=True), 1.0)
        prob = (ex * (1.0 / total)).astype(BF)
        ctxh[row] = jnp.dot(prob, v[...], preferred_element_type=F32).astype(BF)
        lse[row] = peak * (SCALE * LOG2E) + jnp.log2(total)
        return carry

    def attend_send(d, carry):
        attend_rows(d, carry)
        hop(d).start()
        return carry

    oc = []

    def swap_plane(c):
        go.ready(c)
        z = place_of(c, 0) // 4
        here = oall.at[pl.ds(4 * z, 4), pl.ds(pl.multiple_of(core * hr, hr), hr)]
        oc.append(push_pair(here, here, os_.at[c], or_.at[c]))

    lax.fori_loop(1, 6, attend_send, 0)
    go.over(0)
    go.far(2)
    go.near(3)
    lax.fori_loop(6, 12, attend_send, 0)
    swap_plane(0)
    swap_plane(1)
    lax.fori_loop(12, 16, attend_send, 0)
    attend_rows(0, 0)
    stay = pltpu.make_async_copy(ctxh.at[blk(me)], ctx.at[:, blk(me)], co)
    stay.start()
    go.over(2)
    swap_plane(2)
    swap_plane(3)
    g.end()
    go.end()
    own.wait()
    for c in mc:
        c.wait()
    for l in range(3):
        src = w_ref.at[half(l, core)]

        @pl.when(lax.rem(3 * me + l, 16) != me)
        def _():
            pltpu.make_async_copy(src, src, ws.at[l]).wait()

    for p in pc:
        p.wait_send()
    for c in saves:
        c.wait()
    stay.wait()
    for d in range(1, 16):
        hop(d).wait()
    for c in oc:
        c.wait()


def front(tokens, gain, meta, w, wo, cosf, sinf, seg, sk, cid):
    rows, width = tokens.shape
    seq = cosf.shape[0]
    sem = lambda *shape: pltpu.SemaphoreType.DMA(shape) if shape else pltpu.SemaphoreType.DMA
    b = lambda *shape: jax.ShapeDtypeStruct(shape, BF)
    f = lambda *shape: jax.ShapeDtypeStruct(shape, F32)
    v = lambda *shape: pltpu.VMEM(shape, BF)
    return pl.pallas_call(
        front_kernel,
        out_shape=[
            b(16, rows, width), f(16, *meta.shape), b(3 * HD, width),
            b(seq, HD), b(seq, HD), b(seq, HD), f(seq, 1), b(rows, width), b(16, rows, width),
        ],
        in_specs=[VM, VM] + [ANY] * 3 + [VM] * 4,
        out_specs=[ANY] * 3 + [VM] * 4 + [ANY] * 2,
        scratch_shapes=[v(rows, width), v(16, rows, width), v(3 * HD, width), v(seq, HD)]
        + [sem(16), sem(16), sem(), sem(3), sem(3), sem(3), sem(3), sem(), sem()]
        + [sem(16), sem(16), sem(), sem(4), sem(4)]
        + GATHER_SEMS * 2,
        compiler_params=params(cid),
        name="front",
    )(tokens, gain, meta, w, wo, cosf, sinf, seg, sk)


SLOTS = 80
COLS = 512


def place_of(k, j):
    me = lax.axis_index("dp")
    z, y, x = me // 4, (me // 2) % 2, me % 2
    zk = [z, z + 1 - 2 * (z % 2), (z + 2) % 4, 3 - z][k]
    jy, jx = j // 2, j % 2
    return zk * 4 + (y + jy - 2 * y * jy) * 2 + (x + jx - 2 * x * jx)


def expert_kernel(
    ctx, wout, tok, gain, cot, meta, cap, wg_h, wu_h, wd_h,
    att, n2g, p1, xr_o, pg_o, hid_o, gg_o, ug_o,
    n2, rank, coef, pick, sw, nall, call, part, stage, wg, wu, wd, xr, pg, hid, gg, ug, rd, rx, ry, rz, rv,
    wosem, wsem, osem, psem, *sems,
):
    rows, width = ctx.shape
    wload = pltpu.make_async_copy(wout, part, wosem)
    wload.start()
    barrier(gather_targets())
    gn = Gather(n2, nall, rows, sems[:11])
    gc = Gather(cot, call, rows, sems[11:22])
    sc = Scatter(part, n2g, rows, (rd, rx, ry, rz, rv), sems[22:])
    gc.begin()
    loads = [pltpu.make_async_copy(a, b, wsem.at[i]) for i, (a, b) in enumerate([(wg_h, wg), (wu_h, wu), (wd_h, wd)])]
    me = lax.axis_index("dp").astype(F32)
    hits = [meta[:, r, :] == me for r in range(TOPK)]
    member = sum(h.astype(F32) for h in hits)
    coef[...] = sum(jnp.where(h, meta[:, TOPK + r, :], 0.0) for r, h in enumerate(hits))
    i0, i1 = lax.broadcasted_iota(jnp.int32, (HD, HD), 0), lax.broadcasted_iota(jnp.int32, (HD, HD), 1)
    local = dot(member.astype(BF), (i0 < i1).astype(BF), 1, 0)
    count = jnp.broadcast_to(jnp.sum(member, 1, keepdims=True), member.shape).astype(BF)
    j0, j1 = lax.broadcasted_iota(jnp.int32, (16, 16), 0), lax.broadcasted_iota(jnp.int32, (16, 16), 1)
    before = dot((j1 < j0).astype(BF), count, 1, 0)
    kept = (member > 0.0) & (local + before < cap[0].astype(F32))
    rank[...] = jnp.where(kept, local, -1.0)
    wload.wait()

    def attend_cols(t, carry):
        w = part[pl.ds(2 * t, 2)].reshape(2 * rows, width)
        att[:, pl.ds(pl.multiple_of(t * 2 * rows, 2 * rows), 2 * rows)] = dot(ctx[...], w, 1, 1)
        return carry

    lax.fori_loop(0, 8, attend_cols, 0)
    n2[...] = rmsnorm(tok[...].astype(F32) + att[...], gain[...]).astype(BF)
    gn.begin()
    for c in loads:
        c.start()
    saves = []
    both = lambda name, k: [getattr(g, name)(k) for g in (gn, gc)]
    both("near", 1)
    both("far", 0)
    both("near", 2)
    both("over", 0)
    for i, k in enumerate(ORDER):
        both("ready", k)
        if k == 1:
            both("far", 2)
            both("near", 3)
        if k == 0:
            sc.near(1)
            both("over", 2)
        if k == 3:
            sc.near(0)
            sc.along(1)
        if k == 2:
            sc.near(3)
            sc.along(0)
        for c in saves:
            c.wait()
        if i == 0:
            for c in loads:
                c.wait()

        def collect(j, carry):
            b = place_of(k, j)
            to = pl.ds(pl.multiple_of(j * SLOTS, SLOTS), SLOTS)
            s0 = lax.broadcasted_iota(jnp.int32, (SLOTS, rows), 0).astype(F32)
            mine = s0 == rank[pl.ds(b, 1), :]
            sw[to, :] = jnp.sum(jnp.where(mine, coef[pl.ds(b, 1), :], 0.0), 1, keepdims=True)
            pick[to, :] = mine.astype(BF)

            def cols(n, c):
                w = pl.ds(pl.multiple_of(n * 512, 512), 512)
                xr[to, w] = dot(pick[to, :], nall[b, :, w], 1, 0).astype(BF)
                pg[to, w] = (dot(pick[to, :], call[b, :, w], 1, 0) * sw[to, :]).astype(BF)
                return c

            return lax.fori_loop(0, width // 512, cols, carry)

        lax.fori_loop(0, 4, collect, 0)

        def inner(n, carry):
            w = pl.ds(pl.multiple_of(n * COLS, COLS), COLS)
            gate = dot(xr[...], wg[:, w], 1, 0)
            up = dot(xr[...], wu[:, w], 1, 0)
            hg = dot(pg[...], wd[w, :], 1, 1)
            sig = jax.nn.sigmoid(gate)
            hid[:, w] = (gate * sig * up).astype(BF)
            gg[:, w] = (hg * up * sig * (1.0 + gate * (1.0 - sig))).astype(BF)
            ug[:, w] = (hg * gate * sig).astype(BF)
            return carry

        lax.fori_loop(0, hid.shape[1] // COLS, inner, 0)

        def outer(n, carry):
            w = pl.ds(pl.multiple_of(n * COLS, COLS), COLS)
            eo = dot(hid[...], wd[:, w], 1, 0).astype(BF).astype(F32)
            rg = (dot(gg[...], wg[w, :], 1, 1) + dot(ug[...], wu[w, :], 1, 1)).astype(BF)
            for j in range(4):
                b = place_of(k, j)
                cut = slice(j * SLOTS, (j + 1) * SLOTS)
                weighted = (eo[cut] * sw[cut]).astype(BF)
                stage[j, :, w] = dot(pick[cut], weighted, 0, 0).astype(BF)
                part[b, :, w] = dot(pick[cut], rg[cut], 0, 0).astype(BF)
            return carry

        lax.fori_loop(0, xr.shape[1] // COLS, outer, 0)
        if k % 2:
            sc.lift(k)
        else:
            sc.far(k)
        saves = [
            pltpu.make_async_copy(a, o.at[k], osem.at[i])
            for i, (a, o) in enumerate([(xr, xr_o), (pg, pg_o), (hid, hid_o), (gg, gg_o), (ug, ug_o)])
        ] + [pltpu.make_async_copy(stage.at[j], p1.at[place_of(k, j)], psem.at[j]) for j in range(4)]
        for c in saves:
            c.start()
    gn.end()
    gc.end()
    sc.near(2)
    sc.along(3)
    sc.along(2)
    sc.end()
    for c in saves:
        c.wait()


def expert(ctx, wout, tokens, gain, cot, meta, cap, wg, wu, wd, cid):
    rows, width = ctx.shape
    ff = wg.shape[1]
    chunk = 4 * SLOTS
    save = lambda w: jax.ShapeDtypeStruct((4, chunk, w), BF)
    v = lambda *shape: pltpu.VMEM(shape, BF)
    f = lambda *shape: pltpu.VMEM(shape, F32)
    return pl.pallas_call(
        expert_kernel,
        out_shape=[
            jax.ShapeDtypeStruct((rows, width), F32),
            jax.ShapeDtypeStruct((rows, width), F32),
            jax.ShapeDtypeStruct((16, rows, width), BF),
            save(width), save(width), save(ff), save(ff), save(ff),
        ],
        in_specs=[VM, ANY, VM, VM, ANY, VM, pl.BlockSpec(memory_space=pltpu.SMEM), ANY, ANY, ANY],
        out_specs=[VM, VM] + [ANY] * 6,
        scratch_shapes=[
            v(rows, width), f(16, rows), f(16, rows), v(chunk, rows), f(chunk, 1),
            v(16, rows, width), v(16, rows, width), v(16, rows, width), v(4, rows, width),
            v(width, ff), v(width, ff), v(ff, width),
            v(chunk, width), v(chunk, width), v(chunk, ff), v(chunk, ff), v(chunk, ff),
        ]
        + scatter_bufs(rows, width)
        + [pltpu.SemaphoreType.DMA, pltpu.SemaphoreType.DMA((3,)), pltpu.SemaphoreType.DMA((5,)), pltpu.SemaphoreType.DMA((4,))]
        + GATHER_SEMS * 2
        + SCATTER_SEMS,
        compiler_params=params(cid, 62),
        name="expert",
    )(ctx, wout, tokens, gain, cot, meta, cap, wg, wu, wd)


TILE = (256, 1024)


def weights_kernel(
    p1, xr_h, pg_h, hid_h, gg_h, ug_h, wout, n2g, tok, att, cot, gain,
    mix, gate_o, up_o, down_o, ag, mg, gain_g, cgh,
    part, wo, cg, xr, pg, hid, gg, ug, give, got, rd, rx, ry, rz, rv, lsem, wsem, gs, gr, os_, cs, cr, co, *sems,
):
    me = lax.axis_index("dp")
    blk = lambda b: pl.ds(pl.multiple_of(b * HD, HD), HD)
    loads = [
        pltpu.make_async_copy(a, b, lsem.at[i])
        for i, (a, b) in enumerate(
            [(p1, part), (xr_h, xr), (gg_h, gg), (ug_h, ug), (hid_h, hid), (pg_h, pg)]
        )
    ]
    column_load = lambda t: pltpu.make_async_copy(
        wout.at[:, pl.ds(pl.multiple_of(t * HD, HD), HD)], wo.at[lax.rem(t, 2)], wsem.at[lax.rem(t, 2)]
    )
    column_load(0).start()
    for c in loads:
        c.start()
    gain_g[...] = jnp.zeros_like(gain_g)

    def middle_rows(i, carry):
        rows = pl.ds(pl.multiple_of(i * 16, 16), 16)
        back, gains = rmsnorm_pull(tok[rows].astype(F32) + att[rows], gain[...], n2g[rows])
        gain_g[...] += jnp.sum(gains, 0, keepdims=True)
        grad = cot[rows].astype(F32) + back
        mg[rows] = grad
        ag[rows] = grad.astype(BF)
        return carry

    lax.fori_loop(0, tok.shape[0] // 16, middle_rows, 0)
    barrier([lax.rem(me + d, 16) for d in range(1, 16)], pair=True)
    sc = Scatter(part, mix, part.shape[1], (rd, rx, ry, rz, rv), sems)
    loads[0].wait()
    sc.lift(1)
    sc.lift(3)
    sc.near(3)
    sc.near(1)
    tiles = cg.shape[1] // HD

    def context_cols(t, carry):
        @pl.when(t + 1 < tiles)
        def _():
            column_load(t + 1).start()

        column_load(t).wait()
        cols = pl.ds(pl.multiple_of(t * HD, HD), HD)
        cg[:, cols] = dot(ag[...], wo[lax.rem(t, 2)], 1, 0).astype(BF)
        return carry

    lax.fori_loop(0, tiles, context_cols, 0)

    def hop(d):
        to = lax.rem(me + d, 16)
        return pltpu.make_async_remote_copy(
            src_ref=cg.at[:, blk(to)], dst_ref=cgh.at[blk(me)], send_sem=cs.at[d], recv_sem=cr.at[d],
            device_id={"dp": to}, device_id_type=MESH,
        )

    for d in range(1, 16):
        hop(d).start()
    stay = pltpu.make_async_copy(cg.at[:, blk(me)], cgh.at[blk(me)], co)
    stay.start()
    sc.far(2)
    sc.far(0)
    for c in loads[1:]:
        c.wait()
    r, w = TILE
    strip = lambda a, t, size: a[:, pl.ds(pl.multiple_of(t * size, size), size)]

    def product(m, t):
        left = strip((xr, hid)[m], t, r).T
        for e in range(2):
            yield dot(left, (gg, ug)[e][...] if m == 0 else pg[:, e * w : (e + 1) * w], 1, 0)

    def home(m, t, e):
        rows = pl.ds(pl.multiple_of(t * r, r), r)
        return (gate_o, up_o)[e].at[rows] if m == 0 else down_o.at[rows, pl.ds(e * w, w)]

    def sent(m, t):
        s = lax.rem(t, 2)
        return pltpu.make_async_remote_copy(
            src_ref=give.at[s], dst_ref=got.at[8 * m + t], send_sem=gs.at[s], recv_sem=gr.at[8 * m + t],
            device_id={"grp": partner()}, device_id_type=MESH,
        )

    def saved(m, t):
        s = lax.rem(t, 2)
        return [pltpu.make_async_copy(got.at[8 * m + t, e], home(m, t, e), os_.at[s, e]) for e in range(2)]

    def finish(m, t):
        s = lax.rem(t, 2)
        sent(m, t).wait_recv()
        got[8 * m + t] = (give[s].astype(F32) + got[8 * m + t].astype(F32)).astype(BF)
        for c in saved(m, t):
            c.start()

    def free(m, t):
        sent(m, t).wait_send()
        for c in saved(m, t):
            c.wait()

    def body(m, start):
        def step(t, carry):
            s = lax.rem(t, 2)

            @pl.when(t >= start + 2)
            def _():
                free(m, t - 2)

            for e, tile in enumerate(product(m, t)):
                give[s, e] = tile.astype(BF)
            sent(m, t).start()

            @pl.when(t >= start + 1)
            def _():
                finish(m, t - 1)

            return carry

        return step

    for i, (m, start) in enumerate(((0, 0), (0, 4), (1, 0))):
        lax.fori_loop(start, start + 4, body(m, start), 0)
        finish(m, start + 3)
        free(m, start + 2)
        free(m, start + 3)
        if i == 0:
            sc.near(2)
            sc.near(0)
            sc.along(3)
        if i == 1:
            sc.along(1)
            sc.along(2)
    sc.along(0)
    sc.end()
    stay.wait()
    for d in range(1, 16):
        hop(d).wait()


def expert_weights(p1, xr, pg, hid, gg, ug, wout, n2g, tokens, att, cot, gain, cid):
    _, rows, width = p1.shape
    n, ff = gg.shape
    seq = wout.shape[0]
    r, w = TILE
    v = lambda *shape: pltpu.VMEM(shape, BF)
    sem = lambda *shape: pltpu.SemaphoreType.DMA(shape) if shape else pltpu.SemaphoreType.DMA
    b = lambda *shape: jax.ShapeDtypeStruct(shape, BF)
    f = lambda *shape: jax.ShapeDtypeStruct(shape, F32)
    return pl.pallas_call(
        weights_kernel,
        out_shape=[
            f(rows, width), b(width, ff), b(width, ff), b(ff, width), b(rows, width), f(rows, width), f(1, width),
            b(16 * rows, HD),
        ],
        in_specs=[ANY] * 7 + [VM] * 5,
        out_specs=[VM] + [ANY] * 3 + [VM] * 3 + [ANY],
        scratch_shapes=[
            v(16, rows, width), v(2, seq, HD), v(rows, width),
            v(n, width), v(n, width), v(n, ff), v(n, ff), v(n, ff), v(2, 2, r, w), v(12, 2, r, w),
        ]
        + scatter_bufs(rows, width)
        + [sem(6), sem(2), sem(2), sem(12), sem(2, 2), sem(16), sem(16), sem()]
        + SCATTER_SEMS,
        compiler_params=params(cid, 63),
        name="expert_weights",
    )(p1, xr, pg, hid, gg, ug, wout, n2g, tokens, att, cot, gain)


def back_kernel(
    cgh, q, k, v, seg, sk, lse, cosf, sinf, wh, nall, ag, ctx,
    ngrad, out_t, qkv_t,
    dkt, dvt, pgrad, pgt, opair, osum, ostage, ord_, orx, ory, orz,
    part, rd, rx, ry, rz, ntile, qpart, qpair,
    lo, ops, opr, ofs, ofr, nsem, qs, qr, ts, tr, fs, fr, *sems,
):
    me = lax.axis_index("dp")
    core = lax.axis_index("grp") % 2
    hr = HD // 2
    mine, other = pl.multiple_of(core * hr, hr), pl.multiple_of((1 - core) * hr, hr)
    blk = lambda b: pl.ds(pl.multiple_of(b * HD, HD), HD)
    barrier([lax.rem(me + d, 16) for d in range(1, 16)], pair=True)
    tiles = [
        pltpu.make_async_copy(nall.at[:, pl.ds(t * 256, 256)], ntile.at[t % 2], nsem.at[t % 2])
        for t in range(wh.shape[1] // 256)
    ]

    pairs = {}
    for j in (3, 1, 2, 0):
        for kk in range(4):
            part[4 * j + kk] = dot(ag[:, blk(place_of(kk, j))], ctx[...], 0, 0).astype(BF)
        group = pl.ds(4 * j, 4)
        pairs[j] = push_pair(part.at[group, pl.ds(other, hr)], opair.at[group], ops.at[j], opr.at[j])
    dkt[...] = jnp.zeros_like(dkt)
    dvt[...] = jnp.zeros_like(dvt)
    so = PlainScatter(opair, osum, hr, (ord_, orx, ory, orz), sems[:10])
    so.at = {name: [4 * j + kk for kk in range(4)] for j, name in enumerate(("col", "X", "Y", "D"))}
    sn = PlainScatter(part, ngrad, HD, (rd, rx, ry, rz), sems[10:20])
    def out_pair(j):
        pairs[j].wait_recv()

        def add(b, carry):
            opair[b] = (opair[b].astype(F32) + part[b, pl.ds(mine, hr)].astype(F32)).astype(BF)
            return carry

        lax.fori_loop(4 * j, 4 * j + 4, add, 0)

    def attend_rows(i, carry):
        row = blk(i)
        s = dot(q[row], k[...], 1, 1)
        prob = jnp.where(column(seg, i) == sk[...], jnp.exp2(s * (SCALE * LOG2E) - lse[row]), 0.0)
        dp = dot(cgh[row], v[...], 1, 1)
        delta = jnp.sum(prob * dp, -1, keepdims=True)
        ds = (prob * (dp - delta)).astype(BF)
        dq = dot(ds, k[...], 1, 0) * SCALE
        dq = dq * cosf[row] - pltpu.roll(dq, HD // 2, 1) * sinf[row]
        pgrad[row, :HD] = dq.astype(BF)
        pgt[:HD, row] = dq.T.astype(BF)
        dkt[...] += dot(q[row], ds, 0, 0)
        dvt[...] += dot(cgh[row], prob.astype(BF), 0, 0)
        return carry

    n = q.shape[0] // HD
    q4 = n // 4
    lax.fori_loop(0, q4 // 2, attend_rows, 0)
    out_pair(3)
    for j in FAR_FIRST:
        so.far(j)
    lax.fori_loop(q4 // 2, 2 * q4, attend_rows, 0)
    out_pair(1)
    out_pair(2)
    so.near(3)
    so.near(2)
    lax.fori_loop(2 * q4, 3 * q4, attend_rows, 0)
    so.near(1)
    so.near(0)
    out_pair(0)
    lax.fori_loop(3 * q4, n, attend_rows, 0)
    for c in pairs.values():
        c.wait_send()

    def turn_back(i, carry):
        row = blk(i)
        dk = dkt[:, row].T * SCALE
        dk = dk * cosf[row] - pltpu.roll(dk, HD // 2, 1) * sinf[row]
        pgrad[row, HD : 2 * HD] = dk.astype(BF)
        pgt[HD : 2 * HD, row] = dk.T.astype(BF)
        dv = dvt[:, row]
        pgrad[row, 2 * HD :] = dv.T.astype(BF)
        pgt[2 * HD :, row] = dv.astype(BF)
        return carry

    lax.fori_loop(0, n, turn_back, 0)
    tiles[0].start()

    def back_block(j, kk):
        b = place_of(kk, j)
        part[b] = dot(pgrad[blk(b)], wh[...], 1, 0).astype(BF)

    for kk in FAR_FIRST:
        back_block(3, kk)
        sn.far(kk)
    for j in FAR_FIRST:
        so.along(j)
    for t, c in enumerate(tiles):
        if t + 1 < len(tiles):
            tiles[t + 1].start()
        c.wait()
        qpart[:, t * 256 : (t + 1) * 256] = dot(pgt[...], ntile[t % 2], 1, 0).astype(BF)
    qc = [push_pair(qpart.at[pl.ds(s * HD + other, hr)], qpair.at[s], qs.at[s], qr.at[s]) for s in range(3)]
    so.end()
    ostage[...] = osum[...].astype(BF)
    keep = pltpu.make_async_copy(ostage, out_t.at[pl.ds(mine, hr)], lo)
    keep.start()
    give = push_pair(ostage, out_t.at[pl.ds(mine, hr)], ofs, ofr)
    for kk in FAR_FIRST:
        back_block(1, kk)
        back_block(2, kk)
        sn.near(kk)
    for s in range(3):
        qc[s].wait_recv()
        qpair[s] = (qpair[s].astype(F32) + qpart[pl.ds(s * HD + mine, hr)].astype(F32)).astype(BF)
        b = 16 * s + me
        to, slot = b // 3, lax.rem(b, 3)
        dst = qkv_t.at[pl.ds(pl.multiple_of(slot * HD + core * hr, hr), hr)]

        @pl.when(to != me)
        def _():
            push(qpair.at[s], dst, ts.at[s], tr.at[slot], to)

        @pl.when(to == me)
        def _():
            pltpu.make_async_copy(qpair.at[s], dst, tr.at[slot]).start()

    for kk in FAR_FIRST:
        back_block(0, kk)
    for kk in FAR_FIRST:
        sn.along(kk)
    fc = []
    for s in range(3):
        here = qkv_t.at[pl.ds(pl.multiple_of(s * HD + core * hr, hr), hr)]
        pltpu.make_async_copy(here, here, tr.at[s]).wait()
        fc.append(push_pair(here, here, fs.at[s], fr.at[s]))
    sn.end()
    for s in range(3):

        @pl.when((16 * s + me) // 3 != me)
        def _():
            pltpu.make_async_copy(qpair.at[s], qpair.at[s], ts.at[s]).wait()

    keep.wait()
    give.wait()
    for c in qc:
        c.wait_send()
    for c in fc:
        c.wait()


def back(cgh, q, k, v, seg, sk, lse, cosf, sinf, wh, nall, ag, ctx, cid):
    rows, width = ag.shape
    seq = q.shape[0]
    vb = lambda *shape: pltpu.VMEM(shape, BF)
    vf = lambda *shape: pltpu.VMEM(shape, F32)
    sem = lambda *shape: pltpu.SemaphoreType.DMA(shape) if shape else pltpu.SemaphoreType.DMA
    return pl.pallas_call(
        back_kernel,
        out_shape=[
            jax.ShapeDtypeStruct((rows, width), F32),
            jax.ShapeDtypeStruct((rows, width), BF),
            jax.ShapeDtypeStruct((3 * HD, width), BF),
        ],
        in_specs=[VM] * 10 + [ANY, VM, VM],
        out_specs=[VM, ANY, ANY],
        scratch_shapes=[
            vf(HD, seq), vf(HD, seq), vb(seq, 3 * HD), vb(3 * HD, seq),
            vb(16, rows // 2, width), vf(rows // 2, width), vb(rows // 2, width),
        ]
        + plain_bufs(rows // 2, width)
        + [vb(16, rows, width)]
        + plain_bufs(rows, width)
        + [vb(2, seq, 256), vb(3 * HD, width), vb(3, HD // 2, width)]
        + [sem(), sem(4), sem(4), sem(), sem(), sem(2), sem(3), sem(3), sem(3), sem(3), sem(3), sem(3)]
        + SCATTER_SEMS * 2,
        compiler_params=params(cid, 62),
        name="back",
    )(cgh, q, k, v, seg, sk, lse, cosf, sinf, wh, nall, ag, ctx)


def total_kernel(x, dp_o, pair_o, got, fromp, ss, rs, ps, pr):
    me = lax.axis_index("dp")
    barrier([lax.rem(me + d, 16) for d in range(1, 16)], pair=True)
    sent = [push(x, got.at[me], ss.at[d], rs.at[d], lax.rem(me + d, 16)) for d in range(1, 16)]
    got[me] = x[...]
    for c in sent:
        c.wait_recv()
    acc = got[0]
    for j in range(1, 16):
        acc = acc + got[j]
    dp_o[...] = acc
    c = push_pair(dp_o, fromp, ps, pr)
    c.wait()
    pair_o[...] = acc + fromp[...]
    for c in sent:
        c.wait_send()


def total(x, cid):
    sem = pltpu.SemaphoreType.DMA
    return pl.pallas_call(
        total_kernel,
        out_shape=[jax.ShapeDtypeStruct(x.shape, F32)] * 2,
        in_specs=[VM],
        out_specs=[VM, VM],
        scratch_shapes=[pltpu.VMEM((16,) + x.shape, F32), pltpu.VMEM(x.shape, F32), sem((16,)), sem((16,)), sem, sem],
        compiler_params=params(cid, 16),
        name="total",
    )(x)


def rotary_tables(length):
    freq = (THETA ** (-(np.arange(HD // 2) * 2.0 / HD))).astype(np.float32)
    angle = (np.arange(length, dtype=np.float32)[:, None] * freq[None, :]).astype(np.float64)
    cos, sin = np.cos(angle).astype(np.float32), np.sin(angle).astype(np.float32)
    return np.concatenate([cos, cos], 1), np.concatenate([-sin, sin], 1)


def per_device(
    tokens, segments, routes, route_weight, capacity, norm_gain,
    qkv_weight, out_weight, gate_weight, up_weight, down_weight, cotangent,
):
    rows, width = tokens.shape
    seq = segments.shape[0]
    me = lax.axis_index("dp")
    gain1_row, gain2_row = norm_gain[:1], norm_gain[1:]
    stream = tokens.astype(F32)
    meta = jnp.concatenate([routes.astype(F32).T, route_weight.T], 0)
    seg = segments.astype(F32).reshape(16, rows)
    sk = jnp.where(segments == 0, -1.0, segments.astype(F32))[None, :]
    cos_table, sin_table = rotary_tables(seq)
    normed_all, meta_all, w_head, q, k, v, lse, context, dense_out = front(
        tokens, gain1_row, meta, qkv_weight, out_weight, cos_table, sin_table, seg, sk, 0
    )
    attended, n2g, mix_part, xr, pg, hidden, gg, ug = expert(
        context, dense_out, tokens, gain2_row, cotangent, meta_all, capacity,
        gate_weight[0], up_weight[0], down_weight[0], 3,
    )
    flat = lambda a: a.reshape(-1, a.shape[2])
    mixture, gate_g, up_g, down_g, attended_grad, middle_grad, gain2, cgh = expert_weights(
        mix_part, flat(xr), flat(pg), flat(hidden), flat(gg), flat(ug), flat(dense_out),
        n2g, tokens, attended, cotangent, gain2_row, 5,
    )
    layer = stream + attended + mixture
    own_seg = lax.dynamic_slice_in_dim(segments, me * rows, rows)
    valid = (own_seg != 0).astype(F32)
    sums = jnp.stack(
        [
            jnp.sum(valid * jnp.sum(layer * layer, -1)),
            jnp.sum(valid * jnp.sum(attended * attended, -1)),
            jnp.sum(valid * jnp.sum(mixture * mixture, -1)),
            jnp.sum(valid) * width,
        ]
    )
    normed_grad, out_total, qkv_total = back(
        cgh, q, k, v, seg, sk, lse, cos_table, sin_table, w_head, flat(normed_all), attended_grad, context, 6
    )
    sg, gain1 = rmsnorm_pull(stream, gain1_row, normed_grad)
    tokens_grad = middle_grad + sg
    small = jnp.concatenate([jnp.sum(gain1, 0), gain2[0], sums, jnp.zeros((1024 - sums.size,), F32)]).reshape(-1, HD)
    in_group, in_pair = total(small, 4)
    seq_sums = in_group.reshape(-1)[2 * width : 2 * width + 4]
    gain_pair = in_pair.reshape(-1)[: 2 * width].reshape(2, width)
    stat_row = jnp.sqrt(seq_sums[:3] / seq_sums[3]).reshape(1, 3)
    groups = lax.axis_size("grp")
    over = lambda a: a.astype(F32) if groups == 2 else lax.psum(a.astype(BF), "grp").astype(F32) * 0.5
    return (
        layer.astype(BF),
        tokens_grad,
        over(qkv_total),
        over(out_total),
        over(gate_g)[None],
        over(up_g)[None],
        over(down_g)[None],
        gain_pair if groups == 2 else lax.psum(gain_pair, "grp") * 0.5,
        stat_row,
    )


def solution(mesh):
    both = ("grp", "dp")
    in_specs = (
        P(both, None), P("grp"), P(both, None), P(both, None), P(), P(),
        P("dp", None), P("dp", None), P("dp", None, None), P("dp", None, None), P("dp", None, None),
        P(both, None),
    )
    out_specs = (
        P(both, None), P(both, None), P("dp", None), P("dp", None),
        P("dp", None, None), P("dp", None, None), P("dp", None, None), P(), P("grp", None),
    )
    return jax.shard_map(per_device, mesh=mesh, in_specs=in_specs, out_specs=out_specs, check_vma=False)
```

```python
import functools

import jax
import jax.numpy as jnp
import numpy as np
from jax import lax
from jax.experimental import pallas as pl
from jax.experimental.pallas import tpu as pltpu
from jax.sharding import PartitionSpec as P

H = 16
HD = 128
TOPK = 8
EPS = 1e-06
THETA = 50000.0
MESH = pl.DeviceIdType.MESH
MIB = 2**20
BF = jnp.bfloat16
F32 = jnp.float32
SCALE = HD**-0.5
LOG2E = 1.4426950408889634


def places():
    me = lax.axis_index("dp")
    z, y, x = me // 4, (me // 2) % 2, me % 2
    xor = [z, z + 1 - 2 * (z % 2), (z + 2) % 4, 3 - z]
    at = lambda k, yy, xx: xor[k] * 4 + yy * 2 + xx
    return dict(
        me=me,
        col=[at(k, y, x) for k in range(4)],
        X=[at(k, y, 1 - x) for k in range(4)],
        Y=[at(k, 1 - y, x) for k in range(4)],
        D=[at(k, 1 - y, 1 - x) for k in range(4)],
    )


def barrier(targets, pair=False):
    sem = pltpu.get_barrier_semaphore()
    for t in targets:
        pl.semaphore_signal(sem, inc=1, device_id={"dp": t}, device_id_type=MESH)
    count = len(targets)
    if pair:
        pl.semaphore_signal(sem, inc=1, device_id={"grp": partner()}, device_id_type=MESH)
        count += 1
    pl.semaphore_wait(sem, count)


def partner():
    g = lax.axis_index("grp")
    return g + 1 - 2 * (g % 2)


def push(src, dst, send, recv, to):
    c = pltpu.make_async_remote_copy(
        src_ref=src, dst_ref=dst, send_sem=send, recv_sem=recv,
        device_id={"dp": to}, device_id_type=MESH,
    )
    c.start()
    return c


def push_pair(src, dst, send, recv):
    c = pltpu.make_async_remote_copy(
        src_ref=src, dst_ref=dst, send_sem=send, recv_sem=recv,
        device_id={"grp": partner()}, device_id_type=MESH,
    )
    c.start()
    return c


ORDER = (1, 0, 3, 2)
GATHER_SEMS = (
    [pltpu.SemaphoreType.DMA((4,))] * 6 + [pltpu.SemaphoreType.DMA((4, 2))] * 2 + [pltpu.SemaphoreType.DMA]
    + [pltpu.SemaphoreType.DMA((4,))] * 2
)


class Gather:
    def __init__(self, src, dst, rows, sems, first=0):
        self.src, self.dst, self.rows, self.sems, self.first, self.p = src, dst, rows, sems, first, places()

    def block(self, b):
        return self.dst.at[b, pl.ds(self.first, self.rows)]

    def part(self, b, h):
        half = self.rows // 2
        return self.dst.at[b, pl.ds(self.first + h * half, half)]

    def begin(self):
        zs, zr, xs, xr, ys, yr, _, _, own, _, _ = self.sems
        p, src = self.p, self.src
        me = p["me"]
        self.mine = pltpu.make_async_copy(src, self.block(me), own)
        self.mine.start()
        self.xc = {0: push(src, self.block(me), xs.at[0], xr.at[0], p["X"][0])}
        self.yc = {0: push(src, self.block(me), ys.at[0], yr.at[0], p["Y"][0])}
        self.zc = {k: push(src, self.block(me), zs.at[k], zr.at[k], p["col"][k]) for k in (1, 2, 3)}
        self.dc, self.vc = {}, {}

    def near(self, k):
        _, _, xs, xr, ys, yr = self.sems[:6]
        p = self.p
        self.zc[k].wait_recv()
        b = self.block(p["col"][k])
        self.xc[k] = push(b, b, xs.at[k], xr.at[k], p["X"][0])
        self.yc[k] = push(b, b, ys.at[k], yr.at[k], p["Y"][0])

    def far(self, k):
        ds, dr = self.sems[6:8]
        p = self.p
        b = self.part(p["X"][k], 0)
        self.xc[k].wait_recv()
        self.dc[k, 0] = push(b, b, ds.at[k, 0], dr.at[k, 0], p["Y"][0])
        b = self.part(p["Y"][k], 1)
        self.yc[k].wait_recv()
        self.dc[k, 1] = push(b, b, ds.at[k, 1], dr.at[k, 1], p["X"][0])

    def over(self, k):
        vs, vr = self.sems[9:11]
        self.dc[k, 0].wait_recv()
        self.dc[k, 1].wait_recv()
        b = self.block(self.p["D"][k])
        self.vc[k] = push(b, b, vs.at[k], vr.at[k], self.p["col"][1])

    def ready(self, k):
        if k == 0:
            self.mine.wait()
        if k % 2:
            self.xc[k].wait_recv()
            self.yc[k].wait_recv()
            self.vc[k - 1].wait_recv()

    def end(self):
        for group in (self.xc, self.yc, self.zc, self.dc, self.vc):
            for c in group.values():
                c.wait_send()


def gather_targets():
    p = places()
    return [p["col"][1], p["col"][2], p["col"][3], p["X"][0], p["Y"][0]]


SCATTER_SEMS = [pltpu.SemaphoreType.DMA((4, 2))] * 2 + [pltpu.SemaphoreType.DMA((4,))] * 8


def scatter_bufs(rows, width):
    return [
        pltpu.VMEM((4, rows // 2, width), BF),
        pltpu.VMEM((4, rows, width), BF),
        pltpu.VMEM((4, rows, width), BF),
        pltpu.VMEM((4, rows, width), BF),
        pltpu.VMEM((2, rows, width), BF),
    ]


class Scatter:
    def __init__(self, part, out, rows, bufs, sems):
        self.part, self.out, self.half, self.bufs, self.sems, self.p = part, out, rows // 2, bufs, sems, places()
        self.at = self.p
        self.da, self.db, self.xc, self.yc, self.zc, self.vc = {}, {}, {}, {}, {}, {}

    def lift(self, k):
        vs, vr = self.sems[8:]
        self.vc[k] = push(self.part.at[self.p["D"][k]], self.bufs[4].at[k // 2], vs.at[k], vr.at[k], self.p["col"][1])

    def far(self, k):
        ds, dr = self.sems[:2]
        rd, h, p, part = self.bufs[0], self.half, self.p, self.part
        b = p["D"][k]
        self.vc[k + 1].wait_recv()
        part[b] = (part[b].astype(F32) + self.bufs[4][k // 2].astype(F32)).astype(BF)
        self.da[k] = push(part.at[b, pl.ds(0, h)], rd.at[k], ds.at[k, 0], dr.at[k, 0], p["Y"][0])
        self.db[k] = push(part.at[b, pl.ds(h, h)], rd.at[k + 1], ds.at[k, 1], dr.at[k, 1], p["X"][0])

    def near(self, k):
        xs, xr, ys, yr = self.sems[2:6]
        rd, rx, ry = self.bufs[:3]
        part, h, p = self.part, self.half, self.p
        b = p["X"][k]
        if k % 2 == 0:
            self.da[k].wait_recv()
            part[b, pl.ds(0, h)] = (part[b, pl.ds(0, h)].astype(F32) + rd[k].astype(F32)).astype(BF)
        self.xc[k] = push(part.at[b], rx.at[k], xs.at[k], xr.at[k], p["X"][0])
        b = p["Y"][k]
        if k % 2 == 0:
            self.db[k].wait_recv()
            part[b, pl.ds(h, h)] = (part[b, pl.ds(h, h)].astype(F32) + rd[k + 1].astype(F32)).astype(BF)
        self.yc[k] = push(part.at[b], ry.at[k], ys.at[k], yr.at[k], p["Y"][0])

    def along(self, k):
        zs, zr = self.sems[6:8]
        rx, ry, rz = self.bufs[1:4]
        part = self.part
        b = self.p["col"][k]
        self.xc[k].wait_recv()
        self.yc[k].wait_recv()
        total = part[b].astype(F32) + rx[k].astype(F32) + ry[k].astype(F32)
        if k:
            part[b] = total.astype(BF)
            self.zc[k] = push(part.at[b], rz.at[k], zs.at[k], zr.at[k], b)
        else:
            self.out[...] = total

    def end(self):
        for k in (1, 2, 3):
            self.zc[k].wait_recv()
            self.out[...] += self.bufs[3][k].astype(F32)
        for group in (self.da, self.db, self.xc, self.yc, self.zc, self.vc):
            for c in group.values():
                c.wait_send()


class PlainScatter(Scatter):
    def far(self, k):
        ds, dr = self.sems[:2]
        rd, h, p = self.bufs[0], self.half, self.p
        b = self.at["D"][k]
        self.da[k] = push(self.part.at[b, pl.ds(0, h)], rd.at[2 * k], ds.at[k, 0], dr.at[k, 0], p["Y"][0])
        self.db[k] = push(self.part.at[b, pl.ds(h, h)], rd.at[2 * k + 1], ds.at[k, 1], dr.at[k, 1], p["X"][0])

    def near(self, k):
        xs, xr, ys, yr = self.sems[2:6]
        rd, rx, ry = self.bufs[:3]
        part, h, p = self.part, self.half, self.p
        b = self.at["X"][k]
        self.da[k].wait_recv()
        part[b, pl.ds(0, h)] = (part[b, pl.ds(0, h)].astype(F32) + rd[2 * k].astype(F32)).astype(BF)
        self.xc[k] = push(part.at[b], rx.at[k], xs.at[k], xr.at[k], p["X"][0])
        b = self.at["Y"][k]
        self.db[k].wait_recv()
        part[b, pl.ds(h, h)] = (part[b, pl.ds(h, h)].astype(F32) + rd[2 * k + 1].astype(F32)).astype(BF)
        self.yc[k] = push(part.at[b], ry.at[k], ys.at[k], yr.at[k], p["Y"][0])

    def along(self, k):
        zs, zr = self.sems[6:8]
        rx, ry, rz = self.bufs[1:4]
        part, b = self.part, self.at["col"][k]
        self.xc[k].wait_recv()
        self.yc[k].wait_recv()
        total = part[b].astype(F32) + rx[k].astype(F32) + ry[k].astype(F32)
        if k:
            part[b] = total.astype(BF)
            self.zc[k] = push(part.at[b], rz.at[k], zs.at[k], zr.at[k], self.p["col"][k])
        else:
            self.out[...] = total


def plain_bufs(rows, width):
    return [pltpu.VMEM((8, rows // 2, width), BF)] + scatter_bufs(rows, width)[1:4]


FAR_FIRST = (3, 2, 1, 0)


ANY = pl.BlockSpec(memory_space=pl.ANY)
VM = pl.BlockSpec(memory_space=pltpu.VMEM)


def params(cid, vmem=60):
    return pltpu.CompilerParams(collective_id=cid, has_side_effects=True, vmem_limit_bytes=vmem * MIB)


def rmsnorm(field, gain_row):
    return field * lax.rsqrt(jnp.mean(field * field, -1, keepdims=True) + EPS) * gain_row


def rmsnorm_pull(field, gain_row, grad):
    r = lax.rsqrt(jnp.mean(field * field, -1, keepdims=True) + EPS)
    scaled = grad * gain_row
    back = r * scaled - field * (r * r * r * jnp.mean(scaled * field, -1, keepdims=True))
    return back, grad * field * r


def column(rows, b):
    return jnp.broadcast_to(rows[pl.ds(b, 1), :], (8, rows.shape[1])).T[:, :1]


def dot(a, b, ca, cb):
    return lax.dot_general(a, b, (((ca,), (cb,)), ((), ())), preferred_element_type=F32)


def front_kernel(
    tok, gain, m_ref, w_ref, o_ref, cosf, sinf, seg, sk,
    nall_o, mall, wh_o, q, k, v, lse, ctx, oall,
    n_ref, nall, wh, ctxh, ms, mr, mo, ws, wr, ps, pr, wo, no, cs, cr, co, os_, or_, *sems,
):
    me = lax.axis_index("dp")
    core = lax.axis_index("grp") % 2
    hr = HD // 2
    blk = lambda b: pl.ds(pl.multiple_of(b * HD, HD), HD)
    half = lambda s, c: pl.ds(pl.multiple_of(s * HD + c * hr, hr), hr)
    n_ref[...] = rmsnorm(tok[...].astype(F32), gain[...]).astype(BF)
    barrier([lax.rem(me + d, 16) for d in range(1, 16)], pair=True)
    g = Gather(n_ref, nall, n_ref.shape[0], sems[:11])
    go = Gather(o_ref.at[half(0, core)], oall, hr, sems[11:], pl.multiple_of(core * hr, hr))
    g.begin()
    own = pltpu.make_async_copy(m_ref, mall.at[me], mo)
    own.start()
    mc = [push(m_ref, mall.at[me], ms.at[d], mr.at[d], lax.rem(me + d, 16)) for d in range(1, 16)]
    for l in range(3):
        b = 3 * me + l
        to, slot = lax.rem(b, 16), b // 16
        src, dst = w_ref.at[half(l, core)], wh.at[half(slot, core)]

        @pl.when(to != me)
        def _():
            push(src, dst, ws.at[l], wr.at[slot], to)

        @pl.when(to == me)
        def _():
            pltpu.make_async_copy(src, dst, wr.at[slot]).start()

    def project(b, carry):
        row = blk(b)
        out = dot(nall[b], wh[...], 1, 1)
        turn = lambda a: (a * cosf[row] + pltpu.roll(a, HD // 2, 1) * sinf[row]).astype(BF)
        q[row] = turn(out[:, :HD])
        k[row] = turn(out[:, HD : 2 * HD])
        v[row] = out[:, 2 * HD :].astype(BF)
        return carry

    def project_plane(c):
        lax.fori_loop(0, 4, lambda j, carry: project(place_of(c, j), carry), 0)

    g.near(1)
    g.far(0)
    g.near(2)
    g.over(0)
    g.far(2)
    g.near(3)
    go.begin()
    g.over(2)
    pc = []
    for s in range(3):
        dst = wh.at[half(s, core)]
        pltpu.make_async_copy(dst, dst, wr.at[s]).wait()
        pc.append(push_pair(dst, dst, ps.at[s], pr.at[s]))
    go.near(1)
    for p in pc:
        p.wait_recv()
    g.ready(0)
    project_plane(0)
    g.ready(1)
    project_plane(1)
    g.ready(2)
    project_plane(2)
    go.far(0)
    go.near(2)
    g.ready(3)
    project_plane(3)
    saves = [pltpu.make_async_copy(nall, nall_o, no), pltpu.make_async_copy(wh, wh_o, wo)]
    for c in saves:
        c.start()

    def hop(d):
        to = lax.rem(me + d, 16)
        return pltpu.make_async_remote_copy(
            src_ref=ctxh.at[blk(to)], dst_ref=ctx.at[:, blk(me)], send_sem=cs.at[d], recv_sem=cr.at[d],
            device_id={"dp": to}, device_id_type=MESH,
        )

    def attend_rows(d, carry):
        b = lax.rem(me + d, 16)
        row = blk(b)
        s = dot(q[row], k[...], 1, 1)
        s = jnp.where(column(seg, b) == sk[...], s, -1e30)
        peak = jnp.maximum(jnp.max(s, -1, keepdims=True), -1e29)
        ex = jnp.exp2((s - peak) * (SCALE * LOG2E))
        total = jnp.maximum(jnp.sum(ex, -1, keepdims=True), 1.0)
        prob = (ex * (1.0 / total)).astype(BF)
        ctxh[row] = jnp.dot(prob, v[...], preferred_element_type=F32).astype(BF)
        lse[row] = peak * (SCALE * LOG2E) + jnp.log2(total)
        return carry

    def attend_send(d, carry):
        attend_rows(d, carry)
        hop(d).start()
        return carry

    oc = []

    def swap_plane(c):
        go.ready(c)
        z = place_of(c, 0) // 4
        here = oall.at[pl.ds(4 * z, 4), pl.ds(pl.multiple_of(core * hr, hr), hr)]
        oc.append(push_pair(here, here, os_.at[c], or_.at[c]))

    lax.fori_loop(1, 6, attend_send, 0)
    go.over(0)
    go.far(2)
    go.near(3)
    lax.fori_loop(6, 12, attend_send, 0)
    swap_plane(0)
    swap_plane(1)
    lax.fori_loop(12, 16, attend_send, 0)
    attend_rows(0, 0)
    stay = pltpu.make_async_copy(ctxh.at[blk(me)], ctx.at[:, blk(me)], co)
    stay.start()
    go.over(2)
    swap_plane(2)
    swap_plane(3)
    g.end()
    go.end()
    own.wait()
    for c in mc:
        c.wait()
    for l in range(3):
        src = w_ref.at[half(l, core)]

        @pl.when(lax.rem(3 * me + l, 16) != me)
        def _():
            pltpu.make_async_copy(src, src, ws.at[l]).wait()

    for p in pc:
        p.wait_send()
    for c in saves:
        c.wait()
    stay.wait()
    for d in range(1, 16):
        hop(d).wait()
    for c in oc:
        c.wait()


def front(tokens, gain, meta, w, wo, cosf, sinf, seg, sk, cid):
    rows, width = tokens.shape
    seq = cosf.shape[0]
    sem = lambda *shape: pltpu.SemaphoreType.DMA(shape) if shape else pltpu.SemaphoreType.DMA
    b = lambda *shape: jax.ShapeDtypeStruct(shape, BF)
    f = lambda *shape: jax.ShapeDtypeStruct(shape, F32)
    v = lambda *shape: pltpu.VMEM(shape, BF)
    return pl.pallas_call(
        front_kernel,
        out_shape=[
            b(16, rows, width), f(16, *meta.shape), b(3 * HD, width),
            b(seq, HD), b(seq, HD), b(seq, HD), f(seq, 1), b(rows, width), b(16, rows, width),
        ],
        in_specs=[VM, VM] + [ANY] * 3 + [VM] * 4,
        out_specs=[ANY] * 3 + [VM] * 4 + [ANY] * 2,
        scratch_shapes=[v(rows, width), v(16, rows, width), v(3 * HD, width), v(seq, HD)]
        + [sem(16), sem(16), sem(), sem(3), sem(3), sem(3), sem(3), sem(), sem()]
        + [sem(16), sem(16), sem(), sem(4), sem(4)]
        + GATHER_SEMS * 2,
        compiler_params=params(cid),
        name="front",
    )(tokens, gain, meta, w, wo, cosf, sinf, seg, sk)


SLOTS = 80
COLS = 512


def place_of(k, j):
    me = lax.axis_index("dp")
    z, y, x = me // 4, (me // 2) % 2, me % 2
    zk = [z, z + 1 - 2 * (z % 2), (z + 2) % 4, 3 - z][k]
    jy, jx = j // 2, j % 2
    return zk * 4 + (y + jy - 2 * y * jy) * 2 + (x + jx - 2 * x * jx)


def expert_kernel(
    ctx, wout, tok, gain, cot, meta, cap, wg_h, wu_h, wd_h,
    att, n2g, p1, xr_o, pg_o, hid_o, gg_o, ug_o,
    n2, rank, coef, pick, sw, nall, call, part, stage, wg, wu, wd, xr, pg, hid, gg, ug, rd, rx, ry, rz, rv,
    wosem, wsem, osem, psem, *sems,
):
    rows, width = ctx.shape
    wload = pltpu.make_async_copy(wout, part, wosem)
    wload.start()
    barrier(gather_targets())
    gn = Gather(n2, nall, rows, sems[:11])
    gc = Gather(cot, call, rows, sems[11:22])
    sc = Scatter(part, n2g, rows, (rd, rx, ry, rz, rv), sems[22:])
    gc.begin()
    loads = [pltpu.make_async_copy(a, b, wsem.at[i]) for i, (a, b) in enumerate([(wg_h, wg), (wu_h, wu), (wd_h, wd)])]
    me = lax.axis_index("dp").astype(F32)
    hits = [meta[:, r, :] == me for r in range(TOPK)]
    member = sum(h.astype(F32) for h in hits)
    coef[...] = sum(jnp.where(h, meta[:, TOPK + r, :], 0.0) for r, h in enumerate(hits))
    i0, i1 = lax.broadcasted_iota(jnp.int32, (HD, HD), 0), lax.broadcasted_iota(jnp.int32, (HD, HD), 1)
    local = dot(member.astype(BF), (i0 < i1).astype(BF), 1, 0)
    count = jnp.broadcast_to(jnp.sum(member, 1, keepdims=True), member.shape).astype(BF)
    j0, j1 = lax.broadcasted_iota(jnp.int32, (16, 16), 0), lax.broadcasted_iota(jnp.int32, (16, 16), 1)
    before = dot((j1 < j0).astype(BF), count, 1, 0)
    kept = (member > 0.0) & (local + before < cap[0].astype(F32))
    rank[...] = jnp.where(kept, local, -1.0)
    wload.wait()

    def attend_cols(t, carry):
        w = part[pl.ds(2 * t, 2)].reshape(2 * rows, width)
        att[:, pl.ds(pl.multiple_of(t * 2 * rows, 2 * rows), 2 * rows)] = dot(ctx[...], w, 1, 1)
        return carry

    lax.fori_loop(0, 8, attend_cols, 0)
    n2[...] = rmsnorm(tok[...].astype(F32) + att[...], gain[...]).astype(BF)
    gn.begin()
    for c in loads:
        c.start()
    saves = []
    both = lambda name, k: [getattr(g, name)(k) for g in (gn, gc)]
    both("near", 1)
    both("far", 0)
    both("near", 2)
    both("over", 0)
    for i, k in enumerate(ORDER):
        both("ready", k)
        if k == 1:
            both("far", 2)
            both("near", 3)
        if k == 0:
            sc.near(1)
            both("over", 2)
        if k == 3:
            sc.near(0)
            sc.along(1)
        if k == 2:
            sc.near(3)
            sc.along(0)
        for c in saves:
            c.wait()
        if i == 0:
            for c in loads:
                c.wait()

        def collect(j, carry):
            b = place_of(k, j)
            to = pl.ds(pl.multiple_of(j * SLOTS, SLOTS), SLOTS)
            s0 = lax.broadcasted_iota(jnp.int32, (SLOTS, rows), 0).astype(F32)
            mine = s0 == rank[pl.ds(b, 1), :]
            sw[to, :] = jnp.sum(jnp.where(mine, coef[pl.ds(b, 1), :], 0.0), 1, keepdims=True)
            pick[to, :] = mine.astype(BF)

            def cols(n, c):
                w = pl.ds(pl.multiple_of(n * 512, 512), 512)
                xr[to, w] = dot(pick[to, :], nall[b, :, w], 1, 0).astype(BF)
                pg[to, w] = (dot(pick[to, :], call[b, :, w], 1, 0) * sw[to, :]).astype(BF)
                return c

            return lax.fori_loop(0, width // 512, cols, carry)

        lax.fori_loop(0, 4, collect, 0)

        def inner(n, carry):
            w = pl.ds(pl.multiple_of(n * COLS, COLS), COLS)
            gate = dot(xr[...], wg[:, w], 1, 0)
            up = dot(xr[...], wu[:, w], 1, 0)
            hg = dot(pg[...], wd[w, :], 1, 1)
            sig = jax.nn.sigmoid(gate)
            hid[:, w] = (gate * sig * up).astype(BF)
            gg[:, w] = (hg * up * sig * (1.0 + gate * (1.0 - sig))).astype(BF)
            ug[:, w] = (hg * gate * sig).astype(BF)
            return carry

        lax.fori_loop(0, hid.shape[1] // COLS, inner, 0)

        def outer(n, carry):
            w = pl.ds(pl.multiple_of(n * COLS, COLS), COLS)
            eo = dot(hid[...], wd[:, w], 1, 0).astype(BF).astype(F32)
            rg = (dot(gg[...], wg[w, :], 1, 1) + dot(ug[...], wu[w, :], 1, 1)).astype(BF)
            for j in range(4):
                b = place_of(k, j)
                cut = slice(j * SLOTS, (j + 1) * SLOTS)
                weighted = (eo[cut] * sw[cut]).astype(BF)
                stage[j, :, w] = dot(pick[cut], weighted, 0, 0).astype(BF)
                part[b, :, w] = dot(pick[cut], rg[cut], 0, 0).astype(BF)
            return carry

        lax.fori_loop(0, xr.shape[1] // COLS, outer, 0)
        if k % 2:
            sc.lift(k)
        else:
            sc.far(k)
        saves = [
            pltpu.make_async_copy(a, o.at[k], osem.at[i])
            for i, (a, o) in enumerate([(xr, xr_o), (pg, pg_o), (hid, hid_o), (gg, gg_o), (ug, ug_o)])
        ] + [pltpu.make_async_copy(stage.at[j], p1.at[place_of(k, j)], psem.at[j]) for j in range(4)]
        for c in saves:
            c.start()
    gn.end()
    gc.end()
    sc.near(2)
    sc.along(3)
    sc.along(2)
    sc.end()
    for c in saves:
        c.wait()


def expert(ctx, wout, tokens, gain, cot, meta, cap, wg, wu, wd, cid):
    rows, width = ctx.shape
    ff = wg.shape[1]
    chunk = 4 * SLOTS
    save = lambda w: jax.ShapeDtypeStruct((4, chunk, w), BF)
    v = lambda *shape: pltpu.VMEM(shape, BF)
    f = lambda *shape: pltpu.VMEM(shape, F32)
    return pl.pallas_call(
        expert_kernel,
        out_shape=[
            jax.ShapeDtypeStruct((rows, width), F32),
            jax.ShapeDtypeStruct((rows, width), F32),
            jax.ShapeDtypeStruct((16, rows, width), BF),
            save(width), save(width), save(ff), save(ff), save(ff),
        ],
        in_specs=[VM, ANY, VM, VM, ANY, VM, pl.BlockSpec(memory_space=pltpu.SMEM), ANY, ANY, ANY],
        out_specs=[VM, VM] + [ANY] * 6,
        scratch_shapes=[
            v(rows, width), f(16, rows), f(16, rows), v(chunk, rows), f(chunk, 1),
            v(16, rows, width), v(16, rows, width), v(16, rows, width), v(4, rows, width),
            v(width, ff), v(width, ff), v(ff, width),
            v(chunk, width), v(chunk, width), v(chunk, ff), v(chunk, ff), v(chunk, ff),
        ]
        + scatter_bufs(rows, width)
        + [pltpu.SemaphoreType.DMA, pltpu.SemaphoreType.DMA((3,)), pltpu.SemaphoreType.DMA((5,)), pltpu.SemaphoreType.DMA((4,))]
        + GATHER_SEMS * 2
        + SCATTER_SEMS,
        compiler_params=params(cid, 62),
        name="expert",
    )(ctx, wout, tokens, gain, cot, meta, cap, wg, wu, wd)


TILE = (256, 1024)


def weights_kernel(
    p1, xr_h, pg_h, hid_h, gg_h, ug_h, wout, n2g, tok, att, cot, gain,
    mix, gate_o, up_o, down_o, ag, mg, gain_g, cgh,
    part, wo, cg, xr, pg, hid, gg, ug, give, got, rd, rx, ry, rz, rv, lsem, wsem, gs, gr, os_, cs, cr, co, *sems,
):
    me = lax.axis_index("dp")
    blk = lambda b: pl.ds(pl.multiple_of(b * HD, HD), HD)
    loads = [
        pltpu.make_async_copy(a, b, lsem.at[i])
        for i, (a, b) in enumerate(
            [(p1, part), (xr_h, xr), (gg_h, gg), (ug_h, ug), (hid_h, hid), (pg_h, pg)]
        )
    ]
    column_load = lambda t: pltpu.make_async_copy(
        wout.at[:, pl.ds(pl.multiple_of(t * HD, HD), HD)], wo.at[lax.rem(t, 2)], wsem.at[lax.rem(t, 2)]
    )
    column_load(0).start()
    for c in loads:
        c.start()
    gain_g[...] = jnp.zeros_like(gain_g)

    def middle_rows(i, carry):
        rows = pl.ds(pl.multiple_of(i * 16, 16), 16)
        back, gains = rmsnorm_pull(tok[rows].astype(F32) + att[rows], gain[...], n2g[rows])
        gain_g[...] += jnp.sum(gains, 0, keepdims=True)
        grad = cot[rows].astype(F32) + back
        mg[rows] = grad
        ag[rows] = grad.astype(BF)
        return carry

    lax.fori_loop(0, tok.shape[0] // 16, middle_rows, 0)
    barrier([lax.rem(me + d, 16) for d in range(1, 16)], pair=True)
    sc = Scatter(part, mix, part.shape[1], (rd, rx, ry, rz, rv), sems)
    loads[0].wait()
    sc.lift(1)
    sc.lift(3)
    sc.near(3)
    sc.near(1)
    tiles = cg.shape[1] // HD

    def context_cols(t, carry):
        @pl.when(t + 1 < tiles)
        def _():
            column_load(t + 1).start()

        column_load(t).wait()
        cols = pl.ds(pl.multiple_of(t * HD, HD), HD)
        cg[:, cols] = dot(ag[...], wo[lax.rem(t, 2)], 1, 0).astype(BF)
        return carry

    lax.fori_loop(0, tiles, context_cols, 0)

    def hop(d):
        to = lax.rem(me + d, 16)
        return pltpu.make_async_remote_copy(
            src_ref=cg.at[:, blk(to)], dst_ref=cgh.at[blk(me)], send_sem=cs.at[d], recv_sem=cr.at[d],
            device_id={"dp": to}, device_id_type=MESH,
        )

    for d in range(1, 16):
        hop(d).start()
    stay = pltpu.make_async_copy(cg.at[:, blk(me)], cgh.at[blk(me)], co)
    stay.start()
    sc.far(2)
    sc.far(0)
    for c in loads[1:]:
        c.wait()
    r, w = TILE
    strip = lambda a, t, size: a[:, pl.ds(pl.multiple_of(t * size, size), size)]

    def product(m, t):
        left = strip((xr, hid)[m], t, r).T
        for e in range(2):
            yield dot(left, (gg, ug)[e][...] if m == 0 else pg[:, e * w : (e + 1) * w], 1, 0)

    def home(m, t, e):
        rows = pl.ds(pl.multiple_of(t * r, r), r)
        return (gate_o, up_o)[e].at[rows] if m == 0 else down_o.at[rows, pl.ds(e * w, w)]

    def sent(m, t):
        s = lax.rem(t, 2)
        return pltpu.make_async_remote_copy(
            src_ref=give.at[s], dst_ref=got.at[8 * m + t], send_sem=gs.at[s], recv_sem=gr.at[8 * m + t],
            device_id={"grp": partner()}, device_id_type=MESH,
        )

    def saved(m, t):
        s = lax.rem(t, 2)
        return [pltpu.make_async_copy(got.at[8 * m + t, e], home(m, t, e), os_.at[s, e]) for e in range(2)]

    def finish(m, t):
        s = lax.rem(t, 2)
        sent(m, t).wait_recv()
        got[8 * m + t] = (give[s].astype(F32) + got[8 * m + t].astype(F32)).astype(BF)
        for c in saved(m, t):
            c.start()

    def free(m, t):
        sent(m, t).wait_send()
        for c in saved(m, t):
            c.wait()

    def body(m, start):
        def step(t, carry):
            s = lax.rem(t, 2)

            @pl.when(t >= start + 2)
            def _():
                free(m, t - 2)

            for e, tile in enumerate(product(m, t)):
                give[s, e] = tile.astype(BF)
            sent(m, t).start()

            @pl.when(t >= start + 1)
            def _():
                finish(m, t - 1)

            return carry

        return step

    for i, (m, start) in enumerate(((0, 0), (0, 4), (1, 0))):
        lax.fori_loop(start, start + 4, body(m, start), 0)
        finish(m, start + 3)
        free(m, start + 2)
        free(m, start + 3)
        if i == 0:
            sc.near(2)
            sc.near(0)
            sc.along(3)
        if i == 1:
            sc.along(1)
            sc.along(2)
    sc.along(0)
    sc.end()
    stay.wait()
    for d in range(1, 16):
        hop(d).wait()


def expert_weights(p1, xr, pg, hid, gg, ug, wout, n2g, tokens, att, cot, gain, cid):
    _, rows, width = p1.shape
    n, ff = gg.shape
    seq = wout.shape[0]
    r, w = TILE
    v = lambda *shape: pltpu.VMEM(shape, BF)
    sem = lambda *shape: pltpu.SemaphoreType.DMA(shape) if shape else pltpu.SemaphoreType.DMA
    b = lambda *shape: jax.ShapeDtypeStruct(shape, BF)
    f = lambda *shape: jax.ShapeDtypeStruct(shape, F32)
    return pl.pallas_call(
        weights_kernel,
        out_shape=[
            f(rows, width), b(width, ff), b(width, ff), b(ff, width), b(rows, width), f(rows, width), f(1, width),
            b(16 * rows, HD),
        ],
        in_specs=[ANY] * 7 + [VM] * 5,
        out_specs=[VM] + [ANY] * 3 + [VM] * 3 + [ANY],
        scratch_shapes=[
            v(16, rows, width), v(2, seq, HD), v(rows, width),
            v(n, width), v(n, width), v(n, ff), v(n, ff), v(n, ff), v(2, 2, r, w), v(12, 2, r, w),
        ]
        + scatter_bufs(rows, width)
        + [sem(6), sem(2), sem(2), sem(12), sem(2, 2), sem(16), sem(16), sem()]
        + SCATTER_SEMS,
        compiler_params=params(cid, 63),
        name="expert_weights",
    )(p1, xr, pg, hid, gg, ug, wout, n2g, tokens, att, cot, gain)


def back_kernel(
    cgh, q, k, v, seg, sk, lse, cosf, sinf, wh, nall, ag, ctx,
    tok, att, mix, mg, gain1, gain2,
    layer_o, tok_g, stat_o, gain_o, out_t, qkv_t,
    ngrad, valid, gsum, early, late, early_got, late_got, both, both_got,
    es, er, hs, hr_, bs, br,
    dkt, dvt, pgrad, pgt, opair, osum, ostage, ord_, orx, ory, orz,
    part, rd, rx, ry, rz, ntile, qpart, qpair,
    lo, ops, opr, ofs, ofr, nsem, qs, qr, ts, tr, fs, fr, *sems,
):
    me = lax.axis_index("dp")
    core = lax.axis_index("grp") % 2
    hr = HD // 2
    mine, other = pl.multiple_of(core * hr, hr), pl.multiple_of((1 - core) * hr, hr)
    blk = lambda b: pl.ds(pl.multiple_of(b * HD, HD), HD)
    barrier([lax.rem(me + d, 16) for d in range(1, 16)], pair=True)
    tiles = [
        pltpu.make_async_copy(nall.at[:, pl.ds(t * 256, 256)], ntile.at[t % 2], nsem.at[t % 2])
        for t in range(wh.shape[1] // 256)
    ]

    pairs = {}
    for j in (3, 1, 2, 0):
        for kk in range(4):
            part[4 * j + kk] = dot(ag[:, blk(place_of(kk, j))], ctx[...], 0, 0).astype(BF)
        group = pl.ds(4 * j, 4)
        pairs[j] = push_pair(part.at[group, pl.ds(other, hr)], opair.at[group], ops.at[j], opr.at[j])
    strips = [slice(e * HD, (e + 1) * HD) for e in range(16)]
    valid[...] = (column(seg, me) != 0.0).astype(F32)
    early[...] = jnp.zeros_like(early)
    for e, cut in enumerate(strips):
        early[e : e + 1, :] = gain2[:, cut]
    early[19:20, :] = jnp.broadcast_to(jnp.sum(valid[...], 0, keepdims=True) * 16.0, (1, HD))

    def layer_rows(i, carry):
        rows = pl.ds(pl.multiple_of(i * 16, 16), 16)
        layer = tok[rows].astype(F32) + att[rows] + mix[rows]
        layer_o[rows] = layer.astype(BF)
        for e, field in enumerate((layer, att[rows], mix[rows])):
            square = field * field * valid[rows]
            early[16 + e : 17 + e, :] += jnp.sum(sum(square[:, cut] for cut in strips), 0, keepdims=True)
        return carry

    lax.fori_loop(0, HD // 16, layer_rows, 0)
    others = [lax.rem(me + d, 16) for d in range(1, 16)]
    sends = [push(early, early_got.at[me], es.at[d + 1], er.at[d + 1], to) for d, to in enumerate(others)]
    early_got[me] = early[...]
    dkt[...] = jnp.zeros_like(dkt)
    dvt[...] = jnp.zeros_like(dvt)
    so = PlainScatter(opair, osum, hr, (ord_, orx, ory, orz), sems[:10])
    so.at = {name: [4 * j + kk for kk in range(4)] for j, name in enumerate(("col", "X", "Y", "D"))}
    sn = PlainScatter(part, ngrad, HD, (rd, rx, ry, rz), sems[10:20])
    def out_pair(j):
        pairs[j].wait_recv()

        def add(b, carry):
            opair[b] = (opair[b].astype(F32) + part[b, pl.ds(mine, hr)].astype(F32)).astype(BF)
            return carry

        lax.fori_loop(4 * j, 4 * j + 4, add, 0)

    def attend_rows(i, carry):
        row = blk(i)
        s = dot(q[row], k[...], 1, 1)
        prob = jnp.where(column(seg, i) == sk[...], jnp.exp2(s * (SCALE * LOG2E) - lse[row]), 0.0)
        dp = dot(cgh[row], v[...], 1, 1)
        delta = jnp.sum(prob * dp, -1, keepdims=True)
        ds = (prob * (dp - delta)).astype(BF)
        dq = dot(ds, k[...], 1, 0) * SCALE
        dq = dq * cosf[row] - pltpu.roll(dq, HD // 2, 1) * sinf[row]
        pgrad[row, :HD] = dq.astype(BF)
        pgt[:HD, row] = dq.T.astype(BF)
        dkt[...] += dot(q[row], ds, 0, 0)
        dvt[...] += dot(cgh[row], prob.astype(BF), 0, 0)
        return carry

    n = q.shape[0] // HD
    q4 = n // 4
    lax.fori_loop(0, q4 // 2, attend_rows, 0)
    out_pair(3)
    for j in FAR_FIRST:
        so.far(j)
    lax.fori_loop(q4 // 2, 2 * q4, attend_rows, 0)
    out_pair(1)
    out_pair(2)
    so.near(3)
    so.near(2)
    lax.fori_loop(2 * q4, 3 * q4, attend_rows, 0)
    so.near(1)
    so.near(0)
    out_pair(0)
    lax.fori_loop(3 * q4, n, attend_rows, 0)
    for c in pairs.values():
        c.wait_send()

    def turn_back(i, carry):
        row = blk(i)
        dk = dkt[:, row].T * SCALE
        dk = dk * cosf[row] - pltpu.roll(dk, HD // 2, 1) * sinf[row]
        pgrad[row, HD : 2 * HD] = dk.astype(BF)
        pgt[HD : 2 * HD, row] = dk.T.astype(BF)
        dv = dvt[:, row]
        pgrad[row, 2 * HD :] = dv.T.astype(BF)
        pgt[2 * HD :, row] = dv.astype(BF)
        return carry

    lax.fori_loop(0, n, turn_back, 0)
    tiles[0].start()

    def back_block(j, kk):
        b = place_of(kk, j)
        part[b] = dot(pgrad[blk(b)], wh[...], 1, 0).astype(BF)

    for kk in FAR_FIRST:
        back_block(3, kk)
        sn.far(kk)
    for j in FAR_FIRST:
        so.along(j)
    for t, c in enumerate(tiles):
        if t + 1 < len(tiles):
            tiles[t + 1].start()
        c.wait()
        qpart[:, t * 256 : (t + 1) * 256] = dot(pgt[...], ntile[t % 2], 1, 0).astype(BF)
    qc = [push_pair(qpart.at[pl.ds(s * HD + other, hr)], qpair.at[s], qs.at[s], qr.at[s]) for s in range(3)]
    so.end()
    ostage[...] = osum[...].astype(BF)
    keep = pltpu.make_async_copy(ostage, out_t.at[pl.ds(mine, hr)], lo)
    keep.start()
    give = push_pair(ostage, out_t.at[pl.ds(mine, hr)], ofs, ofr)
    for kk in FAR_FIRST:
        back_block(1, kk)
        back_block(2, kk)
        sn.near(kk)
    for s in range(3):
        qc[s].wait_recv()
        qpair[s] = (qpair[s].astype(F32) + qpart[pl.ds(s * HD + mine, hr)].astype(F32)).astype(BF)
        b = 16 * s + me
        to, slot = b // 3, lax.rem(b, 3)
        dst = qkv_t.at[pl.ds(pl.multiple_of(slot * HD + core * hr, hr), hr)]

        @pl.when(to != me)
        def _():
            push(qpair.at[s], dst, ts.at[s], tr.at[slot], to)

        @pl.when(to == me)
        def _():
            pltpu.make_async_copy(qpair.at[s], dst, tr.at[slot]).start()

    for kk in FAR_FIRST:
        back_block(0, kk)
    for kk in FAR_FIRST:
        sn.along(kk)
    fc = []
    for s in range(3):
        here = qkv_t.at[pl.ds(pl.multiple_of(s * HD + core * hr, hr), hr)]
        pltpu.make_async_copy(here, here, tr.at[s]).wait()
        fc.append(push_pair(here, here, fs.at[s], fr.at[s]))
    sn.end()
    for s in range(3):

        @pl.when((16 * s + me) // 3 != me)
        def _():
            pltpu.make_async_copy(qpair.at[s], qpair.at[s], ts.at[s]).wait()

    gsum[...] = jnp.zeros_like(gsum)

    def norm_rows(i, carry):
        rows = pl.ds(pl.multiple_of(i * 16, 16), 16)
        pull, gains = rmsnorm_pull(tok[rows].astype(F32), gain1[...], ngrad[rows])
        tok_g[rows] = mg[rows] + pull
        gsum[...] += jnp.sum(gains, 0, keepdims=True)
        return carry

    lax.fori_loop(0, HD // 16, norm_rows, 0)
    for e, cut in enumerate(strips):
        late[e : e + 1, :] = gsum[:, cut]
    sends += [push(late, late_got.at[me], hs.at[d + 1], hr_.at[d + 1], to) for d, to in enumerate(others)]
    late_got[me] = late[...]
    for c in sends:
        c.wait_recv()

    def over_devices(got):
        total = got[0]
        for e in range(1, 16):
            total = total + got[e]
        return total

    both[:16, :] = over_devices(late_got)
    first = over_devices(early_got)
    both[16:, :] = first[:16]
    stat_o[...] = first[16:]
    across = push_pair(both, both_got, bs, br)
    across.wait()
    gain_o[...] = both[...] + both_got[...]
    for c in sends:
        c.wait_send()
    keep.wait()
    give.wait()
    for c in qc:
        c.wait_send()
    for c in fc:
        c.wait()


def back(cgh, q, k, v, seg, sk, lse, cosf, sinf, wh, nall, ag, ctx, tok, att, mix, mg, gain1, gain2, cid):
    rows, width = ag.shape
    seq = q.shape[0]
    vb = lambda *shape: pltpu.VMEM(shape, BF)
    vf = lambda *shape: pltpu.VMEM(shape, F32)
    sem = lambda *shape: pltpu.SemaphoreType.DMA(shape) if shape else pltpu.SemaphoreType.DMA
    return pl.pallas_call(
        back_kernel,
        out_shape=[
            jax.ShapeDtypeStruct((rows, width), BF),
            jax.ShapeDtypeStruct((rows, width), F32),
            jax.ShapeDtypeStruct((8, HD), F32),
            jax.ShapeDtypeStruct((32, HD), F32),
            jax.ShapeDtypeStruct((rows, width), BF),
            jax.ShapeDtypeStruct((3 * HD, width), BF),
        ],
        in_specs=[VM] * 10 + [ANY] + [VM] * 8,
        out_specs=[VM] * 4 + [ANY, ANY],
        scratch_shapes=[
            vf(rows, width), vf(rows, 1), vf(1, width), vf(24, HD), vf(16, HD), vf(16, 24, HD), vf(16, 16, HD),
            vf(32, HD), vf(32, HD), sem(16), sem(16), sem(16), sem(16), sem(), sem(),
            vf(HD, seq), vf(HD, seq), vb(seq, 3 * HD), vb(3 * HD, seq),
            vb(16, rows // 2, width), vf(rows // 2, width), vb(rows // 2, width),
        ]
        + plain_bufs(rows // 2, width)
        + [vb(16, rows, width)]
        + plain_bufs(rows, width)
        + [vb(2, seq, 256), vb(3 * HD, width), vb(3, HD // 2, width)]
        + [sem(), sem(4), sem(4), sem(), sem(), sem(2), sem(3), sem(3), sem(3), sem(3), sem(3), sem(3)]
        + SCATTER_SEMS * 2,
        compiler_params=params(cid, 62),
        name="back",
    )(cgh, q, k, v, seg, sk, lse, cosf, sinf, wh, nall, ag, ctx, tok, att, mix, mg, gain1, gain2)


def rotary_tables(length):
    freq = (THETA ** (-(np.arange(HD // 2) * 2.0 / HD))).astype(np.float32)
    angle = (np.arange(length, dtype=np.float32)[:, None] * freq[None, :]).astype(np.float64)
    cos, sin = np.cos(angle).astype(np.float32), np.sin(angle).astype(np.float32)
    return np.concatenate([cos, cos], 1), np.concatenate([-sin, sin], 1)


def per_device(
    tokens, segments, routes, route_weight, capacity, norm_gain,
    qkv_weight, out_weight, gate_weight, up_weight, down_weight, cotangent,
):
    rows, width = tokens.shape
    seq = segments.shape[0]
    gain1_row, gain2_row = norm_gain[:1], norm_gain[1:]
    meta = jnp.concatenate([routes.astype(F32).T, route_weight.T], 0)
    seg = segments.astype(F32).reshape(16, rows)
    sk = jnp.where(segments == 0, -1.0, segments.astype(F32))[None, :]
    cos_table, sin_table = rotary_tables(seq)
    normed_all, meta_all, w_head, q, k, v, lse, context, dense_out = front(
        tokens, gain1_row, meta, qkv_weight, out_weight, cos_table, sin_table, seg, sk, 0
    )
    attended, n2g, mix_part, xr, pg, hidden, gg, ug = expert(
        context, dense_out, tokens, gain2_row, cotangent, meta_all, capacity,
        gate_weight[0], up_weight[0], down_weight[0], 3,
    )
    flat = lambda a: a.reshape(-1, a.shape[2])
    mixture, gate_g, up_g, down_g, attended_grad, middle_grad, gain2, cgh = expert_weights(
        mix_part, flat(xr), flat(pg), flat(hidden), flat(gg), flat(ug), flat(dense_out),
        n2g, tokens, attended, cotangent, gain2_row, 5,
    )
    layer_out, tokens_grad, stat_lanes, gain_pair, out_total, qkv_total = back(
        cgh, q, k, v, seg, sk, lse, cos_table, sin_table, w_head, flat(normed_all), attended_grad, context,
        tokens, attended, mixture, middle_grad, gain1_row, gain2, 6,
    )
    seq_sums = jnp.sum(stat_lanes, 1)
    gain_pair = gain_pair.reshape(2, width)
    stat_row = jnp.sqrt(seq_sums[:3] / seq_sums[3]).reshape(1, 3)
    groups = lax.axis_size("grp")
    over = lambda a: a.astype(F32) if groups == 2 else lax.psum(a.astype(BF), "grp").astype(F32) * 0.5
    return (
        layer_out,
        tokens_grad,
        over(qkv_total),
        over(out_total),
        over(gate_g)[None],
        over(up_g)[None],
        over(down_g)[None],
        gain_pair if groups == 2 else lax.psum(gain_pair, "grp") * 0.5,
        stat_row,
    )


def solution(mesh):
    both = ("grp", "dp")
    in_specs = (
        P(both, None), P("grp"), P(both, None), P(both, None), P(), P(),
        P("dp", None), P("dp", None), P("dp", None, None), P("dp", None, None), P("dp", None, None),
        P(both, None),
    )
    out_specs = (
        P(both, None), P(both, None), P("dp", None), P("dp", None),
        P("dp", None, None), P("dp", None, None), P("dp", None, None), P(), P("grp", None),
    )
    return jax.shard_map(per_device, mesh=mesh, in_specs=in_specs, out_specs=out_specs, check_vma=False)
```

```python
import functools

import jax
import jax.numpy as jnp
import numpy as np
from jax import lax
from jax.experimental import pallas as pl
from jax.experimental.pallas import tpu as pltpu
from jax.sharding import PartitionSpec as P

H = 16
HD = 128
TOPK = 8
EPS = 1e-06
THETA = 50000.0
MESH = pl.DeviceIdType.MESH
MIB = 2**20
BF = jnp.bfloat16
F32 = jnp.float32
SCALE = HD**-0.5
LOG2E = 1.4426950408889634


def places():
    me = lax.axis_index("dp")
    z, y, x = me // 4, (me // 2) % 2, me % 2
    xor = [z, z + 1 - 2 * (z % 2), (z + 2) % 4, 3 - z]
    at = lambda k, yy, xx: xor[k] * 4 + yy * 2 + xx
    return dict(
        me=me,
        col=[at(k, y, x) for k in range(4)],
        X=[at(k, y, 1 - x) for k in range(4)],
        Y=[at(k, 1 - y, x) for k in range(4)],
        D=[at(k, 1 - y, 1 - x) for k in range(4)],
    )


def barrier(targets, pair=False):
    sem = pltpu.get_barrier_semaphore()
    for t in targets:
        pl.semaphore_signal(sem, inc=1, device_id={"dp": t}, device_id_type=MESH)
    count = len(targets)
    if pair:
        pl.semaphore_signal(sem, inc=1, device_id={"grp": partner()}, device_id_type=MESH)
        count += 1
    pl.semaphore_wait(sem, count)


def partner():
    g = lax.axis_index("grp")
    return g + 1 - 2 * (g % 2)


def push(src, dst, send, recv, to):
    c = pltpu.make_async_remote_copy(
        src_ref=src, dst_ref=dst, send_sem=send, recv_sem=recv,
        device_id={"dp": to}, device_id_type=MESH,
    )
    c.start()
    return c


def push_pair(src, dst, send, recv):
    c = pltpu.make_async_remote_copy(
        src_ref=src, dst_ref=dst, send_sem=send, recv_sem=recv,
        device_id={"grp": partner()}, device_id_type=MESH,
    )
    c.start()
    return c


ORDER = (1, 0, 3, 2)
GATHER_SEMS = (
    [pltpu.SemaphoreType.DMA((4,))] * 6 + [pltpu.SemaphoreType.DMA((4, 2))] * 2 + [pltpu.SemaphoreType.DMA]
    + [pltpu.SemaphoreType.DMA((4,))] * 2
)


class Gather:
    def __init__(self, src, dst, rows, sems, first=0):
        self.src, self.dst, self.rows, self.sems, self.first, self.p = src, dst, rows, sems, first, places()

    def block(self, b):
        return self.dst.at[b, pl.ds(self.first, self.rows)]

    def part(self, b, h):
        half = self.rows // 2
        return self.dst.at[b, pl.ds(self.first + h * half, half)]

    def begin(self):
        zs, zr, xs, xr, ys, yr, _, _, own, _, _ = self.sems
        p, src = self.p, self.src
        me = p["me"]
        self.mine = pltpu.make_async_copy(src, self.block(me), own)
        self.mine.start()
        self.xc = {0: push(src, self.block(me), xs.at[0], xr.at[0], p["X"][0])}
        self.yc = {0: push(src, self.block(me), ys.at[0], yr.at[0], p["Y"][0])}
        self.zc = {k: push(src, self.block(me), zs.at[k], zr.at[k], p["col"][k]) for k in (1, 2)}
        self.dc, self.vc = {}, {}

    def near(self, k):
        _, _, xs, xr, ys, yr = self.sems[:6]
        p = self.p
        self.zc[k].wait_recv()
        b = self.block(p["col"][k])
        if k == 2:
            zs, zr = self.sems[:2]
            self.zc[3] = push(b, b, zs.at[3], zr.at[3], p["col"][1])
        self.xc[k] = push(b, b, xs.at[k], xr.at[k], p["X"][0])
        self.yc[k] = push(b, b, ys.at[k], yr.at[k], p["Y"][0])

    def far(self, k):
        ds, dr = self.sems[6:8]
        p = self.p
        b = self.part(p["X"][k], 0)
        self.xc[k].wait_recv()
        self.dc[k, 0] = push(b, b, ds.at[k, 0], dr.at[k, 0], p["Y"][0])
        b = self.part(p["Y"][k], 1)
        self.yc[k].wait_recv()
        self.dc[k, 1] = push(b, b, ds.at[k, 1], dr.at[k, 1], p["X"][0])

    def over(self, k):
        vs, vr = self.sems[9:11]
        self.dc[k, 0].wait_recv()
        self.dc[k, 1].wait_recv()
        b = self.block(self.p["D"][k])
        self.vc[k] = push(b, b, vs.at[k], vr.at[k], self.p["col"][1])

    def ready(self, k):
        if k == 0:
            self.mine.wait()
        if k % 2:
            self.xc[k].wait_recv()
            self.yc[k].wait_recv()
            self.vc[k - 1].wait_recv()

    def end(self):
        for group in (self.xc, self.yc, self.zc, self.dc, self.vc):
            for c in group.values():
                c.wait_send()


def gather_targets():
    p = places()
    return [p["col"][1], p["col"][2], p["col"][3], p["X"][0], p["Y"][0]]


SCATTER_SEMS = [pltpu.SemaphoreType.DMA((4, 2))] * 2 + [pltpu.SemaphoreType.DMA((4,))] * 8


def scatter_bufs(rows, width):
    return [
        pltpu.VMEM((4, rows // 2, width), BF),
        pltpu.VMEM((4, rows, width), BF),
        pltpu.VMEM((4, rows, width), BF),
        pltpu.VMEM((4, rows, width), BF),
        pltpu.VMEM((2, rows, width), BF),
    ]


class Scatter:
    def __init__(self, part, out, rows, bufs, sems):
        self.part, self.out, self.half, self.bufs, self.sems, self.p = part, out, rows // 2, bufs, sems, places()
        self.at = self.p
        self.da, self.db, self.xc, self.yc, self.zc, self.vc = {}, {}, {}, {}, {}, {}

    def lift(self, k):
        vs, vr = self.sems[8:]
        self.vc[k] = push(self.part.at[self.p["D"][k]], self.bufs[4].at[k // 2], vs.at[k], vr.at[k], self.p["col"][1])

    def far(self, k):
        ds, dr = self.sems[:2]
        rd, h, p, part = self.bufs[0], self.half, self.p, self.part
        b = p["D"][k]
        self.vc[k + 1].wait_recv()
        part[b] = (part[b].astype(F32) + self.bufs[4][k // 2].astype(F32)).astype(BF)
        self.da[k] = push(part.at[b, pl.ds(0, h)], rd.at[k], ds.at[k, 0], dr.at[k, 0], p["Y"][0])
        self.db[k] = push(part.at[b, pl.ds(h, h)], rd.at[k + 1], ds.at[k, 1], dr.at[k, 1], p["X"][0])

    def near(self, k):
        xs, xr, ys, yr = self.sems[2:6]
        rd, rx, ry = self.bufs[:3]
        part, h, p = self.part, self.half, self.p
        b = p["X"][k]
        if k % 2 == 0:
            self.da[k].wait_recv()
            part[b, pl.ds(0, h)] = (part[b, pl.ds(0, h)].astype(F32) + rd[k].astype(F32)).astype(BF)
        self.xc[k] = push(part.at[b], rx.at[k], xs.at[k], xr.at[k], p["X"][0])
        b = p["Y"][k]
        if k % 2 == 0:
            self.db[k].wait_recv()
            part[b, pl.ds(h, h)] = (part[b, pl.ds(h, h)].astype(F32) + rd[k + 1].astype(F32)).astype(BF)
        self.yc[k] = push(part.at[b], ry.at[k], ys.at[k], yr.at[k], p["Y"][0])

    def along(self, k):
        zs, zr = self.sems[6:8]
        rx, ry, rz = self.bufs[1:4]
        part = self.part
        b = self.p["col"][k]
        self.xc[k].wait_recv()
        self.yc[k].wait_recv()
        total = part[b].astype(F32) + rx[k].astype(F32) + ry[k].astype(F32)
        if k == 2:
            self.zc[3].wait_recv()
            total = total + rz[3].astype(F32)
        if k:
            part[b] = total.astype(BF)
            self.zc[k] = push(part.at[b], rz.at[k], zs.at[k], zr.at[k], self.p["col"][1 if k == 3 else k])
        else:
            self.out[...] = total

    def end(self):
        self.zc[1].wait_recv()
        self.zc[2].wait_recv()
        self.out[...] += self.bufs[3][1].astype(F32) + self.bufs[3][2].astype(F32)
        for group in (self.da, self.db, self.xc, self.yc, self.zc, self.vc):
            for c in group.values():
                c.wait_send()


class PlainScatter(Scatter):
    def far(self, k):
        ds, dr = self.sems[:2]
        rd, h, p = self.bufs[0], self.half, self.p
        b = self.at["D"][k]
        self.da[k] = push(self.part.at[b, pl.ds(0, h)], rd.at[2 * k], ds.at[k, 0], dr.at[k, 0], p["Y"][0])
        self.db[k] = push(self.part.at[b, pl.ds(h, h)], rd.at[2 * k + 1], ds.at[k, 1], dr.at[k, 1], p["X"][0])

    def near(self, k):
        xs, xr, ys, yr = self.sems[2:6]
        rd, rx, ry = self.bufs[:3]
        part, h, p = self.part, self.half, self.p
        b = self.at["X"][k]
        self.da[k].wait_recv()
        part[b, pl.ds(0, h)] = (part[b, pl.ds(0, h)].astype(F32) + rd[2 * k].astype(F32)).astype(BF)
        self.xc[k] = push(part.at[b], rx.at[k], xs.at[k], xr.at[k], p["X"][0])
        b = self.at["Y"][k]
        self.db[k].wait_recv()
        part[b, pl.ds(h, h)] = (part[b, pl.ds(h, h)].astype(F32) + rd[2 * k + 1].astype(F32)).astype(BF)
        self.yc[k] = push(part.at[b], ry.at[k], ys.at[k], yr.at[k], p["Y"][0])

    def along(self, k):
        zs, zr = self.sems[6:8]
        rx, ry, rz = self.bufs[1:4]
        part, b = self.part, self.at["col"][k]
        self.xc[k].wait_recv()
        self.yc[k].wait_recv()
        total = part[b].astype(F32) + rx[k].astype(F32) + ry[k].astype(F32)
        if k == 2:
            self.zc[3].wait_recv()
            total = total + rz[3].astype(F32)
        if k:
            part[b] = total.astype(BF)
            self.zc[k] = push(part.at[b], rz.at[k], zs.at[k], zr.at[k], self.p["col"][1 if k == 3 else k])
        else:
            self.out[...] = total


def plain_bufs(rows, width):
    return [pltpu.VMEM((8, rows // 2, width), BF)] + scatter_bufs(rows, width)[1:4]


FAR_FIRST = (3, 2, 1, 0)


ANY = pl.BlockSpec(memory_space=pl.ANY)
VM = pl.BlockSpec(memory_space=pltpu.VMEM)


def params(cid, vmem=60):
    return pltpu.CompilerParams(collective_id=cid, has_side_effects=True, vmem_limit_bytes=vmem * MIB)


def rmsnorm(field, gain_row):
    return field * lax.rsqrt(jnp.mean(field * field, -1, keepdims=True) + EPS) * gain_row


def rmsnorm_pull(field, gain_row, grad):
    r = lax.rsqrt(jnp.mean(field * field, -1, keepdims=True) + EPS)
    scaled = grad * gain_row
    back = r * scaled - field * (r * r * r * jnp.mean(scaled * field, -1, keepdims=True))
    return back, grad * field * r


def column(rows, b):
    return jnp.broadcast_to(rows[pl.ds(b, 1), :], (8, rows.shape[1])).T[:, :1]


def dot(a, b, ca, cb):
    return lax.dot_general(a, b, (((ca,), (cb,)), ((), ())), preferred_element_type=F32)


def front_kernel(
    tok, gain, m_ref, w_ref, o_ref, cosf, sinf, seg, sk,
    nall_o, mall, wh_o, q, k, v, lse, ctx, oall,
    n_ref, nall, wh, ctxh, ms, mr, mo, ws, wr, ps, pr, wo, no, cs, cr, co, os_, or_, *sems,
):
    me = lax.axis_index("dp")
    core = lax.axis_index("grp") % 2
    hr = HD // 2
    blk = lambda b: pl.ds(pl.multiple_of(b * HD, HD), HD)
    half = lambda s, c: pl.ds(pl.multiple_of(s * HD + c * hr, hr), hr)
    n_ref[...] = rmsnorm(tok[...].astype(F32), gain[...]).astype(BF)
    barrier([lax.rem(me + d, 16) for d in range(1, 16)], pair=True)
    g = Gather(n_ref, nall, n_ref.shape[0], sems[:11])
    go = Gather(o_ref.at[half(0, core)], oall, hr, sems[11:], pl.multiple_of(core * hr, hr))
    g.begin()
    own = pltpu.make_async_copy(m_ref, mall.at[me], mo)
    own.start()
    mc = [push(m_ref, mall.at[me], ms.at[d], mr.at[d], lax.rem(me + d, 16)) for d in range(1, 16)]
    for l in range(3):
        b = 3 * me + l
        to, slot = lax.rem(b, 16), b // 16
        src, dst = w_ref.at[half(l, core)], wh.at[half(slot, core)]

        @pl.when(to != me)
        def _():
            push(src, dst, ws.at[l], wr.at[slot], to)

        @pl.when(to == me)
        def _():
            pltpu.make_async_copy(src, dst, wr.at[slot]).start()

    def project(b, carry):
        row = blk(b)
        out = dot(nall[b], wh[...], 1, 1)
        turn = lambda a: (a * cosf[row] + pltpu.roll(a, HD // 2, 1) * sinf[row]).astype(BF)
        q[row] = turn(out[:, :HD])
        k[row] = turn(out[:, HD : 2 * HD])
        v[row] = out[:, 2 * HD :].astype(BF)
        return carry

    def project_plane(c):
        lax.fori_loop(0, 4, lambda j, carry: project(place_of(c, j), carry), 0)

    g.near(1)
    g.far(0)
    g.near(2)
    g.over(0)
    g.far(2)
    g.near(3)
    go.begin()
    g.over(2)
    pc = []
    for s in range(3):
        dst = wh.at[half(s, core)]
        pltpu.make_async_copy(dst, dst, wr.at[s]).wait()
        pc.append(push_pair(dst, dst, ps.at[s], pr.at[s]))
    go.near(1)
    for p in pc:
        p.wait_recv()
    g.ready(0)
    project_plane(0)
    g.ready(1)
    project_plane(1)
    g.ready(2)
    project_plane(2)
    go.far(0)
    go.near(2)
    g.ready(3)
    project_plane(3)
    saves = [pltpu.make_async_copy(nall, nall_o, no), pltpu.make_async_copy(wh, wh_o, wo)]
    for c in saves:
        c.start()

    def hop(d):
        to = lax.rem(me + d, 16)
        return pltpu.make_async_remote_copy(
            src_ref=ctxh.at[blk(to)], dst_ref=ctx.at[:, blk(me)], send_sem=cs.at[d], recv_sem=cr.at[d],
            device_id={"dp": to}, device_id_type=MESH,
        )

    def attend_rows(d, carry):
        b = lax.rem(me + d, 16)
        row = blk(b)
        s = dot(q[row], k[...], 1, 1)
        s = jnp.where(column(seg, b) == sk[...], s, -1e30)
        peak = jnp.maximum(jnp.max(s, -1, keepdims=True), -1e29)
        ex = jnp.exp2((s - peak) * (SCALE * LOG2E))
        total = jnp.maximum(jnp.sum(ex, -1, keepdims=True), 1.0)
        prob = (ex * (1.0 / total)).astype(BF)
        ctxh[row] = jnp.dot(prob, v[...], preferred_element_type=F32).astype(BF)
        lse[row] = peak * (SCALE * LOG2E) + jnp.log2(total)
        return carry

    def attend_send(d, carry):
        attend_rows(d, carry)
        hop(d).start()
        return carry

    oc = []

    def swap_plane(c):
        go.ready(c)
        z = place_of(c, 0) // 4
        here = oall.at[pl.ds(4 * z, 4), pl.ds(pl.multiple_of(core * hr, hr), hr)]
        oc.append(push_pair(here, here, os_.at[c], or_.at[c]))

    lax.fori_loop(1, 6, attend_send, 0)
    go.over(0)
    go.far(2)
    go.near(3)
    lax.fori_loop(6, 12, attend_send, 0)
    swap_plane(0)
    swap_plane(1)
    lax.fori_loop(12, 16, attend_send, 0)
    attend_rows(0, 0)
    stay = pltpu.make_async_copy(ctxh.at[blk(me)], ctx.at[:, blk(me)], co)
    stay.start()
    go.over(2)
    swap_plane(2)
    swap_plane(3)
    g.end()
    go.end()
    own.wait()
    for c in mc:
        c.wait()
    for l in range(3):
        src = w_ref.at[half(l, core)]

        @pl.when(lax.rem(3 * me + l, 16) != me)
        def _():
            pltpu.make_async_copy(src, src, ws.at[l]).wait()

    for p in pc:
        p.wait_send()
    for c in saves:
        c.wait()
    stay.wait()
    for d in range(1, 16):
        hop(d).wait()
    for c in oc:
        c.wait()


def front(tokens, gain, meta, w, wo, cosf, sinf, seg, sk, cid):
    rows, width = tokens.shape
    seq = cosf.shape[0]
    sem = lambda *shape: pltpu.SemaphoreType.DMA(shape) if shape else pltpu.SemaphoreType.DMA
    b = lambda *shape: jax.ShapeDtypeStruct(shape, BF)
    f = lambda *shape: jax.ShapeDtypeStruct(shape, F32)
    v = lambda *shape: pltpu.VMEM(shape, BF)
    return pl.pallas_call(
        front_kernel,
        out_shape=[
            b(16, rows, width), f(16, *meta.shape), b(3 * HD, width),
            b(seq, HD), b(seq, HD), b(seq, HD), f(seq, 1), b(rows, width), b(16, rows, width),
        ],
        in_specs=[VM, VM] + [ANY] * 3 + [VM] * 4,
        out_specs=[ANY] * 3 + [VM] * 4 + [ANY] * 2,
        scratch_shapes=[v(rows, width), v(16, rows, width), v(3 * HD, width), v(seq, HD)]
        + [sem(16), sem(16), sem(), sem(3), sem(3), sem(3), sem(3), sem(), sem()]
        + [sem(16), sem(16), sem(), sem(4), sem(4)]
        + GATHER_SEMS * 2,
        compiler_params=params(cid),
        name="front",
    )(tokens, gain, meta, w, wo, cosf, sinf, seg, sk)


SLOTS = 80
COLS = 512


def place_of(k, j):
    me = lax.axis_index("dp")
    z, y, x = me // 4, (me // 2) % 2, me % 2
    zk = [z, z + 1 - 2 * (z % 2), (z + 2) % 4, 3 - z][k]
    jy, jx = j // 2, j % 2
    return zk * 4 + (y + jy - 2 * y * jy) * 2 + (x + jx - 2 * x * jx)


def expert_kernel(
    ctx, wout, tok, gain, cot, meta, cap, wg_h, wu_h, wd_h,
    att, n2g, p1, xr_o, pg_o, hid_o, gg_o, ug_o,
    n2, rank, coef, pick, sw, nall, call, part, stage, wg, wu, wd, xr, pg, hid, gg, ug, rd, rx, ry, rz, rv,
    wosem, wsem, osem, psem, *sems,
):
    rows, width = ctx.shape
    wload = pltpu.make_async_copy(wout, part, wosem)
    wload.start()
    barrier(gather_targets())
    gn = Gather(n2, nall, rows, sems[:11])
    gc = Gather(cot, call, rows, sems[11:22])
    sc = Scatter(part, n2g, rows, (rd, rx, ry, rz, rv), sems[22:])
    gc.begin()
    loads = [pltpu.make_async_copy(a, b, wsem.at[i]) for i, (a, b) in enumerate([(wg_h, wg), (wu_h, wu), (wd_h, wd)])]
    me = lax.axis_index("dp").astype(F32)
    hits = [meta[:, r, :] == me for r in range(TOPK)]
    member = sum(h.astype(F32) for h in hits)
    coef[...] = sum(jnp.where(h, meta[:, TOPK + r, :], 0.0) for r, h in enumerate(hits))
    i0, i1 = lax.broadcasted_iota(jnp.int32, (HD, HD), 0), lax.broadcasted_iota(jnp.int32, (HD, HD), 1)
    local = dot(member.astype(BF), (i0 < i1).astype(BF), 1, 0)
    count = jnp.broadcast_to(jnp.sum(member, 1, keepdims=True), member.shape).astype(BF)
    j0, j1 = lax.broadcasted_iota(jnp.int32, (16, 16), 0), lax.broadcasted_iota(jnp.int32, (16, 16), 1)
    before = dot((j1 < j0).astype(BF), count, 1, 0)
    kept = (member > 0.0) & (local + before < cap[0].astype(F32))
    rank[...] = jnp.where(kept, local, -1.0)
    wload.wait()

    def attend_cols(t, carry):
        w = part[pl.ds(2 * t, 2)].reshape(2 * rows, width)
        att[:, pl.ds(pl.multiple_of(t * 2 * rows, 2 * rows), 2 * rows)] = dot(ctx[...], w, 1, 1)
        return carry

    lax.fori_loop(0, 8, attend_cols, 0)
    n2[...] = rmsnorm(tok[...].astype(F32) + att[...], gain[...]).astype(BF)
    gn.begin()
    for c in loads:
        c.start()
    saves = []
    both = lambda name, k: [getattr(g, name)(k) for g in (gn, gc)]
    both("near", 1)
    both("far", 0)
    both("near", 2)
    both("over", 0)
    for i, k in enumerate(ORDER):
        both("ready", k)
        if k == 1:
            both("far", 2)
            both("near", 3)
        if k == 0:
            sc.near(1)
            both("over", 2)
        if k == 3:
            sc.near(0)
            sc.along(1)
        if k == 2:
            sc.near(3)
            sc.along(0)
        for c in saves:
            c.wait()
        if i == 0:
            for c in loads:
                c.wait()

        def collect(j, carry):
            b = place_of(k, j)
            to = pl.ds(pl.multiple_of(j * SLOTS, SLOTS), SLOTS)
            s0 = lax.broadcasted_iota(jnp.int32, (SLOTS, rows), 0).astype(F32)
            mine = s0 == rank[pl.ds(b, 1), :]
            sw[to, :] = jnp.sum(jnp.where(mine, coef[pl.ds(b, 1), :], 0.0), 1, keepdims=True)
            pick[to, :] = mine.astype(BF)

            def cols(n, c):
                w = pl.ds(pl.multiple_of(n * 512, 512), 512)
                xr[to, w] = dot(pick[to, :], nall[b, :, w], 1, 0).astype(BF)
                pg[to, w] = (dot(pick[to, :], call[b, :, w], 1, 0) * sw[to, :]).astype(BF)
                return c

            return lax.fori_loop(0, width // 512, cols, carry)

        lax.fori_loop(0, 4, collect, 0)

        def inner(n, carry):
            w = pl.ds(pl.multiple_of(n * COLS, COLS), COLS)
            gate = dot(xr[...], wg[:, w], 1, 0)
            up = dot(xr[...], wu[:, w], 1, 0)
            hg = dot(pg[...], wd[w, :], 1, 1)
            sig = jax.nn.sigmoid(gate)
            hid[:, w] = (gate * sig * up).astype(BF)
            gg[:, w] = (hg * up * sig * (1.0 + gate * (1.0 - sig))).astype(BF)
            ug[:, w] = (hg * gate * sig).astype(BF)
            return carry

        lax.fori_loop(0, hid.shape[1] // COLS, inner, 0)

        def outer(n, carry):
            w = pl.ds(pl.multiple_of(n * COLS, COLS), COLS)
            eo = dot(hid[...], wd[:, w], 1, 0).astype(BF).astype(F32)
            rg = (dot(gg[...], wg[w, :], 1, 1) + dot(ug[...], wu[w, :], 1, 1)).astype(BF)
            for j in range(4):
                b = place_of(k, j)
                cut = slice(j * SLOTS, (j + 1) * SLOTS)
                weighted = (eo[cut] * sw[cut]).astype(BF)
                stage[j, :, w] = dot(pick[cut], weighted, 0, 0).astype(BF)
                part[b, :, w] = dot(pick[cut], rg[cut], 0, 0).astype(BF)
            return carry

        lax.fori_loop(0, xr.shape[1] // COLS, outer, 0)
        if k % 2:
            sc.lift(k)
        else:
            sc.far(k)
        saves = [
            pltpu.make_async_copy(a, o.at[k], osem.at[i])
            for i, (a, o) in enumerate([(xr, xr_o), (pg, pg_o), (hid, hid_o), (gg, gg_o), (ug, ug_o)])
        ] + [pltpu.make_async_copy(stage.at[j], p1.at[place_of(k, j)], psem.at[j]) for j in range(4)]
        for c in saves:
            c.start()
    gn.end()
    gc.end()
    sc.near(2)
    sc.along(3)
    sc.along(2)
    sc.end()
    for c in saves:
        c.wait()


def expert(ctx, wout, tokens, gain, cot, meta, cap, wg, wu, wd, cid):
    rows, width = ctx.shape
    ff = wg.shape[1]
    chunk = 4 * SLOTS
    save = lambda w: jax.ShapeDtypeStruct((4, chunk, w), BF)
    v = lambda *shape: pltpu.VMEM(shape, BF)
    f = lambda *shape: pltpu.VMEM(shape, F32)
    return pl.pallas_call(
        expert_kernel,
        out_shape=[
            jax.ShapeDtypeStruct((rows, width), F32),
            jax.ShapeDtypeStruct((rows, width), F32),
            jax.ShapeDtypeStruct((16, rows, width), BF),
            save(width), save(width), save(ff), save(ff), save(ff),
        ],
        in_specs=[VM, ANY, VM, VM, ANY, VM, pl.BlockSpec(memory_space=pltpu.SMEM), ANY, ANY, ANY],
        out_specs=[VM, VM] + [ANY] * 6,
        scratch_shapes=[
            v(rows, width), f(16, rows), f(16, rows), v(chunk, rows), f(chunk, 1),
            v(16, rows, width), v(16, rows, width), v(16, rows, width), v(4, rows, width),
            v(width, ff), v(width, ff), v(ff, width),
            v(chunk, width), v(chunk, width), v(chunk, ff), v(chunk, ff), v(chunk, ff),
        ]
        + scatter_bufs(rows, width)
        + [pltpu.SemaphoreType.DMA, pltpu.SemaphoreType.DMA((3,)), pltpu.SemaphoreType.DMA((5,)), pltpu.SemaphoreType.DMA((4,))]
        + GATHER_SEMS * 2
        + SCATTER_SEMS,
        compiler_params=params(cid, 62),
        name="expert",
    )(ctx, wout, tokens, gain, cot, meta, cap, wg, wu, wd)


TILE = (256, 1024)


def weights_kernel(
    p1, xr_h, pg_h, hid_h, gg_h, ug_h, wout, n2g, tok, att, cot, gain,
    mix, gate_o, up_o, down_o, ag, mg, gain_g, cgh,
    part, wo, cg, xr, pg, hid, gg, ug, give, got, rd, rx, ry, rz, rv, lsem, wsem, gs, gr, os_, cs, cr, co, *sems,
):
    me = lax.axis_index("dp")
    blk = lambda b: pl.ds(pl.multiple_of(b * HD, HD), HD)
    loads = [
        pltpu.make_async_copy(a, b, lsem.at[i])
        for i, (a, b) in enumerate(
            [(p1, part), (xr_h, xr), (gg_h, gg), (ug_h, ug), (hid_h, hid), (pg_h, pg)]
        )
    ]
    column_load = lambda t: pltpu.make_async_copy(
        wout.at[:, pl.ds(pl.multiple_of(t * HD, HD), HD)], wo.at[lax.rem(t, 2)], wsem.at[lax.rem(t, 2)]
    )
    column_load(0).start()
    for c in loads:
        c.start()
    gain_g[...] = jnp.zeros_like(gain_g)

    def middle_rows(i, carry):
        rows = pl.ds(pl.multiple_of(i * 16, 16), 16)
        back, gains = rmsnorm_pull(tok[rows].astype(F32) + att[rows], gain[...], n2g[rows])
        gain_g[...] += jnp.sum(gains, 0, keepdims=True)
        grad = cot[rows].astype(F32) + back
        mg[rows] = grad
        ag[rows] = grad.astype(BF)
        return carry

    lax.fori_loop(0, tok.shape[0] // 16, middle_rows, 0)
    barrier([lax.rem(me + d, 16) for d in range(1, 16)], pair=True)
    sc = Scatter(part, mix, part.shape[1], (rd, rx, ry, rz, rv), sems)
    loads[0].wait()
    sc.lift(1)
    sc.lift(3)
    sc.near(3)
    sc.near(1)
    tiles = cg.shape[1] // HD

    def context_cols(t, carry):
        @pl.when(t + 1 < tiles)
        def _():
            column_load(t + 1).start()

        column_load(t).wait()
        cols = pl.ds(pl.multiple_of(t * HD, HD), HD)
        cg[:, cols] = dot(ag[...], wo[lax.rem(t, 2)], 1, 0).astype(BF)
        return carry

    lax.fori_loop(0, tiles, context_cols, 0)

    def hop(d):
        to = lax.rem(me + d, 16)
        return pltpu.make_async_remote_copy(
            src_ref=cg.at[:, blk(to)], dst_ref=cgh.at[blk(me)], send_sem=cs.at[d], recv_sem=cr.at[d],
            device_id={"dp": to}, device_id_type=MESH,
        )

    for d in range(1, 16):
        hop(d).start()
    stay = pltpu.make_async_copy(cg.at[:, blk(me)], cgh.at[blk(me)], co)
    stay.start()
    sc.far(2)
    sc.far(0)
    for c in loads[1:]:
        c.wait()
    r, w = TILE
    strip = lambda a, t, size: a[:, pl.ds(pl.multiple_of(t * size, size), size)]

    def product(m, t):
        left = strip((xr, hid)[m], t, r).T
        for e in range(2):
            yield dot(left, (gg, ug)[e][...] if m == 0 else pg[:, e * w : (e + 1) * w], 1, 0)

    def home(m, t, e):
        rows = pl.ds(pl.multiple_of(t * r, r), r)
        return (gate_o, up_o)[e].at[rows] if m == 0 else down_o.at[rows, pl.ds(e * w, w)]

    def sent(m, t):
        s = lax.rem(t, 2)
        return pltpu.make_async_remote_copy(
            src_ref=give.at[s], dst_ref=got.at[8 * m + t], send_sem=gs.at[s], recv_sem=gr.at[8 * m + t],
            device_id={"grp": partner()}, device_id_type=MESH,
        )

    def saved(m, t):
        s = lax.rem(t, 2)
        return [pltpu.make_async_copy(got.at[8 * m + t, e], home(m, t, e), os_.at[s, e]) for e in range(2)]

    def finish(m, t):
        s = lax.rem(t, 2)
        sent(m, t).wait_recv()
        got[8 * m + t] = (give[s].astype(F32) + got[8 * m + t].astype(F32)).astype(BF)
        for c in saved(m, t):
            c.start()

    def free(m, t):
        sent(m, t).wait_send()
        for c in saved(m, t):
            c.wait()

    def body(m, start):
        def step(t, carry):
            s = lax.rem(t, 2)

            @pl.when(t >= start + 2)
            def _():
                free(m, t - 2)

            for e, tile in enumerate(product(m, t)):
                give[s, e] = tile.astype(BF)
            sent(m, t).start()

            @pl.when(t >= start + 1)
            def _():
                finish(m, t - 1)

            return carry

        return step

    for i, (m, start) in enumerate(((0, 0), (0, 4), (1, 0))):
        lax.fori_loop(start, start + 4, body(m, start), 0)
        finish(m, start + 3)
        free(m, start + 2)
        free(m, start + 3)
        if i == 0:
            sc.near(2)
            sc.near(0)
            sc.along(3)
        if i == 1:
            sc.along(1)
            sc.along(2)
    sc.along(0)
    sc.end()
    stay.wait()
    for d in range(1, 16):
        hop(d).wait()


def expert_weights(p1, xr, pg, hid, gg, ug, wout, n2g, tokens, att, cot, gain, cid):
    _, rows, width = p1.shape
    n, ff = gg.shape
    seq = wout.shape[0]
    r, w = TILE
    v = lambda *shape: pltpu.VMEM(shape, BF)
    sem = lambda *shape: pltpu.SemaphoreType.DMA(shape) if shape else pltpu.SemaphoreType.DMA
    b = lambda *shape: jax.ShapeDtypeStruct(shape, BF)
    f = lambda *shape: jax.ShapeDtypeStruct(shape, F32)
    return pl.pallas_call(
        weights_kernel,
        out_shape=[
            f(rows, width), b(width, ff), b(width, ff), b(ff, width), b(rows, width), f(rows, width), f(1, width),
            b(16 * rows, HD),
        ],
        in_specs=[ANY] * 7 + [VM] * 5,
        out_specs=[VM] + [ANY] * 3 + [VM] * 3 + [ANY],
        scratch_shapes=[
            v(16, rows, width), v(2, seq, HD), v(rows, width),
            v(n, width), v(n, width), v(n, ff), v(n, ff), v(n, ff), v(2, 2, r, w), v(12, 2, r, w),
        ]
        + scatter_bufs(rows, width)
        + [sem(6), sem(2), sem(2), sem(12), sem(2, 2), sem(16), sem(16), sem()]
        + SCATTER_SEMS,
        compiler_params=params(cid, 63),
        name="expert_weights",
    )(p1, xr, pg, hid, gg, ug, wout, n2g, tokens, att, cot, gain)


def back_kernel(
    cgh, q, k, v, seg, sk, lse, cosf, sinf, wh, nall, ag, ctx,
    tok, att, mix, mg, gain1, gain2,
    layer_o, tok_g, stat_o, gain_o, out_t, qkv_t,
    ngrad, valid, gsum, early, late, early_got, late_got, both, both_got,
    es, er, hs, hr_, bs, br,
    dkt, dvt, pgrad, pgt, opair, osum, ostage, ord_, orx, ory, orz,
    part, rd, rx, ry, rz, ntile, qpart, qpair,
    lo, ops, opr, ofs, ofr, nsem, qs, qr, ts, tr, fs, fr, *sems,
):
    me = lax.axis_index("dp")
    core = lax.axis_index("grp") % 2
    hr = HD // 2
    mine, other = pl.multiple_of(core * hr, hr), pl.multiple_of((1 - core) * hr, hr)
    blk = lambda b: pl.ds(pl.multiple_of(b * HD, HD), HD)
    barrier([lax.rem(me + d, 16) for d in range(1, 16)], pair=True)
    tiles = [
        pltpu.make_async_copy(nall.at[:, pl.ds(t * 256, 256)], ntile.at[t % 2], nsem.at[t % 2])
        for t in range(wh.shape[1] // 256)
    ]

    pairs = {}
    for j in (3, 1, 2, 0):
        for kk in range(4):
            part[4 * j + kk] = dot(ag[:, blk(place_of(kk, j))], ctx[...], 0, 0).astype(BF)
        group = pl.ds(4 * j, 4)
        pairs[j] = push_pair(part.at[group, pl.ds(other, hr)], opair.at[group], ops.at[j], opr.at[j])
    dkt[...] = jnp.zeros_like(dkt)
    dvt[...] = jnp.zeros_like(dvt)
    so = PlainScatter(opair, osum, hr, (ord_, orx, ory, orz), sems[:10])
    so.at = {name: [4 * j + kk for kk in range(4)] for j, name in enumerate(("col", "X", "Y", "D"))}
    sn = PlainScatter(part, ngrad, HD, (rd, rx, ry, rz), sems[10:20])
    def out_pair(j):
        pairs[j].wait_recv()

        def add(b, carry):
            opair[b] = (opair[b].astype(F32) + part[b, pl.ds(mine, hr)].astype(F32)).astype(BF)
            return carry

        lax.fori_loop(4 * j, 4 * j + 4, add, 0)

    def attend_rows(i, carry):
        row = blk(i)
        s = dot(q[row], k[...], 1, 1)
        prob = jnp.where(column(seg, i) == sk[...], jnp.exp2(s * (SCALE * LOG2E) - lse[row]), 0.0)
        dp = dot(cgh[row], v[...], 1, 1)
        delta = jnp.sum(prob * dp, -1, keepdims=True)
        ds = (prob * (dp - delta)).astype(BF)
        dq = dot(ds, k[...], 1, 0) * SCALE
        dq = dq * cosf[row] - pltpu.roll(dq, HD // 2, 1) * sinf[row]
        pgrad[row, :HD] = dq.astype(BF)
        pgt[:HD, row] = dq.T.astype(BF)
        dkt[...] += dot(q[row], ds, 0, 0)
        dvt[...] += dot(cgh[row], prob.astype(BF), 0, 0)
        return carry

    n = q.shape[0] // HD
    q4 = n // 4
    lax.fori_loop(0, q4 // 2, attend_rows, 0)
    out_pair(3)
    for j in FAR_FIRST:
        so.far(j)
    lax.fori_loop(q4 // 2, 2 * q4, attend_rows, 0)
    out_pair(1)
    out_pair(2)
    so.near(3)
    so.near(2)
    lax.fori_loop(2 * q4, 3 * q4, attend_rows, 0)
    so.near(1)
    so.near(0)
    out_pair(0)
    lax.fori_loop(3 * q4, n, attend_rows, 0)
    for c in pairs.values():
        c.wait_send()

    def turn_back(i, carry):
        row = blk(i)
        dk = dkt[:, row].T * SCALE
        dk = dk * cosf[row] - pltpu.roll(dk, HD // 2, 1) * sinf[row]
        pgrad[row, HD : 2 * HD] = dk.astype(BF)
        pgt[HD : 2 * HD, row] = dk.T.astype(BF)
        dv = dvt[:, row]
        pgrad[row, 2 * HD :] = dv.T.astype(BF)
        pgt[2 * HD :, row] = dv.astype(BF)
        return carry

    lax.fori_loop(0, n, turn_back, 0)
    tiles[0].start()

    def back_block(j, kk):
        b = place_of(kk, j)
        part[b] = dot(pgrad[blk(b)], wh[...], 1, 0).astype(BF)

    for kk in FAR_FIRST:
        back_block(3, kk)
        sn.far(kk)
    for j in FAR_FIRST:
        so.along(j)
    for t, c in enumerate(tiles):
        if t + 1 < len(tiles):
            tiles[t + 1].start()
        c.wait()
        qpart[:, t * 256 : (t + 1) * 256] = dot(pgt[...], ntile[t % 2], 1, 0).astype(BF)
    qc = [push_pair(qpart.at[pl.ds(s * HD + other, hr)], qpair.at[s], qs.at[s], qr.at[s]) for s in range(3)]
    for kk in FAR_FIRST:
        back_block(1, kk)
        back_block(2, kk)
        sn.near(kk)
    so.end()
    ostage[...] = osum[...].astype(BF)
    keep = pltpu.make_async_copy(ostage, out_t.at[pl.ds(mine, hr)], lo)
    keep.start()
    give = push_pair(ostage, out_t.at[pl.ds(mine, hr)], ofs, ofr)
    for s in range(3):
        qc[s].wait_recv()
        qpair[s] = (qpair[s].astype(F32) + qpart[pl.ds(s * HD + mine, hr)].astype(F32)).astype(BF)
        b = 16 * s + me
        to, slot = b // 3, lax.rem(b, 3)
        dst = qkv_t.at[pl.ds(pl.multiple_of(slot * HD + core * hr, hr), hr)]

        @pl.when(to != me)
        def _():
            push(qpair.at[s], dst, ts.at[s], tr.at[slot], to)

        @pl.when(to == me)
        def _():
            pltpu.make_async_copy(qpair.at[s], dst, tr.at[slot]).start()

    for kk in FAR_FIRST:
        back_block(0, kk)
    strips = [slice(e * HD, (e + 1) * HD) for e in range(16)]
    valid[...] = (column(seg, me) != 0.0).astype(F32)
    early[...] = jnp.zeros_like(early)
    for e, cut in enumerate(strips):
        early[e : e + 1, :] = gain2[:, cut]
    early[19:20, :] = jnp.broadcast_to(jnp.sum(valid[...], 0, keepdims=True) * 16.0, (1, HD))

    def layer_rows(i, carry):
        rows = pl.ds(pl.multiple_of(i * 16, 16), 16)
        layer = tok[rows].astype(F32) + att[rows] + mix[rows]
        layer_o[rows] = layer.astype(BF)
        for e, field in enumerate((layer, att[rows], mix[rows])):
            square = field * field * valid[rows]
            early[16 + e : 17 + e, :] += jnp.sum(sum(square[:, cut] for cut in strips), 0, keepdims=True)
        return carry

    lax.fori_loop(0, HD // 16, layer_rows, 0)
    others = [lax.rem(me + d, 16) for d in range(1, 16)]
    sends = [push(early, early_got.at[me], es.at[d + 1], er.at[d + 1], to) for d, to in enumerate(others)]
    early_got[me] = early[...]
    for kk in FAR_FIRST:
        sn.along(kk)
    fc = []
    for s in range(3):
        here = qkv_t.at[pl.ds(pl.multiple_of(s * HD + core * hr, hr), hr)]
        pltpu.make_async_copy(here, here, tr.at[s]).wait()
        fc.append(push_pair(here, here, fs.at[s], fr.at[s]))
    sn.end()
    for s in range(3):

        @pl.when((16 * s + me) // 3 != me)
        def _():
            pltpu.make_async_copy(qpair.at[s], qpair.at[s], ts.at[s]).wait()

    gsum[...] = jnp.zeros_like(gsum)

    def norm_rows(i, carry):
        rows = pl.ds(pl.multiple_of(i * 16, 16), 16)
        pull, gains = rmsnorm_pull(tok[rows].astype(F32), gain1[...], ngrad[rows])
        tok_g[rows] = mg[rows] + pull
        gsum[...] += jnp.sum(gains, 0, keepdims=True)
        return carry

    lax.fori_loop(0, HD // 16, norm_rows, 0)
    for e, cut in enumerate(strips):
        late[e : e + 1, :] = gsum[:, cut]
    sends += [push(late, late_got.at[me], hs.at[d + 1], hr_.at[d + 1], to) for d, to in enumerate(others)]
    late_got[me] = late[...]
    for c in sends:
        c.wait_recv()

    def over_devices(got):
        total = got[0]
        for e in range(1, 16):
            total = total + got[e]
        return total

    both[:16, :] = over_devices(late_got)
    first = over_devices(early_got)
    both[16:, :] = first[:16]
    stat_o[...] = first[16:]
    across = push_pair(both, both_got, bs, br)
    across.wait()
    gain_o[...] = both[...] + both_got[...]
    for c in sends:
        c.wait_send()
    keep.wait()
    give.wait()
    for c in qc:
        c.wait_send()
    for c in fc:
        c.wait()


def back(cgh, q, k, v, seg, sk, lse, cosf, sinf, wh, nall, ag, ctx, tok, att, mix, mg, gain1, gain2, cid):
    rows, width = ag.shape
    seq = q.shape[0]
    vb = lambda *shape: pltpu.VMEM(shape, BF)
    vf = lambda *shape: pltpu.VMEM(shape, F32)
    sem = lambda *shape: pltpu.SemaphoreType.DMA(shape) if shape else pltpu.SemaphoreType.DMA
    return pl.pallas_call(
        back_kernel,
        out_shape=[
            jax.ShapeDtypeStruct((rows, width), BF),
            jax.ShapeDtypeStruct((rows, width), F32),
            jax.ShapeDtypeStruct((8, HD), F32),
            jax.ShapeDtypeStruct((32, HD), F32),
            jax.ShapeDtypeStruct((rows, width), BF),
            jax.ShapeDtypeStruct((3 * HD, width), BF),
        ],
        in_specs=[VM] * 10 + [ANY] + [VM] * 8,
        out_specs=[VM] * 4 + [ANY, ANY],
        scratch_shapes=[
            vf(rows, width), vf(rows, 1), vf(1, width), vf(24, HD), vf(16, HD), vf(16, 24, HD), vf(16, 16, HD),
            vf(32, HD), vf(32, HD), sem(16), sem(16), sem(16), sem(16), sem(), sem(),
            vf(HD, seq), vf(HD, seq), vb(seq, 3 * HD), vb(3 * HD, seq),
            vb(16, rows // 2, width), vf(rows // 2, width), vb(rows // 2, width),
        ]
        + plain_bufs(rows // 2, width)
        + [vb(16, rows, width)]
        + plain_bufs(rows, width)
        + [vb(2, seq, 256), vb(3 * HD, width), vb(3, HD // 2, width)]
        + [sem(), sem(4), sem(4), sem(), sem(), sem(2), sem(3), sem(3), sem(3), sem(3), sem(3), sem(3)]
        + SCATTER_SEMS * 2,
        compiler_params=params(cid, 62),
        name="back",
    )(cgh, q, k, v, seg, sk, lse, cosf, sinf, wh, nall, ag, ctx, tok, att, mix, mg, gain1, gain2)


def rotary_tables(length):
    freq = (THETA ** (-(np.arange(HD // 2) * 2.0 / HD))).astype(np.float32)
    angle = (np.arange(length, dtype=np.float32)[:, None] * freq[None, :]).astype(np.float64)
    cos, sin = np.cos(angle).astype(np.float32), np.sin(angle).astype(np.float32)
    return np.concatenate([cos, cos], 1), np.concatenate([-sin, sin], 1)


def per_device(
    tokens, segments, routes, route_weight, capacity, norm_gain,
    qkv_weight, out_weight, gate_weight, up_weight, down_weight, cotangent,
):
    rows, width = tokens.shape
    seq = segments.shape[0]
    gain1_row, gain2_row = norm_gain[:1], norm_gain[1:]
    meta = jnp.concatenate([routes.astype(F32).T, route_weight.T], 0)
    seg = segments.astype(F32).reshape(16, rows)
    sk = jnp.where(segments == 0, -1.0, segments.astype(F32))[None, :]
    cos_table, sin_table = rotary_tables(seq)
    normed_all, meta_all, w_head, q, k, v, lse, context, dense_out = front(
        tokens, gain1_row, meta, qkv_weight, out_weight, cos_table, sin_table, seg, sk, 0
    )
    attended, n2g, mix_part, xr, pg, hidden, gg, ug = expert(
        context, dense_out, tokens, gain2_row, cotangent, meta_all, capacity,
        gate_weight[0], up_weight[0], down_weight[0], 3,
    )
    flat = lambda a: a.reshape(-1, a.shape[2])
    mixture, gate_g, up_g, down_g, attended_grad, middle_grad, gain2, cgh = expert_weights(
        mix_part, flat(xr), flat(pg), flat(hidden), flat(gg), flat(ug), flat(dense_out),
        n2g, tokens, attended, cotangent, gain2_row, 5,
    )
    layer_out, tokens_grad, stat_lanes, gain_pair, out_total, qkv_total = back(
        cgh, q, k, v, seg, sk, lse, cos_table, sin_table, w_head, flat(normed_all), attended_grad, context,
        tokens, attended, mixture, middle_grad, gain1_row, gain2, 6,
    )
    seq_sums = jnp.sum(stat_lanes, 1)
    gain_pair = gain_pair.reshape(2, width)
    stat_row = jnp.sqrt(seq_sums[:3] / seq_sums[3]).reshape(1, 3)
    groups = lax.axis_size("grp")
    over = lambda a: a.astype(F32) if groups == 2 else lax.psum(a.astype(BF), "grp").astype(F32) * 0.5
    return (
        layer_out,
        tokens_grad,
        over(qkv_total),
        over(out_total),
        over(gate_g)[None],
        over(up_g)[None],
        over(down_g)[None],
        gain_pair if groups == 2 else lax.psum(gain_pair, "grp") * 0.5,
        stat_row,
    )


def solution(mesh):
    both = ("grp", "dp")
    in_specs = (
        P(both, None), P("grp"), P(both, None), P(both, None), P(), P(),
        P("dp", None), P("dp", None), P("dp", None, None), P("dp", None, None), P("dp", None, None),
        P(both, None),
    )
    out_specs = (
        P(both, None), P(both, None), P("dp", None), P("dp", None),
        P("dp", None, None), P("dp", None, None), P("dp", None, None), P(), P("grp", None),
    )
    return jax.shard_map(per_device, mesh=mesh, in_specs=in_specs, out_specs=out_specs, check_vma=False)
```

```python
import functools

import jax
import jax.numpy as jnp
import numpy as np
from jax import lax
from jax.experimental import pallas as pl
from jax.experimental.pallas import tpu as pltpu
from jax.sharding import PartitionSpec as P

H = 16
HD = 128
TOPK = 8
EPS = 1e-06
THETA = 50000.0
MESH = pl.DeviceIdType.MESH
MIB = 2**20
BF = jnp.bfloat16
F32 = jnp.float32
SCALE = HD**-0.5
LOG2E = 1.4426950408889634


def places():
    me = lax.axis_index("dp")
    z, y, x = me // 4, (me // 2) % 2, me % 2
    xor = [z, z + 1 - 2 * (z % 2), (z + 2) % 4, 3 - z]
    at = lambda k, yy, xx: xor[k] * 4 + yy * 2 + xx
    return dict(
        me=me,
        col=[at(k, y, x) for k in range(4)],
        X=[at(k, y, 1 - x) for k in range(4)],
        Y=[at(k, 1 - y, x) for k in range(4)],
        D=[at(k, 1 - y, 1 - x) for k in range(4)],
    )


def barrier(targets, pair=False):
    sem = pltpu.get_barrier_semaphore()
    for t in targets:
        pl.semaphore_signal(sem, inc=1, device_id={"dp": t}, device_id_type=MESH)
    count = len(targets)
    if pair:
        pl.semaphore_signal(sem, inc=1, device_id={"grp": partner()}, device_id_type=MESH)
        count += 1
    pl.semaphore_wait(sem, count)


def partner():
    g = lax.axis_index("grp")
    return g + 1 - 2 * (g % 2)


def push(src, dst, send, recv, to):
    c = pltpu.make_async_remote_copy(
        src_ref=src, dst_ref=dst, send_sem=send, recv_sem=recv,
        device_id={"dp": to}, device_id_type=MESH,
    )
    c.start()
    return c


def push_pair(src, dst, send, recv):
    c = pltpu.make_async_remote_copy(
        src_ref=src, dst_ref=dst, send_sem=send, recv_sem=recv,
        device_id={"grp": partner()}, device_id_type=MESH,
    )
    c.start()
    return c


ORDER = (1, 0, 3, 2)
GATHER_SEMS = (
    [pltpu.SemaphoreType.DMA((4,))] * 6 + [pltpu.SemaphoreType.DMA((4, 2))] * 2 + [pltpu.SemaphoreType.DMA]
    + [pltpu.SemaphoreType.DMA((4,))] * 2
)


class Gather:
    def __init__(self, src, dst, rows, sems, first=0):
        self.src, self.dst, self.rows, self.sems, self.first, self.p = src, dst, rows, sems, first, places()

    def block(self, b):
        return self.dst.at[b, pl.ds(self.first, self.rows)]

    def part(self, b, h):
        half = self.rows // 2
        return self.dst.at[b, pl.ds(self.first + h * half, half)]

    def begin(self):
        zs, zr, xs, xr, ys, yr, _, _, own, _, _ = self.sems
        p, src = self.p, self.src
        me = p["me"]
        self.mine = pltpu.make_async_copy(src, self.block(me), own)
        self.mine.start()
        self.xc = {0: push(src, self.block(me), xs.at[0], xr.at[0], p["X"][0])}
        self.yc = {0: push(src, self.block(me), ys.at[0], yr.at[0], p["Y"][0])}
        self.zc = {k: push(src, self.block(me), zs.at[k], zr.at[k], p["col"][k]) for k in (1, 2)}
        self.dc, self.vc = {}, {}

    def near(self, k):
        _, _, xs, xr, ys, yr = self.sems[:6]
        p = self.p
        self.zc[k].wait_recv()
        b = self.block(p["col"][k])
        if k == 2:
            zs, zr = self.sems[:2]
            self.zc[3] = push(b, b, zs.at[3], zr.at[3], p["col"][1])
        self.xc[k] = push(b, b, xs.at[k], xr.at[k], p["X"][0])
        self.yc[k] = push(b, b, ys.at[k], yr.at[k], p["Y"][0])

    def far(self, k):
        ds, dr = self.sems[6:8]
        p = self.p
        b = self.part(p["X"][k], 0)
        self.xc[k].wait_recv()
        self.dc[k, 0] = push(b, b, ds.at[k, 0], dr.at[k, 0], p["Y"][0])
        b = self.part(p["Y"][k], 1)
        self.yc[k].wait_recv()
        self.dc[k, 1] = push(b, b, ds.at[k, 1], dr.at[k, 1], p["X"][0])

    def over(self, k):
        vs, vr = self.sems[9:11]
        self.dc[k, 0].wait_recv()
        self.dc[k, 1].wait_recv()
        b = self.block(self.p["D"][k])
        self.vc[k] = push(b, b, vs.at[k], vr.at[k], self.p["col"][1])

    def ready(self, k):
        if k == 0:
            self.mine.wait()
        if k % 2:
            self.xc[k].wait_recv()
            self.yc[k].wait_recv()
            self.vc[k - 1].wait_recv()

    def end(self):
        for group in (self.xc, self.yc, self.zc, self.dc, self.vc):
            for c in group.values():
                c.wait_send()


def gather_targets():
    p = places()
    return [p["col"][1], p["col"][2], p["col"][3], p["X"][0], p["Y"][0]]


SCATTER_SEMS = [pltpu.SemaphoreType.DMA((4, 2))] * 2 + [pltpu.SemaphoreType.DMA((4,))] * 8


def scatter_bufs(rows, width):
    return [
        pltpu.VMEM((4, rows // 2, width), BF),
        pltpu.VMEM((4, rows, width), BF),
        pltpu.VMEM((4, rows, width), BF),
        pltpu.VMEM((4, rows, width), BF),
        pltpu.VMEM((2, rows, width), BF),
    ]


class Scatter:
    def __init__(self, part, out, rows, bufs, sems):
        self.part, self.out, self.half, self.bufs, self.sems, self.p = part, out, rows // 2, bufs, sems, places()
        self.at = self.p
        self.da, self.db, self.xc, self.yc, self.zc, self.vc = {}, {}, {}, {}, {}, {}

    def lift(self, k):
        vs, vr = self.sems[8:]
        self.vc[k] = push(self.part.at[self.p["D"][k]], self.bufs[4].at[k // 2], vs.at[k], vr.at[k], self.p["col"][1])

    def far(self, k):
        ds, dr = self.sems[:2]
        rd, h, p, part = self.bufs[0], self.half, self.p, self.part
        b = p["D"][k]
        self.vc[k + 1].wait_recv()
        part[b] = (part[b].astype(F32) + self.bufs[4][k // 2].astype(F32)).astype(BF)
        self.da[k] = push(part.at[b, pl.ds(0, h)], rd.at[k], ds.at[k, 0], dr.at[k, 0], p["Y"][0])
        self.db[k] = push(part.at[b, pl.ds(h, h)], rd.at[k + 1], ds.at[k, 1], dr.at[k, 1], p["X"][0])

    def near(self, k):
        xs, xr, ys, yr = self.sems[2:6]
        rd, rx, ry = self.bufs[:3]
        part, h, p = self.part, self.half, self.p
        b = p["X"][k]
        if k % 2 == 0:
            self.da[k].wait_recv()
            part[b, pl.ds(0, h)] = (part[b, pl.ds(0, h)].astype(F32) + rd[k].astype(F32)).astype(BF)
        self.xc[k] = push(part.at[b], rx.at[k], xs.at[k], xr.at[k], p["X"][0])
        b = p["Y"][k]
        if k % 2 == 0:
            self.db[k].wait_recv()
            part[b, pl.ds(h, h)] = (part[b, pl.ds(h, h)].astype(F32) + rd[k + 1].astype(F32)).astype(BF)
        self.yc[k] = push(part.at[b], ry.at[k], ys.at[k], yr.at[k], p["Y"][0])

    def along(self, k):
        zs, zr = self.sems[6:8]
        rx, ry, rz = self.bufs[1:4]
        part = self.part
        b = self.p["col"][k]
        self.xc[k].wait_recv()
        self.yc[k].wait_recv()
        total = part[b].astype(F32) + rx[k].astype(F32) + ry[k].astype(F32)
        if k == 2:
            self.zc[3].wait_recv()
            total = total + rz[3].astype(F32)
        if k:
            part[b] = total.astype(BF)
            self.zc[k] = push(part.at[b], rz.at[k], zs.at[k], zr.at[k], self.p["col"][1 if k == 3 else k])
        else:
            self.out[...] = total

    def end(self):
        self.zc[1].wait_recv()
        self.zc[2].wait_recv()
        self.out[...] += self.bufs[3][1].astype(F32) + self.bufs[3][2].astype(F32)
        for group in (self.da, self.db, self.xc, self.yc, self.zc, self.vc):
            for c in group.values():
                c.wait_send()


class PlainScatter(Scatter):
    def far(self, k):
        ds, dr = self.sems[:2]
        rd, h, p = self.bufs[0], self.half, self.p
        b = self.at["D"][k]
        self.da[k] = push(self.part.at[b, pl.ds(0, h)], rd.at[2 * k], ds.at[k, 0], dr.at[k, 0], p["Y"][0])
        self.db[k] = push(self.part.at[b, pl.ds(h, h)], rd.at[2 * k + 1], ds.at[k, 1], dr.at[k, 1], p["X"][0])

    def near(self, k):
        xs, xr, ys, yr = self.sems[2:6]
        rd, rx, ry = self.bufs[:3]
        part, h, p = self.part, self.half, self.p
        b = self.at["X"][k]
        self.da[k].wait_recv()
        part[b, pl.ds(0, h)] = (part[b, pl.ds(0, h)].astype(F32) + rd[2 * k].astype(F32)).astype(BF)
        self.xc[k] = push(part.at[b], rx.at[k], xs.at[k], xr.at[k], p["X"][0])
        b = self.at["Y"][k]
        self.db[k].wait_recv()
        part[b, pl.ds(h, h)] = (part[b, pl.ds(h, h)].astype(F32) + rd[2 * k + 1].astype(F32)).astype(BF)
        self.yc[k] = push(part.at[b], ry.at[k], ys.at[k], yr.at[k], p["Y"][0])

    def along(self, k):
        zs, zr = self.sems[6:8]
        rx, ry, rz = self.bufs[1:4]
        part, b = self.part, self.at["col"][k]
        self.xc[k].wait_recv()
        self.yc[k].wait_recv()
        total = part[b].astype(F32) + rx[k].astype(F32) + ry[k].astype(F32)
        if k == 2:
            self.zc[3].wait_recv()
            total = total + rz[3].astype(F32)
        if k:
            part[b] = total.astype(BF)
            self.zc[k] = push(part.at[b], rz.at[k], zs.at[k], zr.at[k], self.p["col"][1 if k == 3 else k])
        else:
            self.out[...] = total


def plain_bufs(rows, width):
    return [pltpu.VMEM((8, rows // 2, width), BF)] + scatter_bufs(rows, width)[1:4]


FAR_FIRST = (3, 2, 1, 0)


ANY = pl.BlockSpec(memory_space=pl.ANY)
VM = pl.BlockSpec(memory_space=pltpu.VMEM)


def params(cid, vmem=60):
    return pltpu.CompilerParams(collective_id=cid, has_side_effects=True, vmem_limit_bytes=vmem * MIB)


def rmsnorm(field, gain_row):
    return field * lax.rsqrt(jnp.mean(field * field, -1, keepdims=True) + EPS) * gain_row


def rmsnorm_pull(field, gain_row, grad):
    r = lax.rsqrt(jnp.mean(field * field, -1, keepdims=True) + EPS)
    scaled = grad * gain_row
    back = r * scaled - field * (r * r * r * jnp.mean(scaled * field, -1, keepdims=True))
    return back, grad * field * r


def column(rows, b):
    return jnp.broadcast_to(rows[pl.ds(b, 1), :], (8, rows.shape[1])).T[:, :1]


def dot(a, b, ca, cb):
    return lax.dot_general(a, b, (((ca,), (cb,)), ((), ())), preferred_element_type=F32)


def front_kernel(
    tok, gain, m_ref, w_ref, o_ref, cosf, sinf, seg, sk,
    nall_o, mall, wh_o, q, k, v, lse, ctx, oall,
    n_ref, nall, wh, ctxh, ms, mr, mo, ws, wr, ps, pr, wo, no, cs, cr, co, os_, or_, *sems,
):
    me = lax.axis_index("dp")
    core = lax.axis_index("grp") % 2
    hr = HD // 2
    blk = lambda b: pl.ds(pl.multiple_of(b * HD, HD), HD)
    half = lambda s, c: pl.ds(pl.multiple_of(s * HD + c * hr, hr), hr)
    n_ref[...] = rmsnorm(tok[...].astype(F32), gain[...]).astype(BF)
    barrier([lax.rem(me + d, 16) for d in range(1, 16)], pair=True)
    g = Gather(n_ref, nall, n_ref.shape[0], sems[:11])
    go = Gather(o_ref.at[half(0, core)], oall, hr, sems[11:], pl.multiple_of(core * hr, hr))
    g.begin()
    own = pltpu.make_async_copy(m_ref, mall.at[me], mo)
    own.start()
    mc = [push(m_ref, mall.at[me], ms.at[d], mr.at[d], lax.rem(me + d, 16)) for d in range(1, 16)]
    for l in range(3):
        b = 3 * me + l
        to, slot = lax.rem(b, 16), b // 16
        src, dst = w_ref.at[half(l, core)], wh.at[half(slot, core)]

        @pl.when(to != me)
        def _():
            push(src, dst, ws.at[l], wr.at[slot], to)

        @pl.when(to == me)
        def _():
            pltpu.make_async_copy(src, dst, wr.at[slot]).start()

    def project(b, carry):
        row = blk(b)
        out = dot(nall[b], wh[...], 1, 1)
        turn = lambda a: (a * cosf[row] + pltpu.roll(a, HD // 2, 1) * sinf[row]).astype(BF)
        q[row] = turn(out[:, :HD])
        k[row] = turn(out[:, HD : 2 * HD])
        v[row] = out[:, 2 * HD :].astype(BF)
        return carry

    def project_plane(c):
        lax.fori_loop(0, 4, lambda j, carry: project(place_of(c, j), carry), 0)

    g.near(1)
    g.far(0)
    g.near(2)
    g.over(0)
    g.far(2)
    g.near(3)
    go.begin()
    g.over(2)
    pc = []
    for s in range(3):
        dst = wh.at[half(s, core)]
        pltpu.make_async_copy(dst, dst, wr.at[s]).wait()
        pc.append(push_pair(dst, dst, ps.at[s], pr.at[s]))
    go.near(1)
    for p in pc:
        p.wait_recv()
    g.ready(0)
    project_plane(0)
    g.ready(1)
    project_plane(1)
    g.ready(2)
    project_plane(2)
    go.far(0)
    go.near(2)
    g.ready(3)
    project_plane(3)
    saves = [pltpu.make_async_copy(nall, nall_o, no), pltpu.make_async_copy(wh, wh_o, wo)]
    for c in saves:
        c.start()

    def hop(d):
        to = lax.rem(me + d, 16)
        return pltpu.make_async_remote_copy(
            src_ref=ctxh.at[blk(to)], dst_ref=ctx.at[:, blk(me)], send_sem=cs.at[d], recv_sem=cr.at[d],
            device_id={"dp": to}, device_id_type=MESH,
        )

    def attend_rows(d, carry):
        b = lax.rem(me + d, 16)
        row = blk(b)
        s = dot(q[row], k[...], 1, 1)
        s = jnp.where(column(seg, b) == sk[...], s, -1e30)
        peak = jnp.maximum(jnp.max(s, -1, keepdims=True), -1e29)
        ex = jnp.exp2((s - peak) * (SCALE * LOG2E))
        total = jnp.maximum(jnp.sum(ex, -1, keepdims=True), 1.0)
        prob = (ex * (1.0 / total)).astype(BF)
        ctxh[row] = jnp.dot(prob, v[...], preferred_element_type=F32).astype(BF)
        lse[row] = peak * (SCALE * LOG2E) + jnp.log2(total)
        return carry

    def attend_send(d, carry):
        attend_rows(d, carry)
        hop(d).start()
        return carry

    oc = []

    def swap_plane(c):
        go.ready(c)
        z = place_of(c, 0) // 4
        here = oall.at[pl.ds(4 * z, 4), pl.ds(pl.multiple_of(core * hr, hr), hr)]
        oc.append(push_pair(here, here, os_.at[c], or_.at[c]))

    lax.fori_loop(1, 6, attend_send, 0)
    go.over(0)
    go.far(2)
    go.near(3)
    lax.fori_loop(6, 12, attend_send, 0)
    swap_plane(0)
    swap_plane(1)
    lax.fori_loop(12, 16, attend_send, 0)
    attend_rows(0, 0)
    stay = pltpu.make_async_copy(ctxh.at[blk(me)], ctx.at[:, blk(me)], co)
    stay.start()
    go.over(2)
    swap_plane(2)
    swap_plane(3)
    g.end()
    go.end()
    own.wait()
    for c in mc:
        c.wait()
    for l in range(3):
        src = w_ref.at[half(l, core)]

        @pl.when(lax.rem(3 * me + l, 16) != me)
        def _():
            pltpu.make_async_copy(src, src, ws.at[l]).wait()

    for p in pc:
        p.wait_send()
    for c in saves:
        c.wait()
    stay.wait()
    for d in range(1, 16):
        hop(d).wait()
    for c in oc:
        c.wait()


def front(tokens, gain, meta, w, wo, cosf, sinf, seg, sk, cid):
    rows, width = tokens.shape
    seq = cosf.shape[0]
    sem = lambda *shape: pltpu.SemaphoreType.DMA(shape) if shape else pltpu.SemaphoreType.DMA
    b = lambda *shape: jax.ShapeDtypeStruct(shape, BF)
    f = lambda *shape: jax.ShapeDtypeStruct(shape, F32)
    v = lambda *shape: pltpu.VMEM(shape, BF)
    return pl.pallas_call(
        front_kernel,
        out_shape=[
            b(16, rows, width), f(16, *meta.shape), b(3 * HD, width),
            b(seq, HD), b(seq, HD), b(seq, HD), f(seq, 1), b(rows, width), b(16, rows, width),
        ],
        in_specs=[VM, VM] + [ANY] * 3 + [VM] * 4,
        out_specs=[ANY] * 3 + [VM] * 4 + [ANY] * 2,
        scratch_shapes=[v(rows, width), v(16, rows, width), v(3 * HD, width), v(seq, HD)]
        + [sem(16), sem(16), sem(), sem(3), sem(3), sem(3), sem(3), sem(), sem()]
        + [sem(16), sem(16), sem(), sem(4), sem(4)]
        + GATHER_SEMS * 2,
        compiler_params=params(cid),
        name="front",
    )(tokens, gain, meta, w, wo, cosf, sinf, seg, sk)


SLOTS = 80
COLS = 512


def place_of(k, j):
    me = lax.axis_index("dp")
    z, y, x = me // 4, (me // 2) % 2, me % 2
    zk = [z, z + 1 - 2 * (z % 2), (z + 2) % 4, 3 - z][k]
    jy, jx = j // 2, j % 2
    return zk * 4 + (y + jy - 2 * y * jy) * 2 + (x + jx - 2 * x * jx)


def expert_kernel(
    ctx, wout, tok, gain, cot, meta, cap, wg_h, wu_h, wd_h,
    att, n2g, p1, xr_o, pg_o, hid_o, gg_o, ug_o,
    n2, rank, coef, pick, sw, nall, call, part, stage, wg, wu, wd, xr, pg, hid, gg, ug, rd, rx, ry, rz, rv,
    wosem, wsem, osem, psem, *sems,
):
    rows, width = ctx.shape
    wload = pltpu.make_async_copy(wout, part, wosem)
    wload.start()
    barrier(gather_targets())
    gn = Gather(n2, nall, rows, sems[:11])
    gc = Gather(cot, call, rows, sems[11:22])
    sc = Scatter(part, n2g, rows, (rd, rx, ry, rz, rv), sems[22:])
    gc.begin()
    loads = [pltpu.make_async_copy(a, b, wsem.at[i]) for i, (a, b) in enumerate([(wg_h, wg), (wu_h, wu), (wd_h, wd)])]
    me = lax.axis_index("dp").astype(F32)
    hits = [meta[:, r, :] == me for r in range(TOPK)]
    member = sum(h.astype(F32) for h in hits)
    coef[...] = sum(jnp.where(h, meta[:, TOPK + r, :], 0.0) for r, h in enumerate(hits))
    i0, i1 = lax.broadcasted_iota(jnp.int32, (HD, HD), 0), lax.broadcasted_iota(jnp.int32, (HD, HD), 1)
    local = dot(member.astype(BF), (i0 < i1).astype(BF), 1, 0)
    count = jnp.broadcast_to(jnp.sum(member, 1, keepdims=True), member.shape).astype(BF)
    j0, j1 = lax.broadcasted_iota(jnp.int32, (16, 16), 0), lax.broadcasted_iota(jnp.int32, (16, 16), 1)
    before = dot((j1 < j0).astype(BF), count, 1, 0)
    kept = (member > 0.0) & (local + before < cap[0].astype(F32))
    rank[...] = jnp.where(kept, local, -1.0)
    wload.wait()

    def attend_cols(t, carry):
        w = part[pl.ds(2 * t, 2)].reshape(2 * rows, width)
        att[:, pl.ds(pl.multiple_of(t * 2 * rows, 2 * rows), 2 * rows)] = dot(ctx[...], w, 1, 1)
        return carry

    lax.fori_loop(0, 8, attend_cols, 0)
    n2[...] = rmsnorm(tok[...].astype(F32) + att[...], gain[...]).astype(BF)
    gn.begin()
    for c in loads:
        c.start()
    saves = []
    both = lambda name, k: [getattr(g, name)(k) for g in (gn, gc)]
    both("near", 1)
    both("far", 0)
    both("near", 2)
    both("over", 0)
    for i, k in enumerate(ORDER):
        both("ready", k)
        if k == 1:
            both("far", 2)
            both("near", 3)
        if k == 0:
            sc.near(1)
            both("over", 2)
        if k == 3:
            sc.near(0)
            sc.along(1)
        if k == 2:
            sc.near(3)
            sc.along(0)
        for c in saves:
            c.wait()
        if i == 0:
            for c in loads:
                c.wait()

        def collect(j, carry):
            b = place_of(k, j)
            to = pl.ds(pl.multiple_of(j * SLOTS, SLOTS), SLOTS)
            s0 = lax.broadcasted_iota(jnp.int32, (SLOTS, rows), 0).astype(F32)
            mine = s0 == rank[pl.ds(b, 1), :]
            sw[to, :] = jnp.sum(jnp.where(mine, coef[pl.ds(b, 1), :], 0.0), 1, keepdims=True)
            pick[to, :] = mine.astype(BF)

            def cols(n, c):
                w = pl.ds(pl.multiple_of(n * 512, 512), 512)
                xr[to, w] = dot(pick[to, :], nall[b, :, w], 1, 0).astype(BF)
                pg[to, w] = (dot(pick[to, :], call[b, :, w], 1, 0) * sw[to, :]).astype(BF)
                return c

            return lax.fori_loop(0, width // 512, cols, carry)

        lax.fori_loop(0, 4, collect, 0)

        def inner(n, carry):
            w = pl.ds(pl.multiple_of(n * COLS, COLS), COLS)
            gate = dot(xr[...], wg[:, w], 1, 0)
            up = dot(xr[...], wu[:, w], 1, 0)
            hg = dot(pg[...], wd[w, :], 1, 1)
            sig = jax.nn.sigmoid(gate)
            hid[:, w] = (gate * sig * up).astype(BF)
            gg[:, w] = (hg * up * sig * (1.0 + gate * (1.0 - sig))).astype(BF)
            ug[:, w] = (hg * gate * sig).astype(BF)
            return carry

        lax.fori_loop(0, hid.shape[1] // COLS, inner, 0)

        def outer(n, carry):
            w = pl.ds(pl.multiple_of(n * COLS, COLS), COLS)
            eo = dot(hid[...], wd[:, w], 1, 0).astype(BF).astype(F32)
            rg = (dot(gg[...], wg[w, :], 1, 1) + dot(ug[...], wu[w, :], 1, 1)).astype(BF)
            for j in range(4):
                b = place_of(k, j)
                cut = slice(j * SLOTS, (j + 1) * SLOTS)
                weighted = (eo[cut] * sw[cut]).astype(BF)
                stage[j, :, w] = dot(pick[cut], weighted, 0, 0).astype(BF)
                part[b, :, w] = dot(pick[cut], rg[cut], 0, 0).astype(BF)
            return carry

        if k == 2:
            sc.along(3)
        lax.fori_loop(0, xr.shape[1] // COLS, outer, 0)
        if k % 2:
            sc.lift(k)
        else:
            sc.far(k)
        saves = [
            pltpu.make_async_copy(a, o.at[k], osem.at[i])
            for i, (a, o) in enumerate([(xr, xr_o), (pg, pg_o), (hid, hid_o), (gg, gg_o), (ug, ug_o)])
        ] + [pltpu.make_async_copy(stage.at[j], p1.at[place_of(k, j)], psem.at[j]) for j in range(4)]
        for c in saves:
            c.start()
    gn.end()
    gc.end()
    sc.near(2)
    sc.along(2)
    sc.end()
    for c in saves:
        c.wait()


def expert(ctx, wout, tokens, gain, cot, meta, cap, wg, wu, wd, cid):
    rows, width = ctx.shape
    ff = wg.shape[1]
    chunk = 4 * SLOTS
    save = lambda w: jax.ShapeDtypeStruct((4, chunk, w), BF)
    v = lambda *shape: pltpu.VMEM(shape, BF)
    f = lambda *shape: pltpu.VMEM(shape, F32)
    return pl.pallas_call(
        expert_kernel,
        out_shape=[
            jax.ShapeDtypeStruct((rows, width), F32),
            jax.ShapeDtypeStruct((rows, width), F32),
            jax.ShapeDtypeStruct((16, rows, width), BF),
            save(width), save(width), save(ff), save(ff), save(ff),
        ],
        in_specs=[VM, ANY, VM, VM, ANY, VM, pl.BlockSpec(memory_space=pltpu.SMEM), ANY, ANY, ANY],
        out_specs=[VM, VM] + [ANY] * 6,
        scratch_shapes=[
            v(rows, width), f(16, rows), f(16, rows), v(chunk, rows), f(chunk, 1),
            v(16, rows, width), v(16, rows, width), v(16, rows, width), v(4, rows, width),
            v(width, ff), v(width, ff), v(ff, width),
            v(chunk, width), v(chunk, width), v(chunk, ff), v(chunk, ff), v(chunk, ff),
        ]
        + scatter_bufs(rows, width)
        + [pltpu.SemaphoreType.DMA, pltpu.SemaphoreType.DMA((3,)), pltpu.SemaphoreType.DMA((5,)), pltpu.SemaphoreType.DMA((4,))]
        + GATHER_SEMS * 2
        + SCATTER_SEMS,
        compiler_params=params(cid, 62),
        name="expert",
    )(ctx, wout, tokens, gain, cot, meta, cap, wg, wu, wd)


TILE = (256, 1024)


def weights_kernel(
    p1, xr_h, pg_h, hid_h, gg_h, ug_h, wout, n2g, tok, att, cot, gain,
    mix, gate_o, up_o, down_o, ag, mg, gain_g, cgh,
    part, wo, cg, xr, pg, hid, gg, ug, give, got, rd, rx, ry, rz, rv, lsem, wsem, gs, gr, os_, cs, cr, co, *sems,
):
    me = lax.axis_index("dp")
    blk = lambda b: pl.ds(pl.multiple_of(b * HD, HD), HD)
    loads = [
        pltpu.make_async_copy(a, b, lsem.at[i])
        for i, (a, b) in enumerate(
            [(p1, part), (xr_h, xr), (gg_h, gg), (ug_h, ug), (hid_h, hid), (pg_h, pg)]
        )
    ]
    column_load = lambda t: pltpu.make_async_copy(
        wout.at[:, pl.ds(pl.multiple_of(t * HD, HD), HD)], wo.at[lax.rem(t, 2)], wsem.at[lax.rem(t, 2)]
    )
    column_load(0).start()
    for c in loads:
        c.start()
    gain_g[...] = jnp.zeros_like(gain_g)

    def middle_rows(i, carry):
        rows = pl.ds(pl.multiple_of(i * 16, 16), 16)
        back, gains = rmsnorm_pull(tok[rows].astype(F32) + att[rows], gain[...], n2g[rows])
        gain_g[...] += jnp.sum(gains, 0, keepdims=True)
        grad = cot[rows].astype(F32) + back
        mg[rows] = grad
        ag[rows] = grad.astype(BF)
        return carry

    lax.fori_loop(0, tok.shape[0] // 16, middle_rows, 0)
    barrier([lax.rem(me + d, 16) for d in range(1, 16)], pair=True)
    sc = Scatter(part, mix, part.shape[1], (rd, rx, ry, rz, rv), sems)
    loads[0].wait()
    sc.lift(1)
    sc.lift(3)
    sc.near(3)
    sc.near(1)
    tiles = cg.shape[1] // HD

    def context_cols(t, carry):
        @pl.when(t + 1 < tiles)
        def _():
            column_load(t + 1).start()

        column_load(t).wait()
        cols = pl.ds(pl.multiple_of(t * HD, HD), HD)
        cg[:, cols] = dot(ag[...], wo[lax.rem(t, 2)], 1, 0).astype(BF)
        return carry

    lax.fori_loop(0, tiles, context_cols, 0)

    def hop(d):
        to = lax.rem(me + d, 16)
        return pltpu.make_async_remote_copy(
            src_ref=cg.at[:, blk(to)], dst_ref=cgh.at[blk(me)], send_sem=cs.at[d], recv_sem=cr.at[d],
            device_id={"dp": to}, device_id_type=MESH,
        )

    for d in range(1, 16):
        hop(d).start()
    stay = pltpu.make_async_copy(cg.at[:, blk(me)], cgh.at[blk(me)], co)
    stay.start()
    sc.far(2)
    sc.far(0)
    for c in loads[1:]:
        c.wait()
    r, w = TILE
    strip = lambda a, t, size: a[:, pl.ds(pl.multiple_of(t * size, size), size)]

    def product(m, t):
        left = strip((xr, hid)[m], t, r).T
        for e in range(2):
            yield dot(left, (gg, ug)[e][...] if m == 0 else pg[:, e * w : (e + 1) * w], 1, 0)

    def home(m, t, e):
        rows = pl.ds(pl.multiple_of(t * r, r), r)
        return (gate_o, up_o)[e].at[rows] if m == 0 else down_o.at[rows, pl.ds(e * w, w)]

    def sent(m, t):
        s = lax.rem(t, 2)
        return pltpu.make_async_remote_copy(
            src_ref=give.at[s], dst_ref=got.at[8 * m + t], send_sem=gs.at[s], recv_sem=gr.at[8 * m + t],
            device_id={"grp": partner()}, device_id_type=MESH,
        )

    def saved(m, t):
        s = lax.rem(t, 2)
        return [pltpu.make_async_copy(got.at[8 * m + t, e], home(m, t, e), os_.at[s, e]) for e in range(2)]

    def finish(m, t):
        s = lax.rem(t, 2)
        sent(m, t).wait_recv()
        got[8 * m + t] = (give[s].astype(F32) + got[8 * m + t].astype(F32)).astype(BF)
        for c in saved(m, t):
            c.start()

    def free(m, t):
        sent(m, t).wait_send()
        for c in saved(m, t):
            c.wait()

    def body(m, start):
        def step(t, carry):
            s = lax.rem(t, 2)

            @pl.when(t >= start + 2)
            def _():
                free(m, t - 2)

            for e, tile in enumerate(product(m, t)):
                give[s, e] = tile.astype(BF)
            sent(m, t).start()

            @pl.when(t >= start + 1)
            def _():
                finish(m, t - 1)

            return carry

        return step

    for i, (m, start) in enumerate(((0, 0), (0, 4), (1, 0))):
        lax.fori_loop(start, start + 4, body(m, start), 0)
        finish(m, start + 3)
        free(m, start + 2)
        free(m, start + 3)
        if i == 0:
            sc.near(2)
            sc.near(0)
            sc.along(3)
        if i == 1:
            sc.along(1)
            sc.along(2)
    sc.along(0)
    sc.end()
    stay.wait()
    for d in range(1, 16):
        hop(d).wait()


def expert_weights(p1, xr, pg, hid, gg, ug, wout, n2g, tokens, att, cot, gain, cid):
    _, rows, width = p1.shape
    n, ff = gg.shape
    seq = wout.shape[0]
    r, w = TILE
    v = lambda *shape: pltpu.VMEM(shape, BF)
    sem = lambda *shape: pltpu.SemaphoreType.DMA(shape) if shape else pltpu.SemaphoreType.DMA
    b = lambda *shape: jax.ShapeDtypeStruct(shape, BF)
    f = lambda *shape: jax.ShapeDtypeStruct(shape, F32)
    return pl.pallas_call(
        weights_kernel,
        out_shape=[
            f(rows, width), b(width, ff), b(width, ff), b(ff, width), b(rows, width), f(rows, width), f(1, width),
            b(16 * rows, HD),
        ],
        in_specs=[ANY] * 7 + [VM] * 5,
        out_specs=[VM] + [ANY] * 3 + [VM] * 3 + [ANY],
        scratch_shapes=[
            v(16, rows, width), v(2, seq, HD), v(rows, width),
            v(n, width), v(n, width), v(n, ff), v(n, ff), v(n, ff), v(2, 2, r, w), v(12, 2, r, w),
        ]
        + scatter_bufs(rows, width)
        + [sem(6), sem(2), sem(2), sem(12), sem(2, 2), sem(16), sem(16), sem()]
        + SCATTER_SEMS,
        compiler_params=params(cid, 63),
        name="expert_weights",
    )(p1, xr, pg, hid, gg, ug, wout, n2g, tokens, att, cot, gain)


def back_kernel(
    cgh, q, k, v, seg, sk, lse, cosf, sinf, wh, nall, ag, ctx,
    tok, att, mix, mg, gain1, gain2,
    layer_o, tok_g, stat_o, gain_o, out_t, qkv_t,
    ngrad, valid, gsum, early, late, early_got, late_got, both, both_got,
    es, er, hs, hr_, bs, br,
    dkt, dvt, pgrad, pgt, opair, osum, ostage, ord_, orx, ory, orz,
    part, rd, rx, ry, rz, ntile, qpart, qpair,
    lo, ops, opr, ofs, ofr, nsem, qs, qr, ts, tr, fs, fr, *sems,
):
    me = lax.axis_index("dp")
    core = lax.axis_index("grp") % 2
    hr = HD // 2
    mine, other = pl.multiple_of(core * hr, hr), pl.multiple_of((1 - core) * hr, hr)
    blk = lambda b: pl.ds(pl.multiple_of(b * HD, HD), HD)
    barrier([lax.rem(me + d, 16) for d in range(1, 16)], pair=True)
    tiles = [
        pltpu.make_async_copy(nall.at[:, pl.ds(t * 256, 256)], ntile.at[t % 2], nsem.at[t % 2])
        for t in range(wh.shape[1] // 256)
    ]

    pairs = {}
    for j in (3, 1, 2, 0):
        for kk in range(4):
            part[4 * j + kk] = dot(ag[:, blk(place_of(kk, j))], ctx[...], 0, 0).astype(BF)
        group = pl.ds(4 * j, 4)
        pairs[j] = push_pair(part.at[group, pl.ds(other, hr)], opair.at[group], ops.at[j], opr.at[j])
    dkt[...] = jnp.zeros_like(dkt)
    dvt[...] = jnp.zeros_like(dvt)
    so = PlainScatter(opair, osum, hr, (ord_, orx, ory, orz), sems[:10])
    so.at = {name: [4 * j + kk for kk in range(4)] for j, name in enumerate(("col", "X", "Y", "D"))}
    sn = PlainScatter(part, ngrad, HD, (rd, rx, ry, rz), sems[10:20])
    def out_pair(j):
        pairs[j].wait_recv()

        def add(b, carry):
            opair[b] = (opair[b].astype(F32) + part[b, pl.ds(mine, hr)].astype(F32)).astype(BF)
            return carry

        lax.fori_loop(4 * j, 4 * j + 4, add, 0)

    def attend_rows(i, carry):
        row = blk(i)
        s = dot(q[row], k[...], 1, 1)
        prob = jnp.where(column(seg, i) == sk[...], jnp.exp2(s * (SCALE * LOG2E) - lse[row]), 0.0)
        dp = dot(cgh[row], v[...], 1, 1)
        delta = jnp.sum(prob * dp, -1, keepdims=True)
        ds = (prob * (dp - delta)).astype(BF)
        dq = dot(ds, k[...], 1, 0) * SCALE
        dq = dq * cosf[row] - pltpu.roll(dq, HD // 2, 1) * sinf[row]
        pgrad[row, :HD] = dq.astype(BF)
        pgt[:HD, row] = dq.T.astype(BF)
        dkt[...] += dot(q[row], ds, 0, 0)
        dvt[...] += dot(cgh[row], prob.astype(BF), 0, 0)
        return carry

    n = q.shape[0] // HD
    q4 = n // 4
    lax.fori_loop(0, q4 // 2, attend_rows, 0)
    out_pair(3)
    for j in FAR_FIRST:
        so.far(j)
    lax.fori_loop(q4 // 2, 2 * q4, attend_rows, 0)
    out_pair(1)
    out_pair(2)
    so.near(3)
    so.near(2)
    lax.fori_loop(2 * q4, 3 * q4, attend_rows, 0)
    so.near(1)
    so.near(0)
    out_pair(0)
    lax.fori_loop(3 * q4, n, attend_rows, 0)
    for c in pairs.values():
        c.wait_send()

    def turn_back(i, carry):
        row = blk(i)
        dk = dkt[:, row].T * SCALE
        dk = dk * cosf[row] - pltpu.roll(dk, HD // 2, 1) * sinf[row]
        pgrad[row, HD : 2 * HD] = dk.astype(BF)
        pgt[HD : 2 * HD, row] = dk.T.astype(BF)
        dv = dvt[:, row]
        pgrad[row, 2 * HD :] = dv.T.astype(BF)
        pgt[2 * HD :, row] = dv.astype(BF)
        return carry

    lax.fori_loop(0, n, turn_back, 0)
    tiles[0].start()

    def back_block(j, kk):
        b = place_of(kk, j)
        part[b] = dot(pgrad[blk(b)], wh[...], 1, 0).astype(BF)

    for kk in FAR_FIRST:
        back_block(3, kk)
        sn.far(kk)
    for j in FAR_FIRST:
        so.along(j)
    for t, c in enumerate(tiles):
        if t + 1 < len(tiles):
            tiles[t + 1].start()
        c.wait()
        qpart[:, t * 256 : (t + 1) * 256] = dot(pgt[...], ntile[t % 2], 1, 0).astype(BF)
    qc = [push_pair(qpart.at[pl.ds(s * HD + other, hr)], qpair.at[s], qs.at[s], qr.at[s]) for s in range(3)]
    for kk in FAR_FIRST:
        back_block(1, kk)
        back_block(2, kk)
        sn.near(kk)
    so.end()
    ostage[...] = osum[...].astype(BF)
    keep = pltpu.make_async_copy(ostage, out_t.at[pl.ds(mine, hr)], lo)
    keep.start()
    give = push_pair(ostage, out_t.at[pl.ds(mine, hr)], ofs, ofr)
    for s in range(3):
        qc[s].wait_recv()
        qpair[s] = (qpair[s].astype(F32) + qpart[pl.ds(s * HD + mine, hr)].astype(F32)).astype(BF)
        b = 16 * s + me
        to, slot = b // 3, lax.rem(b, 3)
        dst = qkv_t.at[pl.ds(pl.multiple_of(slot * HD + core * hr, hr), hr)]

        @pl.when(to != me)
        def _():
            push(qpair.at[s], dst, ts.at[s], tr.at[slot], to)

        @pl.when(to == me)
        def _():
            pltpu.make_async_copy(qpair.at[s], dst, tr.at[slot]).start()

    for kk in FAR_FIRST:
        back_block(0, kk)
    strips = [slice(e * HD, (e + 1) * HD) for e in range(16)]
    valid[...] = (column(seg, me) != 0.0).astype(F32)
    early[...] = jnp.zeros_like(early)
    for e, cut in enumerate(strips):
        early[e : e + 1, :] = gain2[:, cut]
    early[19:20, :] = jnp.broadcast_to(jnp.sum(valid[...], 0, keepdims=True) * 16.0, (1, HD))

    def layer_rows(i, carry):
        rows = pl.ds(pl.multiple_of(i * 16, 16), 16)
        layer = tok[rows].astype(F32) + att[rows] + mix[rows]
        layer_o[rows] = layer.astype(BF)
        for e, field in enumerate((layer, att[rows], mix[rows])):
            square = field * field * valid[rows]
            early[16 + e : 17 + e, :] += jnp.sum(sum(square[:, cut] for cut in strips), 0, keepdims=True)
        return carry

    lax.fori_loop(0, HD // 16, layer_rows, 0)
    others = [lax.rem(me + d, 16) for d in range(1, 16)]
    sends = [push(early, early_got.at[me], es.at[d + 1], er.at[d + 1], to) for d, to in enumerate(others)]
    early_got[me] = early[...]
    for kk in FAR_FIRST:
        sn.along(kk)
    fc = []
    for s in range(3):
        here = qkv_t.at[pl.ds(pl.multiple_of(s * HD + core * hr, hr), hr)]
        pltpu.make_async_copy(here, here, tr.at[s]).wait()
        fc.append(push_pair(here, here, fs.at[s], fr.at[s]))
    sn.end()
    for s in range(3):

        @pl.when((16 * s + me) // 3 != me)
        def _():
            pltpu.make_async_copy(qpair.at[s], qpair.at[s], ts.at[s]).wait()

    gsum[...] = jnp.zeros_like(gsum)

    def norm_rows(i, carry):
        rows = pl.ds(pl.multiple_of(i * 16, 16), 16)
        pull, gains = rmsnorm_pull(tok[rows].astype(F32), gain1[...], ngrad[rows])
        tok_g[rows] = mg[rows] + pull
        gsum[...] += jnp.sum(gains, 0, keepdims=True)
        return carry

    lax.fori_loop(0, HD // 16, norm_rows, 0)
    for e, cut in enumerate(strips):
        late[e : e + 1, :] = gsum[:, cut]
    sends += [push(late, late_got.at[me], hs.at[d + 1], hr_.at[d + 1], to) for d, to in enumerate(others)]
    late_got[me] = late[...]
    for c in sends:
        c.wait_recv()

    def over_devices(got):
        total = got[0]
        for e in range(1, 16):
            total = total + got[e]
        return total

    both[:16, :] = over_devices(late_got)
    first = over_devices(early_got)
    both[16:, :] = first[:16]
    stat_o[...] = first[16:]
    across = push_pair(both, both_got, bs, br)
    across.wait()
    gain_o[...] = both[...] + both_got[...]
    for c in sends:
        c.wait_send()
    keep.wait()
    give.wait()
    for c in qc:
        c.wait_send()
    for c in fc:
        c.wait()


def back(cgh, q, k, v, seg, sk, lse, cosf, sinf, wh, nall, ag, ctx, tok, att, mix, mg, gain1, gain2, cid):
    rows, width = ag.shape
    seq = q.shape[0]
    vb = lambda *shape: pltpu.VMEM(shape, BF)
    vf = lambda *shape: pltpu.VMEM(shape, F32)
    sem = lambda *shape: pltpu.SemaphoreType.DMA(shape) if shape else pltpu.SemaphoreType.DMA
    return pl.pallas_call(
        back_kernel,
        out_shape=[
            jax.ShapeDtypeStruct((rows, width), BF),
            jax.ShapeDtypeStruct((rows, width), F32),
            jax.ShapeDtypeStruct((8, HD), F32),
            jax.ShapeDtypeStruct((32, HD), F32),
            jax.ShapeDtypeStruct((rows, width), BF),
            jax.ShapeDtypeStruct((3 * HD, width), BF),
        ],
        in_specs=[VM] * 10 + [ANY] + [VM] * 8,
        out_specs=[VM] * 4 + [ANY, ANY],
        scratch_shapes=[
            vf(rows, width), vf(rows, 1), vf(1, width), vf(24, HD), vf(16, HD), vf(16, 24, HD), vf(16, 16, HD),
            vf(32, HD), vf(32, HD), sem(16), sem(16), sem(16), sem(16), sem(), sem(),
            vf(HD, seq), vf(HD, seq), vb(seq, 3 * HD), vb(3 * HD, seq),
            vb(16, rows // 2, width), vf(rows // 2, width), vb(rows // 2, width),
        ]
        + plain_bufs(rows // 2, width)
        + [vb(16, rows, width)]
        + plain_bufs(rows, width)
        + [vb(2, seq, 256), vb(3 * HD, width), vb(3, HD // 2, width)]
        + [sem(), sem(4), sem(4), sem(), sem(), sem(2), sem(3), sem(3), sem(3), sem(3), sem(3), sem(3)]
        + SCATTER_SEMS * 2,
        compiler_params=params(cid, 62),
        name="back",
    )(cgh, q, k, v, seg, sk, lse, cosf, sinf, wh, nall, ag, ctx, tok, att, mix, mg, gain1, gain2)


def rotary_tables(length):
    freq = (THETA ** (-(np.arange(HD // 2) * 2.0 / HD))).astype(np.float32)
    angle = (np.arange(length, dtype=np.float32)[:, None] * freq[None, :]).astype(np.float64)
    cos, sin = np.cos(angle).astype(np.float32), np.sin(angle).astype(np.float32)
    return np.concatenate([cos, cos], 1), np.concatenate([-sin, sin], 1)


def per_device(
    tokens, segments, routes, route_weight, capacity, norm_gain,
    qkv_weight, out_weight, gate_weight, up_weight, down_weight, cotangent,
):
    rows, width = tokens.shape
    seq = segments.shape[0]
    gain1_row, gain2_row = norm_gain[:1], norm_gain[1:]
    meta = jnp.concatenate([routes.astype(F32).T, route_weight.T], 0)
    seg = segments.astype(F32).reshape(16, rows)
    sk = jnp.where(segments == 0, -1.0, segments.astype(F32))[None, :]
    cos_table, sin_table = rotary_tables(seq)
    normed_all, meta_all, w_head, q, k, v, lse, context, dense_out = front(
        tokens, gain1_row, meta, qkv_weight, out_weight, cos_table, sin_table, seg, sk, 0
    )
    attended, n2g, mix_part, xr, pg, hidden, gg, ug = expert(
        context, dense_out, tokens, gain2_row, cotangent, meta_all, capacity,
        gate_weight[0], up_weight[0], down_weight[0], 3,
    )
    flat = lambda a: a.reshape(-1, a.shape[2])
    mixture, gate_g, up_g, down_g, attended_grad, middle_grad, gain2, cgh = expert_weights(
        mix_part, flat(xr), flat(pg), flat(hidden), flat(gg), flat(ug), flat(dense_out),
        n2g, tokens, attended, cotangent, gain2_row, 5,
    )
    layer_out, tokens_grad, stat_lanes, gain_pair, out_total, qkv_total = back(
        cgh, q, k, v, seg, sk, lse, cos_table, sin_table, w_head, flat(normed_all), attended_grad, context,
        tokens, attended, mixture, middle_grad, gain1_row, gain2, 6,
    )
    seq_sums = jnp.sum(stat_lanes, 1)
    gain_pair = gain_pair.reshape(2, width)
    stat_row = jnp.sqrt(seq_sums[:3] / seq_sums[3]).reshape(1, 3)
    groups = lax.axis_size("grp")
    over = lambda a: a.astype(F32) if groups == 2 else lax.psum(a.astype(BF), "grp").astype(F32) * 0.5
    return (
        layer_out,
        tokens_grad,
        over(qkv_total),
        over(out_total),
        over(gate_g)[None],
        over(up_g)[None],
        over(down_g)[None],
        gain_pair if groups == 2 else lax.psum(gain_pair, "grp") * 0.5,
        stat_row,
    )


def solution(mesh):
    both = ("grp", "dp")
    in_specs = (
        P(both, None), P("grp"), P(both, None), P(both, None), P(), P(),
        P("dp", None), P("dp", None), P("dp", None, None), P("dp", None, None), P("dp", None, None),
        P(both, None),
    )
    out_specs = (
        P(both, None), P(both, None), P("dp", None), P("dp", None),
        P("dp", None, None), P("dp", None, None), P("dp", None, None), P(), P("grp", None),
    )
    return jax.shard_map(per_device, mesh=mesh, in_specs=in_specs, out_specs=out_specs, check_vma=False)
```
